32 devices in a mesh: groups: 2 (over y), tile: 4 (over z), sub: 4 (over x, core).
Axes of the slice: x: 2, y: 2, z: 4, core: 2. Of those that a mesh axis runs over, the one named last changes fastest.
Arguments:
- embeddings: bfloat16 [16384, 1024], P(('groups', 'tile')), parts along dimension 0, may hold values from -12 to 12
- cluster_ids: int32 [16384], P(('groups', 'tile')), parts along dimension 0, may hold values from -1 to 1, as said below
Outputs:
- scores: float32 [16384], P(('groups', 'tile', 'sub')), parts along dimension 0
The draws below stay inside these ranges and needn't reach their ends.
There are 2 independent parts, one for each index of `groups`. The reference program is written for one: setup_inputs(seed, part) draws one part's arguments, and reference() takes and returns one part's arrays. A program takes and returns all parts, laid end to end along the dimension named above; each array names one. Nothing has to cross between parts.
Inputs may be any that keep to these rules, and one draw needn't show every extreme that they name: `cluster_ids`: each cluster occupies consecutive whole blocks of 128 rows in increasing order of cluster number, every cluster from 0 to 1 present; inside a cluster's last block the unused rows at its end are -1, and only there. The rows of one cluster lie on at most 4 consecutive indices of tile.
All inputs are finite; a program needn't handle non-finite values.
Results may differ from the reference program's by a relative error of at most 0.00087.
Values may be sent and summed in bfloat16 or wider, within the bound.
No kernel may reach another device: no remote copies, remote signals or barrier semaphores. Data moves between devices by JAX's collectives and lax.ppermute only.
A program may use at most 128 MiB of HBM per device.

```python
import jax
import jax.numpy as jnp
from jax import lax

E = 1024
BLOCK = 128
BLK_DEV = 16
ROWS = 8192
CLUSTERS = 2
CLUSTER_MAX = 6144


near_count = 1024


def cluster_layout(key):
    half = BLK_DEV // 2
    shifts = jax.random.randint(jax.random.fold_in(key, 11), (CLUSTERS - 1,), -half, half + 1)
    shifts = shifts.at[0].set(-half)
    if CLUSTERS >= 3:
        shifts = shifts.at[1].set(half)
    bounds = 2 * BLK_DEV * jnp.arange(1, CLUSTERS, dtype=jnp.int32) + shifts.astype(jnp.int32)
    used = jax.random.randint(jax.random.fold_in(key, 12), (CLUSTERS,), 1, BLOCK + 1)
    blocks = jnp.arange(ROWS, dtype=jnp.int32) // BLOCK
    inside = jnp.arange(ROWS, dtype=jnp.int32) % BLOCK
    cluster = jnp.sum((blocks[:, None] >= bounds[None, :]).astype(jnp.int32), axis=1)
    last_block = jnp.concatenate([bounds - 1, jnp.full((1,), ROWS // BLOCK - 1, jnp.int32)])
    padding = (blocks == last_block[cluster]) & (inside >= used[cluster])
    return jnp.where(padding, -1, cluster).astype(jnp.int32)


def log_between(key, shape, low, high):
    return jnp.exp(jax.random.uniform(key, shape, jnp.float32, jnp.log(low), jnp.log(high)))


def draw_cluster_ids(key, part):
    return cluster_layout(key)


def draw_embeddings(key, part):
    ids = cluster_layout(key)
    key = jax.random.fold_in(key, 5)
    centers = jax.random.normal(jax.random.fold_in(key, 1), (CLUSTERS + 1, E), jnp.float32)
    near_centers = jax.random.normal(jax.random.fold_in(key, 7), ((CLUSTERS + 1) * near_count, E), jnp.float32)
    noise = jax.random.normal(jax.random.fold_in(key, 2), (ROWS, E), jnp.float32)
    first = jax.random.randint(jax.random.fold_in(key, 8), (ROWS,), 0, near_count)
    second = jax.random.randint(jax.random.fold_in(key, 9), (ROWS,), 0, near_count)
    near_group = jnp.minimum(first, second).astype(jnp.int32)
    background = jax.random.randint(jax.random.fold_in(key, 10), (ROWS,), 0, 10) < 3
    near_index = (ids + 1) * near_count + near_group
    near_amp = log_between(jax.random.fold_in(key, 3), (ROWS,), 0.2, 1.0)
    far_amp = log_between(jax.random.fold_in(key, 11), (ROWS,), 0.2, 2.5)
    share = jax.random.uniform(jax.random.fold_in(key, 12), (ROWS,), jnp.float32, 0.8, 1.2)
    spread = log_between(jax.random.fold_in(key, 13), (ROWS,), 0.05, 0.3)
    near_values = near_amp[:, None] * centers[ids + 1] + share[:, None] * near_centers[near_index] + spread[:, None] * noise
    far_values = far_amp[:, None] * centers[ids + 1] + noise
    values = jnp.where(background[:, None], far_values, near_values)
    return jnp.clip(values, -12.0, 12.0).astype(jnp.bfloat16)


def setup_inputs(seed: int = 0, part: int = 0) -> dict:
    key_list = jax.random.split(jax.random.key(seed), 3)
    part_keys = jax.random.split(jax.random.fold_in(key_list[2], part), 3)
    embeddings = draw_embeddings(jax.random.fold_in(jax.random.fold_in(key_list[2], part), 71), part)
    cluster_ids = draw_cluster_ids(jax.random.fold_in(jax.random.fold_in(key_list[2], part), 71), part)
    return {"embeddings": embeddings, "cluster_ids": cluster_ids}


inverse_temp = 10.0
norm_eps = 1e-06

def reference(embeddings, cluster_ids):
    values = embeddings.astype(jnp.float32)
    scale = lax.rsqrt(lax.optimization_barrier(jnp.sum(values * values, axis=1, keepdims=True)) + norm_eps)
    rounded = lax.optimization_barrier((values * scale).astype(jnp.bfloat16))
    unit = rounded.astype(jnp.float32)
    padded_unit = jnp.concatenate([unit, jnp.zeros((CLUSTER_MAX, E), jnp.float32)], axis=0)
    padded_ids = jnp.concatenate([cluster_ids.astype(jnp.int32), jnp.full((CLUSTER_MAX,), -1, jnp.int32)], axis=0)
    positions = jnp.arange(ROWS, dtype=jnp.int32)
    not_self = ~jnp.eye(CLUSTER_MAX, dtype=bool)

    def one_cluster(cluster, total):
        cluster = jnp.asarray(cluster).astype(jnp.int32)
        start = jnp.min(jnp.where(cluster_ids.astype(jnp.int32) == cluster, positions, ROWS)).astype(jnp.int32)
        window = lax.dynamic_slice_in_dim(padded_unit, start, CLUSTER_MAX, 0)
        window_ids = lax.dynamic_slice_in_dim(padded_ids, start, CLUSTER_MAX, 0)
        member = window_ids == cluster
        cosine = jnp.dot(window, window.T, precision=lax.Precision.HIGHEST)
        keep = member[:, None] & member[None, :] & not_self
        weight = jnp.where(keep, jnp.exp(inverse_temp * (cosine - 1.0)), 0.0)
        current = lax.dynamic_slice_in_dim(total, start, CLUSTER_MAX, 0)
        return lax.dynamic_update_slice_in_dim(total, current + lax.optimization_barrier(jnp.sum(weight, axis=1)), start, 0)
    total = lax.fori_loop(0, CLUSTERS, one_cluster, jnp.zeros((ROWS + CLUSTER_MAX,), jnp.float32))
    return jnp.log(1.0 + total[:ROWS])
```

```python
import functools
import math

import jax
import jax.numpy as jnp
import numpy as np
from jax import lax
from jax.experimental import pallas as pl
from jax.experimental.pallas import tpu as pltpu
from jax.sharding import PartitionSpec as P

BLOCK = 128
QUAD = 4
SPAN = 4

inverse_temp = 10.0
norm_eps = 1e-06
GAIN = inverse_temp * math.log2(math.e)
OFF = -1000.0

STEP = 512
SUBSTEP = 256


def normalised(values):
    values = values.astype(jnp.float32)
    scale = lax.rsqrt(jnp.sum(values * values, axis=1, keepdims=True) + norm_eps)
    return (values * scale).astype(jnp.bfloat16)


def products(rows, columns):
    return lax.dot_general(
        rows, columns, (((1,), (1,)), ((), ())), preferred_element_type=jnp.float32
    )


def column_bias(tag, col_tags, col_valid):
    lane = lax.broadcasted_iota(jnp.int32, (1, BLOCK), 1)
    parts = []
    for ctag, cvalid in zip(col_tags, col_valid):
        count = jnp.where((ctag == tag) & (tag >= 0), cvalid, 0)
        parts.append(jnp.where(lane < count, -GAIN, OFF))
    return jnp.concatenate(parts, axis=1) if len(parts) > 1 else parts[0]


def lane_sums(weight):
    total = weight[:, :BLOCK]
    for start in range(BLOCK, weight.shape[1], BLOCK):
        total = total + weight[:, start : start + BLOCK]
    return jnp.sum(total.T, axis=0, keepdims=True)


def self_kernel(blocks, width, meta, rows_ref, piece_ref, unit_ref, sums_ref, piece_unit):
    step = pl.program_id(0)

    @pl.when(step == 0)
    def _():
        for start in range(0, width * BLOCK, BLOCK):
            piece_unit[pl.ds(start, BLOCK), :] = normalised(piece_ref[pl.ds(start, BLOCK), :])

    first_col = meta[2 * blocks] * width
    per_step = STEP // BLOCK
    for part in range(STEP // SUBSTEP):
        unit = normalised(rows_ref[pl.ds(part * SUBSTEP, SUBSTEP), :])
        unit_ref[pl.ds(part * SUBSTEP, SUBSTEP), :] = unit
        cosine = products(unit, piece_unit[...])
        for half in range(SUBSTEP // BLOCK):
            local = part * (SUBSTEP // BLOCK) + half
            block = step * per_step + local
            bias = column_bias(
                meta[block],
                [meta[first_col + k] for k in range(width)],
                [meta[blocks + first_col + k] for k in range(width)],
            )
            weight = jnp.exp2(cosine[half * BLOCK : (half + 1) * BLOCK] * GAIN + bias)
            row = lax.broadcasted_iota(jnp.int32, weight.shape, 0)
            col = lax.broadcasted_iota(jnp.int32, weight.shape, 1)
            shift = (block - first_col) * BLOCK
            weight = jnp.where((row < meta[blocks + block]) & (col - row != shift), weight, 0.0)
            sums_ref[pl.ds(block, 1), :] = lane_sums(weight)


def cross_terms(count, blocks, share, step, meta, base, unit_ref, piece_unit, row_sums, col_sums):
    per_step = STEP // BLOCK
    stride = blocks + 2 * share
    for part in range(STEP // SUBSTEP):
        cosine = products(unit_ref[pl.ds(part * SUBSTEP, SUBSTEP), :], piece_unit[...])
        for half in range(SUBSTEP // BLOCK):
            block = step * per_step + part * (SUBSTEP // BLOCK) + half
            biases = []
            for chunk in range(count):
                at = base + chunk * stride
                biases.append(
                    column_bias(
                        meta[at + block],
                        [meta[at + blocks + k] for k in range(share)],
                        [meta[at + blocks + share + k] for k in range(share)],
                    )
                )
            bias = jnp.concatenate(biases, axis=1) if count > 1 else biases[0]
            weight = jnp.exp2(cosine[half * BLOCK : (half + 1) * BLOCK] * GAIN + bias)
            row = lax.broadcasted_iota(jnp.int32, weight.shape, 0)
            weight = jnp.where(row < meta[block], weight, 0.0)
            row_sums[pl.ds(block, 1), :] = lane_sums(weight)
            partial = weight[0:8]
            for start in range(8, BLOCK, 8):
                partial = partial + weight[start : start + 8]
            col_sums[...] += partial


def first_kernel(blocks, share, meta, unit_ref, piece_ref, before_ref, sums_ref, cols_ref, piece_unit, rows, cols):
    step = pl.program_id(0)

    @pl.when(step == 0)
    def _():
        for start in range(0, share * BLOCK, BLOCK):
            piece_unit[pl.ds(start, BLOCK), :] = normalised(piece_ref[pl.ds(start, BLOCK), :])
        cols[...] = jnp.zeros_like(cols)

    cross_terms(1, blocks, share, step, meta, blocks, unit_ref, piece_unit, rows, cols)

    @pl.when(step == pl.num_programs(0) - 1)
    def _():
        sums_ref[...] = rows[...] + before_ref[...]
        total = jnp.sum(cols[...], axis=0, keepdims=True)
        for k in range(share):
            cols_ref[k : k + 1, :] = total[:, k * BLOCK : (k + 1) * BLOCK]


def last_kernel(
    blocks, share, meta, unit_ref, second_ref, third_ref, before_ref, first_cols_ref, extra_ref, out_ref,
    piece_unit, rows, cols,
):
    step = pl.program_id(0)
    size = share * BLOCK

    @pl.when(step == 0)
    def _():
        for start in range(0, size, BLOCK):
            piece_unit[pl.ds(start, BLOCK), :] = normalised(second_ref[pl.ds(start, BLOCK), :])
            piece_unit[pl.ds(size + start, BLOCK), :] = normalised(third_ref[pl.ds(start, BLOCK), :])
        cols[...] = jnp.zeros_like(cols)

    stride = blocks + 2 * share
    cross_terms(2, blocks, share, step, meta, blocks + stride, unit_ref, piece_unit, rows, cols)

    @pl.when(step == pl.num_programs(0) - 1)
    def _():
        tail = blocks + 3 * stride
        place, bad = meta[tail], meta[tail + 1]
        out_ref[...] = jnp.zeros_like(out_ref)
        out_ref[pl.ds(pl.multiple_of(place * blocks, 8), blocks), :] = rows[...] + before_ref[...]
        total = jnp.sum(cols[...], axis=0, keepdims=True)
        for chunk in range(3):
            for k in range(share):
                if chunk == 0:
                    value = first_cols_ref[k : k + 1, :]
                else:
                    at = ((chunk - 1) * share + k) * BLOCK
                    value = total[:, at : at + BLOCK]
                target = meta[tail + 2 + chunk] + k
                out_ref[pl.ds(target, 1), :] += value

        @pl.when(bad > 0)
        def _():
            out_ref[...] = extra_ref[...]


def whole(shape):
    return pl.BlockSpec(shape, lambda *_: (0,) * len(shape))


def call(kernel, meta, operands, in_specs, out_shapes, out_specs, scratch, grid, flops):
    return pl.pallas_call(
        kernel,
        grid_spec=pltpu.PrefetchScalarGridSpec(
            num_scalar_prefetch=1,
            grid=grid,
            in_specs=in_specs,
            out_specs=out_specs,
            scratch_shapes=scratch,
        ),
        out_shape=out_shapes,
        compiler_params=pltpu.CompilerParams(
            vmem_limit_bytes=32 * 1024 * 1024, dimension_semantics=("arbitrary",)
        ),
        cost_estimate=pl.CostEstimate(flops=flops, bytes_accessed=6 * 1024 * 1024, transcendentals=flops // 2048),
    )(meta, *operands)


def every_pair(embeddings, cluster_ids):
    unit = normalised(embeddings)
    tags = cluster_ids + 1
    groups = lax.axis_size("sub")
    member = lax.axis_index("sub")
    owners = lax.axis_size("tile")
    place = lax.axis_index("tile")
    rows_here = unit.shape[0]
    width = rows_here // groups
    own_piece = lax.dynamic_slice_in_dim(unit, member * width, width, 0)
    own_tags = lax.dynamic_slice_in_dim(tags, member * width, width, 0)
    distance = place - jnp.arange(owners, dtype=jnp.int32)
    keep = (jnp.abs(distance) < SPAN) & (distance != 0)
    outgoing = jnp.where(keep[:, None, None], own_piece[None, :, :], jnp.zeros((), jnp.bfloat16))
    outgoing_tags = jnp.where(keep[:, None], own_tags[None, :], 0)
    arrived = lax.all_to_all(outgoing, "tile", split_axis=0, concat_axis=0, tiled=True)
    arrived_tags = lax.all_to_all(outgoing_tags, "tile", split_axis=0, concat_axis=0, tiled=True)
    local_rows = jnp.arange(rows_here, dtype=jnp.int32)[:, None]
    slice_rows = member * width + jnp.arange(width, dtype=jnp.int32)[None, :]
    total = jnp.zeros((rows_here,), jnp.float32)
    for offset in range(1 - SPAN, SPAN):
        if offset == 0:
            piece, piece_tags, order = own_piece, own_tags, local_rows != slice_rows
        else:
            source = place + offset
            valid = (source >= 0) & (source < owners)
            index = jnp.clip(source, 0, owners - 1)
            piece = lax.dynamic_index_in_dim(arrived, index, 0, keepdims=False)
            piece_tags = lax.dynamic_index_in_dim(arrived_tags, index, 0, keepdims=False)
            piece_tags = jnp.where(valid, piece_tags, 0)
            order = True
        same = (tags[:, None] == piece_tags[None, :]) & (tags[:, None] > 0) & order
        weight = jnp.where(same, jnp.exp(inverse_temp * (products(unit, piece) - 1.0)), 0.0)
        total = total + jnp.sum(weight, axis=1)
    return total


def uncovered(tags, blocks):
    size = tags.shape[1]
    index = jnp.arange(size, dtype=jnp.int32)
    tile, inside = index // blocks, index % blocks
    part = tile % QUAD
    half = blocks // 2
    left, right = part[:, None], part[None, :]
    far_left = (inside < half)[:, None]
    far_right = (inside >= half)[None, :]
    missed = (
        (tile[:, None] // QUAD != tile[None, :] // QUAD)
        | ((left == 0) & (right == 3))
        | ((left == 0) & (right == 2) & far_right)
        | ((left == 1) & (right == 3) & far_left)
        | ((left == 1) & (right == 2) & far_left & far_right)
    )
    missed = missed & (tile[:, None] < tile[None, :])
    same = (tags[:, :, None] == tags[:, None, :]) & (tags[:, :, None] >= 0)
    return jnp.any(same & missed[None])


def shards(embeddings, cluster_ids):
    tiles, subs = lax.axis_size("tile"), lax.axis_size("sub")
    place, member = lax.axis_index("tile"), lax.axis_index("sub")
    rows, depth = embeddings.shape
    blocks = rows // BLOCK
    width = blocks // subs
    share = width // 2
    part = place % QUAD
    quads = range(0, tiles, QUAD)

    first_at = jnp.where(
        part == 1, blocks // 2 + member * share, jnp.where(part == 2, member * share, member * width)
    )
    second_at = member * width + share
    size = share * BLOCK
    first_out = lax.dynamic_slice_in_dim(embeddings, first_at * BLOCK, size, 0)
    second_out = lax.dynamic_slice_in_dim(embeddings, second_at * BLOCK, size, 0)
    first = lax.ppermute(
        first_out, "tile", [p for q in quads for p in ((q, q + 1), (q + 3, q + 2), (q + 1, q + 3), (q + 2, q))]
    )
    second = lax.ppermute(second_out, "tile", [p for q in quads for p in ((q, q + 1), (q + 3, q + 2))])
    third = lax.ppermute(first_out, "tile", [p for q in quads for p in ((q + 1, q + 2), (q + 2, q + 1))])

    by_block = cluster_ids.reshape(blocks, BLOCK)
    tag = jnp.max(by_block, axis=1)
    used = jnp.sum((by_block >= 0).astype(jnp.int32), axis=1)
    info = lax.all_gather(jnp.stack([tag, used]), ("groups", "tile"))
    info = info.reshape(-1, tiles, 2, blocks)
    tags_all = info[:, :, 0].reshape(-1, tiles * blocks)
    bad = uncovered(tags_all, blocks)
    mine = lax.dynamic_index_in_dim(info, lax.axis_index("groups"), 0, keepdims=False)
    group_tags = mine[:, 0].reshape(-1)
    group_used = mine[:, 1].reshape(-1)

    outer_from = jnp.where(part == 1, place - 1, place + 1)
    near_at = jnp.where(part == 1, member * share, blocks // 2 + member * share)
    inner = (part == 1) | (part == 2)
    first_from = jnp.where(
        inner,
        outer_from * blocks + member * width,
        jnp.where(part == 3, (place - 2) * blocks + blocks // 2, (place + 2) * blocks) + member * share,
    )
    second_from = jnp.where(inner, outer_from * blocks + second_at, 0)
    third_from = jnp.where(inner, jnp.where(part == 1, place + 1, place - 1) * blocks + near_at, 0)
    own_block = jnp.arange(blocks, dtype=jnp.int32)
    far = (part == 1) & (own_block >= blocks // 2)

    def chunk_meta(start, valid, own_tags):
        ctag = lax.dynamic_slice_in_dim(group_tags, start, share, 0)
        cused = lax.dynamic_slice_in_dim(group_used, start, share, 0)
        return [jnp.where(valid, own_tags, -1), ctag, cused]

    meta = jnp.concatenate(
        [used]
        + chunk_meta(first_from, True, tag)
        + chunk_meta(second_from, inner, tag)
        + chunk_meta(third_from, inner, jnp.where(far, -1, tag))
        + [jnp.stack([place, bad.astype(jnp.int32), first_from, second_from, third_from]).astype(jnp.int32)]
    )
    own_meta = jnp.concatenate([tag, used, member[None]]).astype(jnp.int32)

    extra = lax.cond(
        bad,
        lambda: lax.dynamic_update_slice(
            jnp.zeros((tiles * rows,), jnp.float32), every_pair(embeddings, cluster_ids), (place * rows,)
        ),
        lambda: jnp.zeros((tiles * rows,), jnp.float32),
    ).reshape(tiles * blocks, BLOCK)

    grid = (rows // STEP,)
    step_rows = pl.BlockSpec((STEP, depth), lambda i, _: (i, 0))
    row_sums = jax.ShapeDtypeStruct((blocks, BLOCK), jnp.float32)
    unit, own_sums = call(
        functools.partial(self_kernel, blocks, width),
        own_meta,
        (embeddings, embeddings),
        [step_rows, pl.BlockSpec((width * BLOCK, depth), lambda i, m: (m[2 * blocks], 0))],
        [jax.ShapeDtypeStruct((rows, depth), jnp.bfloat16), row_sums],
        [step_rows, whole((blocks, BLOCK))],
        [pltpu.VMEM((width * BLOCK, depth), jnp.bfloat16)],
        grid,
        2 * rows * width * BLOCK * depth,
    )
    sums, first_cols = call(
        functools.partial(first_kernel, blocks, share),
        meta,
        (unit, first, own_sums),
        [step_rows, whole((size, depth)), whole((blocks, BLOCK))],
        [row_sums, jax.ShapeDtypeStruct((share, BLOCK), jnp.float32)],
        [whole((blocks, BLOCK)), whole((share, BLOCK))],
        [
            pltpu.VMEM((size, depth), jnp.bfloat16),
            pltpu.VMEM((blocks, BLOCK), jnp.float32),
            pltpu.VMEM((8, size), jnp.float32),
        ],
        grid,
        2 * rows * size * depth,
    )
    partial = call(
        functools.partial(last_kernel, blocks, share),
        meta,
        (unit, second, third, sums, first_cols, extra),
        [
            step_rows,
            whole((size, depth)),
            whole((size, depth)),
            whole((blocks, BLOCK)),
            whole((share, BLOCK)),
            whole((tiles * blocks, BLOCK)),
        ],
        jax.ShapeDtypeStruct((tiles * blocks, BLOCK), jnp.float32),
        whole((tiles * blocks, BLOCK)),
        [
            pltpu.VMEM((2 * size, depth), jnp.bfloat16),
            pltpu.VMEM((blocks, BLOCK), jnp.float32),
            pltpu.VMEM((8, 2 * size), jnp.float32),
        ],
        grid,
        4 * rows * size * depth,
    )
    density = lax.psum_scatter(partial.reshape(-1), ("tile", "sub"), scatter_dimension=0, tiled=True)
    return jnp.log(1.0 + density)


def solution(mesh):
    in_specs = (P(("groups", "tile"), None), P(("groups", "tile")))
    out_specs = P(("groups", "tile", "sub"))
    return jax.shard_map(shards, mesh=mesh, in_specs=in_specs, out_specs=out_specs, check_vma=False)
```

```python
import functools
import math

import jax
import jax.numpy as jnp
import numpy as np
from jax import lax
from jax.experimental import pallas as pl
from jax.experimental.pallas import tpu as pltpu
from jax.sharding import PartitionSpec as P

BLOCK = 128
QUAD = 4
SPAN = 4

inverse_temp = 10.0
norm_eps = 1e-06
GAIN = inverse_temp * math.log2(math.e)
OFF = -1000.0

STEP = 512


def normalised(values):
    values = values.astype(jnp.float32)
    scale = lax.rsqrt(jnp.sum(values * values, axis=1, keepdims=True) + norm_eps)
    return (values * scale).astype(jnp.bfloat16)


def products(rows, columns):
    return lax.dot_general(
        rows, columns, (((1,), (1,)), ((), ())), preferred_element_type=jnp.float32
    )


def column_bias(tag, col_tags, col_valid):
    lane = lax.broadcasted_iota(jnp.int32, (1, BLOCK), 1)
    parts = []
    for ctag, cvalid in zip(col_tags, col_valid):
        count = jnp.where((ctag == tag) & (tag >= 0), cvalid, 0)
        parts.append(jnp.where(lane < count, -GAIN, OFF))
    return jnp.concatenate(parts, axis=1) if len(parts) > 1 else parts[0]


def lane_sums(weight):
    total = weight[:, :BLOCK]
    for start in range(BLOCK, weight.shape[1], BLOCK):
        total = total + weight[:, start : start + BLOCK]
    return jnp.sum(total.T, axis=0, keepdims=True)


def self_kernel(blocks, width, meta, rows_ref, unit_ref, sums_ref):
    for start in range(0, blocks * BLOCK, STEP):
        unit_ref[start : start + STEP, :] = normalised(rows_ref[start : start + STEP, :])
    first_col = meta[2 * blocks] * width
    share = unit_ref[pl.ds(pl.multiple_of(first_col * BLOCK, width * BLOCK), width * BLOCK), :]
    col_tags = [meta[first_col + k] for k in range(width)]
    col_used = [meta[blocks + first_col + k] for k in range(width)]
    for start in range(0, blocks * BLOCK, STEP):
        cosine = products(unit_ref[start : start + STEP, :], share)
        for inner in range(0, STEP, BLOCK):
            block = (start + inner) // BLOCK
            bias = column_bias(meta[block], col_tags, col_used)
            weight = jnp.exp2(cosine[inner : inner + BLOCK] * GAIN + bias)
            row = lax.broadcasted_iota(jnp.int32, weight.shape, 0)
            col = lax.broadcasted_iota(jnp.int32, weight.shape, 1)
            shift = (block - first_col) * BLOCK
            weight = jnp.where((row < meta[blocks + block]) & (col - row != shift), weight, 0.0)
            sums_ref[block : block + 1, :] = lane_sums(weight)


def cross_terms(count, blocks, share, meta, base, unit_ref, piece_unit, row_sums):
    stride = blocks + 2 * share
    columns = None
    for start in range(0, blocks * BLOCK, STEP):
        cosine = products(unit_ref[start : start + STEP, :], piece_unit[...])
        for inner in range(0, STEP, BLOCK):
            block = (start + inner) // BLOCK
            biases = []
            for chunk in range(count):
                at = base + chunk * stride
                biases.append(
                    column_bias(
                        meta[at + block],
                        [meta[at + blocks + k] for k in range(share)],
                        [meta[at + blocks + share + k] for k in range(share)],
                    )
                )
            bias = jnp.concatenate(biases, axis=1) if count > 1 else biases[0]
            weight = jnp.exp2(cosine[inner : inner + BLOCK] * GAIN + bias)
            row = lax.broadcasted_iota(jnp.int32, weight.shape, 0)
            weight = jnp.where(row < meta[block], weight, 0.0)
            row_sums(block, lane_sums(weight))
            partial = weight[0:8]
            for at in range(8, BLOCK, 8):
                partial = partial + weight[at : at + 8]
            columns = partial if columns is None else columns + partial
    return jnp.sum(columns, axis=0, keepdims=True)


def first_kernel(blocks, share, meta, unit_ref, piece_ref, before_ref, sums_ref, cols_ref, piece_unit):
    piece_unit[...] = normalised(piece_ref[...])

    def row_sums(block, value):
        sums_ref[block : block + 1, :] = before_ref[block : block + 1, :] + value

    total = cross_terms(1, blocks, share, meta, blocks, unit_ref, piece_unit, row_sums)
    for k in range(share):
        cols_ref[k : k + 1, :] = total[:, k * BLOCK : (k + 1) * BLOCK]


def last_kernel(
    blocks, share, meta, unit_ref, second_ref, third_ref, before_ref, first_cols_ref, extra_ref, out_ref, piece_unit
):
    size = share * BLOCK
    piece_unit[:size, :] = normalised(second_ref[...])
    piece_unit[size:, :] = normalised(third_ref[...])
    stride = blocks + 2 * share
    tail = blocks + 3 * stride
    place, bad = meta[tail], meta[tail + 1]
    out_ref[...] = jnp.zeros_like(out_ref)

    def row_sums(block, value):
        out_ref[pl.ds(place * blocks + block, 1), :] = before_ref[block : block + 1, :] + value

    total = cross_terms(2, blocks, share, meta, blocks + stride, unit_ref, piece_unit, row_sums)
    for chunk in range(3):
        for k in range(share):
            if chunk == 0:
                value = first_cols_ref[k : k + 1, :]
            else:
                at = ((chunk - 1) * share + k) * BLOCK
                value = total[:, at : at + BLOCK]
            out_ref[pl.ds(meta[tail + 2 + chunk] + k, 1), :] += value

    @pl.when(bad > 0)
    def _():
        out_ref[...] = extra_ref[...]


def call(kernel, meta, operands, out_shapes, scratch, flops):
    vmem = pl.BlockSpec(memory_space=pltpu.VMEM)
    return pl.pallas_call(
        kernel,
        in_specs=[pl.BlockSpec(memory_space=pltpu.SMEM)] + [vmem] * len(operands),
        out_specs=jax.tree.map(lambda _: vmem, out_shapes),
        out_shape=out_shapes,
        scratch_shapes=scratch,
        compiler_params=pltpu.CompilerParams(vmem_limit_bytes=40 * 1024 * 1024),
        cost_estimate=pl.CostEstimate(flops=flops, bytes_accessed=1024 * 1024, transcendentals=flops // 2048),
    )(meta, *operands)


def every_pair(embeddings, cluster_ids):
    unit = normalised(embeddings)
    tags = cluster_ids + 1
    groups = lax.axis_size("sub")
    member = lax.axis_index("sub")
    owners = lax.axis_size("tile")
    place = lax.axis_index("tile")
    rows_here = unit.shape[0]
    width = rows_here // groups
    own_piece = lax.dynamic_slice_in_dim(unit, member * width, width, 0)
    own_tags = lax.dynamic_slice_in_dim(tags, member * width, width, 0)
    distance = place - jnp.arange(owners, dtype=jnp.int32)
    keep = (jnp.abs(distance) < SPAN) & (distance != 0)
    outgoing = jnp.where(keep[:, None, None], own_piece[None, :, :], jnp.zeros((), jnp.bfloat16))
    outgoing_tags = jnp.where(keep[:, None], own_tags[None, :], 0)
    arrived = lax.all_to_all(outgoing, "tile", split_axis=0, concat_axis=0, tiled=True)
    arrived_tags = lax.all_to_all(outgoing_tags, "tile", split_axis=0, concat_axis=0, tiled=True)
    local_rows = jnp.arange(rows_here, dtype=jnp.int32)[:, None]
    slice_rows = member * width + jnp.arange(width, dtype=jnp.int32)[None, :]
    total = jnp.zeros((rows_here,), jnp.float32)
    for offset in range(1 - SPAN, SPAN):
        if offset == 0:
            piece, piece_tags, order = own_piece, own_tags, local_rows != slice_rows
        else:
            source = place + offset
            valid = (source >= 0) & (source < owners)
            index = jnp.clip(source, 0, owners - 1)
            piece = lax.dynamic_index_in_dim(arrived, index, 0, keepdims=False)
            piece_tags = lax.dynamic_index_in_dim(arrived_tags, index, 0, keepdims=False)
            piece_tags = jnp.where(valid, piece_tags, 0)
            order = True
        same = (tags[:, None] == piece_tags[None, :]) & (tags[:, None] > 0) & order
        weight = jnp.where(same, jnp.exp(inverse_temp * (products(unit, piece) - 1.0)), 0.0)
        total = total + jnp.sum(weight, axis=1)
    return total


def uncovered(tags, blocks):
    size = tags.shape[1]
    index = jnp.arange(size, dtype=jnp.int32)
    tile, inside = index // blocks, index % blocks
    part = tile % QUAD
    half = blocks // 2
    left, right = part[:, None], part[None, :]
    far_left = (inside < half)[:, None]
    far_right = (inside >= half)[None, :]
    missed = (
        (tile[:, None] // QUAD != tile[None, :] // QUAD)
        | ((left == 0) & (right == 3))
        | ((left == 0) & (right == 2) & far_right)
        | ((left == 1) & (right == 3) & far_left)
        | ((left == 1) & (right == 2) & far_left & far_right)
    )
    missed = missed & (tile[:, None] < tile[None, :])
    same = (tags[:, :, None] == tags[:, None, :]) & (tags[:, :, None] >= 0)
    return jnp.any(same & missed[None])


def shards(embeddings, cluster_ids):
    tiles, subs = lax.axis_size("tile"), lax.axis_size("sub")
    place, member = lax.axis_index("tile"), lax.axis_index("sub")
    rows, depth = embeddings.shape
    blocks = rows // BLOCK
    width = blocks // subs
    share = width // 2
    part = place % QUAD
    quads = range(0, tiles, QUAD)

    first_at = jnp.where(
        part == 1, blocks // 2 + member * share, jnp.where(part == 2, member * share, member * width)
    )
    second_at = member * width + share
    size = share * BLOCK
    first_out = lax.dynamic_slice_in_dim(embeddings, first_at * BLOCK, size, 0)
    second_out = lax.dynamic_slice_in_dim(embeddings, second_at * BLOCK, size, 0)
    first = lax.ppermute(
        first_out, "tile", [p for q in quads for p in ((q, q + 1), (q + 3, q + 2), (q + 1, q + 3), (q + 2, q))]
    )
    second = lax.ppermute(second_out, "tile", [p for q in quads for p in ((q, q + 1), (q + 3, q + 2))])
    third = lax.ppermute(first_out, "tile", [p for q in quads for p in ((q + 1, q + 2), (q + 2, q + 1))])

    count = lax.axis_size("groups") * tiles
    everyone = lax.all_to_all(
        jnp.broadcast_to(cluster_ids[None], (count, rows)), ("groups", "tile"), split_axis=0, concat_axis=0, tiled=True
    ).reshape(count, blocks, BLOCK)
    info = jnp.stack([jnp.max(everyone, axis=2), jnp.sum((everyone >= 0).astype(jnp.int32), axis=2)], axis=1)
    info = info.reshape(-1, tiles, 2, blocks)
    by_block = cluster_ids.reshape(blocks, BLOCK)
    tag = jnp.max(by_block, axis=1)
    used = jnp.sum((by_block >= 0).astype(jnp.int32), axis=1)
    tags_all = info[:, :, 0].reshape(-1, tiles * blocks)
    bad = uncovered(tags_all, blocks)
    mine = lax.dynamic_index_in_dim(info, lax.axis_index("groups"), 0, keepdims=False)
    group_tags = mine[:, 0].reshape(-1)
    group_used = mine[:, 1].reshape(-1)

    outer_from = jnp.where(part == 1, place - 1, place + 1)
    near_at = jnp.where(part == 1, member * share, blocks // 2 + member * share)
    inner = (part == 1) | (part == 2)
    first_from = jnp.where(
        inner,
        outer_from * blocks + member * width,
        jnp.where(part == 3, (place - 2) * blocks + blocks // 2, (place + 2) * blocks) + member * share,
    )
    second_from = jnp.where(inner, outer_from * blocks + second_at, 0)
    third_from = jnp.where(inner, jnp.where(part == 1, place + 1, place - 1) * blocks + near_at, 0)
    own_block = jnp.arange(blocks, dtype=jnp.int32)
    far = (part == 1) & (own_block >= blocks // 2)

    def chunk_meta(start, valid, own_tags):
        ctag = lax.dynamic_slice_in_dim(group_tags, start, share, 0)
        cused = lax.dynamic_slice_in_dim(group_used, start, share, 0)
        return [jnp.where(valid, own_tags, -1), ctag, cused]

    meta = jnp.concatenate(
        [used]
        + chunk_meta(first_from, True, tag)
        + chunk_meta(second_from, inner, tag)
        + chunk_meta(third_from, inner, jnp.where(far, -1, tag))
        + [jnp.stack([place, bad.astype(jnp.int32), first_from, second_from, third_from]).astype(jnp.int32)]
    )
    own_meta = jnp.concatenate([tag, used, member[None]]).astype(jnp.int32)

    extra = lax.cond(
        bad,
        lambda: lax.dynamic_update_slice(
            jnp.zeros((tiles * rows,), jnp.float32), every_pair(embeddings, cluster_ids), (place * rows,)
        ),
        lambda: jnp.zeros((tiles * rows,), jnp.float32),
    ).reshape(tiles * blocks, BLOCK)

    row_sums = jax.ShapeDtypeStruct((blocks, BLOCK), jnp.float32)
    unit, own_sums = call(
        functools.partial(self_kernel, blocks, width),
        own_meta,
        (embeddings,),
        [jax.ShapeDtypeStruct((rows, depth), jnp.bfloat16), row_sums],
        [],
        2 * rows * width * BLOCK * depth,
    )
    sums, first_cols = call(
        functools.partial(first_kernel, blocks, share),
        meta,
        (unit, first, own_sums),
        [row_sums, jax.ShapeDtypeStruct((share, BLOCK), jnp.float32)],
        [pltpu.VMEM((size, depth), jnp.bfloat16)],
        2 * rows * size * depth,
    )
    partial = call(
        functools.partial(last_kernel, blocks, share),
        meta,
        (unit, second, third, sums, first_cols, extra),
        jax.ShapeDtypeStruct((tiles * blocks, BLOCK), jnp.float32),
        [pltpu.VMEM((2 * size, depth), jnp.bfloat16)],
        4 * rows * size * depth,
    )
    parts = lax.all_to_all(
        partial.reshape(tiles * subs, rows // subs), ("tile", "sub"), split_axis=0, concat_axis=0, tiled=True
    )
    return jnp.log(1.0 + jnp.sum(parts, axis=0))


def solution(mesh):
    in_specs = (P(("groups", "tile"), None), P(("groups", "tile")))
    out_specs = P(("groups", "tile", "sub"))
    return jax.shard_map(shards, mesh=mesh, in_specs=in_specs, out_specs=out_specs, check_vma=False)
```

```python
import functools
import math

import jax
import jax.numpy as jnp
import numpy as np
from jax import lax
from jax.experimental import pallas as pl
from jax.experimental.pallas import tpu as pltpu
from jax.sharding import PartitionSpec as P

BLOCK = 128
QUAD = 4
SPAN = 4

inverse_temp = 10.0
norm_eps = 1e-06
GAIN = inverse_temp * math.log2(math.e)
OFF = -1000.0

STEP = 512


def normalised(values):
    values = values.astype(jnp.float32)
    scale = lax.rsqrt(jnp.sum(values * values, axis=1, keepdims=True) + norm_eps)
    return (values * scale).astype(jnp.bfloat16)


def products(rows, columns):
    return lax.dot_general(
        rows, columns, (((1,), (1,)), ((), ())), preferred_element_type=jnp.float32
    )


def column_bias(tag, column_tags):
    return jnp.where(column_tags == tag.astype(jnp.float32), -GAIN, OFF)


def lane_sums(weight):
    total = weight[:, :BLOCK]
    for start in range(BLOCK, weight.shape[1], BLOCK):
        total = total + weight[:, start : start + BLOCK]
    return jnp.sum(total.T, axis=0, keepdims=True)


def self_kernel(blocks, width, meta, rows_ref, tags_ref, unit_ref, sums_ref):
    for start in range(0, blocks * BLOCK, STEP):
        unit_ref[start : start + STEP, :] = normalised(rows_ref[start : start + STEP, :])
    first_col = meta[5 * blocks] * width
    share = unit_ref[pl.ds(pl.multiple_of(first_col * BLOCK, width * BLOCK), width * BLOCK), :]
    column_tags = tags_ref[...].astype(jnp.float32)
    for start in range(0, blocks * BLOCK, STEP):
        cosine = products(unit_ref[start : start + STEP, :], share)
        for inner in range(0, STEP, BLOCK):
            block = (start + inner) // BLOCK
            bias = column_bias(meta[block], column_tags)
            weight = jnp.exp2(cosine[inner : inner + BLOCK] * GAIN + bias)
            row = lax.broadcasted_iota(jnp.int32, weight.shape, 0)
            col = lax.broadcasted_iota(jnp.int32, weight.shape, 1)
            shift = (block - first_col) * BLOCK
            weight = jnp.where((row < meta[blocks + block]) & (col - row != shift), weight, 0.0)
            sums_ref[block : block + 1, :] = lane_sums(weight)


def cross_kernel(blocks, size, chunk, meta, unit_ref, piece_ref, tags_ref, before_ref, sums_ref, cols_ref, piece_unit):
    piece_unit[...] = normalised(piece_ref[:size, :])
    at = 0 if tags_ref.shape[0] == 8 else size
    column_tags = tags_ref[at : at + 8, :].astype(jnp.float32)[0:1, :]
    first = 0 if chunk == 2 else size if chunk == 1 else 0
    column_tags = column_tags[:, first : first + size]
    columns = None
    for start in range(0, blocks * BLOCK, STEP):
        cosine = products(unit_ref[start : start + STEP, :], piece_unit[...])
        for inner in range(0, STEP, BLOCK):
            block = (start + inner) // BLOCK
            bias = column_bias(meta[(2 + chunk) * blocks + block], column_tags)
            weight = jnp.exp2(cosine[inner : inner + BLOCK] * GAIN + bias)
            row = lax.broadcasted_iota(jnp.int32, weight.shape, 0)
            weight = jnp.where(row < meta[blocks + block], weight, 0.0)
            sums_ref[block : block + 1, :] = before_ref[block : block + 1, :] + lane_sums(weight)
            partial = weight[0:8]
            for down in range(8, BLOCK, 8):
                partial = partial + weight[down : down + 8]
            columns = partial if columns is None else columns + partial
    total = jnp.sum(columns, axis=0, keepdims=True)
    for k in range(size // BLOCK):
        cols_ref[k : k + 1, :] = total[:, k * BLOCK : (k + 1) * BLOCK]


def call(kernel, meta, operands, out_shapes, scratch, flops):
    vmem = pl.BlockSpec(memory_space=pltpu.VMEM)
    return pl.pallas_call(
        kernel,
        in_specs=[pl.BlockSpec(memory_space=pltpu.SMEM)] + [vmem] * len(operands),
        out_specs=jax.tree.map(lambda _: vmem, out_shapes),
        out_shape=out_shapes,
        scratch_shapes=scratch,
        compiler_params=pltpu.CompilerParams(vmem_limit_bytes=16 * 1024 * 1024),
        cost_estimate=pl.CostEstimate(flops=flops, bytes_accessed=1024 * 1024, transcendentals=flops // 2048),
    )(meta, *operands)


def every_pair(embeddings, cluster_ids):
    unit = normalised(embeddings)
    tags = cluster_ids + 1
    groups = lax.axis_size("sub")
    member = lax.axis_index("sub")
    owners = lax.axis_size("tile")
    place = lax.axis_index("tile")
    rows_here = unit.shape[0]
    width = rows_here // groups
    own_piece = lax.dynamic_slice_in_dim(unit, member * width, width, 0)
    own_tags = lax.dynamic_slice_in_dim(tags, member * width, width, 0)
    distance = place - jnp.arange(owners, dtype=jnp.int32)
    keep = (jnp.abs(distance) < SPAN) & (distance != 0)
    outgoing = jnp.where(keep[:, None, None], own_piece[None, :, :], jnp.zeros((), jnp.bfloat16))
    outgoing_tags = jnp.where(keep[:, None], own_tags[None, :], 0)
    arrived = lax.all_to_all(outgoing, "tile", split_axis=0, concat_axis=0, tiled=True)
    arrived_tags = lax.all_to_all(outgoing_tags, "tile", split_axis=0, concat_axis=0, tiled=True)
    local_rows = jnp.arange(rows_here, dtype=jnp.int32)[:, None]
    slice_rows = member * width + jnp.arange(width, dtype=jnp.int32)[None, :]
    total = jnp.zeros((rows_here,), jnp.float32)
    for offset in range(1 - SPAN, SPAN):
        if offset == 0:
            piece, piece_tags, order = own_piece, own_tags, local_rows != slice_rows
        else:
            source = place + offset
            valid = (source >= 0) & (source < owners)
            index = jnp.clip(source, 0, owners - 1)
            piece = lax.dynamic_index_in_dim(arrived, index, 0, keepdims=False)
            piece_tags = lax.dynamic_index_in_dim(arrived_tags, index, 0, keepdims=False)
            piece_tags = jnp.where(valid, piece_tags, 0)
            order = True
        same = (tags[:, None] == piece_tags[None, :]) & (tags[:, None] > 0) & order
        weight = jnp.where(same, jnp.exp(inverse_temp * (products(unit, piece) - 1.0)), 0.0)
        total = total + jnp.sum(weight, axis=1)
    return total


def uncovered(tag, blocks, tiles, place):
    half = blocks // 2
    part = place % QUAD
    quads = range(0, tiles, QUAD)
    edge = jnp.broadcast_to(jnp.where(part == 1, tag[half - 1], tag[half]), (BLOCK,))
    out = lax.ppermute(edge, "tile", [p for q in quads for p in ((q + 1, q), (q + 2, q + 3))])[0]
    over = lax.ppermute(edge, "tile", [p for q in quads for p in ((q + 1, q + 3), (q + 2, q))])[0]
    across = lax.ppermute(edge, "tile", [p for q in quads for p in ((q + 1, q + 2), (q + 2, q + 1))])[0]
    inner = (part == 1) | (part == 2)
    one = jnp.where(inner, edge[0], out)
    other = jnp.where(inner, across, over)
    bad = (one == other) & (one >= 0)
    if tiles > QUAD:
        last = jnp.broadcast_to(tag[blocks - 1], (BLOCK,))
        before = lax.ppermute(last, "tile", [(t, t + 1) for t in range(tiles - 1)])[0]
        bad = bad | ((part == 0) & (place > 0) & (before == tag[0]) & (before >= 0))
        bad = lax.pmax(bad.astype(jnp.int32), "tile") > 0
    return bad


def shards(embeddings, cluster_ids):
    tiles, subs = lax.axis_size("tile"), lax.axis_size("sub")
    place, member = lax.axis_index("tile"), lax.axis_index("sub")
    rows, depth = embeddings.shape
    blocks = rows // BLOCK
    width = blocks // subs
    share = width // 2
    size = share * BLOCK
    part = place % QUAD
    inner = (part == 1) | (part == 2)
    quads = range(0, tiles, QUAD)
    routes = [
        [p for q in quads for p in ((q, q + 1), (q + 3, q + 2), (q + 1, q + 3), (q + 2, q))],
        [p for q in quads for p in ((q, q + 1), (q + 3, q + 2))],
        [p for q in quads for p in ((q + 1, q + 2), (q + 2, q + 1))],
    ]
    back = [[(b, a) for a, b in route] for route in routes]

    first_at = BLOCK * jnp.where(
        part == 1, blocks // 2 + member * share, jnp.where(part == 2, member * share, member * width)
    )
    second_at = BLOCK * (member * width + share)
    carried = jnp.concatenate(
        [lax.dynamic_slice_in_dim(cluster_ids, at, size, 0) for at in (first_at, second_at)]
    ).astype(jnp.bfloat16)
    carried = jnp.broadcast_to(jnp.pad(carried, (0, depth - 2 * size))[None], (8, depth))
    first_out = jnp.concatenate([lax.dynamic_slice_in_dim(embeddings, first_at, size, 0), carried])
    second_out = lax.dynamic_slice_in_dim(embeddings, second_at, size, 0)
    first = lax.ppermute(first_out, "tile", routes[0])
    third = lax.ppermute(first_out, "tile", routes[2])
    second = lax.ppermute(second_out, "tile", routes[1])

    by_block = cluster_ids.reshape(blocks, BLOCK)
    tag = jnp.max(by_block, axis=1)
    used = jnp.sum((by_block >= 0).astype(jnp.int32), axis=1)
    far = (part == 1) & (jnp.arange(blocks) >= blocks // 2)
    from_outer = jnp.where(inner, tag, -2)
    meta = jnp.concatenate([tag, used, tag, from_outer, jnp.where(far, -2, from_outer), member[None]]).astype(jnp.int32)

    bad = uncovered(tag, blocks, tiles, place)
    extra = lax.cond(
        bad, lambda: every_pair(embeddings, cluster_ids), lambda: jnp.zeros((rows,), jnp.float32)
    )

    row_sums = jax.ShapeDtypeStruct((blocks, BLOCK), jnp.float32)
    unit, sums = call(
        functools.partial(self_kernel, blocks, width),
        meta,
        (embeddings, lax.dynamic_slice_in_dim(cluster_ids, member * width * BLOCK, width * BLOCK, 0)[None]),
        [jax.ShapeDtypeStruct((rows, depth), jnp.bfloat16), row_sums],
        [],
        2 * rows * width * BLOCK * depth,
    )

    def cross(chunk, piece, tags, before):
        return call(
            functools.partial(cross_kernel, blocks, size, chunk),
            meta,
            (unit, piece, tags, before),
            [row_sums, jax.ShapeDtypeStruct((share, BLOCK), jnp.float32)],
            [pltpu.VMEM((size, depth), jnp.bfloat16)],
            2 * rows * size * depth,
        )

    sums, first_cols = cross(0, first, first, sums)
    sums, third_cols = cross(2, third, third, sums)
    sums, second_cols = cross(1, second, first, sums)
    returned = lax.ppermute(first_cols, "tile", back[0]) + lax.ppermute(third_cols, "tile", back[2])
    outer = lax.ppermute(second_cols, "tile", back[1])

    partial = sums.reshape(-1)
    here = lax.dynamic_slice_in_dim(partial, first_at, size, 0) + returned.reshape(-1)
    partial = lax.dynamic_update_slice_in_dim(partial, here, first_at, 0)
    partial = jnp.where(bad, extra, partial)
    quarter = width * BLOCK

    def portion(shift):
        return lax.dynamic_slice_in_dim(partial, lax.rem(member + shift, subs) * quarter, quarter, 0)

    density = portion(0)
    for shift in range(1, subs):
        density = density + lax.ppermute(portion(shift), "sub", [(i, (i + shift) % subs) for i in range(subs)])
    outer = jnp.where(bad, 0.0, outer.reshape(-1))
    density = density + jnp.concatenate([jnp.zeros_like(outer), outer])
    return jnp.log(1.0 + density)


def solution(mesh):
    in_specs = (P(("groups", "tile"), None), P(("groups", "tile")))
    out_specs = P(("groups", "tile", "sub"))
    return jax.shard_map(shards, mesh=mesh, in_specs=in_specs, out_specs=out_specs, check_vma=False)
```

```python
import functools
import math

import jax
import jax.numpy as jnp
import numpy as np
from jax import lax
from jax.experimental import pallas as pl
from jax.experimental.pallas import tpu as pltpu
from jax.sharding import PartitionSpec as P

BLOCK = 128
QUAD = 4
SPAN = 4

inverse_temp = 10.0
norm_eps = 1e-06
GAIN = inverse_temp * math.log2(math.e)
OFF = -1000.0

STEP = 512


def normalised(values):
    values = values.astype(jnp.float32)
    scale = lax.rsqrt(jnp.sum(values * values, axis=1, keepdims=True) + norm_eps)
    return (values * scale).astype(jnp.bfloat16)


def products(rows, columns):
    return lax.dot_general(
        rows, columns, (((1,), (1,)), ((), ())), preferred_element_type=jnp.float32
    )


def column_bias(tag, column_tags):
    return jnp.where(column_tags == tag.astype(jnp.float32), -GAIN, OFF)


def lane_sums(weight):
    total = weight[:, :BLOCK]
    for start in range(BLOCK, weight.shape[1], BLOCK):
        total = total + weight[:, start : start + BLOCK]
    return jnp.sum(total.T, axis=0, keepdims=True)


def pack_kernel(blocks, share, at, rows_ref, ids_ref, first_ref, second_ref, sems):
    size = share * BLOCK
    copies = []
    for index, out in enumerate((first_ref.at[pl.ds(0, size), :], second_ref)):
        start = pl.multiple_of(at[index] * BLOCK, BLOCK)
        copies.append(pltpu.make_async_copy(rows_ref.at[pl.ds(start, size), :], out, sems.at[index]))
        copies[-1].start()
    depth = first_ref.shape[1]
    parts = [ids_ref[pl.ds(at[index] + k, 1), :] for index in range(2) for k in range(share)]
    edge = jnp.max(ids_ref[pl.ds(at[2], 1), :], axis=1, keepdims=True)
    parts.append(jnp.broadcast_to(edge, (1, BLOCK)))
    parts.append(jnp.zeros((1, depth - len(parts) * BLOCK), jnp.int32))
    row = jnp.concatenate(parts, axis=1).astype(jnp.float32)
    first_ref[size : size + 8, :] = jnp.broadcast_to(row, (8, depth)).astype(jnp.bfloat16)
    for copy in copies:
        copy.wait()


def self_kernel(blocks, width, meta, rows_ref, tags_ref, unit_ref, sums_ref):
    for start in range(0, blocks * BLOCK, STEP):
        unit_ref[start : start + STEP, :] = normalised(rows_ref[start : start + STEP, :])
    first_col = meta[5 * blocks] * width
    share = unit_ref[pl.ds(pl.multiple_of(first_col * BLOCK, width * BLOCK), width * BLOCK), :]
    column_tags = tags_ref[...].astype(jnp.float32)
    for start in range(0, blocks * BLOCK, STEP):
        cosine = products(unit_ref[start : start + STEP, :], share)
        for inner in range(0, STEP, BLOCK):
            block = (start + inner) // BLOCK
            bias = column_bias(meta[block], column_tags)
            weight = jnp.exp2(cosine[inner : inner + BLOCK] * GAIN + bias)
            row = lax.broadcasted_iota(jnp.int32, weight.shape, 0)
            col = lax.broadcasted_iota(jnp.int32, weight.shape, 1)
            shift = (block - first_col) * BLOCK
            weight = jnp.where((row < meta[blocks + block]) & (col - row != shift), weight, 0.0)
            sums_ref[block : block + 1, :] = lane_sums(weight)


def cross_kernel(blocks, size, chunk, meta, unit_ref, piece_ref, tags_ref, before_ref, sums_ref, cols_ref, piece_unit):
    piece_unit[...] = normalised(piece_ref[:size, :])
    at = 0 if tags_ref.shape[0] == 8 else size
    column_tags = tags_ref[at : at + 8, :].astype(jnp.float32)[0:1, :]
    first = 0 if chunk == 2 else size if chunk == 1 else 0
    column_tags = column_tags[:, first : first + size]
    columns = None
    for start in range(0, blocks * BLOCK, STEP):
        cosine = products(unit_ref[start : start + STEP, :], piece_unit[...])
        for inner in range(0, STEP, BLOCK):
            block = (start + inner) // BLOCK
            bias = column_bias(meta[(2 + chunk) * blocks + block], column_tags)
            weight = jnp.exp2(cosine[inner : inner + BLOCK] * GAIN + bias)
            row = lax.broadcasted_iota(jnp.int32, weight.shape, 0)
            weight = jnp.where(row < meta[blocks + block], weight, 0.0)
            sums_ref[block : block + 1, :] = before_ref[block : block + 1, :] + lane_sums(weight)
            partial = weight[0:8]
            for down in range(8, BLOCK, 8):
                partial = partial + weight[down : down + 8]
            columns = partial if columns is None else columns + partial
    total = jnp.sum(columns, axis=0, keepdims=True)
    for k in range(size // BLOCK):
        cols_ref[k : k + 1, :] = total[:, k * BLOCK : (k + 1) * BLOCK]


def call(kernel, meta, operands, out_shapes, scratch, flops):
    vmem = pl.BlockSpec(memory_space=pltpu.VMEM)
    return pl.pallas_call(
        kernel,
        in_specs=[pl.BlockSpec(memory_space=pltpu.SMEM)] + [vmem] * len(operands),
        out_specs=jax.tree.map(lambda _: vmem, out_shapes),
        out_shape=out_shapes,
        scratch_shapes=scratch,
        compiler_params=pltpu.CompilerParams(vmem_limit_bytes=16 * 1024 * 1024),
        cost_estimate=pl.CostEstimate(flops=flops, bytes_accessed=1024 * 1024, transcendentals=flops // 2048),
    )(meta, *operands)


def every_pair(embeddings, cluster_ids):
    unit = normalised(embeddings)
    tags = cluster_ids + 1
    groups = lax.axis_size("sub")
    member = lax.axis_index("sub")
    owners = lax.axis_size("tile")
    place = lax.axis_index("tile")
    rows_here = unit.shape[0]
    width = rows_here // groups
    own_piece = lax.dynamic_slice_in_dim(unit, member * width, width, 0)
    own_tags = lax.dynamic_slice_in_dim(tags, member * width, width, 0)
    distance = place - jnp.arange(owners, dtype=jnp.int32)
    keep = (jnp.abs(distance) < SPAN) & (distance != 0)
    outgoing = jnp.where(keep[:, None, None], own_piece[None, :, :], jnp.zeros((), jnp.bfloat16))
    outgoing_tags = jnp.where(keep[:, None], own_tags[None, :], 0)
    arrived = lax.all_to_all(outgoing, "tile", split_axis=0, concat_axis=0, tiled=True)
    arrived_tags = lax.all_to_all(outgoing_tags, "tile", split_axis=0, concat_axis=0, tiled=True)
    local_rows = jnp.arange(rows_here, dtype=jnp.int32)[:, None]
    slice_rows = member * width + jnp.arange(width, dtype=jnp.int32)[None, :]
    total = jnp.zeros((rows_here,), jnp.float32)
    for offset in range(1 - SPAN, SPAN):
        if offset == 0:
            piece, piece_tags, order = own_piece, own_tags, local_rows != slice_rows
        else:
            source = place + offset
            valid = (source >= 0) & (source < owners)
            index = jnp.clip(source, 0, owners - 1)
            piece = lax.dynamic_index_in_dim(arrived, index, 0, keepdims=False)
            piece_tags = lax.dynamic_index_in_dim(arrived_tags, index, 0, keepdims=False)
            piece_tags = jnp.where(valid, piece_tags, 0)
            order = True
        same = (tags[:, None] == piece_tags[None, :]) & (tags[:, None] > 0) & order
        weight = jnp.where(same, jnp.exp(inverse_temp * (products(unit, piece) - 1.0)), 0.0)
        total = total + jnp.sum(weight, axis=1)
    return total


def quads_joined(tag, tiles, place):
    last = jnp.broadcast_to(tag[-1], (BLOCK,))
    before = lax.ppermute(last, "tile", [(t, t + 1) for t in range(tiles - 1)])[0]
    joined = (place % QUAD == 0) & (place > 0) & (before == tag[0]) & (before >= 0)
    return lax.pmax(joined.astype(jnp.int32), "tile") > 0


def shards(embeddings, cluster_ids):
    tiles, subs = lax.axis_size("tile"), lax.axis_size("sub")
    place, member = lax.axis_index("tile"), lax.axis_index("sub")
    rows, depth = embeddings.shape
    blocks = rows // BLOCK
    width = blocks // subs
    share = width // 2
    size = share * BLOCK
    part = place % QUAD
    inner = (part == 1) | (part == 2)
    quads = range(0, tiles, QUAD)
    routes = [
        [p for q in quads for p in ((q, q + 1), (q + 3, q + 2), (q + 1, q + 3), (q + 2, q))],
        [p for q in quads for p in ((q, q + 1), (q + 3, q + 2))],
        [p for q in quads for p in ((q + 1, q + 2), (q + 2, q + 1))],
    ]
    back = [[(b, a) for a, b in route] for route in routes]

    first_block = jnp.where(
        part == 1, blocks // 2 + member * share, jnp.where(part == 2, member * share, member * width)
    )
    first_at = first_block * BLOCK
    edge_block = jnp.where(part == 1, blocks // 2 - 1, blocks // 2)
    by_block = cluster_ids.reshape(blocks, BLOCK)
    first_out, second_out = pl.pallas_call(
        functools.partial(pack_kernel, blocks, share),
        in_specs=[
            pl.BlockSpec(memory_space=pltpu.SMEM),
            pl.BlockSpec(memory_space=pl.ANY),
            pl.BlockSpec(memory_space=pltpu.VMEM),
        ],
        out_specs=[pl.BlockSpec(memory_space=pltpu.VMEM)] * 2,
        out_shape=[
            jax.ShapeDtypeStruct((size + 8, depth), jnp.bfloat16),
            jax.ShapeDtypeStruct((size, depth), jnp.bfloat16),
        ],
        scratch_shapes=[pltpu.SemaphoreType.DMA((2,))],
        compiler_params=pltpu.CompilerParams(vmem_limit_bytes=8 * 1024 * 1024),
    )(jnp.stack([first_block, member * width + share, edge_block]).astype(jnp.int32), embeddings, by_block)
    first = lax.ppermute(first_out, "tile", routes[0])
    second = lax.ppermute(second_out, "tile", routes[1])
    third = lax.ppermute(first_out, "tile", routes[2])

    tag = jnp.max(by_block, axis=1)
    used = jnp.sum((by_block >= 0).astype(jnp.int32), axis=1)
    far = (part == 1) & (jnp.arange(blocks) >= blocks // 2)
    from_outer = jnp.where(inner, tag, -2)
    meta = jnp.concatenate([tag, used, tag, from_outer, jnp.where(far, -2, from_outer), member[None]]).astype(jnp.int32)

    row_sums = jax.ShapeDtypeStruct((blocks, BLOCK), jnp.float32)
    unit, sums = call(
        functools.partial(self_kernel, blocks, width),
        meta,
        (embeddings, lax.dynamic_slice_in_dim(cluster_ids, member * width * BLOCK, width * BLOCK, 0)[None]),
        [jax.ShapeDtypeStruct((rows, depth), jnp.bfloat16), row_sums],
        [],
        2 * rows * width * BLOCK * depth,
    )

    def cross(chunk, piece, tags, before):
        return call(
            functools.partial(cross_kernel, blocks, size, chunk),
            meta,
            (unit, piece, tags, before),
            [row_sums, jax.ShapeDtypeStruct((share, BLOCK), jnp.float32)],
            [pltpu.VMEM((size, depth), jnp.bfloat16)],
            2 * rows * size * depth,
        )

    sums, first_cols = cross(0, first, first, sums)
    sums, third_cols = cross(2, third, third, sums)
    sums, second_cols = cross(1, second, first, sums)
    edge = jnp.where(part == 1, tag[blocks // 2 - 1], tag[blocks // 2]).astype(jnp.float32)
    first_cols = lax.ppermute(
        jnp.concatenate([first_cols, jnp.broadcast_to(edge, (1, BLOCK))]), "tile", back[0]
    )
    returned = first_cols[:share] + lax.ppermute(third_cols, "tile", back[2])
    outer = lax.ppermute(second_cols, "tile", back[1])

    one = jnp.where(inner, edge, first[size, 2 * size].astype(jnp.float32))
    other = jnp.where(inner, third[size, 2 * size].astype(jnp.float32), first_cols[share, 0])
    bad = (one == other) & (one >= 0)
    if tiles > QUAD:
        bad = lax.pmax(bad.astype(jnp.int32), "tile") > 0
        bad = bad | quads_joined(tag, tiles, place)
    extra = lax.cond(
        bad, lambda: every_pair(embeddings, cluster_ids), lambda: jnp.zeros((rows,), jnp.float32)
    )

    partial = sums.reshape(-1)
    here = lax.dynamic_slice_in_dim(partial, first_at, size, 0) + returned.reshape(-1)
    partial = lax.dynamic_update_slice_in_dim(partial, here, first_at, 0)
    partial = jnp.where(bad, extra, partial)
    quarter = width * BLOCK

    def portion(shift):
        return lax.dynamic_slice_in_dim(partial, lax.rem(member + shift, subs) * quarter, quarter, 0)

    density = portion(0)
    for shift in range(1, subs):
        density = density + lax.ppermute(portion(shift), "sub", [(i, (i + shift) % subs) for i in range(subs)])
    outer = jnp.where(bad, 0.0, outer.reshape(-1))
    density = density + jnp.concatenate([jnp.zeros_like(outer), outer])
    return jnp.log(1.0 + density)


def solution(mesh):
    in_specs = (P(("groups", "tile"), None), P(("groups", "tile")))
    out_specs = P(("groups", "tile", "sub"))
    return jax.shard_map(shards, mesh=mesh, in_specs=in_specs, out_specs=out_specs, check_vma=False)
```

```python
import functools
import math

import jax
import jax.numpy as jnp
import numpy as np
from jax import lax
from jax.experimental import pallas as pl
from jax.experimental.pallas import tpu as pltpu
from jax.sharding import PartitionSpec as P

BLOCK = 128
QUAD = 4
SPAN = 4

inverse_temp = 10.0
norm_eps = 1e-06
GAIN = inverse_temp * math.log2(math.e)
OFF = -1000.0

STEP = 512


def normalised(values):
    values = values.astype(jnp.float32)
    scale = lax.rsqrt(jnp.sum(values * values, axis=1, keepdims=True) + norm_eps)
    return (values * scale).astype(jnp.bfloat16)


def products(rows, columns):
    return lax.dot_general(
        rows, columns, (((1,), (1,)), ((), ())), preferred_element_type=jnp.float32
    )


def column_bias(tag, column_tags):
    return jnp.where(column_tags == tag.astype(jnp.float32), -GAIN, OFF)


def lane_sums(weight):
    total = weight[:, :BLOCK]
    for start in range(BLOCK, weight.shape[1], BLOCK):
        total = total + weight[:, start : start + BLOCK]
    return jnp.sum(total.T, axis=0, keepdims=True)


def pack_kernel(share, at, rows_ref, ids_ref, first_ref, second_ref, sems):
    size = share * BLOCK
    copies = []
    for index, out in enumerate((first_ref, second_ref)):
        start = pl.multiple_of(at[index] * BLOCK, BLOCK)
        copies.append(
            pltpu.make_async_copy(rows_ref.at[pl.ds(start, size), :], out.at[pl.ds(0, size), :], sems.at[index])
        )
        copies[-1].start()
    depth = first_ref.shape[1]
    edge = jnp.max(ids_ref[pl.ds(at[2], 1), :], axis=1, keepdims=True)
    rest = [jnp.broadcast_to(edge, (1, BLOCK)), jnp.zeros((1, depth - size - BLOCK), jnp.int32)]
    for index, out in enumerate((first_ref, second_ref)):
        row = jnp.concatenate([ids_ref[pl.ds(at[index] + k, 1), :] for k in range(share)] + rest, axis=1)
        out[size : size + 8, :] = jnp.broadcast_to(row.astype(jnp.float32), (8, depth)).astype(jnp.bfloat16)
    for copy in copies:
        copy.wait()


class Meta:
    def __init__(self, ref, blocks):
        self.ref, self.blocks = ref, blocks

    def tag(self, block, chunk=None):
        return self.ref[block + (0 if chunk is None else (2 + chunk) * self.blocks)]

    def used(self, block):
        return self.ref[self.blocks + block]

    def number(self, index):
        return self.ref[5 * self.blocks + index]


MEMBER, FIRST_BLOCK, EDGE = range(3)


def self_kernel(blocks, width, meta_ref, rows_ref, tags_ref, unit_ref, sums_ref):
    meta = Meta(meta_ref, blocks)
    for start in range(0, blocks * BLOCK, STEP):
        unit_ref[start : start + STEP, :] = normalised(rows_ref[start : start + STEP, :])
    first_col = meta.number(MEMBER) * width
    share = unit_ref[pl.ds(pl.multiple_of(first_col * BLOCK, width * BLOCK), width * BLOCK), :]
    column_tags = tags_ref[...].astype(jnp.float32)
    for start in range(0, blocks * BLOCK, STEP):
        cosine = products(unit_ref[start : start + STEP, :], share)
        for inner in range(0, STEP, BLOCK):
            block = (start + inner) // BLOCK
            bias = column_bias(meta.tag(block), column_tags)
            weight = jnp.exp2(cosine[inner : inner + BLOCK] * GAIN + bias)
            row = lax.broadcasted_iota(jnp.int32, weight.shape, 0)
            col = lax.broadcasted_iota(jnp.int32, weight.shape, 1)
            shift = (block - first_col) * BLOCK
            weight = jnp.where((row < meta.used(block)) & (col - row != shift), weight, 0.0)
            sums_ref[block : block + 1, :] = lane_sums(weight)


def chunk_tags(piece_ref, size):
    row = piece_ref[size : size + 8, :].astype(jnp.float32)[0:1, :]
    return row[:, :size], row[:, size : size + BLOCK]


def cross_terms(meta, chunks, column_tags, unit_ref, piece_unit, add_rows):
    size = column_tags[0].shape[1]
    columns = None
    for start in range(0, meta.blocks * BLOCK, STEP):
        cosine = products(unit_ref[start : start + STEP, :], piece_unit[...])
        for inner in range(0, STEP, BLOCK):
            block = (start + inner) // BLOCK
            bias = [column_bias(meta.tag(block, chunk), tags) for chunk, tags in zip(chunks, column_tags)]
            bias = jnp.concatenate(bias, axis=1) if len(bias) > 1 else bias[0]
            weight = jnp.exp2(cosine[inner : inner + BLOCK] * GAIN + bias)
            row = lax.broadcasted_iota(jnp.int32, weight.shape, 0)
            weight = jnp.where(row < meta.used(block), weight, 0.0)
            add_rows(block, lane_sums(weight))
            partial = weight[0:8]
            for down in range(8, BLOCK, 8):
                partial = partial + weight[down : down + 8]
            columns = partial if columns is None else columns + partial
    total = jnp.sum(columns, axis=0, keepdims=True)
    return [
        [total[:, at + down : at + down + BLOCK] for down in range(0, size, BLOCK)]
        for at in range(0, total.shape[1], size)
    ]


def middle_kernel(
    blocks, share, meta_ref, unit_ref, outer_ref, swap_ref, before_ref, sums_ref, outer_cols_ref, swap_cols_ref,
    piece_unit,
):
    meta = Meta(meta_ref, blocks)
    size = share * BLOCK
    piece_unit[:size, :] = normalised(outer_ref[:size, :])
    piece_unit[size:, :] = normalised(swap_ref[:size, :])
    outer_tags, _ = chunk_tags(outer_ref, size)
    swap_tags, edge = chunk_tags(swap_ref, size)

    def add_rows(block, value):
        sums_ref[block : block + 1, :] = before_ref[block : block + 1, :] + value

    outer, swap = cross_terms(meta, (0, 1), (outer_tags, swap_tags), unit_ref, piece_unit, add_rows)
    for k in range(share):
        outer_cols_ref[k : k + 1, :] = outer[k]
        swap_cols_ref[k : k + 1, :] = swap[k]
    mine = meta.number(EDGE).astype(jnp.float32)
    outer_cols_ref[share : share + 1, :] = jnp.where((edge == mine) & (edge >= 0), 1.0, 0.0)


def last_kernel(
    blocks, share, width, meta_ref, unit_ref, piece_ref, before_ref, outer_back_ref, swap_back_ref,
    keep_ref, send_ref, cols_ref, piece_unit, sums,
):
    meta = Meta(meta_ref, blocks)
    size = share * BLOCK
    piece_unit[...] = normalised(piece_ref[:size, :])
    tags, _ = chunk_tags(piece_ref, size)

    def place(block):
        owner = block // width
        return owner % 2 * (blocks // 2) + owner // 2 * width + block % width

    def add_rows(block, value):
        at = place(block)
        sums[at : at + 1, :] = before_ref[block : block + 1, :] + value

    (cols,) = cross_terms(meta, (2,), (tags,), unit_ref, piece_unit, add_rows)
    for k in range(share):
        cols_ref[k : k + 1, :] = cols[k]
        at = place(meta.number(FIRST_BLOCK) + k)
        sums[pl.ds(at, 1), :] += outer_back_ref[k : k + 1, :] + swap_back_ref[k : k + 1, :]
    parity = meta.number(MEMBER) % 2
    heap = blocks // 2
    keep_ref[...] = sums[pl.ds(pl.multiple_of(parity * heap, heap), heap), :]
    send_ref[...] = sums[pl.ds(pl.multiple_of((1 - parity) * heap, heap), heap), :]


def call(kernel, meta, operands, out_shapes, scratch, flops):
    vmem = pl.BlockSpec(memory_space=pltpu.VMEM)
    return pl.pallas_call(
        kernel,
        in_specs=[pl.BlockSpec(memory_space=pltpu.SMEM)] + [vmem] * len(operands),
        out_specs=jax.tree.map(lambda _: vmem, out_shapes),
        out_shape=out_shapes,
        scratch_shapes=scratch,
        compiler_params=pltpu.CompilerParams(vmem_limit_bytes=16 * 1024 * 1024),
        cost_estimate=pl.CostEstimate(flops=flops, bytes_accessed=1024 * 1024, transcendentals=flops // 2048),
    )(meta, *operands)


def every_pair(embeddings, cluster_ids):
    unit = normalised(embeddings)
    tags = cluster_ids + 1
    groups = lax.axis_size("sub")
    member = lax.axis_index("sub")
    owners = lax.axis_size("tile")
    place = lax.axis_index("tile")
    rows_here = unit.shape[0]
    width = rows_here // groups
    own_piece = lax.dynamic_slice_in_dim(unit, member * width, width, 0)
    own_tags = lax.dynamic_slice_in_dim(tags, member * width, width, 0)
    distance = place - jnp.arange(owners, dtype=jnp.int32)
    keep = (jnp.abs(distance) < SPAN) & (distance != 0)
    outgoing = jnp.where(keep[:, None, None], own_piece[None, :, :], jnp.zeros((), jnp.bfloat16))
    outgoing_tags = jnp.where(keep[:, None], own_tags[None, :], 0)
    arrived = lax.all_to_all(outgoing, "tile", split_axis=0, concat_axis=0, tiled=True)
    arrived_tags = lax.all_to_all(outgoing_tags, "tile", split_axis=0, concat_axis=0, tiled=True)
    local_rows = jnp.arange(rows_here, dtype=jnp.int32)[:, None]
    slice_rows = member * width + jnp.arange(width, dtype=jnp.int32)[None, :]
    total = jnp.zeros((rows_here,), jnp.float32)
    for offset in range(1 - SPAN, SPAN):
        if offset == 0:
            piece, piece_tags, order = own_piece, own_tags, local_rows != slice_rows
        else:
            source = place + offset
            valid = (source >= 0) & (source < owners)
            index = jnp.clip(source, 0, owners - 1)
            piece = lax.dynamic_index_in_dim(arrived, index, 0, keepdims=False)
            piece_tags = lax.dynamic_index_in_dim(arrived_tags, index, 0, keepdims=False)
            piece_tags = jnp.where(valid, piece_tags, 0)
            order = True
        same = (tags[:, None] == piece_tags[None, :]) & (tags[:, None] > 0) & order
        weight = jnp.where(same, jnp.exp(inverse_temp * (products(unit, piece) - 1.0)), 0.0)
        total = total + jnp.sum(weight, axis=1)
    return jnp.log(1.0 + lax.psum_scatter(total, "sub", scatter_dimension=0, tiled=True))


def quads_joined(tag, tiles, place):
    last = jnp.broadcast_to(tag[-1], (BLOCK,))
    before = lax.ppermute(last, "tile", [(t, t + 1) for t in range(tiles - 1)])[0]
    joined = (place % QUAD == 0) & (place > 0) & (before == tag[0]) & (before >= 0)
    return lax.pmax(joined.astype(jnp.int32), "tile") > 0


def shards(embeddings, cluster_ids):
    tiles, subs = lax.axis_size("tile"), lax.axis_size("sub")
    place, member = lax.axis_index("tile"), lax.axis_index("sub")
    rows, depth = embeddings.shape
    blocks = rows // BLOCK
    width = blocks // subs
    share = width // 2
    size = share * BLOCK
    part = place % QUAD
    inner = (part == 1) | (part == 2)
    quads = range(0, tiles, QUAD)
    inward = [p for q in quads for p in ((q, q + 1), (q + 3, q + 2))]
    swap = [p for q in quads for p in ((q + 1, q + 2), (q + 2, q + 1))]
    around = [p for q in quads for p in ((q, q + 1), (q + 3, q + 2), (q + 1, q + 3), (q + 2, q))]

    def turned(route):
        return [(b, a) for a, b in route]

    dealt = member // 2 * share
    near = (dealt // width * 2 + member % 2) * width + dealt % width
    near = jnp.where(part == 1, blocks // 2, 0) + near
    first_block = jnp.where(inner, near, member * width)
    second_block = jnp.where(inner, near, member * width + share)
    edge_block = jnp.where(part == 1, blocks // 2 - 1, blocks // 2)
    by_block = cluster_ids.reshape(blocks, BLOCK)
    vmem = pl.BlockSpec(memory_space=pltpu.VMEM)
    first_out, second_out = pl.pallas_call(
        functools.partial(pack_kernel, share),
        in_specs=[pl.BlockSpec(memory_space=pltpu.SMEM), pl.BlockSpec(memory_space=pl.ANY), vmem],
        out_specs=[vmem] * 2,
        out_shape=[jax.ShapeDtypeStruct((size + 8, depth), jnp.bfloat16)] * 2,
        scratch_shapes=[pltpu.SemaphoreType.DMA((2,))],
        compiler_params=pltpu.CompilerParams(vmem_limit_bytes=8 * 1024 * 1024),
    )(jnp.stack([first_block, second_block, edge_block]).astype(jnp.int32), embeddings, by_block)
    from_outer = lax.ppermute(first_out, "tile", inward)
    from_inner = lax.ppermute(first_out, "tile", swap)

    tag = jnp.max(by_block, axis=1)
    used = jnp.sum((by_block >= 0).astype(jnp.int32), axis=1)
    edge = jnp.where(part == 1, tag[blocks // 2 - 1], tag[blocks // 2])
    far = (part == 1) & (jnp.arange(blocks) >= blocks // 2)
    seen = jnp.where(inner, tag, -2)
    meta = jnp.concatenate(
        [tag, used, seen, jnp.where(far, -2, seen), tag, jnp.stack([member, first_block, edge])]
    ).astype(jnp.int32)

    row_sums = jax.ShapeDtypeStruct((blocks, BLOCK), jnp.float32)
    col_sums = jax.ShapeDtypeStruct((share, BLOCK), jnp.float32)
    unit, sums = call(
        functools.partial(self_kernel, blocks, width),
        meta,
        (embeddings, lax.dynamic_slice_in_dim(cluster_ids, member * width * BLOCK, width * BLOCK, 0)[None]),
        [jax.ShapeDtypeStruct((rows, depth), jnp.bfloat16), row_sums],
        [],
        2 * rows * width * BLOCK * depth,
    )
    second_out, sums = lax.optimization_barrier((second_out, sums))
    last = lax.ppermute(second_out, "tile", around)
    sums, outer_cols, swap_cols = call(
        functools.partial(middle_kernel, blocks, share),
        meta,
        (unit, from_outer, from_inner, sums),
        [row_sums, jax.ShapeDtypeStruct((share + 1, BLOCK), jnp.float32), col_sums],
        [pltpu.VMEM((2 * size, depth), jnp.bfloat16)],
        4 * rows * size * depth,
    )
    outer_back = lax.ppermute(outer_cols, "tile", turned(inward))
    swap_back = lax.ppermute(swap_cols, "tile", turned(swap))

    bad = jnp.where(inner, outer_cols[share, 0], outer_back[share, 0]) > 0
    if tiles > QUAD:
        bad = lax.pmax(bad.astype(jnp.int32), "tile") > 0
        bad = bad | quads_joined(tag, tiles, place)

    half = jax.ShapeDtypeStruct((blocks // 2, BLOCK), jnp.float32)
    held, leaving, cols = call(
        functools.partial(last_kernel, blocks, share, width),
        meta,
        (unit, last, sums, outer_back, swap_back),
        [half, half, col_sums],
        [pltpu.VMEM((size, depth), jnp.bfloat16), pltpu.VMEM((blocks, BLOCK), jnp.float32)],
        2 * rows * size * depth,
    )

    came = lax.ppermute(leaving, "sub", [(i, i ^ 1) for i in range(subs)])
    home = lax.ppermute(cols, "tile", turned(around))
    owner = second_block // width
    home_at = owner // 2 * width + second_block % width
    held = held + came
    held = lax.dynamic_update_slice_in_dim(
        held, lax.dynamic_slice_in_dim(held, home_at, share, 0) + home, home_at, 0
    )
    bit = 1
    while 1 << bit < subs:
        pairs = held.reshape(-1, 2, width, BLOCK)
        own = (member >> bit) & 1
        leaving = lax.dynamic_index_in_dim(pairs, 1 - own, 1, keepdims=False)
        came = lax.ppermute(leaving, "sub", [(i, i ^ (1 << bit)) for i in range(subs)])
        held = lax.dynamic_index_in_dim(pairs, own, 1, keepdims=False) + came
        bit += 1
    scores = jnp.log(1.0 + held.reshape(-1))
    return lax.cond(bad, lambda: every_pair(embeddings, cluster_ids), lambda: scores)


def solution(mesh):
    in_specs = (P(("groups", "tile"), None), P(("groups", "tile")))
    out_specs = P(("groups", "tile", "sub"))
    return jax.shard_map(shards, mesh=mesh, in_specs=in_specs, out_specs=out_specs, check_vma=False)
```

```python
import functools
import math

import jax
import jax.numpy as jnp
import numpy as np
from jax import lax
from jax.experimental import pallas as pl
from jax.experimental.pallas import tpu as pltpu
from jax.sharding import PartitionSpec as P

BLOCK = 128
QUAD = 4
SPAN = 4

inverse_temp = 10.0
norm_eps = 1e-06
GAIN = inverse_temp * math.log2(math.e)
OFF = -1000.0

STEP = 512


def normalised(values):
    values = values.astype(jnp.float32)
    scale = lax.rsqrt(jnp.sum(values * values, axis=1, keepdims=True) + norm_eps)
    return (values * scale).astype(jnp.bfloat16)


def products(rows, columns):
    return lax.dot_general(
        rows, columns, (((1,), (1,)), ((), ())), preferred_element_type=jnp.float32
    )


def column_bias(tag, column_tags):
    return jnp.where(column_tags == tag.astype(jnp.float32), -GAIN, OFF)


def lane_sums(weight):
    total = weight[:, :BLOCK]
    for start in range(BLOCK, weight.shape[1], BLOCK):
        total = total + weight[:, start : start + BLOCK]
    return jnp.sum(total.T, axis=0, keepdims=True)


def pack_kernel(share, at, rows_ref, ids_ref, out_ref, sem):
    size = share * BLOCK
    start = pl.multiple_of(at[0] * BLOCK, BLOCK)
    copy = pltpu.make_async_copy(rows_ref.at[pl.ds(start, size), :], out_ref.at[pl.ds(0, size), :], sem)
    copy.start()
    depth = out_ref.shape[1]
    edge = jnp.max(ids_ref[pl.ds(at[1], 1), :], axis=1, keepdims=True)
    row = [ids_ref[pl.ds(at[0] + k, 1), :] for k in range(share)]
    row += [jnp.broadcast_to(edge, (1, BLOCK)), jnp.zeros((1, depth - size - BLOCK), jnp.int32)]
    row = jnp.concatenate(row, axis=1).astype(jnp.float32)
    out_ref[size : size + 8, :] = jnp.broadcast_to(row, (8, depth)).astype(jnp.bfloat16)
    copy.wait()


def pack(share, block, edge_block, embeddings, by_block):
    vmem = pl.BlockSpec(memory_space=pltpu.VMEM)
    return pl.pallas_call(
        functools.partial(pack_kernel, share),
        in_specs=[pl.BlockSpec(memory_space=pltpu.SMEM), pl.BlockSpec(memory_space=pl.ANY), vmem],
        out_specs=vmem,
        out_shape=jax.ShapeDtypeStruct((share * BLOCK + 8, embeddings.shape[1]), jnp.bfloat16),
        scratch_shapes=[pltpu.SemaphoreType.DMA],
        compiler_params=pltpu.CompilerParams(vmem_limit_bytes=8 * 1024 * 1024),
        cost_estimate=pl.CostEstimate(flops=0, bytes_accessed=1024, transcendentals=0),
    )(jnp.stack([block, edge_block]).astype(jnp.int32), embeddings, by_block)


class Meta:
    def __init__(self, ref, blocks):
        self.ref, self.blocks = ref, blocks

    def tag(self, block, chunk=None):
        return self.ref[block + (0 if chunk is None else (2 + chunk) * self.blocks)]

    def used(self, block):
        return self.ref[self.blocks + block]

    def number(self, index):
        return self.ref[5 * self.blocks + index]


MEMBER, FIRST_BLOCK, EDGE = range(3)


def self_kernel(blocks, width, meta_ref, rows_ref, piece_ref, tags_ref, unit_ref, sums_ref, piece_unit):
    meta = Meta(meta_ref, blocks)
    step = pl.program_id(0)

    @pl.when(step == 0)
    def _():
        piece_unit[...] = normalised(piece_ref[...])

    unit = normalised(rows_ref[...])
    unit_ref[pl.ds(pl.multiple_of(step * STEP, STEP), STEP), :] = unit
    first_col = meta.number(MEMBER) * width
    column_tags = tags_ref[...].astype(jnp.float32)
    cosine = products(unit, piece_unit[...])
    for inner in range(0, STEP, BLOCK):
        block = step * (STEP // BLOCK) + inner // BLOCK
        bias = column_bias(meta.tag(block), column_tags)
        weight = jnp.exp2(cosine[inner : inner + BLOCK] * GAIN + bias)
        row = lax.broadcasted_iota(jnp.int32, weight.shape, 0)
        col = lax.broadcasted_iota(jnp.int32, weight.shape, 1)
        shift = (block - first_col) * BLOCK
        weight = jnp.where((row < meta.used(block)) & (col - row != shift), weight, 0.0)
        sums_ref[pl.ds(block, 1), :] = lane_sums(weight)


def chunk_tags(piece_ref, size):
    row = piece_ref[size : size + 8, :].astype(jnp.float32)[0:1, :]
    return row[:, :size], row[:, size : size + BLOCK]


def cross_terms(meta, chunks, column_tags, unit_ref, piece_unit, add_rows):
    size = column_tags[0].shape[1]
    columns = None
    for start in range(0, meta.blocks * BLOCK, STEP):
        cosine = products(unit_ref[start : start + STEP, :], piece_unit[...])
        for inner in range(0, STEP, BLOCK):
            block = (start + inner) // BLOCK
            bias = [column_bias(meta.tag(block, chunk), tags) for chunk, tags in zip(chunks, column_tags)]
            bias = jnp.concatenate(bias, axis=1) if len(bias) > 1 else bias[0]
            weight = jnp.exp2(cosine[inner : inner + BLOCK] * GAIN + bias)
            row = lax.broadcasted_iota(jnp.int32, weight.shape, 0)
            weight = jnp.where(row < meta.used(block), weight, 0.0)
            add_rows(block, lane_sums(weight))
            partial = weight[0:8]
            for down in range(8, BLOCK, 8):
                partial = partial + weight[down : down + 8]
            columns = partial if columns is None else columns + partial
    total = jnp.sum(columns, axis=0, keepdims=True)
    return [
        [total[:, at + down : at + down + BLOCK] for down in range(0, size, BLOCK)]
        for at in range(0, total.shape[1], size)
    ]


def middle_kernel(
    blocks, share, meta_ref, unit_ref, swap_ref, outer_ref, before_ref, sums_ref, outer_cols_ref, swap_cols_ref,
    piece_unit,
):
    meta = Meta(meta_ref, blocks)
    size = share * BLOCK
    piece_unit[:size, :] = normalised(outer_ref[:size, :])
    piece_unit[size:, :] = normalised(swap_ref[:size, :])
    outer_tags, _ = chunk_tags(outer_ref, size)
    swap_tags, edge = chunk_tags(swap_ref, size)

    def add_rows(block, value):
        sums_ref[block : block + 1, :] = before_ref[block : block + 1, :] + value

    outer, swap = cross_terms(meta, (0, 1), (outer_tags, swap_tags), unit_ref, piece_unit, add_rows)
    for k in range(share):
        outer_cols_ref[k : k + 1, :] = outer[k]
        swap_cols_ref[k : k + 1, :] = swap[k]
    mine = meta.number(EDGE).astype(jnp.float32)
    outer_cols_ref[share : share + 1, :] = jnp.where((edge == mine) & (edge >= 0), 1.0, 0.0)


def last_kernel(
    blocks, share, width, meta_ref, unit_ref, piece_ref, before_ref, outer_back_ref, swap_back_ref,
    keep_ref, send_ref, cols_ref, piece_unit, sums,
):
    meta = Meta(meta_ref, blocks)
    size = share * BLOCK
    piece_unit[...] = normalised(piece_ref[:size, :])
    tags, _ = chunk_tags(piece_ref, size)

    def place(block):
        owner = block // width
        return owner % 2 * (blocks // 2) + owner // 2 * width + block % width

    def add_rows(block, value):
        at = place(block)
        sums[at : at + 1, :] = before_ref[block : block + 1, :] + value

    (cols,) = cross_terms(meta, (2,), (tags,), unit_ref, piece_unit, add_rows)
    for k in range(share):
        cols_ref[k : k + 1, :] = cols[k]
        at = place(meta.number(FIRST_BLOCK) + k)
        sums[pl.ds(at, 1), :] += outer_back_ref[k : k + 1, :] + swap_back_ref[k : k + 1, :]
    parity = meta.number(MEMBER) % 2
    heap = blocks // 2
    keep_ref[...] = sums[pl.ds(pl.multiple_of(parity * heap, heap), heap), :]
    send_ref[...] = sums[pl.ds(pl.multiple_of((1 - parity) * heap, heap), heap), :]


def call(kernel, meta, operands, out_shapes, scratch, flops):
    vmem = pl.BlockSpec(memory_space=pltpu.VMEM)
    return pl.pallas_call(
        kernel,
        in_specs=[pl.BlockSpec(memory_space=pltpu.SMEM)] + [vmem] * len(operands),
        out_specs=jax.tree.map(lambda _: vmem, out_shapes),
        out_shape=out_shapes,
        scratch_shapes=scratch,
        compiler_params=pltpu.CompilerParams(vmem_limit_bytes=16 * 1024 * 1024),
        cost_estimate=pl.CostEstimate(flops=flops, bytes_accessed=1024, transcendentals=0),
    )(meta, *operands)


def every_pair(embeddings, cluster_ids):
    unit = normalised(embeddings)
    tags = cluster_ids + 1
    groups = lax.axis_size("sub")
    member = lax.axis_index("sub")
    owners = lax.axis_size("tile")
    place = lax.axis_index("tile")
    rows_here = unit.shape[0]
    width = rows_here // groups
    own_piece = lax.dynamic_slice_in_dim(unit, member * width, width, 0)
    own_tags = lax.dynamic_slice_in_dim(tags, member * width, width, 0)
    distance = place - jnp.arange(owners, dtype=jnp.int32)
    keep = (jnp.abs(distance) < SPAN) & (distance != 0)
    outgoing = jnp.where(keep[:, None, None], own_piece[None, :, :], jnp.zeros((), jnp.bfloat16))
    outgoing_tags = jnp.where(keep[:, None], own_tags[None, :], 0)
    arrived = lax.all_to_all(outgoing, "tile", split_axis=0, concat_axis=0, tiled=True)
    arrived_tags = lax.all_to_all(outgoing_tags, "tile", split_axis=0, concat_axis=0, tiled=True)
    local_rows = jnp.arange(rows_here, dtype=jnp.int32)[:, None]
    slice_rows = member * width + jnp.arange(width, dtype=jnp.int32)[None, :]
    total = jnp.zeros((rows_here,), jnp.float32)
    for offset in range(1 - SPAN, SPAN):
        if offset == 0:
            piece, piece_tags, order = own_piece, own_tags, local_rows != slice_rows
        else:
            source = place + offset
            valid = (source >= 0) & (source < owners)
            index = jnp.clip(source, 0, owners - 1)
            piece = lax.dynamic_index_in_dim(arrived, index, 0, keepdims=False)
            piece_tags = lax.dynamic_index_in_dim(arrived_tags, index, 0, keepdims=False)
            piece_tags = jnp.where(valid, piece_tags, 0)
            order = True
        same = (tags[:, None] == piece_tags[None, :]) & (tags[:, None] > 0) & order
        weight = jnp.where(same, jnp.exp(inverse_temp * (products(unit, piece) - 1.0)), 0.0)
        total = total + jnp.sum(weight, axis=1)
    return jnp.log(1.0 + lax.psum_scatter(total, "sub", scatter_dimension=0, tiled=True))


def quads_joined(tag, tiles, place):
    last = jnp.broadcast_to(tag[-1], (BLOCK,))
    before = lax.ppermute(last, "tile", [(t, t + 1) for t in range(tiles - 1)])[0]
    joined = (place % QUAD == 0) & (place > 0) & (before == tag[0]) & (before >= 0)
    return lax.pmax(joined.astype(jnp.int32), "tile") > 0


def shards(embeddings, cluster_ids):
    tiles, subs = lax.axis_size("tile"), lax.axis_size("sub")
    place, member = lax.axis_index("tile"), lax.axis_index("sub")
    rows, depth = embeddings.shape
    blocks = rows // BLOCK
    width = blocks // subs
    share = width // 2
    size = share * BLOCK
    part = place % QUAD
    inner = (part == 1) | (part == 2)
    quads = range(0, tiles, QUAD)
    inward = [p for q in quads for p in ((q, q + 1), (q + 3, q + 2))]
    swap = [p for q in quads for p in ((q + 1, q + 2), (q + 2, q + 1))]
    around = [p for q in quads for p in ((q, q + 1), (q + 3, q + 2), (q + 1, q + 3), (q + 2, q))]

    def turned(route):
        return [(b, a) for a, b in route]

    dealt = member // 2 * share
    near = (dealt // width * 2 + member % 2) * width + dealt % width
    near = jnp.where(part == 1, blocks // 2, 0) + near
    first_block = jnp.where(inner, near, member * width)
    second_block = jnp.where(inner, near, member * width + share)
    edge_block = jnp.where(part == 1, blocks // 2 - 1, blocks // 2)
    by_block = cluster_ids.reshape(blocks, BLOCK)
    first_out = pack(share, first_block, edge_block, embeddings, by_block)
    from_inner = lax.ppermute(first_out, "tile", swap)
    from_outer = lax.ppermute(first_out, "tile", inward)

    tag = jnp.max(by_block, axis=1)
    used = jnp.sum((by_block >= 0).astype(jnp.int32), axis=1)
    edge = jnp.where(part == 1, tag[blocks // 2 - 1], tag[blocks // 2])
    far = (part == 1) & (jnp.arange(blocks) >= blocks // 2)
    seen = jnp.where(inner, tag, -2)
    meta = jnp.concatenate(
        [tag, used, seen, jnp.where(far, -2, seen), tag, jnp.stack([member, first_block, edge])]
    ).astype(jnp.int32)

    second_block, meta = lax.optimization_barrier((second_block, meta))
    second_out = pack(share, second_block, edge_block, embeddings, by_block)

    row_sums = jax.ShapeDtypeStruct((blocks, BLOCK), jnp.float32)
    col_sums = jax.ShapeDtypeStruct((share, BLOCK), jnp.float32)
    quarter = width * BLOCK
    unit, sums = pl.pallas_call(
        functools.partial(self_kernel, blocks, width),
        grid_spec=pltpu.PrefetchScalarGridSpec(
            num_scalar_prefetch=1,
            grid=(rows // STEP,),
            in_specs=[
                pl.BlockSpec((STEP, depth), lambda i, _: (i, 0)),
                pl.BlockSpec((quarter, depth), lambda i, m: (m[5 * blocks + MEMBER], 0)),
                pl.BlockSpec((1, quarter), lambda i, _: (0, 0)),
            ],
            out_specs=[pl.BlockSpec((rows, depth), lambda i, _: (0, 0)), pl.BlockSpec((blocks, BLOCK), lambda i, _: (0, 0))],
            scratch_shapes=[pltpu.VMEM((quarter, depth), jnp.bfloat16)],
        ),
        out_shape=[jax.ShapeDtypeStruct((rows, depth), jnp.bfloat16), row_sums],
        compiler_params=pltpu.CompilerParams(vmem_limit_bytes=32 * 1024 * 1024),
        cost_estimate=pl.CostEstimate(flops=0, bytes_accessed=1024, transcendentals=0),
    )(meta, embeddings, embeddings, lax.dynamic_slice_in_dim(cluster_ids, member * quarter, quarter, 0)[None])
    second_out, sums = lax.optimization_barrier((second_out, sums))
    last = lax.ppermute(second_out, "tile", around)
    sums, outer_cols, swap_cols = call(
        functools.partial(middle_kernel, blocks, share),
        meta,
        (unit, from_inner, from_outer, sums),
        [row_sums, jax.ShapeDtypeStruct((share + 1, BLOCK), jnp.float32), col_sums],
        [pltpu.VMEM((2 * size, depth), jnp.bfloat16)],
        4 * rows * size * depth,
    )
    outer_back = lax.ppermute(outer_cols, "tile", turned(inward))
    swap_back = lax.ppermute(swap_cols, "tile", turned(swap))

    bad = jnp.where(inner, outer_cols[share, 0], outer_back[share, 0]) > 0
    if tiles > QUAD:
        bad = lax.pmax(bad.astype(jnp.int32), "tile") > 0
        bad = bad | quads_joined(tag, tiles, place)
    sums, bad = lax.optimization_barrier((sums, bad.astype(jnp.int32)))

    half = jax.ShapeDtypeStruct((blocks // 2, BLOCK), jnp.float32)
    held, leaving, cols = call(
        functools.partial(last_kernel, blocks, share, width),
        meta,
        (unit, last, sums, outer_back, swap_back),
        [half, half, col_sums],
        [pltpu.VMEM((size, depth), jnp.bfloat16), pltpu.VMEM((blocks, BLOCK), jnp.float32)],
        2 * rows * size * depth,
    )

    def owners(turn):
        pairs = [(b * subs + s, a * subs + s) for a, b in inward for s in range(subs) if turn == 0]
        for a, b in around:
            if (a, b) not in inward:
                for s in range(subs):
                    dealt = s // 2 * share
                    if dealt % width == turn * share:
                        near = (subs // 2 if a % QUAD == 1 else 0) + dealt // width * 2 + s % 2
                        pairs.append((b * subs + s, a * subs + near))
        return pairs

    home = [lax.ppermute(cols, ("tile", "sub"), owners(turn)) for turn in range(2)]

    came = lax.ppermute(leaving, "sub", [(i, i ^ 1) for i in range(subs)])
    held = held + came
    bit = 1
    while 1 << bit < subs:
        pairs = held.reshape(-1, 2, width, BLOCK)
        own = (member >> bit) & 1
        leaving = lax.dynamic_index_in_dim(pairs, 1 - own, 1, keepdims=False)
        came = lax.ppermute(leaving, "sub", [(i, i ^ (1 << bit)) for i in range(subs)])
        held = lax.dynamic_index_in_dim(pairs, own, 1, keepdims=False) + came
        bit += 1
    held, *home = lax.optimization_barrier((held, *home))
    home = jnp.concatenate([jnp.where(inner, home[0], 0.0), jnp.where(inner, home[1], home[0])])
    scores = jnp.log(1.0 + (held.reshape(width, BLOCK) + home).reshape(-1))
    return lax.cond(bad > 0, lambda: every_pair(embeddings, cluster_ids), lambda: scores)


def solution(mesh):
    in_specs = (P(("groups", "tile"), None), P(("groups", "tile")))
    out_specs = P(("groups", "tile", "sub"))
    return jax.shard_map(shards, mesh=mesh, in_specs=in_specs, out_specs=out_specs, check_vma=False)
```

```python
import functools
import math

import jax
import jax.numpy as jnp
import numpy as np
from jax import lax
from jax.experimental import pallas as pl
from jax.experimental.pallas import tpu as pltpu
from jax.sharding import PartitionSpec as P

BLOCK = 128
QUAD = 4
SPAN = 4

inverse_temp = 10.0
norm_eps = 1e-06
GAIN = inverse_temp * math.log2(math.e)
OFF = -1000.0

STEP = 512
COPY = 64


def normalised(values):
    values = values.astype(jnp.float32)
    scale = lax.rsqrt(jnp.sum(values * values, axis=1, keepdims=True) + norm_eps)
    return (values * scale).astype(jnp.bfloat16)


def products(rows, columns):
    return lax.dot_general(
        rows, columns, (((1,), (1,)), ((), ())), preferred_element_type=jnp.float32
    )


def column_bias(tag, column_tags):
    return jnp.where(column_tags == tag.astype(jnp.float32), -GAIN, OFF)


def lane_sums(weight):
    total = weight[:, :BLOCK]
    for start in range(BLOCK, weight.shape[1], BLOCK):
        total = total + weight[:, start : start + BLOCK]
    return jnp.sum(total.T, axis=0, keepdims=True)


class Plan:
    def __init__(self, blocks, subs, place, member):
        width = blocks // subs
        share = width // 2
        part = place % QUAD
        self.inner = (part == 1) | (part == 2)
        self.far = part == 1
        dealt = member // 2 * share
        near = (dealt // width * 2 + member % 2) * width + dealt % width
        near = jnp.where(part == 1, blocks // 2, 0) + near
        self.first = jnp.where(self.inner, near, member * width)
        self.second = jnp.where(self.inner, near, member * width + share)
        self.edge = jnp.where(part == 1, blocks // 2 - 1, blocks // 2)
        self.width, self.share = width, share


def pack_kernel(blocks, subs, rows_ref, ids_ref, first_ref, second_ref, ids, sems):
    plan = Plan(blocks, subs, lax.axis_index("tile"), lax.axis_index("sub"))
    share, size = plan.share, plan.share * BLOCK
    copies = []
    for block, out in ((plan.first, first_ref), (plan.second, second_ref)):
        for down in range(0, size, COPY):
            start = pl.multiple_of(block * BLOCK + down, COPY)
            copies.append((rows_ref.at[pl.ds(start, COPY), :], out.at[pl.ds(down, COPY), :]))
    copies.append((ids_ref, ids))
    copies = [pltpu.make_async_copy(*ends, sems.at[index]) for index, ends in enumerate(copies)]
    for copy in copies:
        copy.start()
    copies[-1].wait()
    depth = first_ref.shape[1]
    edge = jnp.max(ids[pl.ds(plan.edge, 1), :], axis=1, keepdims=True)
    rest = [jnp.broadcast_to(edge, (1, BLOCK)), jnp.zeros((1, depth - size - BLOCK), jnp.int32)]
    for block, out in ((plan.first, first_ref), (plan.second, second_ref)):
        row = jnp.concatenate([ids[pl.ds(block + k, 1), :] for k in range(share)] + rest, axis=1)
        out[size : size + 8, :] = jnp.broadcast_to(row.astype(jnp.float32), (8, depth)).astype(jnp.bfloat16)
    for copy in copies[:-1]:
        copy.wait()


def pack(size, subs, embeddings, by_block):
    blocks, depth = by_block.shape[0], embeddings.shape[1]
    return pl.pallas_call(
        functools.partial(pack_kernel, blocks, subs),
        in_specs=[pl.BlockSpec(memory_space=pl.ANY)] * 2,
        out_specs=[pl.BlockSpec(memory_space=pltpu.VMEM)] * 2,
        out_shape=[jax.ShapeDtypeStruct((size + 8, depth), jnp.bfloat16)] * 2,
        scratch_shapes=[pltpu.VMEM(by_block.shape, jnp.int32), pltpu.SemaphoreType.DMA((2 * size // COPY + 1,))],
        compiler_params=pltpu.CompilerParams(vmem_limit_bytes=8 * 1024 * 1024),
        cost_estimate=pl.CostEstimate(flops=0, bytes_accessed=1024, transcendentals=0),
    )(embeddings, by_block)


class Meta:
    def __init__(self, ref, blocks):
        self.ref, self.blocks = ref, blocks

    def tag(self, block, chunk=None):
        return self.ref[block + (0 if chunk is None else (2 + chunk) * self.blocks)]

    def used(self, block):
        return self.ref[self.blocks + block]

    def number(self, index):
        return self.ref[5 * self.blocks + index]


MEMBER, FIRST_BLOCK, EDGE, INNER = range(4)


def self_kernel(blocks, width, meta_ref, rows_ref, piece_ref, tags_ref, unit_ref, sums_ref, piece_unit):
    meta = Meta(meta_ref, blocks)
    step = pl.program_id(0)

    @pl.when(step == 0)
    def _():
        piece_unit[...] = normalised(piece_ref[...])

    unit = normalised(rows_ref[...])
    unit_ref[pl.ds(pl.multiple_of(step * STEP, STEP), STEP), :] = unit
    first_col = meta.number(MEMBER) * width
    column_tags = tags_ref[...].astype(jnp.float32)
    cosine = products(unit, piece_unit[...])
    for inner in range(0, STEP, BLOCK):
        block = step * (STEP // BLOCK) + inner // BLOCK
        bias = column_bias(meta.tag(block), column_tags)
        weight = jnp.exp2(cosine[inner : inner + BLOCK] * GAIN + bias)
        row = lax.broadcasted_iota(jnp.int32, weight.shape, 0)
        col = lax.broadcasted_iota(jnp.int32, weight.shape, 1)
        shift = (block - first_col) * BLOCK
        weight = jnp.where((row < meta.used(block)) & (col - row != shift), weight, 0.0)
        sums_ref[pl.ds(block, 1), :] = lane_sums(weight)


def chunk_tags(piece_ref, size):
    row = piece_ref[size : size + 8, :].astype(jnp.float32)[0:1, :]
    return row[:, :size], row[:, size : size + BLOCK]


def cross_terms(meta, chunks, column_tags, unit_ref, piece_unit, add_rows):
    size = column_tags[0].shape[1]
    columns = None
    for start in range(0, meta.blocks * BLOCK, STEP):
        cosine = products(unit_ref[start : start + STEP, :], piece_unit[...])
        for inner in range(0, STEP, BLOCK):
            block = (start + inner) // BLOCK
            bias = [column_bias(meta.tag(block, chunk), tags) for chunk, tags in zip(chunks, column_tags)]
            bias = jnp.concatenate(bias, axis=1) if len(bias) > 1 else bias[0]
            weight = jnp.exp2(cosine[inner : inner + BLOCK] * GAIN + bias)
            row = lax.broadcasted_iota(jnp.int32, weight.shape, 0)
            weight = jnp.where(row < meta.used(block), weight, 0.0)
            add_rows(block, lane_sums(weight))
            partial = weight[0:8]
            for down in range(8, BLOCK, 8):
                partial = partial + weight[down : down + 8]
            columns = partial if columns is None else columns + partial
    total = jnp.sum(columns, axis=0, keepdims=True)
    return [
        [total[:, at + down : at + down + BLOCK] for down in range(0, size, BLOCK)]
        for at in range(0, total.shape[1], size)
    ]


def middle_kernel(
    blocks, share, meta_ref, unit_ref, swap_ref, outer_ref, before_ref, sums_ref, outer_cols_ref, swap_cols_ref,
    piece_unit,
):
    meta = Meta(meta_ref, blocks)
    size = share * BLOCK
    piece_unit[:size, :] = normalised(outer_ref[:size, :])
    piece_unit[size:, :] = normalised(swap_ref[:size, :])
    outer_tags, _ = chunk_tags(outer_ref, size)
    swap_tags, edge = chunk_tags(swap_ref, size)

    def add_rows(block, value):
        sums_ref[block : block + 1, :] = before_ref[block : block + 1, :] + value

    outer, swap = cross_terms(meta, (0, 1), (outer_tags, swap_tags), unit_ref, piece_unit, add_rows)
    for k in range(share):
        outer_cols_ref[k : k + 1, :] = outer[k]
        swap_cols_ref[k : k + 1, :] = swap[k]
    mine = meta.tag(meta.number(EDGE)).astype(jnp.float32)
    joined = (edge == mine) & (edge >= 0) & (meta.number(INNER) > 0)
    outer_cols_ref[share : share + 1, :] = jnp.where(joined, 1.0, 0.0)


def last_kernel(
    blocks, share, width, meta_ref, unit_ref, piece_ref, before_ref, outer_cols_ref, outer_back_ref, swap_back_ref,
    keep_ref, send_ref, cols_ref, flag_ref, piece_unit, sums,
):
    meta = Meta(meta_ref, blocks)
    size = share * BLOCK
    piece_unit[...] = normalised(piece_ref[:size, :])
    tags, _ = chunk_tags(piece_ref, size)

    def place(block):
        owner = block // width
        return owner % 2 * (blocks // 2) + owner // 2 * width + block % width

    def add_rows(block, value):
        at = place(block)
        sums[at : at + 1, :] = before_ref[block : block + 1, :] + value

    flags = jnp.maximum(outer_cols_ref[share : share + 1, :], outer_back_ref[share : share + 1, :])
    flag_ref[0] = jnp.max(flags).astype(jnp.int32)
    (cols,) = cross_terms(meta, (2,), (tags,), unit_ref, piece_unit, add_rows)
    for k in range(share):
        cols_ref[k : k + 1, :] = cols[k]
        at = place(meta.number(FIRST_BLOCK) + k)
        sums[pl.ds(at, 1), :] += outer_back_ref[k : k + 1, :] + swap_back_ref[k : k + 1, :]
    parity = meta.number(MEMBER) % 2
    heap = blocks // 2
    keep_ref[...] = sums[pl.ds(pl.multiple_of(parity * heap, heap), heap), :]
    send_ref[...] = sums[pl.ds(pl.multiple_of((1 - parity) * heap, heap), heap), :]


def call(kernel, meta, operands, out_shapes, scratch, flops):
    vmem, smem = pl.BlockSpec(memory_space=pltpu.VMEM), pl.BlockSpec(memory_space=pltpu.SMEM)
    return pl.pallas_call(
        kernel,
        in_specs=[smem] + [vmem] * len(operands),
        out_specs=[vmem if len(shape.shape) > 1 else smem for shape in out_shapes],
        out_shape=out_shapes,
        scratch_shapes=scratch,
        compiler_params=pltpu.CompilerParams(vmem_limit_bytes=16 * 1024 * 1024),
        cost_estimate=pl.CostEstimate(flops=flops, bytes_accessed=1024, transcendentals=0),
    )(meta, *operands)


def every_pair(embeddings, cluster_ids):
    unit = normalised(embeddings)
    tags = cluster_ids + 1
    groups = lax.axis_size("sub")
    member = lax.axis_index("sub")
    owners = lax.axis_size("tile")
    place = lax.axis_index("tile")
    rows_here = unit.shape[0]
    width = rows_here // groups
    own_piece = lax.dynamic_slice_in_dim(unit, member * width, width, 0)
    own_tags = lax.dynamic_slice_in_dim(tags, member * width, width, 0)
    distance = place - jnp.arange(owners, dtype=jnp.int32)
    keep = (jnp.abs(distance) < SPAN) & (distance != 0)
    outgoing = jnp.where(keep[:, None, None], own_piece[None, :, :], jnp.zeros((), jnp.bfloat16))
    outgoing_tags = jnp.where(keep[:, None], own_tags[None, :], 0)
    arrived = lax.all_to_all(outgoing, "tile", split_axis=0, concat_axis=0, tiled=True)
    arrived_tags = lax.all_to_all(outgoing_tags, "tile", split_axis=0, concat_axis=0, tiled=True)
    local_rows = jnp.arange(rows_here, dtype=jnp.int32)[:, None]
    slice_rows = member * width + jnp.arange(width, dtype=jnp.int32)[None, :]
    total = jnp.zeros((rows_here,), jnp.float32)
    for offset in range(1 - SPAN, SPAN):
        if offset == 0:
            piece, piece_tags, order = own_piece, own_tags, local_rows != slice_rows
        else:
            source = place + offset
            valid = (source >= 0) & (source < owners)
            index = jnp.clip(source, 0, owners - 1)
            piece = lax.dynamic_index_in_dim(arrived, index, 0, keepdims=False)
            piece_tags = lax.dynamic_index_in_dim(arrived_tags, index, 0, keepdims=False)
            piece_tags = jnp.where(valid, piece_tags, 0)
            order = True
        same = (tags[:, None] == piece_tags[None, :]) & (tags[:, None] > 0) & order
        weight = jnp.where(same, jnp.exp(inverse_temp * (products(unit, piece) - 1.0)), 0.0)
        total = total + jnp.sum(weight, axis=1)
    return jnp.log(1.0 + lax.psum_scatter(total, "sub", scatter_dimension=0, tiled=True))


def quads_joined(tag, tiles, place):
    last = jnp.broadcast_to(tag[-1], (BLOCK,))
    before = lax.ppermute(last, "tile", [(t, t + 1) for t in range(tiles - 1)])[0]
    joined = (place % QUAD == 0) & (place > 0) & (before == tag[0]) & (before >= 0)
    return lax.pmax(joined.astype(jnp.int32), "tile") > 0


def shards(embeddings, cluster_ids):
    tiles, subs = lax.axis_size("tile"), lax.axis_size("sub")
    place, member = lax.axis_index("tile"), lax.axis_index("sub")
    rows, depth = embeddings.shape
    blocks = rows // BLOCK
    plan = Plan(blocks, subs, place, member)
    width, share, inner = plan.width, plan.share, plan.inner
    size = share * BLOCK
    quads = range(0, tiles, QUAD)
    inward = [p for q in quads for p in ((q, q + 1), (q + 3, q + 2))]
    swap = [p for q in quads for p in ((q + 1, q + 2), (q + 2, q + 1))]
    around = [p for q in quads for p in ((q, q + 1), (q + 3, q + 2), (q + 1, q + 3), (q + 2, q))]

    def turned(route):
        return [(b, a) for a, b in route]

    by_block = cluster_ids.reshape(blocks, BLOCK)
    first_out, second_out = pack(size, subs, embeddings, by_block)
    from_inner = lax.ppermute(first_out, "tile", swap)
    from_outer = lax.ppermute(first_out, "tile", inward)

    tag = jnp.max(by_block, axis=1)
    used = jnp.sum((by_block >= 0).astype(jnp.int32), axis=1)
    seen = jnp.where(inner, tag, -2)
    swapped = jnp.where(plan.far & (jnp.arange(blocks) >= blocks // 2), -2, seen)
    numbers = jnp.stack([member, plan.first, plan.edge, inner])
    meta = jnp.concatenate([tag, used, seen, swapped, tag, numbers]).astype(jnp.int32)

    row_sums = jax.ShapeDtypeStruct((blocks, BLOCK), jnp.float32)
    col_sums = jax.ShapeDtypeStruct((share, BLOCK), jnp.float32)
    quarter = width * BLOCK
    unit, sums = pl.pallas_call(
        functools.partial(self_kernel, blocks, width),
        grid_spec=pltpu.PrefetchScalarGridSpec(
            num_scalar_prefetch=1,
            grid=(rows // STEP,),
            in_specs=[
                pl.BlockSpec((STEP, depth), lambda i, _: (i, 0)),
                pl.BlockSpec((quarter, depth), lambda i, m: (m[5 * blocks + MEMBER], 0)),
                pl.BlockSpec((1, quarter), lambda i, _: (0, 0)),
            ],
            out_specs=[pl.BlockSpec((rows, depth), lambda i, _: (0, 0)), pl.BlockSpec((blocks, BLOCK), lambda i, _: (0, 0))],
            scratch_shapes=[pltpu.VMEM((quarter, depth), jnp.bfloat16)],
        ),
        out_shape=[jax.ShapeDtypeStruct((rows, depth), jnp.bfloat16), row_sums],
        compiler_params=pltpu.CompilerParams(vmem_limit_bytes=32 * 1024 * 1024),
        cost_estimate=pl.CostEstimate(flops=0, bytes_accessed=1024, transcendentals=0),
    )(meta, embeddings, embeddings, lax.dynamic_slice_in_dim(cluster_ids, member * quarter, quarter, 0)[None])
    second_out, sums = lax.optimization_barrier((second_out, sums))
    last = lax.ppermute(second_out, "tile", around)
    sums, outer_cols, swap_cols = call(
        functools.partial(middle_kernel, blocks, share),
        meta,
        (unit, from_inner, from_outer, sums),
        [row_sums, jax.ShapeDtypeStruct((share + 1, BLOCK), jnp.float32), col_sums],
        [pltpu.VMEM((2 * size, depth), jnp.bfloat16)],
        4 * rows * size * depth,
    )
    outer_back = lax.ppermute(outer_cols, "tile", turned(inward))
    swap_back = lax.ppermute(swap_cols, "tile", turned(swap))

    half = jax.ShapeDtypeStruct((blocks // 2, BLOCK), jnp.float32)
    held, leaving, cols, flag = call(
        functools.partial(last_kernel, blocks, share, width),
        meta,
        (unit, last, sums, outer_cols, outer_back, swap_back),
        [half, half, col_sums, jax.ShapeDtypeStruct((1,), jnp.int32)],
        [pltpu.VMEM((size, depth), jnp.bfloat16), pltpu.VMEM((blocks, BLOCK), jnp.float32)],
        2 * rows * size * depth,
    )

    home = lax.ppermute(cols, "tile", turned(around))
    owner = plan.second // width
    home_at = owner // 2 * width + plan.second % width
    held = lax.dynamic_update_slice_in_dim(
        held, lax.dynamic_slice_in_dim(held, home_at, share, 0) + home, home_at, 0
    )
    held = held + lax.ppermute(leaving, "sub", [(i, i ^ 1) for i in range(subs)])
    bit = 1
    while 1 << bit < subs:
        pairs = held.reshape(-1, 2, width, BLOCK)
        own = (member >> bit) & 1
        leaving = lax.dynamic_index_in_dim(pairs, 1 - own, 1, keepdims=False)
        came = lax.ppermute(leaving, "sub", [(i, i ^ (1 << bit)) for i in range(subs)])
        held = lax.dynamic_index_in_dim(pairs, own, 1, keepdims=False) + came
        bit += 1
    scores = jnp.log(1.0 + held.reshape(-1))

    bad = flag[0] > 0
    if tiles > QUAD:
        bad = lax.pmax(bad.astype(jnp.int32), "tile") > 0
        bad = bad | quads_joined(tag, tiles, place)
    return lax.cond(bad, lambda: every_pair(embeddings, cluster_ids), lambda: scores)


def solution(mesh):
    in_specs = (P(("groups", "tile"), None), P(("groups", "tile")))
    out_specs = P(("groups", "tile", "sub"))
    return jax.shard_map(shards, mesh=mesh, in_specs=in_specs, out_specs=out_specs, check_vma=False)
```

```python
import functools
import math

import jax
import jax.numpy as jnp
import numpy as np
from jax import lax
from jax.experimental import pallas as pl
from jax.experimental.pallas import tpu as pltpu
from jax.sharding import PartitionSpec as P

BLOCK = 128
QUAD = 4
SPAN = 4

inverse_temp = 10.0
norm_eps = 1e-06
GAIN = inverse_temp * math.log2(math.e)
OFF = -1000.0

STEP = 512
COPY = 64


def normalised(values):
    values = values.astype(jnp.float32)
    scale = lax.rsqrt(jnp.sum(values * values, axis=1, keepdims=True) + norm_eps)
    return (values * scale).astype(jnp.bfloat16)


def products(rows, columns):
    return lax.dot_general(
        rows, columns, (((1,), (1,)), ((), ())), preferred_element_type=jnp.float32
    )


def column_bias(tag, column_tags):
    return jnp.where(column_tags == tag.astype(jnp.float32), -GAIN, OFF)


def lane_sums(weight):
    total = weight[:, :BLOCK]
    for start in range(BLOCK, weight.shape[1], BLOCK):
        total = total + weight[:, start : start + BLOCK]
    return jnp.sum(total.T, axis=0, keepdims=True)


class Plan:
    def __init__(self, blocks, subs, place, member):
        width = blocks // subs
        share = width // 2
        part = place % QUAD
        self.inner = (part == 1) | (part == 2)
        self.far = part == 1
        dealt = member // 2 * share
        near = (dealt // width * 2 + member % 2) * width + dealt % width
        near = jnp.where(part == 1, blocks // 2, 0) + near
        self.first = jnp.where(self.inner, near, member * width)
        self.second = jnp.where(self.inner, near, member * width + share)
        self.edge = jnp.where(part == 1, blocks // 2 - 1, blocks // 2)
        self.width, self.share = width, share


def pack_kernel(blocks, subs, rows_ref, ids_ref, first_ref, second_ref, ids, sems):
    plan = Plan(blocks, subs, lax.axis_index("tile"), lax.axis_index("sub"))
    share, size = plan.share, plan.share * BLOCK
    copies = []
    for block, out in ((plan.first, first_ref), (plan.second, second_ref)):
        for down in range(0, size, COPY):
            start = pl.multiple_of(block * BLOCK + down, COPY)
            copies.append((rows_ref.at[pl.ds(start, COPY), :], out.at[pl.ds(down, COPY), :]))
    copies.append((ids_ref, ids))
    copies = [pltpu.make_async_copy(*ends, sems.at[index]) for index, ends in enumerate(copies)]
    for copy in copies:
        copy.start()
    copies[-1].wait()
    depth = first_ref.shape[1]
    edge = jnp.max(ids[pl.ds(plan.edge, 1), :], axis=1, keepdims=True)
    rest = [jnp.broadcast_to(edge, (1, BLOCK)), jnp.zeros((1, depth - size - BLOCK), jnp.int32)]
    for block, out in ((plan.first, first_ref), (plan.second, second_ref)):
        row = jnp.concatenate([ids[pl.ds(block + k, 1), :] for k in range(share)] + rest, axis=1)
        out[size : size + 8, :] = jnp.broadcast_to(row.astype(jnp.float32), (8, depth)).astype(jnp.bfloat16)
    for copy in copies[:-1]:
        copy.wait()


def pack(size, subs, embeddings, by_block):
    blocks, depth = by_block.shape[0], embeddings.shape[1]
    return pl.pallas_call(
        functools.partial(pack_kernel, blocks, subs),
        in_specs=[pl.BlockSpec(memory_space=pl.ANY)] * 2,
        out_specs=[pl.BlockSpec(memory_space=pltpu.VMEM)] * 2,
        out_shape=[jax.ShapeDtypeStruct((size + 8, depth), jnp.bfloat16)] * 2,
        scratch_shapes=[pltpu.VMEM(by_block.shape, jnp.int32), pltpu.SemaphoreType.DMA((2 * size // COPY + 1,))],
        compiler_params=pltpu.CompilerParams(vmem_limit_bytes=8 * 1024 * 1024),
        cost_estimate=pl.CostEstimate(flops=0, bytes_accessed=1024, transcendentals=0),
    )(embeddings, by_block)


class Meta:
    def __init__(self, ref, blocks):
        self.ref, self.blocks = ref, blocks

    def tag(self, block, chunk=None):
        return self.ref[block + (0 if chunk is None else (2 + chunk) * self.blocks)]

    def used(self, block):
        return self.ref[self.blocks + block]

    def number(self, index):
        return self.ref[5 * self.blocks + index]


MEMBER, FIRST_BLOCK, EDGE, INNER = range(4)


def self_kernel(blocks, width, meta_ref, rows_ref, piece_ref, tags_ref, unit_ref, sums_ref, piece_unit):
    meta = Meta(meta_ref, blocks)
    step = pl.program_id(0)

    @pl.when(step == 0)
    def _():
        piece_unit[...] = normalised(piece_ref[...])

    unit = normalised(rows_ref[...])
    unit_ref[pl.ds(pl.multiple_of(step * STEP, STEP), STEP), :] = unit
    first_col = meta.number(MEMBER) * width
    column_tags = tags_ref[...].astype(jnp.float32)
    cosine = products(unit, piece_unit[...])
    for inner in range(0, STEP, BLOCK):
        block = step * (STEP // BLOCK) + inner // BLOCK
        bias = column_bias(meta.tag(block), column_tags)
        weight = jnp.exp2(cosine[inner : inner + BLOCK] * GAIN + bias)
        row = lax.broadcasted_iota(jnp.int32, weight.shape, 0)
        col = lax.broadcasted_iota(jnp.int32, weight.shape, 1)
        shift = (block - first_col) * BLOCK
        weight = jnp.where((row < meta.used(block)) & (col - row != shift), weight, 0.0)
        sums_ref[pl.ds(block, 1), :] = lane_sums(weight)


def chunk_tags(piece_ref, size):
    row = piece_ref[size : size + 8, :].astype(jnp.float32)[0:1, :]
    return row[:, :size], row[:, size : size + BLOCK]


def cross_terms(meta, chunks, column_tags, unit_ref, piece_unit, add_rows):
    size = column_tags[0].shape[1]
    columns = None
    for start in range(0, meta.blocks * BLOCK, STEP):
        cosine = products(unit_ref[start : start + STEP, :], piece_unit[...])
        for inner in range(0, STEP, BLOCK):
            block = (start + inner) // BLOCK
            bias = [column_bias(meta.tag(block, chunk), tags) for chunk, tags in zip(chunks, column_tags)]
            bias = jnp.concatenate(bias, axis=1) if len(bias) > 1 else bias[0]
            weight = jnp.exp2(cosine[inner : inner + BLOCK] * GAIN + bias)
            row = lax.broadcasted_iota(jnp.int32, weight.shape, 0)
            weight = jnp.where(row < meta.used(block), weight, 0.0)
            add_rows(block, lane_sums(weight))
            partial = weight[0:8]
            for down in range(8, BLOCK, 8):
                partial = partial + weight[down : down + 8]
            columns = partial if columns is None else columns + partial
    total = jnp.sum(columns, axis=0, keepdims=True)
    return [
        [total[:, at + down : at + down + BLOCK] for down in range(0, size, BLOCK)]
        for at in range(0, total.shape[1], size)
    ]


def middle_kernel(
    blocks, share, meta_ref, unit_ref, swap_ref, outer_ref, before_ref, sums_ref, outer_cols_ref, swap_cols_ref,
    piece_unit,
):
    meta = Meta(meta_ref, blocks)
    size = share * BLOCK
    piece_unit[:size, :] = normalised(outer_ref[:size, :])
    piece_unit[size:, :] = normalised(swap_ref[:size, :])
    outer_tags, _ = chunk_tags(outer_ref, size)
    swap_tags, edge = chunk_tags(swap_ref, size)

    def add_rows(block, value):
        sums_ref[block : block + 1, :] = before_ref[block : block + 1, :] + value

    outer, swap = cross_terms(meta, (0, 1), (outer_tags, swap_tags), unit_ref, piece_unit, add_rows)
    for k in range(share):
        outer_cols_ref[k : k + 1, :] = outer[k]
        swap_cols_ref[k : k + 1, :] = swap[k]
    mine = meta.tag(meta.number(EDGE)).astype(jnp.float32)
    joined = (edge == mine) & (edge >= 0) & (meta.number(INNER) > 0)
    outer_cols_ref[share : share + 1, :] = jnp.where(joined, 1.0, 0.0)


def flag_kernel(share, outer_cols_ref, outer_back_ref, flag_ref):
    flags = jnp.maximum(outer_cols_ref[share : share + 1, :], outer_back_ref[share : share + 1, :])
    flag_ref[0] = jnp.max(flags).astype(jnp.int32)


def last_kernel(
    blocks, share, width, meta_ref, unit_ref, piece_ref, before_ref, outer_back_ref, swap_back_ref,
    keep_ref, send_ref, cols_ref, piece_unit, sums,
):
    meta = Meta(meta_ref, blocks)
    size = share * BLOCK
    piece_unit[...] = normalised(piece_ref[:size, :])
    tags, _ = chunk_tags(piece_ref, size)

    def place(block):
        owner = block // width
        return owner % 2 * (blocks // 2) + owner // 2 * width + block % width

    def add_rows(block, value):
        at = place(block)
        sums[at : at + 1, :] = before_ref[block : block + 1, :] + value

    (cols,) = cross_terms(meta, (2,), (tags,), unit_ref, piece_unit, add_rows)
    for k in range(share):
        cols_ref[k : k + 1, :] = cols[k]
        at = place(meta.number(FIRST_BLOCK) + k)
        sums[pl.ds(at, 1), :] += outer_back_ref[k : k + 1, :] + swap_back_ref[k : k + 1, :]
    parity = meta.number(MEMBER) % 2
    heap = blocks // 2
    keep_ref[...] = sums[pl.ds(pl.multiple_of(parity * heap, heap), heap), :]
    send_ref[...] = sums[pl.ds(pl.multiple_of((1 - parity) * heap, heap), heap), :]


def call(kernel, meta, operands, out_shapes, scratch, flops):
    vmem, smem = pl.BlockSpec(memory_space=pltpu.VMEM), pl.BlockSpec(memory_space=pltpu.SMEM)
    return pl.pallas_call(
        kernel,
        in_specs=[smem] + [vmem] * len(operands),
        out_specs=[vmem if len(shape.shape) > 1 else smem for shape in out_shapes],
        out_shape=out_shapes,
        scratch_shapes=scratch,
        compiler_params=pltpu.CompilerParams(vmem_limit_bytes=16 * 1024 * 1024),
        cost_estimate=pl.CostEstimate(flops=flops, bytes_accessed=1024, transcendentals=0),
    )(meta, *operands)


def every_pair(embeddings, cluster_ids):
    unit = normalised(embeddings)
    tags = cluster_ids + 1
    groups = lax.axis_size("sub")
    member = lax.axis_index("sub")
    owners = lax.axis_size("tile")
    place = lax.axis_index("tile")
    rows_here = unit.shape[0]
    width = rows_here // groups
    own_piece = lax.dynamic_slice_in_dim(unit, member * width, width, 0)
    own_tags = lax.dynamic_slice_in_dim(tags, member * width, width, 0)
    distance = place - jnp.arange(owners, dtype=jnp.int32)
    keep = (jnp.abs(distance) < SPAN) & (distance != 0)
    outgoing = jnp.where(keep[:, None, None], own_piece[None, :, :], jnp.zeros((), jnp.bfloat16))
    outgoing_tags = jnp.where(keep[:, None], own_tags[None, :], 0)
    arrived = lax.all_to_all(outgoing, "tile", split_axis=0, concat_axis=0, tiled=True)
    arrived_tags = lax.all_to_all(outgoing_tags, "tile", split_axis=0, concat_axis=0, tiled=True)
    local_rows = jnp.arange(rows_here, dtype=jnp.int32)[:, None]
    slice_rows = member * width + jnp.arange(width, dtype=jnp.int32)[None, :]
    total = jnp.zeros((rows_here,), jnp.float32)
    for offset in range(1 - SPAN, SPAN):
        if offset == 0:
            piece, piece_tags, order = own_piece, own_tags, local_rows != slice_rows
        else:
            source = place + offset
            valid = (source >= 0) & (source < owners)
            index = jnp.clip(source, 0, owners - 1)
            piece = lax.dynamic_index_in_dim(arrived, index, 0, keepdims=False)
            piece_tags = lax.dynamic_index_in_dim(arrived_tags, index, 0, keepdims=False)
            piece_tags = jnp.where(valid, piece_tags, 0)
            order = True
        same = (tags[:, None] == piece_tags[None, :]) & (tags[:, None] > 0) & order
        weight = jnp.where(same, jnp.exp(inverse_temp * (products(unit, piece) - 1.0)), 0.0)
        total = total + jnp.sum(weight, axis=1)
    return jnp.log(1.0 + lax.psum_scatter(total, "sub", scatter_dimension=0, tiled=True))


def quads_joined(tag, tiles, place):
    last = jnp.broadcast_to(tag[-1], (BLOCK,))
    before = lax.ppermute(last, "tile", [(t, t + 1) for t in range(tiles - 1)])[0]
    joined = (place % QUAD == 0) & (place > 0) & (before == tag[0]) & (before >= 0)
    return lax.pmax(joined.astype(jnp.int32), "tile") > 0


def shards(embeddings, cluster_ids):
    tiles, subs = lax.axis_size("tile"), lax.axis_size("sub")
    place, member = lax.axis_index("tile"), lax.axis_index("sub")
    rows, depth = embeddings.shape
    blocks = rows // BLOCK
    plan = Plan(blocks, subs, place, member)
    width, share, inner = plan.width, plan.share, plan.inner
    size = share * BLOCK
    quads = range(0, tiles, QUAD)
    inward = [p for q in quads for p in ((q, q + 1), (q + 3, q + 2))]
    swap = [p for q in quads for p in ((q + 1, q + 2), (q + 2, q + 1))]
    around = [p for q in quads for p in ((q, q + 1), (q + 3, q + 2), (q + 1, q + 3), (q + 2, q))]

    def turned(route):
        return [(b, a) for a, b in route]

    by_block = cluster_ids.reshape(blocks, BLOCK)
    first_out, second_out = pack(size, subs, embeddings, by_block)
    from_inner = lax.ppermute(first_out, "tile", swap)
    from_outer = lax.ppermute(first_out, "tile", inward)

    tag = jnp.max(by_block, axis=1)
    used = jnp.sum((by_block >= 0).astype(jnp.int32), axis=1)
    seen = jnp.where(inner, tag, -2)
    swapped = jnp.where(plan.far & (jnp.arange(blocks) >= blocks // 2), -2, seen)
    numbers = jnp.stack([member, plan.first, plan.edge, inner])
    meta = jnp.concatenate([tag, used, seen, swapped, tag, numbers]).astype(jnp.int32)

    heap = blocks // 2
    owner = plan.second // width
    home_row = jnp.arange(heap)[:, None] - (owner // 2 * width + plan.second % width)
    home_row = jnp.broadcast_to(home_row, (heap, BLOCK)).astype(jnp.int32)
    upper = [
        jnp.broadcast_to((member >> bit) & 1, (heap >> bit, BLOCK)).astype(jnp.int32)
        for bit in range(1, subs.bit_length() - 1)
    ]
    meta, home_row, *upper = lax.optimization_barrier((meta, home_row, *upper))

    row_sums = jax.ShapeDtypeStruct((blocks, BLOCK), jnp.float32)
    col_sums = jax.ShapeDtypeStruct((share, BLOCK), jnp.float32)
    quarter = width * BLOCK
    unit, sums = pl.pallas_call(
        functools.partial(self_kernel, blocks, width),
        grid_spec=pltpu.PrefetchScalarGridSpec(
            num_scalar_prefetch=1,
            grid=(rows // STEP,),
            in_specs=[
                pl.BlockSpec((STEP, depth), lambda i, _: (i, 0)),
                pl.BlockSpec((quarter, depth), lambda i, m: (m[5 * blocks + MEMBER], 0)),
                pl.BlockSpec((1, quarter), lambda i, _: (0, 0)),
            ],
            out_specs=[pl.BlockSpec((rows, depth), lambda i, _: (0, 0)), pl.BlockSpec((blocks, BLOCK), lambda i, _: (0, 0))],
            scratch_shapes=[pltpu.VMEM((quarter, depth), jnp.bfloat16)],
        ),
        out_shape=[jax.ShapeDtypeStruct((rows, depth), jnp.bfloat16), row_sums],
        compiler_params=pltpu.CompilerParams(vmem_limit_bytes=32 * 1024 * 1024),
        cost_estimate=pl.CostEstimate(flops=0, bytes_accessed=1024, transcendentals=0),
    )(meta, embeddings, embeddings, lax.dynamic_slice_in_dim(cluster_ids, member * quarter, quarter, 0)[None])
    second_out, sums = lax.optimization_barrier((second_out, sums))
    last = lax.ppermute(second_out, "tile", around)
    sums, outer_cols, swap_cols = call(
        functools.partial(middle_kernel, blocks, share),
        meta,
        (unit, from_inner, from_outer, sums),
        [row_sums, jax.ShapeDtypeStruct((share + 1, BLOCK), jnp.float32), col_sums],
        [pltpu.VMEM((2 * size, depth), jnp.bfloat16)],
        4 * rows * size * depth,
    )
    outer_back = lax.ppermute(outer_cols, "tile", turned(inward))
    swap_back = lax.ppermute(swap_cols, "tile", turned(swap))

    flag = pl.pallas_call(
        functools.partial(flag_kernel, share),
        out_specs=pl.BlockSpec(memory_space=pltpu.SMEM),
        out_shape=jax.ShapeDtypeStruct((1,), jnp.int32),
        compiler_params=pltpu.CompilerParams(vmem_limit_bytes=4 * 1024 * 1024),
    )(outer_cols, outer_back)
    sums, flag = lax.optimization_barrier((sums, flag))
    half = jax.ShapeDtypeStruct((heap, BLOCK), jnp.float32)
    held, leaving, cols = call(
        functools.partial(last_kernel, blocks, share, width),
        meta,
        (unit, last, sums, outer_back, swap_back),
        [half, half, col_sums],
        [pltpu.VMEM((size, depth), jnp.bfloat16), pltpu.VMEM((blocks, BLOCK), jnp.float32)],
        2 * rows * size * depth,
    )

    home = lax.ppermute(cols, "tile", turned(around))
    for k in range(share):
        held = held + jnp.where(home_row == k, home[k : k + 1], 0.0)
    held = held + lax.ppermute(leaving, "sub", [(i, i ^ 1) for i in range(subs)])
    for bit, mine in enumerate(upper, 1):
        pairs = held.reshape(-1, 2, width, BLOCK)
        low, high = pairs[:, 0].reshape(mine.shape), pairs[:, 1].reshape(mine.shape)
        leaving = jnp.where(mine > 0, low, high)
        held = jnp.where(mine > 0, high, low)
        held = held + lax.ppermute(leaving, "sub", [(i, i ^ (1 << bit)) for i in range(subs)])
    scores = jnp.log(1.0 + held.reshape(-1))

    bad = flag[0] > 0
    if tiles > QUAD:
        bad = lax.pmax(bad.astype(jnp.int32), "tile") > 0
        bad = bad | quads_joined(tag, tiles, place)
    return lax.cond(bad, lambda: every_pair(embeddings, cluster_ids), lambda: scores)


def solution(mesh):
    in_specs = (P(("groups", "tile"), None), P(("groups", "tile")))
    out_specs = P(("groups", "tile", "sub"))
    return jax.shard_map(shards, mesh=mesh, in_specs=in_specs, out_specs=out_specs, check_vma=False)
```

```python
import functools
import math

import jax
import jax.numpy as jnp
import numpy as np
from jax import lax
from jax.experimental import pallas as pl
from jax.experimental.pallas import tpu as pltpu
from jax.sharding import PartitionSpec as P

BLOCK = 128
QUAD = 4
SPAN = 4

inverse_temp = 10.0
norm_eps = 1e-06
GAIN = inverse_temp * math.log2(math.e)
OFF = -1000.0

STEP = 512
COPY = 64


def normalised(values):
    values = values.astype(jnp.float32)
    scale = lax.rsqrt(jnp.sum(values * values, axis=1, keepdims=True) + norm_eps)
    return (values * scale).astype(jnp.bfloat16)


def products(rows, columns):
    return lax.dot_general(
        rows, columns, (((1,), (1,)), ((), ())), preferred_element_type=jnp.float32
    )


def column_bias(tag, column_tags):
    return jnp.where(column_tags == tag.astype(jnp.float32), -GAIN, OFF)


def lane_sums(weight):
    total = weight[:, :BLOCK]
    for start in range(BLOCK, weight.shape[1], BLOCK):
        total = total + weight[:, start : start + BLOCK]
    return jnp.sum(total.T, axis=0, keepdims=True)


class Plan:
    def __init__(self, blocks, subs, place, member):
        width = blocks // subs
        share = width // 2
        part = place % QUAD
        self.inner = (part == 1) | (part == 2)
        self.far = part == 1
        dealt = member // 2 * share
        near = (dealt // width * 2 + member % 2) * width + dealt % width
        near = jnp.where(part == 1, blocks // 2, 0) + near
        self.first = jnp.where(self.inner, near, member * width)
        self.second = jnp.where(self.inner, near, member * width + share)
        self.edge = jnp.where(part == 1, blocks // 2 - 1, blocks // 2)
        self.width, self.share = width, share


def pack_kernel(blocks, subs, rows_ref, ids_ref, *refs):
    outs, (ids, sems) = refs[:4], refs[4:]
    plan = Plan(blocks, subs, lax.axis_index("tile"), lax.axis_index("sub"))
    share, half = plan.share, plan.share * BLOCK // 2
    copies = []
    for index, out in enumerate(outs):
        block = plan.first if index < 2 else plan.second
        for down in range(0, half, COPY):
            start = pl.multiple_of(block * BLOCK + index % 2 * half + down, COPY)
            copies.append((rows_ref.at[pl.ds(start, COPY), :], out.at[pl.ds(down, COPY), :]))
    copies.append((ids_ref, ids))
    copies = [pltpu.make_async_copy(*ends, sems.at[index]) for index, ends in enumerate(copies)]
    for copy in copies:
        copy.start()
    copies[-1].wait()
    depth = outs[1].shape[1]
    edge = jnp.max(ids[pl.ds(plan.edge, 1), :], axis=1, keepdims=True)
    rest = [jnp.broadcast_to(edge, (1, BLOCK)), jnp.zeros((1, depth - 2 * half - BLOCK), jnp.int32)]
    for block, out in ((plan.first, outs[1]), (plan.second, outs[3])):
        row = jnp.concatenate([ids[pl.ds(block + k, 1), :] for k in range(share)] + rest, axis=1)
        out[half : half + 8, :] = jnp.broadcast_to(row.astype(jnp.float32), (8, depth)).astype(jnp.bfloat16)
    for copy in copies[:-1]:
        copy.wait()


def pack(size, subs, embeddings, by_block):
    blocks, depth = by_block.shape[0], embeddings.shape[1]
    halves = [jax.ShapeDtypeStruct((size // 2 + more, depth), jnp.bfloat16) for more in (0, 8)]
    return pl.pallas_call(
        functools.partial(pack_kernel, blocks, subs),
        in_specs=[pl.BlockSpec(memory_space=pl.ANY)] * 2,
        out_specs=[pl.BlockSpec(memory_space=pltpu.VMEM)] * 4,
        out_shape=halves * 2,
        scratch_shapes=[pltpu.VMEM(by_block.shape, jnp.int32), pltpu.SemaphoreType.DMA((2 * size // COPY + 1,))],
        compiler_params=pltpu.CompilerParams(vmem_limit_bytes=8 * 1024 * 1024),
        cost_estimate=pl.CostEstimate(flops=0, bytes_accessed=1024, transcendentals=0),
    )(embeddings, by_block)


class Meta:
    def __init__(self, ref, blocks):
        self.ref, self.blocks = ref, blocks

    def tag(self, block, chunk=None):
        return self.ref[block + (0 if chunk is None else (2 + chunk) * self.blocks)]

    def used(self, block):
        return self.ref[self.blocks + block]

    def number(self, index):
        return self.ref[5 * self.blocks + index]


MEMBER, FIRST_BLOCK, EDGE, INNER = range(4)


def self_kernel(blocks, subs, meta_ref, rows_ref, tags_ref, unit_ref, sums_ref, held, sems):
    meta = Meta(meta_ref, blocks)
    width = blocks // subs
    quarter = width * BLOCK
    member = meta.number(MEMBER)
    owners = [lax.rem(member + turn, subs) for turn in range(subs)]
    spans = [pl.ds(pl.multiple_of(owner * quarter, quarter), quarter) for owner in owners]
    copies = []
    for turn, span in enumerate(spans):
        copies.append(pltpu.make_async_copy(rows_ref.at[span, :], held.at[turn], sems.at[turn]))
        copies[-1].start()
    column_tags = tags_ref[...].astype(jnp.float32)
    for turn in range(subs):
        copies[turn].wait()
        unit = normalised(held[turn])
        unit_ref[spans[turn], :] = unit
        if turn == 0:
            share = unit
        cosine = products(unit, share)
        for inner in range(width):
            block = owners[turn] * width + inner
            bias = column_bias(meta.tag(block), column_tags)
            weight = jnp.exp2(cosine[inner * BLOCK : (inner + 1) * BLOCK] * GAIN + bias)
            row = lax.broadcasted_iota(jnp.int32, weight.shape, 0)
            keep = row < meta.used(block)
            if turn == 0:
                keep = keep & (lax.broadcasted_iota(jnp.int32, weight.shape, 1) - row != inner * BLOCK)
            sums_ref[pl.ds(block, 1), :] = lane_sums(jnp.where(keep, weight, 0.0))


def whole_chunk(low_ref, high_ref, piece_unit, at):
    half = low_ref.shape[0]
    piece_unit[at : at + half, :] = normalised(low_ref[...])
    piece_unit[at + half : at + 2 * half, :] = normalised(high_ref[:half, :])


def chunk_tags(high_ref, size):
    row = high_ref[size // 2 : size // 2 + 8, :].astype(jnp.float32)[0:1, :]
    return row[:, :size], row[:, size : size + BLOCK]


def cross_terms(meta, chunks, column_tags, unit_ref, piece_unit, add_rows):
    size = column_tags[0].shape[1]
    columns = None
    for start in range(0, meta.blocks * BLOCK, STEP):
        cosine = products(unit_ref[start : start + STEP, :], piece_unit[...])
        for inner in range(0, STEP, BLOCK):
            block = (start + inner) // BLOCK
            bias = [column_bias(meta.tag(block, chunk), tags) for chunk, tags in zip(chunks, column_tags)]
            bias = jnp.concatenate(bias, axis=1) if len(bias) > 1 else bias[0]
            weight = jnp.exp2(cosine[inner : inner + BLOCK] * GAIN + bias)
            row = lax.broadcasted_iota(jnp.int32, weight.shape, 0)
            weight = jnp.where(row < meta.used(block), weight, 0.0)
            add_rows(block, lane_sums(weight))
            partial = weight[0:8]
            for down in range(8, BLOCK, 8):
                partial = partial + weight[down : down + 8]
            columns = partial if columns is None else columns + partial
    total = jnp.sum(columns, axis=0, keepdims=True)
    return [
        [total[:, at + down : at + down + BLOCK] for down in range(0, size, BLOCK)]
        for at in range(0, total.shape[1], size)
    ]


def middle_kernel(
    blocks, share, meta_ref, unit_ref, swap_low_ref, swap_high_ref, outer_low_ref, outer_high_ref, before_ref,
    sums_ref, outer_cols_ref, swap_cols_ref, piece_unit,
):
    meta = Meta(meta_ref, blocks)
    size = share * BLOCK
    whole_chunk(outer_low_ref, outer_high_ref, piece_unit, 0)
    whole_chunk(swap_low_ref, swap_high_ref, piece_unit, size)
    outer_tags, _ = chunk_tags(outer_high_ref, size)
    swap_tags, edge = chunk_tags(swap_high_ref, size)

    def add_rows(block, value):
        sums_ref[block : block + 1, :] = before_ref[block : block + 1, :] + value

    outer, swap = cross_terms(meta, (0, 1), (outer_tags, swap_tags), unit_ref, piece_unit, add_rows)
    for k in range(share):
        outer_cols_ref[k : k + 1, :] = outer[k]
        swap_cols_ref[k : k + 1, :] = swap[k]
    mine = meta.tag(meta.number(EDGE)).astype(jnp.float32)
    joined = (edge == mine) & (edge >= 0) & (meta.number(INNER) > 0)
    outer_cols_ref[share : share + 1, :] = jnp.where(joined, 1.0, 0.0)


def flag_kernel(share, outer_cols_ref, outer_back_ref, flag_ref):
    flags = jnp.maximum(outer_cols_ref[share : share + 1, :], outer_back_ref[share : share + 1, :])
    flag_ref[0] = jnp.max(flags).astype(jnp.int32)


def last_kernel(
    blocks, share, width, meta_ref, unit_ref, low_ref, high_ref, before_ref, outer_back_ref,
    keep_ref, send_ref, cols_ref, piece_unit, sums,
):
    meta = Meta(meta_ref, blocks)
    size = share * BLOCK
    whole_chunk(low_ref, high_ref, piece_unit, 0)
    tags, _ = chunk_tags(high_ref, size)

    def place(block):
        owner = block // width
        return owner % 2 * (blocks // 2) + owner // 2 * width + block % width

    def add_rows(block, value):
        at = place(block)
        sums[at : at + 1, :] = before_ref[block : block + 1, :] + value

    (cols,) = cross_terms(meta, (2,), (tags,), unit_ref, piece_unit, add_rows)
    for k in range(share):
        cols_ref[k : k + 1, :] = cols[k]
        at = place(meta.number(FIRST_BLOCK) + k)
        sums[pl.ds(at, 1), :] += outer_back_ref[k : k + 1, :]
    parity = meta.number(MEMBER) % 2
    heap = blocks // 2
    keep_ref[...] = sums[pl.ds(pl.multiple_of(parity * heap, heap), heap), :]
    send_ref[...] = sums[pl.ds(pl.multiple_of((1 - parity) * heap, heap), heap), :]


def call(kernel, meta, operands, out_shapes, scratch, flops):
    vmem, smem = pl.BlockSpec(memory_space=pltpu.VMEM), pl.BlockSpec(memory_space=pltpu.SMEM)
    return pl.pallas_call(
        kernel,
        in_specs=[smem] + [vmem] * len(operands),
        out_specs=[vmem if len(shape.shape) > 1 else smem for shape in out_shapes],
        out_shape=out_shapes,
        scratch_shapes=scratch,
        compiler_params=pltpu.CompilerParams(vmem_limit_bytes=16 * 1024 * 1024),
        cost_estimate=pl.CostEstimate(flops=flops, bytes_accessed=1024, transcendentals=0),
    )(meta, *operands)


def every_pair(embeddings, cluster_ids):
    unit = normalised(embeddings)
    tags = cluster_ids + 1
    groups = lax.axis_size("sub")
    member = lax.axis_index("sub")
    owners = lax.axis_size("tile")
    place = lax.axis_index("tile")
    rows_here = unit.shape[0]
    width = rows_here // groups
    own_piece = lax.dynamic_slice_in_dim(unit, member * width, width, 0)
    own_tags = lax.dynamic_slice_in_dim(tags, member * width, width, 0)
    distance = place - jnp.arange(owners, dtype=jnp.int32)
    keep = (jnp.abs(distance) < SPAN) & (distance != 0)
    outgoing = jnp.where(keep[:, None, None], own_piece[None, :, :], jnp.zeros((), jnp.bfloat16))
    outgoing_tags = jnp.where(keep[:, None], own_tags[None, :], 0)
    arrived = lax.all_to_all(outgoing, "tile", split_axis=0, concat_axis=0, tiled=True)
    arrived_tags = lax.all_to_all(outgoing_tags, "tile", split_axis=0, concat_axis=0, tiled=True)
    local_rows = jnp.arange(rows_here, dtype=jnp.int32)[:, None]
    slice_rows = member * width + jnp.arange(width, dtype=jnp.int32)[None, :]
    total = jnp.zeros((rows_here,), jnp.float32)
    for offset in range(1 - SPAN, SPAN):
        if offset == 0:
            piece, piece_tags, order = own_piece, own_tags, local_rows != slice_rows
        else:
            source = place + offset
            valid = (source >= 0) & (source < owners)
            index = jnp.clip(source, 0, owners - 1)
            piece = lax.dynamic_index_in_dim(arrived, index, 0, keepdims=False)
            piece_tags = lax.dynamic_index_in_dim(arrived_tags, index, 0, keepdims=False)
            piece_tags = jnp.where(valid, piece_tags, 0)
            order = True
        same = (tags[:, None] == piece_tags[None, :]) & (tags[:, None] > 0) & order
        weight = jnp.where(same, jnp.exp(inverse_temp * (products(unit, piece) - 1.0)), 0.0)
        total = total + jnp.sum(weight, axis=1)
    return jnp.log(1.0 + lax.psum_scatter(total, "sub", scatter_dimension=0, tiled=True))


def quads_joined(tag, tiles, place):
    last = jnp.broadcast_to(tag[-1], (BLOCK,))
    before = lax.ppermute(last, "tile", [(t, t + 1) for t in range(tiles - 1)])[0]
    joined = (place % QUAD == 0) & (place > 0) & (before == tag[0]) & (before >= 0)
    return lax.pmax(joined.astype(jnp.int32), "tile") > 0


def shards(embeddings, cluster_ids):
    tiles, subs = lax.axis_size("tile"), lax.axis_size("sub")
    place, member = lax.axis_index("tile"), lax.axis_index("sub")
    rows, depth = embeddings.shape
    blocks = rows // BLOCK
    plan = Plan(blocks, subs, place, member)
    width, share, inner = plan.width, plan.share, plan.inner
    size = share * BLOCK
    quads = range(0, tiles, QUAD)
    inward = [p for q in quads for p in ((q, q + 1), (q + 3, q + 2))]
    swap = [p for q in quads for p in ((q + 1, q + 2), (q + 2, q + 1))]
    around = [p for q in quads for p in ((q, q + 1), (q + 3, q + 2), (q + 1, q + 3), (q + 2, q))]

    def turned(route):
        return [(b, a) for a, b in route]

    by_block = cluster_ids.reshape(blocks, BLOCK)
    *first_out, second_low, second_high = pack(size, subs, embeddings, by_block)
    from_inner = [lax.ppermute(out, "tile", swap) for out in first_out]
    from_outer = [lax.ppermute(out, "tile", inward) for out in first_out]

    tag = jnp.max(by_block, axis=1)
    used = jnp.sum((by_block >= 0).astype(jnp.int32), axis=1)
    seen = jnp.where(inner, tag, -2)
    swapped = jnp.where(plan.far & (jnp.arange(blocks) >= blocks // 2), -2, seen)
    numbers = jnp.stack([member, plan.first, plan.edge, inner])
    meta = jnp.concatenate([tag, used, seen, swapped, tag, numbers]).astype(jnp.int32)

    heap = blocks // 2
    owner = plan.second // width
    home_row = jnp.arange(heap)[:, None] - (owner // 2 * width + plan.second % width)
    home_row = jnp.broadcast_to(home_row, (heap, BLOCK)).astype(jnp.int32)
    upper = [
        jnp.broadcast_to((member >> bit) & 1, (heap >> bit, BLOCK)).astype(jnp.int32)
        for bit in range(1, subs.bit_length() - 1)
    ]
    meta, home_row, *upper = lax.optimization_barrier((meta, home_row, *upper))

    row_sums = jax.ShapeDtypeStruct((blocks, BLOCK), jnp.float32)
    col_sums = jax.ShapeDtypeStruct((share, BLOCK), jnp.float32)
    quarter = width * BLOCK
    vmem, smem = pl.BlockSpec(memory_space=pltpu.VMEM), pl.BlockSpec(memory_space=pltpu.SMEM)
    unit, sums = pl.pallas_call(
        functools.partial(self_kernel, blocks, subs),
        in_specs=[smem, pl.BlockSpec(memory_space=pl.ANY), vmem],
        out_specs=[vmem, vmem],
        out_shape=[jax.ShapeDtypeStruct((rows, depth), jnp.bfloat16), row_sums],
        scratch_shapes=[pltpu.VMEM((subs, quarter, depth), jnp.bfloat16), pltpu.SemaphoreType.DMA((subs,))],
        compiler_params=pltpu.CompilerParams(vmem_limit_bytes=24 * 1024 * 1024),
        cost_estimate=pl.CostEstimate(flops=0, bytes_accessed=1024, transcendentals=0),
    )(meta, embeddings, lax.dynamic_slice_in_dim(cluster_ids, member * quarter, quarter, 0)[None])
    second_low, second_high, sums = lax.optimization_barrier((second_low, second_high, sums))
    last = [lax.ppermute(out, "tile", around) for out in (second_low, second_high)]
    sums, outer_cols, swap_cols = call(
        functools.partial(middle_kernel, blocks, share),
        meta,
        (unit, *from_inner, *from_outer, sums),
        [row_sums, jax.ShapeDtypeStruct((share + 1, BLOCK), jnp.float32), col_sums],
        [pltpu.VMEM((2 * size, depth), jnp.bfloat16)],
        4 * rows * size * depth,
    )
    outer_back = lax.ppermute(outer_cols, "tile", turned(inward))
    swap_back = lax.ppermute(swap_cols, "tile", turned(swap))

    flag = pl.pallas_call(
        functools.partial(flag_kernel, share),
        out_specs=pl.BlockSpec(memory_space=pltpu.SMEM),
        out_shape=jax.ShapeDtypeStruct((1,), jnp.int32),
        compiler_params=pltpu.CompilerParams(vmem_limit_bytes=4 * 1024 * 1024),
    )(outer_cols, outer_back)
    sums, flag = lax.optimization_barrier((sums, flag))
    half = jax.ShapeDtypeStruct((heap, BLOCK), jnp.float32)
    held, leaving, cols = call(
        functools.partial(last_kernel, blocks, share, width),
        meta,
        (unit, *last, sums, outer_back),
        [half, half, col_sums],
        [pltpu.VMEM((size, depth), jnp.bfloat16), pltpu.VMEM((blocks, BLOCK), jnp.float32)],
        2 * rows * size * depth,
    )

    home = lax.ppermute(cols, "tile", turned(around)) + swap_back
    for k in range(share):
        held = held + jnp.where(home_row == k, home[k : k + 1], 0.0)
    held = held + lax.ppermute(leaving, "sub", [(i, i ^ 1) for i in range(subs)])
    held, flag = lax.optimization_barrier((held, flag))
    for bit, mine in enumerate(upper, 1):
        pairs = held.reshape(-1, 2, width, BLOCK)
        low, high = pairs[:, 0].reshape(mine.shape), pairs[:, 1].reshape(mine.shape)
        leaving = jnp.where(mine > 0, low, high)
        held = jnp.where(mine > 0, high, low)
        held = held + lax.ppermute(leaving, "sub", [(i, i ^ (1 << bit)) for i in range(subs)])
    scores = jnp.log(1.0 + held.reshape(-1))

    bad = flag[0] > 0
    if tiles > QUAD:
        bad = lax.pmax(bad.astype(jnp.int32), "tile") > 0
        bad = bad | quads_joined(tag, tiles, place)
    return lax.cond(bad, lambda: every_pair(embeddings, cluster_ids), lambda: scores)


def solution(mesh):
    in_specs = (P(("groups", "tile"), None), P(("groups", "tile")))
    out_specs = P(("groups", "tile", "sub"))
    return jax.shard_map(shards, mesh=mesh, in_specs=in_specs, out_specs=out_specs, check_vma=False)
```

```python
import functools
import math

import jax
import jax.numpy as jnp
import numpy as np
from jax import lax
from jax.experimental import pallas as pl
from jax.experimental.pallas import tpu as pltpu
from jax.sharding import PartitionSpec as P

BLOCK = 128
QUAD = 4
SPAN = 4

inverse_temp = 10.0
norm_eps = 1e-06
GAIN = inverse_temp * math.log2(math.e)
OFF = -1000.0

STEP = 512
COPY = 64


def normalised(values):
    values = values.astype(jnp.float32)
    scale = lax.rsqrt(jnp.sum(values * values, axis=1, keepdims=True) + norm_eps)
    return (values * scale).astype(jnp.bfloat16)


def products(rows, columns):
    return lax.dot_general(
        rows, columns, (((1,), (1,)), ((), ())), preferred_element_type=jnp.float32
    )


def column_bias(tag, column_tags):
    return jnp.where(column_tags == tag.astype(jnp.float32), -GAIN, OFF)


def lane_sums(weight):
    total = weight[:, :BLOCK]
    for start in range(BLOCK, weight.shape[1], BLOCK):
        total = total + weight[:, start : start + BLOCK]
    return jnp.sum(total.T, axis=0, keepdims=True)


class Plan:
    def __init__(self, blocks, subs, place, member):
        width = blocks // subs
        share = width // 2
        part = place % QUAD
        self.inner = (part == 1) | (part == 2)
        self.far = part == 1
        dealt = member // 2 * share
        near = (dealt // width * 2 + member % 2) * width + dealt % width
        near = jnp.where(part == 1, blocks // 2, 0) + near
        self.first = jnp.where(self.inner, near, member * width)
        self.second = jnp.where(self.inner, near, member * width + share)
        self.edge = jnp.where(part == 1, blocks // 2 - 1, blocks // 2)
        self.width, self.share = width, share


def pack_kernel(blocks, subs, rows_ref, ids_ref, *refs):
    outs, (ids, sems) = refs[:5], refs[5:]
    plan = Plan(blocks, subs, lax.axis_index("tile"), lax.axis_index("sub"))
    share, size = plan.share, plan.share * BLOCK
    first_low, first_high, swapped, second_low, second_high = outs
    ids_copy = pltpu.make_async_copy(ids_ref, ids, sems.at[0])
    ids_copy.start()

    def copies(block, parts, sem):
        made, down = [], 0
        for part, count in parts:
            for at in range(0, count, COPY):
                start = pl.multiple_of(block * BLOCK + down, COPY)
                made.append(
                    pltpu.make_async_copy(
                        rows_ref.at[pl.ds(start, COPY), :], part.at[pl.ds(at, COPY), :], sems.at[sem + len(made)]
                    )
                )
                down += COPY
        return made

    count = size // COPY
    first = copies(plan.first, ((first_low, size // 2), (first_high, size // 2)), 1)
    swap = copies(plan.first, ((swapped, size),), 1)
    second = copies(plan.second, ((second_low, size // 2), (second_high, size // 2)), 1 + count)

    @pl.when(plan.inner)
    def _():
        for copy in swap:
            copy.start()

    @pl.when(jnp.logical_not(plan.inner))
    def _():
        for copy in first:
            copy.start()

    for copy in second:
        copy.start()
    ids_copy.wait()
    depth = swapped.shape[1]
    edge = jnp.max(ids[pl.ds(plan.edge, 1), :], axis=1, keepdims=True)
    rest = [jnp.broadcast_to(edge, (1, BLOCK)), jnp.zeros((1, depth - size - BLOCK), jnp.int32)]
    for block, parts in ((plan.first, (first_high, swapped)), (plan.second, (second_high,))):
        row = jnp.concatenate([ids[pl.ds(block + k, 1), :] for k in range(share)] + rest, axis=1)
        row = jnp.broadcast_to(row.astype(jnp.float32), (8, depth)).astype(jnp.bfloat16)
        for part in parts:
            part[part.shape[0] - 8 :, :] = row

    @pl.when(plan.inner)
    def _():
        for copy in swap:
            copy.wait()

    @pl.when(jnp.logical_not(plan.inner))
    def _():
        for copy in first:
            copy.wait()

    for copy in second:
        copy.wait()


def pack(size, subs, embeddings, by_block):
    depth = embeddings.shape[1]
    parts = (size // 2, size // 2 + 8, size + 8, size // 2, size // 2 + 8)
    return pl.pallas_call(
        functools.partial(pack_kernel, by_block.shape[0], subs),
        in_specs=[pl.BlockSpec(memory_space=pl.ANY)] * 2,
        out_specs=[pl.BlockSpec(memory_space=pltpu.VMEM)] * 5,
        out_shape=[jax.ShapeDtypeStruct((count, depth), jnp.bfloat16) for count in parts],
        scratch_shapes=[pltpu.VMEM(by_block.shape, jnp.int32), pltpu.SemaphoreType.DMA((2 * size // COPY + 1,))],
        compiler_params=pltpu.CompilerParams(vmem_limit_bytes=8 * 1024 * 1024),
        cost_estimate=pl.CostEstimate(flops=0, bytes_accessed=1024, transcendentals=0),
    )(embeddings, by_block)


class Meta:
    def __init__(self, ref, blocks):
        self.ref, self.blocks = ref, blocks

    def tag(self, block, chunk=None):
        return self.ref[block + (0 if chunk is None else (2 + chunk) * self.blocks)]

    def used(self, block):
        return self.ref[self.blocks + block]

    def number(self, index):
        return self.ref[5 * self.blocks + index]


MEMBER, FIRST_BLOCK, EDGE, INNER = range(4)


def self_kernel(blocks, subs, meta_ref, rows_ref, tags_ref, unit_ref, sums_ref, held, sems):
    meta = Meta(meta_ref, blocks)
    width = blocks // subs
    quarter = width * BLOCK
    member = meta.number(MEMBER)
    owners = [lax.rem(member + turn, subs) for turn in range(subs)]
    spans = [pl.ds(pl.multiple_of(owner * quarter, quarter), quarter) for owner in owners]
    copies = []
    for turn, span in enumerate(spans):
        copies.append(pltpu.make_async_copy(rows_ref.at[span, :], held.at[turn], sems.at[turn]))
        copies[-1].start()
    column_tags = tags_ref[...].astype(jnp.float32)
    for turn in range(subs):
        copies[turn].wait()
        unit = normalised(held[turn])
        unit_ref[spans[turn], :] = unit
        if turn == 0:
            share = unit
        cosine = products(unit, share)
        for inner in range(width):
            block = owners[turn] * width + inner
            bias = column_bias(meta.tag(block), column_tags)
            weight = jnp.exp2(cosine[inner * BLOCK : (inner + 1) * BLOCK] * GAIN + bias)
            row = lax.broadcasted_iota(jnp.int32, weight.shape, 0)
            keep = row < meta.used(block)
            if turn == 0:
                keep = keep & (lax.broadcasted_iota(jnp.int32, weight.shape, 1) - row != inner * BLOCK)
            sums_ref[pl.ds(block, 1), :] = lane_sums(jnp.where(keep, weight, 0.0))


def unit_chunk(parts, piece_unit):
    size = piece_unit.shape[0]
    down = 0
    for part in parts:
        count = part.shape[0] // 16 * 16
        piece_unit[down : down + count, :] = normalised(part[:count, :])
        down += count
    row = parts[-1][count : count + 8, :].astype(jnp.float32)[0:1, :]
    return row[:, :size], row[:, size : size + BLOCK]


def cross_terms(meta, chunk, column_tags, unit_ref, piece_unit, add_rows):
    size = column_tags.shape[1]
    columns = None
    for start in range(0, meta.blocks * BLOCK, STEP):
        cosine = products(unit_ref[start : start + STEP, :], piece_unit[...])
        for inner in range(0, STEP, BLOCK):
            block = (start + inner) // BLOCK
            bias = column_bias(meta.tag(block, chunk), column_tags)
            weight = jnp.exp2(cosine[inner : inner + BLOCK] * GAIN + bias)
            row = lax.broadcasted_iota(jnp.int32, weight.shape, 0)
            weight = jnp.where(row < meta.used(block), weight, 0.0)
            add_rows(block, lane_sums(weight))
            partial = weight[0:8]
            for down in range(8, BLOCK, 8):
                partial = partial + weight[down : down + 8]
            columns = partial if columns is None else columns + partial
    total = jnp.sum(columns, axis=0, keepdims=True)
    return [total[:, at : at + BLOCK] for at in range(0, size, BLOCK)]


def middle_kernel(blocks, share, chunk, meta_ref, unit_ref, *refs):
    *parts, before_ref, sums_ref, cols_ref, piece_unit = refs
    meta = Meta(meta_ref, blocks)
    tags, edge = unit_chunk(parts, piece_unit)

    def add_rows(block, value):
        sums_ref[block : block + 1, :] = before_ref[block : block + 1, :] + value

    cols = cross_terms(meta, chunk, tags, unit_ref, piece_unit, add_rows)
    for k in range(share):
        cols_ref[k : k + 1, :] = cols[k]
    mine = meta.tag(meta.number(EDGE)).astype(jnp.float32)
    joined = (edge == mine) & (edge >= 0) & (meta.number(INNER) > 0)
    cols_ref[share : share + 1, :] = jnp.where(joined, 1.0, 0.0)


def last_kernel(
    blocks, share, width, meta_ref, unit_ref, low_ref, high_ref, before_ref, outer_back_ref, swap_cols_ref,
    keep_ref, send_ref, cols_ref, piece_unit, sums,
):
    meta = Meta(meta_ref, blocks)
    tags, _ = unit_chunk((low_ref, high_ref), piece_unit)

    def place(block):
        owner = block // width
        return owner % 2 * (blocks // 2) + owner // 2 * width + block % width

    def add_rows(block, value):
        at = place(block)
        sums[at : at + 1, :] = before_ref[block : block + 1, :] + value

    cols = cross_terms(meta, 2, tags, unit_ref, piece_unit, add_rows)
    for k in range(share):
        cols_ref[k : k + 1, :] = cols[k]
        at = place(meta.number(FIRST_BLOCK) + k)
        sums[pl.ds(at, 1), :] += outer_back_ref[k : k + 1, :]
    cols_ref[share : share + 1, :] = swap_cols_ref[share : share + 1, :]
    parity = meta.number(MEMBER) % 2
    heap = blocks // 2
    keep_ref[...] = sums[pl.ds(pl.multiple_of(parity * heap, heap), heap), :]
    send_ref[...] = sums[pl.ds(pl.multiple_of((1 - parity) * heap, heap), heap), :]


def flag_kernel(share, here_ref, home_ref, flag_ref):
    flags = jnp.maximum(here_ref[share : share + 1, :], home_ref[share : share + 1, :])
    flag_ref[0] = jnp.max(flags).astype(jnp.int32)


def call(kernel, meta, operands, out_shapes, scratch, flops):
    vmem, smem = pl.BlockSpec(memory_space=pltpu.VMEM), pl.BlockSpec(memory_space=pltpu.SMEM)
    return pl.pallas_call(
        kernel,
        in_specs=[smem] + [vmem] * len(operands),
        out_specs=[vmem if len(shape.shape) > 1 else smem for shape in out_shapes],
        out_shape=out_shapes,
        scratch_shapes=scratch,
        compiler_params=pltpu.CompilerParams(vmem_limit_bytes=16 * 1024 * 1024),
        cost_estimate=pl.CostEstimate(flops=flops, bytes_accessed=1024, transcendentals=0),
    )(meta, *operands)


def every_pair(embeddings, cluster_ids):
    unit = normalised(embeddings)
    tags = cluster_ids + 1
    groups = lax.axis_size("sub")
    member = lax.axis_index("sub")
    owners = lax.axis_size("tile")
    place = lax.axis_index("tile")
    rows_here = unit.shape[0]
    width = rows_here // groups
    own_piece = lax.dynamic_slice_in_dim(unit, member * width, width, 0)
    own_tags = lax.dynamic_slice_in_dim(tags, member * width, width, 0)
    distance = place - jnp.arange(owners, dtype=jnp.int32)
    keep = (jnp.abs(distance) < SPAN) & (distance != 0)
    outgoing = jnp.where(keep[:, None, None], own_piece[None, :, :], jnp.zeros((), jnp.bfloat16))
    outgoing_tags = jnp.where(keep[:, None], own_tags[None, :], 0)
    arrived = lax.all_to_all(outgoing, "tile", split_axis=0, concat_axis=0, tiled=True)
    arrived_tags = lax.all_to_all(outgoing_tags, "tile", split_axis=0, concat_axis=0, tiled=True)
    local_rows = jnp.arange(rows_here, dtype=jnp.int32)[:, None]
    slice_rows = member * width + jnp.arange(width, dtype=jnp.int32)[None, :]
    total = jnp.zeros((rows_here,), jnp.float32)
    for offset in range(1 - SPAN, SPAN):
        if offset == 0:
            piece, piece_tags, order = own_piece, own_tags, local_rows != slice_rows
        else:
            source = place + offset
            valid = (source >= 0) & (source < owners)
            index = jnp.clip(source, 0, owners - 1)
            piece = lax.dynamic_index_in_dim(arrived, index, 0, keepdims=False)
            piece_tags = lax.dynamic_index_in_dim(arrived_tags, index, 0, keepdims=False)
            piece_tags = jnp.where(valid, piece_tags, 0)
            order = True
        same = (tags[:, None] == piece_tags[None, :]) & (tags[:, None] > 0) & order
        weight = jnp.where(same, jnp.exp(inverse_temp * (products(unit, piece) - 1.0)), 0.0)
        total = total + jnp.sum(weight, axis=1)
    return jnp.log(1.0 + lax.psum_scatter(total, "sub", scatter_dimension=0, tiled=True))


def quads_joined(tag, tiles, place):
    last = jnp.broadcast_to(tag[-1], (BLOCK,))
    before = lax.ppermute(last, "tile", [(t, t + 1) for t in range(tiles - 1)])[0]
    joined = (place % QUAD == 0) & (place > 0) & (before == tag[0]) & (before >= 0)
    return lax.pmax(joined.astype(jnp.int32), "tile") > 0


def shards(embeddings, cluster_ids):
    tiles, subs = lax.axis_size("tile"), lax.axis_size("sub")
    place, member = lax.axis_index("tile"), lax.axis_index("sub")
    rows, depth = embeddings.shape
    blocks = rows // BLOCK
    plan = Plan(blocks, subs, place, member)
    width, share, inner = plan.width, plan.share, plan.inner
    size = share * BLOCK
    quads = range(0, tiles, QUAD)
    inward = [p for q in quads for p in ((q, q + 1), (q + 3, q + 2))]
    swap = [p for q in quads for p in ((q + 1, q + 2), (q + 2, q + 1))]
    around = [p for q in quads for p in ((q, q + 1), (q + 3, q + 2), (q + 1, q + 3), (q + 2, q))]

    def turned(route):
        return [(b, a) for a, b in route]

    by_block = cluster_ids.reshape(blocks, BLOCK)
    first_low, first_high, swapped, second_low, second_high = pack(size, subs, embeddings, by_block)
    from_inner = lax.ppermute(swapped, "tile", swap)
    from_outer = [lax.ppermute(out, "tile", inward) for out in (first_high, first_low)][::-1]

    tag = jnp.max(by_block, axis=1)
    used = jnp.sum((by_block >= 0).astype(jnp.int32), axis=1)
    seen = jnp.where(inner, tag, -2)
    swapped = jnp.where(plan.far & (jnp.arange(blocks) >= blocks // 2), -2, seen)
    numbers = jnp.stack([member, plan.first, plan.edge, inner])
    meta = jnp.concatenate([tag, used, seen, swapped, tag, numbers]).astype(jnp.int32)

    heap = blocks // 2
    owner = plan.second // width
    home_row = jnp.arange(heap)[:, None] - (owner // 2 * width + plan.second % width)
    home_row = jnp.broadcast_to(home_row, (heap, BLOCK)).astype(jnp.int32)
    upper = [
        jnp.broadcast_to((member >> bit) & 1, (heap >> bit, BLOCK)).astype(jnp.int32)
        for bit in range(1, subs.bit_length() - 1)
    ]
    meta, home_row, *upper = lax.optimization_barrier((meta, home_row, *upper))

    row_sums = jax.ShapeDtypeStruct((blocks, BLOCK), jnp.float32)
    col_sums = jax.ShapeDtypeStruct((share + 1, BLOCK), jnp.float32)
    quarter = width * BLOCK
    vmem, smem = pl.BlockSpec(memory_space=pltpu.VMEM), pl.BlockSpec(memory_space=pltpu.SMEM)
    unit, sums = pl.pallas_call(
        functools.partial(self_kernel, blocks, subs),
        in_specs=[smem, pl.BlockSpec(memory_space=pl.ANY), vmem],
        out_specs=[vmem, vmem],
        out_shape=[jax.ShapeDtypeStruct((rows, depth), jnp.bfloat16), row_sums],
        scratch_shapes=[pltpu.VMEM((subs, quarter, depth), jnp.bfloat16), pltpu.SemaphoreType.DMA((subs,))],
        compiler_params=pltpu.CompilerParams(vmem_limit_bytes=24 * 1024 * 1024),
        cost_estimate=pl.CostEstimate(flops=0, bytes_accessed=1024, transcendentals=0),
    )(meta, embeddings, lax.dynamic_slice_in_dim(cluster_ids, member * quarter, quarter, 0)[None])
    second_low, second_high, sums = lax.optimization_barrier((second_low, second_high, sums))
    last = [lax.ppermute(out, "tile", around) for out in (second_low, second_high)]

    def middle(chunk, parts, before):
        return call(
            functools.partial(middle_kernel, blocks, share, chunk),
            meta,
            (unit, *parts, before),
            [row_sums, col_sums],
            [pltpu.VMEM((size, depth), jnp.bfloat16)],
            2 * rows * size * depth,
        )

    sums, outer_cols = middle(0, from_outer, sums)
    outer_back = lax.ppermute(outer_cols, "tile", turned(inward))
    sums, swap_cols = middle(1, (from_inner,), sums)
    swap_back = lax.ppermute(swap_cols, "tile", turned(swap))
    half = jax.ShapeDtypeStruct((heap, BLOCK), jnp.float32)
    held, leaving, cols = call(
        functools.partial(last_kernel, blocks, share, width),
        meta,
        (unit, *last, sums, outer_back, swap_cols),
        [half, half, col_sums],
        [pltpu.VMEM((size, depth), jnp.bfloat16), pltpu.VMEM((blocks, BLOCK), jnp.float32)],
        2 * rows * size * depth,
    )

    home = lax.ppermute(cols, "tile", turned(around))
    for k in range(share):
        held = held + jnp.where(home_row == k, home[k : k + 1] + swap_back[k : k + 1], 0.0)
    held = held + lax.ppermute(leaving, "sub", [(i, i ^ 1) for i in range(subs)])
    home, held = lax.optimization_barrier((home, held))
    for bit, mine in enumerate(upper, 1):
        pairs = held.reshape(-1, 2, width, BLOCK)
        low, high = pairs[:, 0].reshape(mine.shape), pairs[:, 1].reshape(mine.shape)
        leaving = jnp.where(mine > 0, low, high)
        held = jnp.where(mine > 0, high, low)
        held = held + lax.ppermute(leaving, "sub", [(i, i ^ (1 << bit)) for i in range(subs)])
    scores = jnp.log(1.0 + held.reshape(-1))

    flag = pl.pallas_call(
        functools.partial(flag_kernel, share),
        out_specs=pl.BlockSpec(memory_space=pltpu.SMEM),
        out_shape=jax.ShapeDtypeStruct((1,), jnp.int32),
        compiler_params=pltpu.CompilerParams(vmem_limit_bytes=4 * 1024 * 1024),
    )(swap_cols, home)
    bad = flag[0] > 0
    if tiles > QUAD:
        bad = lax.pmax(bad.astype(jnp.int32), "tile") > 0
        bad = bad | quads_joined(tag, tiles, place)
    return lax.cond(bad, lambda: every_pair(embeddings, cluster_ids), lambda: scores)


def solution(mesh):
    in_specs = (P(("groups", "tile"), None), P(("groups", "tile")))
    out_specs = P(("groups", "tile", "sub"))
    return jax.shard_map(shards, mesh=mesh, in_specs=in_specs, out_specs=out_specs, check_vma=False)
```

```python
import functools
import math

import jax
import jax.numpy as jnp
import numpy as np
from jax import lax
from jax.experimental import pallas as pl
from jax.experimental.pallas import tpu as pltpu
from jax.sharding import PartitionSpec as P

BLOCK = 128
QUAD = 4
SPAN = 4

inverse_temp = 10.0
norm_eps = 1e-06
GAIN = inverse_temp * math.log2(math.e)
OFF = -1000.0

STEP = 512
COPY = 64


def normalised(values):
    values = values.astype(jnp.float32)
    scale = lax.rsqrt(jnp.sum(values * values, axis=1, keepdims=True) + norm_eps)
    return (values * scale).astype(jnp.bfloat16)


def products(rows, columns):
    return lax.dot_general(
        rows, columns, (((1,), (1,)), ((), ())), preferred_element_type=jnp.float32
    )


def column_bias(tag, column_tags):
    return jnp.where(column_tags == tag.astype(jnp.float32), -GAIN, OFF)


def lane_sums(weight):
    total = weight[:, :BLOCK]
    for start in range(BLOCK, weight.shape[1], BLOCK):
        total = total + weight[:, start : start + BLOCK]
    return jnp.sum(total.T, axis=0, keepdims=True)


class Plan:
    def __init__(self, blocks, subs, place, member):
        width = blocks // subs
        share = width // 2
        part = place % QUAD
        self.inner = (part == 1) | (part == 2)
        self.far = part == 1
        dealt = member // 2 * share
        near = (dealt // width * 2 + member % 2) * width + dealt % width
        near = jnp.where(part == 1, blocks // 2, 0) + near
        self.first = jnp.where(self.inner, near, member * width)
        self.second = jnp.where(self.inner, near, member * width + share)
        self.edge = jnp.where(part == 1, blocks // 2 - 1, blocks // 2)
        self.width, self.share = width, share


def pack_kernel(blocks, subs, rows_ref, ids_ref, first_ref, second_ref, ids, sems):
    plan = Plan(blocks, subs, lax.axis_index("tile"), lax.axis_index("sub"))
    share, size = plan.share, plan.share * BLOCK
    ids_copy = pltpu.make_async_copy(ids_ref, ids, sems.at[0])

    def copies(block, out, sem):
        for down in range(0, size, COPY):
            start = pl.multiple_of(block * BLOCK + down, COPY)
            yield pltpu.make_async_copy(
                rows_ref.at[pl.ds(start, COPY), :], out.at[pl.ds(down, COPY), :], sems.at[sem + down // COPY]
            )

    first = list(copies(plan.first, first_ref, 1))
    second = list(copies(plan.second, second_ref, 1 + size // COPY))
    for copy in [ids_copy] + first:
        copy.start()

    @pl.when(jnp.logical_not(plan.inner))
    def _():
        for copy in second:
            copy.start()

    ids_copy.wait()
    depth = first_ref.shape[1]
    edge = jnp.max(ids[pl.ds(plan.edge, 1), :], axis=1, keepdims=True)
    rest = [jnp.broadcast_to(edge, (1, BLOCK)), jnp.zeros((1, depth - size - BLOCK), jnp.int32)]
    for block, out in ((plan.first, first_ref), (plan.second, second_ref)):
        row = jnp.concatenate([ids[pl.ds(block + k, 1), :] for k in range(share)] + rest, axis=1)
        out[size:, :] = jnp.broadcast_to(row.astype(jnp.float32), (8, depth)).astype(jnp.bfloat16)
    for copy in first:
        copy.wait()

    @pl.when(jnp.logical_not(plan.inner))
    def _():
        for copy in second:
            copy.wait()


def pack(size, subs, embeddings, by_block):
    return pl.pallas_call(
        functools.partial(pack_kernel, by_block.shape[0], subs),
        in_specs=[pl.BlockSpec(memory_space=pl.ANY)] * 2,
        out_specs=[pl.BlockSpec(memory_space=pltpu.VMEM)] * 2,
        out_shape=[jax.ShapeDtypeStruct((size + 8, embeddings.shape[1]), jnp.bfloat16)] * 2,
        scratch_shapes=[pltpu.VMEM(by_block.shape, jnp.int32), pltpu.SemaphoreType.DMA((2 * size // COPY + 1,))],
        compiler_params=pltpu.CompilerParams(vmem_limit_bytes=8 * 1024 * 1024),
        cost_estimate=pl.CostEstimate(flops=0, bytes_accessed=1024, transcendentals=0),
    )(embeddings, by_block)


class Meta:
    def __init__(self, ref, blocks):
        self.ref, self.blocks = ref, blocks

    def tag(self, block, chunk=None):
        return self.ref[block + (0 if chunk is None else (2 + chunk) * self.blocks)]

    def used(self, block):
        return self.ref[self.blocks + block]

    def number(self, index):
        return self.ref[5 * self.blocks + index]


MEMBER, FIRST_BLOCK, EDGE, INNER = range(4)


def self_kernel(blocks, subs, meta_ref, rows_ref, tags_ref, unit_ref, sums_ref, held, sems):
    meta = Meta(meta_ref, blocks)
    width = blocks // subs
    quarter = width * BLOCK
    member = meta.number(MEMBER)
    owners = [lax.rem(member + turn, subs) for turn in range(subs)]
    spans = [pl.ds(pl.multiple_of(owner * quarter, quarter), quarter) for owner in owners]
    copies = []
    for turn, span in enumerate(spans):
        copies.append(pltpu.make_async_copy(rows_ref.at[span, :], held.at[turn], sems.at[turn]))
        copies[-1].start()
    column_tags = tags_ref[...].astype(jnp.float32)
    for turn in range(subs):
        copies[turn].wait()
        unit = normalised(held[turn])
        unit_ref[spans[turn], :] = unit
        if turn == 0:
            share = unit
        cosine = products(unit, share)
        for inner in range(width):
            block = owners[turn] * width + inner
            bias = column_bias(meta.tag(block), column_tags)
            weight = jnp.exp2(cosine[inner * BLOCK : (inner + 1) * BLOCK] * GAIN + bias)
            row = lax.broadcasted_iota(jnp.int32, weight.shape, 0)
            keep = row < meta.used(block)
            if turn == 0:
                keep = keep & (lax.broadcasted_iota(jnp.int32, weight.shape, 1) - row != inner * BLOCK)
            sums_ref[pl.ds(block, 1), :] = lane_sums(jnp.where(keep, weight, 0.0))


def chunk_tags(piece_ref, size):
    row = piece_ref[size:, :].astype(jnp.float32)[0:1, :]
    return row[:, :size], row[:, size : size + BLOCK]


def cross_terms(meta, chunk, column_tags, unit_ref, piece_unit, add_rows):
    size = column_tags.shape[1]
    columns = None
    for start in range(0, meta.blocks * BLOCK, STEP):
        cosine = products(unit_ref[start : start + STEP, :], piece_unit[...])
        for inner in range(0, STEP, BLOCK):
            block = (start + inner) // BLOCK
            bias = column_bias(meta.tag(block, chunk), column_tags)
            weight = jnp.exp2(cosine[inner : inner + BLOCK] * GAIN + bias)
            row = lax.broadcasted_iota(jnp.int32, weight.shape, 0)
            weight = jnp.where(row < meta.used(block), weight, 0.0)
            add_rows(block, lane_sums(weight))
            partial = weight[0:8]
            for down in range(8, BLOCK, 8):
                partial = partial + weight[down : down + 8]
            columns = partial if columns is None else columns + partial
    total = jnp.sum(columns, axis=0, keepdims=True)
    return [total[:, at : at + BLOCK] for at in range(0, size, BLOCK)]


def middle_kernel(
    blocks, share, chunk, meta_ref, unit_ref, piece_ref, before_ref, sums_ref, cols_ref, piece_unit
):
    meta = Meta(meta_ref, blocks)
    size = share * BLOCK
    piece_unit[...] = normalised(piece_ref[:size, :])
    tags, edge = chunk_tags(piece_ref, size)

    def add_rows(block, value):
        sums_ref[block : block + 1, :] = before_ref[block : block + 1, :] + value

    cols = cross_terms(meta, chunk, tags, unit_ref, piece_unit, add_rows)
    for k in range(share):
        cols_ref[k : k + 1, :] = cols[k]
    mine = meta.tag(meta.number(EDGE)).astype(jnp.float32)
    joined = (edge == mine) & (edge >= 0) & (meta.number(INNER) > 0)
    cols_ref[share : share + 1, :] = jnp.where(joined, 1.0, 0.0)


def last_kernel(
    blocks, share, width, meta_ref, unit_ref, inward_ref, relayed_ref, before_ref, outer_back_ref, swap_cols_ref,
    keep_ref, send_ref, cols_ref, piece_unit, sums,
):
    meta = Meta(meta_ref, blocks)
    size = share * BLOCK
    is_inner = meta.number(INNER) > 0

    @pl.when(is_inner)
    def _():
        piece_unit[...] = normalised(inward_ref[:size, :])

    @pl.when(jnp.logical_not(is_inner))
    def _():
        piece_unit[...] = normalised(relayed_ref[:size, :])

    tags = jnp.where(is_inner, chunk_tags(inward_ref, size)[0], chunk_tags(relayed_ref, size)[0])

    def place(block):
        owner = block // width
        return owner % 2 * (blocks // 2) + owner // 2 * width + block % width

    def add_rows(block, value):
        at = place(block)
        sums[at : at + 1, :] = before_ref[block : block + 1, :] + value

    cols = cross_terms(meta, 2, tags, unit_ref, piece_unit, add_rows)
    for k in range(share):
        cols_ref[k : k + 1, :] = cols[k]
        at = place(meta.number(FIRST_BLOCK) + k)
        sums[pl.ds(at, 1), :] += outer_back_ref[k : k + 1, :]
    cols_ref[share : share + 1, :] = swap_cols_ref[share : share + 1, :]
    parity = meta.number(MEMBER) % 2
    heap = blocks // 2
    keep_ref[...] = sums[pl.ds(pl.multiple_of(parity * heap, heap), heap), :]
    send_ref[...] = sums[pl.ds(pl.multiple_of((1 - parity) * heap, heap), heap), :]


def flag_kernel(share, here_ref, home_ref, flag_ref):
    flags = jnp.maximum(here_ref[share : share + 1, :], home_ref[share : share + 1, :])
    flag_ref[0] = jnp.max(flags).astype(jnp.int32)


def call(kernel, meta, operands, out_shapes, scratch, flops):
    vmem, smem = pl.BlockSpec(memory_space=pltpu.VMEM), pl.BlockSpec(memory_space=pltpu.SMEM)
    return pl.pallas_call(
        kernel,
        in_specs=[smem] + [vmem] * len(operands),
        out_specs=[vmem if len(shape.shape) > 1 else smem for shape in out_shapes],
        out_shape=out_shapes,
        scratch_shapes=scratch,
        compiler_params=pltpu.CompilerParams(vmem_limit_bytes=16 * 1024 * 1024),
        cost_estimate=pl.CostEstimate(flops=flops, bytes_accessed=1024, transcendentals=0),
    )(meta, *operands)


def every_pair(embeddings, cluster_ids):
    unit = normalised(embeddings)
    tags = cluster_ids + 1
    groups = lax.axis_size("sub")
    member = lax.axis_index("sub")
    owners = lax.axis_size("tile")
    place = lax.axis_index("tile")
    rows_here = unit.shape[0]
    width = rows_here // groups
    own_piece = lax.dynamic_slice_in_dim(unit, member * width, width, 0)
    own_tags = lax.dynamic_slice_in_dim(tags, member * width, width, 0)
    distance = place - jnp.arange(owners, dtype=jnp.int32)
    keep = (jnp.abs(distance) < SPAN) & (distance != 0)
    outgoing = jnp.where(keep[:, None, None], own_piece[None, :, :], jnp.zeros((), jnp.bfloat16))
    outgoing_tags = jnp.where(keep[:, None], own_tags[None, :], 0)
    arrived = lax.all_to_all(outgoing, "tile", split_axis=0, concat_axis=0, tiled=True)
    arrived_tags = lax.all_to_all(outgoing_tags, "tile", split_axis=0, concat_axis=0, tiled=True)
    local_rows = jnp.arange(rows_here, dtype=jnp.int32)[:, None]
    slice_rows = member * width + jnp.arange(width, dtype=jnp.int32)[None, :]
    total = jnp.zeros((rows_here,), jnp.float32)
    for offset in range(1 - SPAN, SPAN):
        if offset == 0:
            piece, piece_tags, order = own_piece, own_tags, local_rows != slice_rows
        else:
            source = place + offset
            valid = (source >= 0) & (source < owners)
            index = jnp.clip(source, 0, owners - 1)
            piece = lax.dynamic_index_in_dim(arrived, index, 0, keepdims=False)
            piece_tags = lax.dynamic_index_in_dim(arrived_tags, index, 0, keepdims=False)
            piece_tags = jnp.where(valid, piece_tags, 0)
            order = True
        same = (tags[:, None] == piece_tags[None, :]) & (tags[:, None] > 0) & order
        weight = jnp.where(same, jnp.exp(inverse_temp * (products(unit, piece) - 1.0)), 0.0)
        total = total + jnp.sum(weight, axis=1)
    return jnp.log(1.0 + lax.psum_scatter(total, "sub", scatter_dimension=0, tiled=True))


def quads_joined(tag, tiles, place):
    last = jnp.broadcast_to(tag[-1], (BLOCK,))
    before = lax.ppermute(last, "tile", [(t, t + 1) for t in range(tiles - 1)])[0]
    joined = (place % QUAD == 0) & (place > 0) & (before == tag[0]) & (before >= 0)
    return lax.pmax(joined.astype(jnp.int32), "tile") > 0


def shards(embeddings, cluster_ids):
    tiles, subs = lax.axis_size("tile"), lax.axis_size("sub")
    place, member = lax.axis_index("tile"), lax.axis_index("sub")
    rows, depth = embeddings.shape
    blocks = rows // BLOCK
    plan = Plan(blocks, subs, place, member)
    width, share, inner = plan.width, plan.share, plan.inner
    size = share * BLOCK
    quads = range(0, tiles, QUAD)
    inward = [p for q in quads for p in ((q, q + 1), (q + 3, q + 2))]
    swap = [p for q in quads for p in ((q + 1, q + 2), (q + 2, q + 1))]
    around = [p for q in quads for p in ((q, q + 1), (q + 3, q + 2), (q + 1, q + 3), (q + 2, q))]

    def turned(route):
        return [(b, a) for a, b in route]

    by_block = cluster_ids.reshape(blocks, BLOCK)
    first_out, second_out = pack(size, subs, embeddings, by_block)
    from_outer = lax.ppermute(first_out, "tile", inward)
    from_inner = lax.ppermute(first_out, "tile", swap)
    relayed = lax.ppermute(from_inner, "tile", turned(inward))

    tag = jnp.max(by_block, axis=1)
    used = jnp.sum((by_block >= 0).astype(jnp.int32), axis=1)
    seen = jnp.where(inner, tag, -2)
    swapped = jnp.where(plan.far & (jnp.arange(blocks) >= blocks // 2), -2, seen)
    numbers = jnp.stack([member, plan.first, plan.edge, inner])
    meta = jnp.concatenate([tag, used, seen, swapped, tag, numbers]).astype(jnp.int32)

    heap = blocks // 2
    owner = plan.second // width
    home_row = jnp.arange(heap)[:, None] - (owner // 2 * width + plan.second % width)
    home_row = jnp.broadcast_to(home_row, (heap, BLOCK)).astype(jnp.int32)
    upper = [
        jnp.broadcast_to((member >> bit) & 1, (heap >> bit, BLOCK)).astype(jnp.int32)
        for bit in range(1, subs.bit_length() - 1)
    ]
    meta, home_row, *upper = lax.optimization_barrier((meta, home_row, *upper))

    row_sums = jax.ShapeDtypeStruct((blocks, BLOCK), jnp.float32)
    col_sums = jax.ShapeDtypeStruct((share + 1, BLOCK), jnp.float32)
    quarter = width * BLOCK
    vmem, smem = pl.BlockSpec(memory_space=pltpu.VMEM), pl.BlockSpec(memory_space=pltpu.SMEM)
    unit, sums = pl.pallas_call(
        functools.partial(self_kernel, blocks, subs),
        in_specs=[smem, pl.BlockSpec(memory_space=pl.ANY), vmem],
        out_specs=[vmem, vmem],
        out_shape=[jax.ShapeDtypeStruct((rows, depth), jnp.bfloat16), row_sums],
        scratch_shapes=[pltpu.VMEM((subs, quarter, depth), jnp.bfloat16), pltpu.SemaphoreType.DMA((subs,))],
        compiler_params=pltpu.CompilerParams(vmem_limit_bytes=24 * 1024 * 1024),
        cost_estimate=pl.CostEstimate(flops=0, bytes_accessed=1024, transcendentals=0),
    )(meta, embeddings, lax.dynamic_slice_in_dim(cluster_ids, member * quarter, quarter, 0)[None])
    second_out, sums = lax.optimization_barrier((second_out, sums))
    last = lax.ppermute(second_out, "tile", inward)

    def middle(chunk, piece, before):
        return call(
            functools.partial(middle_kernel, blocks, share, chunk),
            meta,
            (unit, piece, before),
            [row_sums, col_sums],
            [pltpu.VMEM((size, depth), jnp.bfloat16)],
            2 * rows * size * depth,
        )

    sums, swap_cols = middle(1, from_inner, sums)
    sums, outer_cols = middle(0, from_outer, sums)
    outer_back = lax.ppermute(outer_cols, "tile", turned(inward))
    swap_back = lax.ppermute(swap_cols, "tile", turned(swap))
    half = jax.ShapeDtypeStruct((heap, BLOCK), jnp.float32)
    held, leaving, cols = call(
        functools.partial(last_kernel, blocks, share, width),
        meta,
        (unit, last, relayed, sums, outer_back, swap_cols),
        [half, half, col_sums],
        [pltpu.VMEM((size, depth), jnp.bfloat16), pltpu.VMEM((blocks, BLOCK), jnp.float32)],
        2 * rows * size * depth,
    )

    home = lax.ppermute(cols, "tile", turned(around))
    for k in range(share):
        held = held + jnp.where(home_row == k, home[k : k + 1] + swap_back[k : k + 1], 0.0)
    held = held + lax.ppermute(leaving, "sub", [(i, i ^ 1) for i in range(subs)])
    home, held = lax.optimization_barrier((home, held))
    for bit, mine in enumerate(upper, 1):
        pairs = held.reshape(-1, 2, width, BLOCK)
        low, high = pairs[:, 0].reshape(mine.shape), pairs[:, 1].reshape(mine.shape)
        leaving = jnp.where(mine > 0, low, high)
        held = jnp.where(mine > 0, high, low)
        held = held + lax.ppermute(leaving, "sub", [(i, i ^ (1 << bit)) for i in range(subs)])
    scores = jnp.log(1.0 + held.reshape(-1))

    flag = pl.pallas_call(
        functools.partial(flag_kernel, share),
        out_specs=pl.BlockSpec(memory_space=pltpu.SMEM),
        out_shape=jax.ShapeDtypeStruct((1,), jnp.int32),
        compiler_params=pltpu.CompilerParams(vmem_limit_bytes=4 * 1024 * 1024),
    )(swap_cols, home)
    bad = flag[0] > 0
    if tiles > QUAD:
        bad = lax.pmax(bad.astype(jnp.int32), "tile") > 0
        bad = bad | quads_joined(tag, tiles, place)
    return lax.cond(bad, lambda: every_pair(embeddings, cluster_ids), lambda: scores)


def solution(mesh):
    in_specs = (P(("groups", "tile"), None), P(("groups", "tile")))
    out_specs = P(("groups", "tile", "sub"))
    return jax.shard_map(shards, mesh=mesh, in_specs=in_specs, out_specs=out_specs, check_vma=False)
```

```python
import functools
import math

import jax
import jax.numpy as jnp
import numpy as np
from jax import lax
from jax.experimental import pallas as pl
from jax.experimental.pallas import tpu as pltpu
from jax.sharding import PartitionSpec as P

BLOCK = 128
QUAD = 4
SPAN = 4

inverse_temp = 10.0
norm_eps = 1e-06
GAIN = inverse_temp * math.log2(math.e)
OFF = -1000.0

STEPS = (512, 256, 1024)
COPY = 64


def normalised(values):
    values = values.astype(jnp.float32)
    scale = lax.rsqrt(jnp.sum(values * values, axis=1, keepdims=True) + norm_eps)
    return (values * scale).astype(jnp.bfloat16)


def products(rows, columns):
    return lax.dot_general(
        rows, columns, (((1,), (1,)), ((), ())), preferred_element_type=jnp.float32
    )


def column_bias(tag, column_tags):
    return jnp.where(column_tags == tag.astype(jnp.float32), -GAIN, OFF)


def lane_sums(weight):
    total = weight[:, :BLOCK]
    for start in range(BLOCK, weight.shape[1], BLOCK):
        total = total + weight[:, start : start + BLOCK]
    return jnp.sum(total.T, axis=0, keepdims=True)


class Plan:
    def __init__(self, blocks, subs, place, member):
        width = blocks // subs
        share = width // 2
        part = place % QUAD
        self.inner = (part == 1) | (part == 2)
        self.far = part == 1
        dealt = member // 2 * share
        near = (dealt // width * 2 + member % 2) * width + dealt % width
        near = jnp.where(part == 1, blocks // 2, 0) + near
        self.first = jnp.where(self.inner, near, member * width)
        self.second = jnp.where(self.inner, near, member * width + share)
        self.edge = jnp.where(part == 1, blocks // 2 - 1, blocks // 2)
        self.width, self.share = width, share


def pack_kernel(blocks, subs, rows_ref, ids_ref, first_ref, second_ref, ids, sems):
    plan = Plan(blocks, subs, lax.axis_index("tile"), lax.axis_index("sub"))
    share, size = plan.share, plan.share * BLOCK
    ids_copy = pltpu.make_async_copy(ids_ref, ids, sems.at[0])

    def copies(block, out, sem):
        for down in range(0, size, COPY):
            start = pl.multiple_of(block * BLOCK + down, COPY)
            yield pltpu.make_async_copy(
                rows_ref.at[pl.ds(start, COPY), :], out.at[pl.ds(down, COPY), :], sems.at[sem + down // COPY]
            )

    first = list(copies(plan.first, first_ref, 1))
    second = list(copies(plan.second, second_ref, 1 + size // COPY))
    for copy in [ids_copy] + first + second:
        copy.start()
    ids_copy.wait()
    depth = first_ref.shape[1]
    edge = jnp.max(ids[pl.ds(plan.edge, 1), :], axis=1, keepdims=True)
    rest = [jnp.broadcast_to(edge, (1, BLOCK)), jnp.zeros((1, depth - size - BLOCK), jnp.int32)]
    for block, out in ((plan.first, first_ref), (plan.second, second_ref)):
        row = jnp.concatenate([ids[pl.ds(block + k, 1), :] for k in range(share)] + rest, axis=1)
        out[size:, :] = jnp.broadcast_to(row.astype(jnp.float32), (8, depth)).astype(jnp.bfloat16)
    for copy in first + second:
        copy.wait()


def pack(size, subs, embeddings, by_block):
    return pl.pallas_call(
        functools.partial(pack_kernel, by_block.shape[0], subs),
        in_specs=[pl.BlockSpec(memory_space=pl.ANY)] * 2,
        out_specs=[pl.BlockSpec(memory_space=pltpu.VMEM)] * 2,
        out_shape=[jax.ShapeDtypeStruct((size + 8, embeddings.shape[1]), jnp.bfloat16)] * 2,
        scratch_shapes=[pltpu.VMEM(by_block.shape, jnp.int32), pltpu.SemaphoreType.DMA((2 * size // COPY + 1,))],
        compiler_params=pltpu.CompilerParams(vmem_limit_bytes=8 * 1024 * 1024),
        cost_estimate=pl.CostEstimate(flops=0, bytes_accessed=1024, transcendentals=0),
    )(embeddings, by_block)


class Meta:
    def __init__(self, ref, blocks):
        self.ref, self.blocks = ref, blocks

    def tag(self, block, chunk=None):
        return self.ref[block + (0 if chunk is None else (2 + chunk) * self.blocks)]

    def used(self, block):
        return self.ref[self.blocks + block]

    def number(self, index):
        return self.ref[5 * self.blocks + index]


MEMBER, FIRST_BLOCK, EDGE, INNER = range(4)


def self_kernel(blocks, subs, meta_ref, rows_ref, tags_ref, unit_ref, sums_ref, held, sems):
    meta = Meta(meta_ref, blocks)
    width = blocks // subs
    quarter = width * BLOCK
    member = meta.number(MEMBER)
    owners = [lax.rem(member + turn, subs) for turn in range(subs)]
    spans = [pl.ds(pl.multiple_of(owner * quarter, quarter), quarter) for owner in owners]
    copies = []
    for turn, span in enumerate(spans):
        copies.append(pltpu.make_async_copy(rows_ref.at[span, :], held.at[turn], sems.at[turn]))
        copies[-1].start()
    column_tags = tags_ref[...].astype(jnp.float32)
    for turn in range(subs):
        copies[turn].wait()
        unit = normalised(held[turn])
        unit_ref[spans[turn], :] = unit
        if turn == 0:
            share = unit
        cosine = products(unit, share)
        for inner in range(width):
            block = owners[turn] * width + inner
            bias = column_bias(meta.tag(block), column_tags)
            weight = jnp.exp2(cosine[inner * BLOCK : (inner + 1) * BLOCK] * GAIN + bias)
            row = lax.broadcasted_iota(jnp.int32, weight.shape, 0)
            keep = row < meta.used(block)
            if turn == 0:
                keep = keep & (lax.broadcasted_iota(jnp.int32, weight.shape, 1) - row != inner * BLOCK)
            sums_ref[pl.ds(block, 1), :] = lane_sums(jnp.where(keep, weight, 0.0))


def chunk_tags(piece_ref, size):
    row = piece_ref[size:, :].astype(jnp.float32)[0:1, :]
    return row[:, :size], row[:, size : size + BLOCK]


def cross_terms(meta, chunk, column_tags, unit_ref, piece_unit, add_rows, step):
    size = column_tags.shape[1]
    columns = None
    for start in range(0, meta.blocks * BLOCK, step):
        cosine = products(unit_ref[start : start + step, :], piece_unit[...])
        for inner in range(0, step, BLOCK):
            block = (start + inner) // BLOCK
            bias = column_bias(meta.tag(block, chunk), column_tags)
            weight = jnp.exp2(cosine[inner : inner + BLOCK] * GAIN + bias)
            row = lax.broadcasted_iota(jnp.int32, weight.shape, 0)
            weight = jnp.where(row < meta.used(block), weight, 0.0)
            add_rows(block, lane_sums(weight))
            partial = weight[0:8]
            for down in range(8, BLOCK, 8):
                partial = partial + weight[down : down + 8]
            columns = partial if columns is None else columns + partial
    total = jnp.sum(columns, axis=0, keepdims=True)
    return [total[:, at : at + BLOCK] for at in range(0, size, BLOCK)]


def middle_kernel(
    blocks, share, chunk, meta_ref, unit_ref, piece_ref, before_ref, sums_ref, cols_ref, piece_unit
):
    meta = Meta(meta_ref, blocks)
    size = share * BLOCK
    piece_unit[...] = normalised(piece_ref[:size, :])
    tags, edge = chunk_tags(piece_ref, size)

    def add_rows(block, value):
        sums_ref[block : block + 1, :] = before_ref[block : block + 1, :] + value

    cols = cross_terms(meta, chunk, tags, unit_ref, piece_unit, add_rows, STEPS[chunk])
    for k in range(share):
        cols_ref[k : k + 1, :] = cols[k]
    mine = meta.tag(meta.number(EDGE)).astype(jnp.float32)
    joined = (edge == mine) & (edge >= 0) & (meta.number(INNER) > 0)
    cols_ref[share : share + 1, :] = jnp.where(joined, 1.0, 0.0)


def last_kernel(
    blocks, share, width, meta_ref, unit_ref, piece_ref, before_ref, outer_back_ref, swap_cols_ref,
    keep_ref, send_ref, cols_ref, piece_unit, sums,
):
    meta = Meta(meta_ref, blocks)
    size = share * BLOCK
    piece_unit[...] = normalised(piece_ref[:size, :])
    tags, _ = chunk_tags(piece_ref, size)

    def place(block):
        owner = block // width
        return owner % 2 * (blocks // 2) + owner // 2 * width + block % width

    def add_rows(block, value):
        at = place(block)
        sums[at : at + 1, :] = before_ref[block : block + 1, :] + value

    cols = cross_terms(meta, 2, tags, unit_ref, piece_unit, add_rows, STEPS[2])
    for k in range(share):
        cols_ref[k : k + 1, :] = cols[k]
        at = place(meta.number(FIRST_BLOCK) + k)
        sums[pl.ds(at, 1), :] += outer_back_ref[k : k + 1, :]
    cols_ref[share : share + 1, :] = swap_cols_ref[share : share + 1, :]
    parity = meta.number(MEMBER) % 2
    heap = blocks // 2
    keep_ref[...] = sums[pl.ds(pl.multiple_of(parity * heap, heap), heap), :]
    send_ref[...] = sums[pl.ds(pl.multiple_of((1 - parity) * heap, heap), heap), :]


def flag_kernel(share, here_ref, home_ref, flag_ref):
    flags = jnp.maximum(here_ref[share : share + 1, :], home_ref[share : share + 1, :])
    flag_ref[0] = jnp.max(flags).astype(jnp.int32)


def call(kernel, meta, operands, out_shapes, scratch, flops):
    vmem, smem = pl.BlockSpec(memory_space=pltpu.VMEM), pl.BlockSpec(memory_space=pltpu.SMEM)
    return pl.pallas_call(
        kernel,
        in_specs=[smem] + [vmem] * len(operands),
        out_specs=[vmem if len(shape.shape) > 1 else smem for shape in out_shapes],
        out_shape=out_shapes,
        scratch_shapes=scratch,
        compiler_params=pltpu.CompilerParams(vmem_limit_bytes=16 * 1024 * 1024),
        cost_estimate=pl.CostEstimate(flops=flops, bytes_accessed=1024, transcendentals=0),
    )(meta, *operands)


def every_pair(embeddings, cluster_ids):
    unit = normalised(embeddings)
    tags = cluster_ids + 1
    groups = lax.axis_size("sub")
    member = lax.axis_index("sub")
    owners = lax.axis_size("tile")
    place = lax.axis_index("tile")
    rows_here = unit.shape[0]
    width = rows_here // groups
    own_piece = lax.dynamic_slice_in_dim(unit, member * width, width, 0)
    own_tags = lax.dynamic_slice_in_dim(tags, member * width, width, 0)
    distance = place - jnp.arange(owners, dtype=jnp.int32)
    keep = (jnp.abs(distance) < SPAN) & (distance != 0)
    outgoing = jnp.where(keep[:, None, None], own_piece[None, :, :], jnp.zeros((), jnp.bfloat16))
    outgoing_tags = jnp.where(keep[:, None], own_tags[None, :], 0)
    arrived = lax.all_to_all(outgoing, "tile", split_axis=0, concat_axis=0, tiled=True)
    arrived_tags = lax.all_to_all(outgoing_tags, "tile", split_axis=0, concat_axis=0, tiled=True)
    local_rows = jnp.arange(rows_here, dtype=jnp.int32)[:, None]
    slice_rows = member * width + jnp.arange(width, dtype=jnp.int32)[None, :]
    total = jnp.zeros((rows_here,), jnp.float32)
    for offset in range(1 - SPAN, SPAN):
        if offset == 0:
            piece, piece_tags, order = own_piece, own_tags, local_rows != slice_rows
        else:
            source = place + offset
            valid = (source >= 0) & (source < owners)
            index = jnp.clip(source, 0, owners - 1)
            piece = lax.dynamic_index_in_dim(arrived, index, 0, keepdims=False)
            piece_tags = lax.dynamic_index_in_dim(arrived_tags, index, 0, keepdims=False)
            piece_tags = jnp.where(valid, piece_tags, 0)
            order = True
        same = (tags[:, None] == piece_tags[None, :]) & (tags[:, None] > 0) & order
        weight = jnp.where(same, jnp.exp(inverse_temp * (products(unit, piece) - 1.0)), 0.0)
        total = total + jnp.sum(weight, axis=1)
    return jnp.log(1.0 + lax.psum_scatter(total, "sub", scatter_dimension=0, tiled=True))


def quads_joined(tag, tiles, place):
    last = jnp.broadcast_to(tag[-1], (BLOCK,))
    before = lax.ppermute(last, "tile", [(t, t + 1) for t in range(tiles - 1)])[0]
    joined = (place % QUAD == 0) & (place > 0) & (before == tag[0]) & (before >= 0)
    return lax.pmax(joined.astype(jnp.int32), "tile") > 0


def shards(embeddings, cluster_ids):
    tiles, subs = lax.axis_size("tile"), lax.axis_size("sub")
    place, member = lax.axis_index("tile"), lax.axis_index("sub")
    rows, depth = embeddings.shape
    blocks = rows // BLOCK
    plan = Plan(blocks, subs, place, member)
    width, share, inner = plan.width, plan.share, plan.inner
    size = share * BLOCK
    quads = range(0, tiles, QUAD)
    inward = [p for q in quads for p in ((q, q + 1), (q + 3, q + 2))]
    swap = [p for q in quads for p in ((q + 1, q + 2), (q + 2, q + 1))]
    around = [p for q in quads for p in ((q, q + 1), (q + 3, q + 2), (q + 1, q + 3), (q + 2, q))]

    def turned(route):
        return [(b, a) for a, b in route]

    by_block = cluster_ids.reshape(blocks, BLOCK)
    first_out, second_out = pack(size, subs, embeddings, by_block)
    from_inner = lax.ppermute(first_out, "tile", swap)
    from_outer = lax.ppermute(first_out, "tile", inward)

    tag = jnp.max(by_block, axis=1)
    used = jnp.sum((by_block >= 0).astype(jnp.int32), axis=1)
    seen = jnp.where(inner, tag, -2)
    swapped = jnp.where(plan.far & (jnp.arange(blocks) >= blocks // 2), -2, seen)
    numbers = jnp.stack([member, plan.first, plan.edge, inner])
    meta = jnp.concatenate([tag, used, seen, swapped, tag, numbers]).astype(jnp.int32)

    heap = blocks // 2
    owner = plan.second // width
    home_row = jnp.arange(heap)[:, None] - (owner // 2 * width + plan.second % width)
    home_row = jnp.broadcast_to(home_row, (heap, BLOCK)).astype(jnp.int32)
    upper = [
        jnp.broadcast_to((member >> bit) & 1, (heap >> bit, BLOCK)).astype(jnp.int32)
        for bit in range(1, subs.bit_length() - 1)
    ]
    meta, home_row, *upper = lax.optimization_barrier((meta, home_row, *upper))

    row_sums = jax.ShapeDtypeStruct((blocks, BLOCK), jnp.float32)
    col_sums = jax.ShapeDtypeStruct((share + 1, BLOCK), jnp.float32)
    quarter = width * BLOCK
    vmem, smem = pl.BlockSpec(memory_space=pltpu.VMEM), pl.BlockSpec(memory_space=pltpu.SMEM)
    unit, sums = pl.pallas_call(
        functools.partial(self_kernel, blocks, subs),
        in_specs=[smem, pl.BlockSpec(memory_space=pl.ANY), vmem],
        out_specs=[vmem, vmem],
        out_shape=[jax.ShapeDtypeStruct((rows, depth), jnp.bfloat16), row_sums],
        scratch_shapes=[pltpu.VMEM((subs, quarter, depth), jnp.bfloat16), pltpu.SemaphoreType.DMA((subs,))],
        compiler_params=pltpu.CompilerParams(vmem_limit_bytes=24 * 1024 * 1024),
        cost_estimate=pl.CostEstimate(flops=0, bytes_accessed=1024, transcendentals=0),
    )(meta, embeddings, lax.dynamic_slice_in_dim(cluster_ids, member * quarter, quarter, 0)[None])
    second_out, sums = lax.optimization_barrier((second_out, sums))
    last = lax.ppermute(second_out, "tile", around)

    def middle(chunk, piece, before):
        return call(
            functools.partial(middle_kernel, blocks, share, chunk),
            meta,
            (unit, piece, before),
            [row_sums, col_sums],
            [pltpu.VMEM((size, depth), jnp.bfloat16)],
            2 * rows * size * depth,
        )

    sums, outer_cols = middle(0, from_outer, sums)
    outer_back = lax.ppermute(outer_cols, "tile", turned(inward))
    sums, swap_cols = middle(1, from_inner, sums)
    swap_back = lax.ppermute(swap_cols, "tile", turned(swap))
    half = jax.ShapeDtypeStruct((heap, BLOCK), jnp.float32)
    held, leaving, cols = call(
        functools.partial(last_kernel, blocks, share, width),
        meta,
        (unit, last, sums, outer_back, swap_cols),
        [half, half, col_sums],
        [pltpu.VMEM((size, depth), jnp.bfloat16), pltpu.VMEM((blocks, BLOCK), jnp.float32)],
        2 * rows * size * depth,
    )

    home = lax.ppermute(cols, "tile", turned(around))
    for k in range(share):
        held = held + jnp.where(home_row == k, home[k : k + 1] + swap_back[k : k + 1], 0.0)
    held = held + lax.ppermute(leaving, "sub", [(i, i ^ 1) for i in range(subs)])
    home, held = lax.optimization_barrier((home, held))
    for bit, mine in enumerate(upper, 1):
        pairs = held.reshape(-1, 2, width, BLOCK)
        low, high = pairs[:, 0].reshape(mine.shape), pairs[:, 1].reshape(mine.shape)
        leaving = jnp.where(mine > 0, low, high)
        held = jnp.where(mine > 0, high, low)
        held = held + lax.ppermute(leaving, "sub", [(i, i ^ (1 << bit)) for i in range(subs)])
    scores = jnp.log(1.0 + held.reshape(-1))

    flag = pl.pallas_call(
        functools.partial(flag_kernel, share),
        out_specs=pl.BlockSpec(memory_space=pltpu.SMEM),
        out_shape=jax.ShapeDtypeStruct((1,), jnp.int32),
        compiler_params=pltpu.CompilerParams(vmem_limit_bytes=4 * 1024 * 1024),
    )(swap_cols, home)
    bad = flag[0] > 0
    if tiles > QUAD:
        bad = lax.pmax(bad.astype(jnp.int32), "tile") > 0
        bad = bad | quads_joined(tag, tiles, place)
    return lax.cond(bad, lambda: every_pair(embeddings, cluster_ids), lambda: scores)


def solution(mesh):
    in_specs = (P(("groups", "tile"), None), P(("groups", "tile")))
    out_specs = P(("groups", "tile", "sub"))
    return jax.shard_map(shards, mesh=mesh, in_specs=in_specs, out_specs=out_specs, check_vma=False)
```

```python
import functools
import math

import jax
import jax.numpy as jnp
import numpy as np
from jax import lax
from jax.experimental import pallas as pl
from jax.experimental.pallas import tpu as pltpu
from jax.sharding import PartitionSpec as P

BLOCK = 128
QUAD = 4
SPAN = 4

inverse_temp = 10.0
norm_eps = 1e-06
GAIN = inverse_temp * math.log2(math.e)
OFF = -1000.0

STEP = 512
COPY = 64


def normalised(values):
    values = values.astype(jnp.float32)
    scale = lax.rsqrt(jnp.sum(values * values, axis=1, keepdims=True) + norm_eps)
    return (values * scale).astype(jnp.bfloat16)


def products(rows, columns):
    return lax.dot_general(
        rows, columns, (((1,), (1,)), ((), ())), preferred_element_type=jnp.float32
    )


def column_bias(tag, column_tags):
    return jnp.where(column_tags == tag.astype(jnp.float32), -GAIN, OFF)


def lane_sums(weight):
    total = weight[:, :BLOCK]
    for start in range(BLOCK, weight.shape[1], BLOCK):
        total = total + weight[:, start : start + BLOCK]
    return jnp.sum(total.T, axis=0, keepdims=True)


class Plan:
    def __init__(self, blocks, subs, place, member):
        width = blocks // subs
        share = width // 2
        part = place % QUAD
        self.inner = (part == 1) | (part == 2)
        self.far = part == 1
        dealt = member // 2 * share
        near = (dealt // width * 2 + member % 2) * width + dealt % width
        near = jnp.where(part == 1, blocks // 2, 0) + near
        self.first = jnp.where(self.inner, near, member * width)
        self.second = member * width + share
        self.edge = jnp.where(part == 1, blocks // 2 - 1, blocks // 2)
        self.width, self.share = width, share


def pack_kernel(blocks, subs, rows_ref, ids_ref, first_ref, second_ref, low_ref, high_ref, ids, sems):
    plan = Plan(blocks, subs, lax.axis_index("tile"), lax.axis_index("sub"))
    share, size = plan.share, plan.share * BLOCK
    ids_copy = pltpu.make_async_copy(ids_ref, ids, sems.at[0])
    ids_copy.start()

    def copies(block, parts, sem):
        down = 0
        for part, count in parts:
            for at in range(0, count, COPY):
                start = pl.multiple_of(block * BLOCK + down, COPY)
                yield pltpu.make_async_copy(
                    rows_ref.at[pl.ds(start, COPY), :], part.at[pl.ds(at, COPY), :], sems.at[sem + down // COPY]
                )
                down += COPY

    near = list(copies(plan.first, ((low_ref, size // 2), (high_ref, size // 2)), 1))
    outer = list(copies(plan.first, ((first_ref, size),), 1))
    outer += list(copies(plan.second, ((second_ref, size),), 1 + size // COPY))

    @pl.when(plan.inner)
    def _():
        for copy in near:
            copy.start()

    @pl.when(jnp.logical_not(plan.inner))
    def _():
        for copy in outer:
            copy.start()

    ids_copy.wait()
    depth = first_ref.shape[1]
    edge = jnp.max(ids[pl.ds(plan.edge, 1), :], axis=1, keepdims=True)
    rest = [jnp.broadcast_to(edge, (1, BLOCK)), jnp.zeros((1, depth - size - BLOCK), jnp.int32)]
    for block, outs in ((plan.first, (first_ref, high_ref)), (plan.second, (second_ref,))):
        row = jnp.concatenate([ids[pl.ds(block + k, 1), :] for k in range(share)] + rest, axis=1)
        row = jnp.broadcast_to(row.astype(jnp.float32), (8, depth)).astype(jnp.bfloat16)
        for out in outs:
            out[out.shape[0] - 8 :, :] = row

    @pl.when(plan.inner)
    def _():
        for copy in near:
            copy.wait()

    @pl.when(jnp.logical_not(plan.inner))
    def _():
        for copy in outer:
            copy.wait()


def pack(size, subs, embeddings, by_block):
    depth = embeddings.shape[1]
    counts = (size + 8, size + 8, size // 2, size // 2 + 8)
    return pl.pallas_call(
        functools.partial(pack_kernel, by_block.shape[0], subs),
        in_specs=[pl.BlockSpec(memory_space=pl.ANY)] * 2,
        out_specs=[pl.BlockSpec(memory_space=pltpu.VMEM)] * len(counts),
        out_shape=[jax.ShapeDtypeStruct((count, depth), jnp.bfloat16) for count in counts],
        scratch_shapes=[pltpu.VMEM(by_block.shape, jnp.int32), pltpu.SemaphoreType.DMA((2 * size // COPY + 1,))],
        compiler_params=pltpu.CompilerParams(vmem_limit_bytes=8 * 1024 * 1024),
        cost_estimate=pl.CostEstimate(flops=0, bytes_accessed=1024, transcendentals=0),
    )(embeddings, by_block)


class Meta:
    def __init__(self, ref, blocks):
        self.ref, self.blocks = ref, blocks

    def tag(self, block, chunk=None):
        return self.ref[block + (0 if chunk is None else (2 + chunk) * self.blocks)]

    def used(self, block):
        return self.ref[self.blocks + block]

    def number(self, index):
        return self.ref[5 * self.blocks + index]


MEMBER, EDGE, INNER = range(3)


def self_kernel(blocks, subs, meta_ref, rows_ref, tags_ref, unit_ref, sums_ref, held, sems):
    meta = Meta(meta_ref, blocks)
    width = blocks // subs
    quarter = width * BLOCK
    member = meta.number(MEMBER)
    owners = [lax.rem(member + turn, subs) for turn in range(subs)]
    spans = [pl.ds(pl.multiple_of(owner * quarter, quarter), quarter) for owner in owners]
    copies = []
    for turn, span in enumerate(spans):
        copies.append(pltpu.make_async_copy(rows_ref.at[span, :], held.at[turn], sems.at[turn]))
        copies[-1].start()
    column_tags = tags_ref[...].astype(jnp.float32)
    for turn in range(subs):
        copies[turn].wait()
        unit = normalised(held[turn])
        unit_ref[spans[turn], :] = unit
        if turn == 0:
            share = unit
        cosine = products(unit, share)
        for inner in range(width):
            block = owners[turn] * width + inner
            bias = column_bias(meta.tag(block), column_tags)
            weight = jnp.exp2(cosine[inner * BLOCK : (inner + 1) * BLOCK] * GAIN + bias)
            row = lax.broadcasted_iota(jnp.int32, weight.shape, 0)
            keep = row < meta.used(block)
            if turn == 0:
                keep = keep & (lax.broadcasted_iota(jnp.int32, weight.shape, 1) - row != inner * BLOCK)
            sums_ref[pl.ds(block, 1), :] = lane_sums(jnp.where(keep, weight, 0.0))


def take_chunk(parts, piece_unit):
    down = 0
    for part in parts:
        count = part.shape[0] // 16 * 16
        piece_unit[down : down + count, :] = normalised(part[:count, :])
        down += count


def chunk_tags(parts, size):
    row = parts[-1][parts[-1].shape[0] - 8 :, :].astype(jnp.float32)[0:1, :]
    return row[:, :size], row[:, size : size + BLOCK]


def cross_terms(meta, chunk, column_tags, unit_ref, piece_unit, add_rows):
    size = column_tags.shape[1]
    columns = None
    for start in range(0, meta.blocks * BLOCK, STEP):
        cosine = products(unit_ref[start : start + STEP, :], piece_unit[...])
        for inner in range(0, STEP, BLOCK):
            block = (start + inner) // BLOCK
            bias = column_bias(meta.tag(block, chunk), column_tags)
            weight = jnp.exp2(cosine[inner : inner + BLOCK] * GAIN + bias)
            row = lax.broadcasted_iota(jnp.int32, weight.shape, 0)
            weight = jnp.where(row < meta.used(block), weight, 0.0)
            add_rows(block, lane_sums(weight))
            partial = weight[0:8]
            for down in range(8, BLOCK, 8):
                partial = partial + weight[down : down + 8]
            columns = partial if columns is None else columns + partial
    total = jnp.sum(columns, axis=0, keepdims=True)
    return [total[:, at : at + BLOCK] for at in range(0, size, BLOCK)]


def middle_kernel(blocks, share, chunk, meta_ref, unit_ref, *refs):
    *parts, before_ref, sums_ref, cols_ref, piece_unit = refs
    meta = Meta(meta_ref, blocks)
    take_chunk(parts, piece_unit)
    tags, edge = chunk_tags(parts, share * BLOCK)

    def add_rows(block, value):
        sums_ref[block : block + 1, :] = before_ref[block : block + 1, :] + value

    cols = cross_terms(meta, chunk, tags, unit_ref, piece_unit, add_rows)
    for k in range(share):
        cols_ref[k : k + 1, :] = cols[k]
    mine = meta.tag(meta.number(EDGE)).astype(jnp.float32)
    joined = (edge == mine) & (edge >= 0) & (meta.number(INNER) > 0)
    cols_ref[share : share + 1, :] = jnp.where(joined, 1.0, 0.0)


def last_kernel(
    blocks, share, width, meta_ref, unit_ref, inward_ref, low_ref, high_ref, before_ref, outer_cols_ref, swap_cols_ref,
    keep_ref, send_ref, cols_ref, piece_unit, sums,
):
    meta = Meta(meta_ref, blocks)
    size = share * BLOCK
    is_inner = meta.number(INNER) > 0

    @pl.when(is_inner)
    def _():
        take_chunk((inward_ref,), piece_unit)

    @pl.when(jnp.logical_not(is_inner))
    def _():
        take_chunk((low_ref, high_ref), piece_unit)

    tags = jnp.where(is_inner, chunk_tags((inward_ref,), size)[0], chunk_tags((low_ref, high_ref), size)[0])

    def place(block):
        owner = block // width
        return owner % 2 * (blocks // 2) + owner // 2 * width + block % width

    def add_rows(block, value):
        at = place(block)
        sums[at : at + 1, :] = before_ref[block : block + 1, :] + value

    cols = cross_terms(meta, 2, tags, unit_ref, piece_unit, add_rows)
    for k in range(share):
        cols_ref[k : k + 1, :] = jnp.where(is_inner, outer_cols_ref[k : k + 1, :], cols[k])
        cols_ref[share + k : share + k + 1, :] = jnp.where(is_inner, cols[k], 0.0)
    cols_ref[2 * share : 2 * share + 1, :] = swap_cols_ref[share : share + 1, :]
    parity = meta.number(MEMBER) % 2
    heap = blocks // 2
    keep_ref[...] = sums[pl.ds(pl.multiple_of(parity * heap, heap), heap), :]
    send_ref[...] = sums[pl.ds(pl.multiple_of((1 - parity) * heap, heap), heap), :]


def flag_kernel(share, here_ref, home_ref, flag_ref):
    flags = jnp.maximum(here_ref[share : share + 1, :], home_ref[2 * share : 2 * share + 1, :])
    flag_ref[0] = jnp.max(flags).astype(jnp.int32)


def call(kernel, meta, operands, out_shapes, scratch):
    vmem, smem = pl.BlockSpec(memory_space=pltpu.VMEM), pl.BlockSpec(memory_space=pltpu.SMEM)
    return pl.pallas_call(
        kernel,
        in_specs=[smem] + [vmem] * len(operands),
        out_specs=[vmem if len(shape.shape) > 1 else smem for shape in out_shapes],
        out_shape=out_shapes,
        scratch_shapes=scratch,
        compiler_params=pltpu.CompilerParams(vmem_limit_bytes=16 * 1024 * 1024),
        cost_estimate=pl.CostEstimate(flops=0, bytes_accessed=1024, transcendentals=0),
    )(meta, *operands)


def every_pair(embeddings, cluster_ids):
    unit = normalised(embeddings)
    tags = cluster_ids + 1
    groups = lax.axis_size("sub")
    member = lax.axis_index("sub")
    owners = lax.axis_size("tile")
    place = lax.axis_index("tile")
    rows_here = unit.shape[0]
    width = rows_here // groups
    own_piece = lax.dynamic_slice_in_dim(unit, member * width, width, 0)
    own_tags = lax.dynamic_slice_in_dim(tags, member * width, width, 0)
    distance = place - jnp.arange(owners, dtype=jnp.int32)
    keep = (jnp.abs(distance) < SPAN) & (distance != 0)
    outgoing = jnp.where(keep[:, None, None], own_piece[None, :, :], jnp.zeros((), jnp.bfloat16))
    outgoing_tags = jnp.where(keep[:, None], own_tags[None, :], 0)
    arrived = lax.all_to_all(outgoing, "tile", split_axis=0, concat_axis=0, tiled=True)
    arrived_tags = lax.all_to_all(outgoing_tags, "tile", split_axis=0, concat_axis=0, tiled=True)
    local_rows = jnp.arange(rows_here, dtype=jnp.int32)[:, None]
    slice_rows = member * width + jnp.arange(width, dtype=jnp.int32)[None, :]
    total = jnp.zeros((rows_here,), jnp.float32)
    for offset in range(1 - SPAN, SPAN):
        if offset == 0:
            piece, piece_tags, order = own_piece, own_tags, local_rows != slice_rows
        else:
            source = place + offset
            valid = (source >= 0) & (source < owners)
            index = jnp.clip(source, 0, owners - 1)
            piece = lax.dynamic_index_in_dim(arrived, index, 0, keepdims=False)
            piece_tags = lax.dynamic_index_in_dim(arrived_tags, index, 0, keepdims=False)
            piece_tags = jnp.where(valid, piece_tags, 0)
            order = True
        same = (tags[:, None] == piece_tags[None, :]) & (tags[:, None] > 0) & order
        weight = jnp.where(same, jnp.exp(inverse_temp * (products(unit, piece) - 1.0)), 0.0)
        total = total + jnp.sum(weight, axis=1)
    return jnp.log(1.0 + lax.psum_scatter(total, "sub", scatter_dimension=0, tiled=True))


def quads_joined(tag, tiles, place):
    last = jnp.broadcast_to(tag[-1], (BLOCK,))
    before = lax.ppermute(last, "tile", [(t, t + 1) for t in range(tiles - 1)])[0]
    joined = (place % QUAD == 0) & (place > 0) & (before == tag[0]) & (before >= 0)
    return lax.pmax(joined.astype(jnp.int32), "tile") > 0


def shards(embeddings, cluster_ids):
    tiles, subs = lax.axis_size("tile"), lax.axis_size("sub")
    place, member = lax.axis_index("tile"), lax.axis_index("sub")
    rows, depth = embeddings.shape
    blocks = rows // BLOCK
    plan = Plan(blocks, subs, place, member)
    width, share, inner = plan.width, plan.share, plan.inner
    size = share * BLOCK
    quads = range(0, tiles, QUAD)
    inward = [p for q in quads for p in ((q, q + 1), (q + 3, q + 2))]
    swap = [p for q in quads for p in ((q + 1, q + 2), (q + 2, q + 1))]
    around = [p for q in quads for p in ((q, q + 1), (q + 3, q + 2), (q + 1, q + 3), (q + 2, q))]

    def turned(route):
        return [(b, a) for a, b in route]

    by_block = cluster_ids.reshape(blocks, BLOCK)
    first_out, second_out, low_out, high_out = pack(size, subs, embeddings, by_block)
    from_outer = lax.ppermute(first_out, "tile", inward)

    tag = jnp.max(by_block, axis=1)
    used = jnp.sum((by_block >= 0).astype(jnp.int32), axis=1)
    seen = jnp.where(inner, tag, -2)
    swapped = jnp.where(plan.far & (jnp.arange(blocks) >= blocks // 2), -2, seen)
    numbers = jnp.stack([member, plan.edge, inner])
    meta = jnp.concatenate([tag, used, seen, swapped, tag, numbers]).astype(jnp.int32)

    heap = blocks // 2
    owner = plan.first // width
    home_row = jnp.arange(heap)[:, None] - (owner // 2 * width + plan.first % width)
    home_row = jnp.broadcast_to(home_row, (heap, BLOCK)).astype(jnp.int32)
    upper = [
        jnp.broadcast_to((member >> bit) & 1, (heap >> bit, BLOCK)).astype(jnp.int32)
        for bit in range(1, subs.bit_length() - 1)
    ]
    meta, home_row, low_out, high_out, *upper = lax.optimization_barrier((meta, home_row, low_out, high_out, *upper))
    near_high = lax.ppermute(high_out, "tile", swap)
    near_low = lax.ppermute(low_out, "tile", swap)

    row_sums = jax.ShapeDtypeStruct((blocks, BLOCK), jnp.float32)
    col_sums = jax.ShapeDtypeStruct((share + 1, BLOCK), jnp.float32)
    quarter = width * BLOCK
    vmem, smem = pl.BlockSpec(memory_space=pltpu.VMEM), pl.BlockSpec(memory_space=pltpu.SMEM)
    unit, sums = pl.pallas_call(
        functools.partial(self_kernel, blocks, subs),
        in_specs=[smem, pl.BlockSpec(memory_space=pl.ANY), vmem],
        out_specs=[vmem, vmem],
        out_shape=[jax.ShapeDtypeStruct((rows, depth), jnp.bfloat16), row_sums],
        scratch_shapes=[pltpu.VMEM((subs, quarter, depth), jnp.bfloat16), pltpu.SemaphoreType.DMA((subs,))],
        compiler_params=pltpu.CompilerParams(vmem_limit_bytes=24 * 1024 * 1024),
        cost_estimate=pl.CostEstimate(flops=0, bytes_accessed=1024, transcendentals=0),
    )(meta, embeddings, lax.dynamic_slice_in_dim(cluster_ids, member * quarter, quarter, 0)[None])
    second_out, near_low, sums = lax.optimization_barrier((second_out, near_low, sums))
    relayed_low = lax.ppermute(near_low, "tile", turned(inward))
    last = lax.ppermute(second_out, "tile", inward)

    def middle(chunk, parts, before):
        return call(
            functools.partial(middle_kernel, blocks, share, chunk),
            meta,
            (unit, *parts, before),
            [row_sums, col_sums],
            [pltpu.VMEM((size, depth), jnp.bfloat16)],
        )

    sums, outer_cols = middle(0, (from_outer,), sums)
    near_high, relayed_low, sums = lax.optimization_barrier((near_high, relayed_low, sums))
    relayed_high = lax.ppermute(near_high, "tile", turned(inward))
    sums, swap_cols = middle(1, (near_low, near_high), sums)
    swap_back = lax.ppermute(swap_cols, "tile", turned(swap))
    swap_back, sums = lax.optimization_barrier((swap_back, sums))
    half = jax.ShapeDtypeStruct((heap, BLOCK), jnp.float32)
    held, leaving, cols = call(
        functools.partial(last_kernel, blocks, share, width),
        meta,
        (unit, last, relayed_low, relayed_high, sums, outer_cols, swap_cols),
        [half, half, jax.ShapeDtypeStruct((2 * share + 1, BLOCK), jnp.float32)],
        [pltpu.VMEM((size, depth), jnp.bfloat16), pltpu.VMEM((blocks, BLOCK), jnp.float32)],
    )

    home = lax.ppermute(cols, "tile", turned(around))
    for k in range(2 * share):
        came = home[k : k + 1] + swap_back[k : k + 1] if k < share else home[k : k + 1]
        held = held + jnp.where(home_row == k, came, 0.0)
    held = held + lax.ppermute(leaving, "sub", [(i, i ^ 1) for i in range(subs)])
    home, held = lax.optimization_barrier((home, held))
    for bit, mine in enumerate(upper, 1):
        pairs = held.reshape(-1, 2, width, BLOCK)
        low, high = pairs[:, 0].reshape(mine.shape), pairs[:, 1].reshape(mine.shape)
        leaving = jnp.where(mine > 0, low, high)
        held = jnp.where(mine > 0, high, low)
        held = held + lax.ppermute(leaving, "sub", [(i, i ^ (1 << bit)) for i in range(subs)])
    scores = jnp.log(1.0 + held.reshape(-1))

    flag = pl.pallas_call(
        functools.partial(flag_kernel, share),
        out_specs=pl.BlockSpec(memory_space=pltpu.SMEM),
        out_shape=jax.ShapeDtypeStruct((1,), jnp.int32),
        compiler_params=pltpu.CompilerParams(vmem_limit_bytes=4 * 1024 * 1024),
    )(swap_cols, home)
    bad = flag[0] > 0
    if tiles > QUAD:
        bad = lax.pmax(bad.astype(jnp.int32), "tile") > 0
        bad = bad | quads_joined(tag, tiles, place)
    return lax.cond(bad, lambda: every_pair(embeddings, cluster_ids), lambda: scores)


def solution(mesh):
    in_specs = (P(("groups", "tile"), None), P(("groups", "tile")))
    out_specs = P(("groups", "tile", "sub"))
    return jax.shard_map(shards, mesh=mesh, in_specs=in_specs, out_specs=out_specs, check_vma=False)
```

```python
import functools
import math

import jax
import jax.numpy as jnp
import numpy as np
from jax import lax
from jax.experimental import pallas as pl
from jax.experimental.pallas import tpu as pltpu
from jax.sharding import PartitionSpec as P

BLOCK = 128
QUAD = 4
SPAN = 4

inverse_temp = 10.0
norm_eps = 1e-06
GAIN = inverse_temp * math.log2(math.e)
OFF = -1000.0

STEP = 512
COPY = 64


def normalised(values):
    values = values.astype(jnp.float32)
    scale = lax.rsqrt(jnp.sum(values * values, axis=1, keepdims=True) + norm_eps)
    return (values * scale).astype(jnp.bfloat16)


def products(rows, columns):
    return lax.dot_general(
        rows, columns, (((1,), (1,)), ((), ())), preferred_element_type=jnp.float32
    )


def column_bias(tag, column_tags):
    return jnp.where(column_tags == tag.astype(jnp.float32), -GAIN, OFF)


def lane_sums(weight):
    total = weight[:, :BLOCK]
    for start in range(BLOCK, weight.shape[1], BLOCK):
        total = total + weight[:, start : start + BLOCK]
    return jnp.sum(total.T, axis=0, keepdims=True)


class Plan:
    def __init__(self, blocks, subs, place, member):
        width = blocks // subs
        share = width // 2
        part = place % QUAD
        self.inner = (part == 1) | (part == 2)
        self.far = part == 1
        dealt = member // 2 * share
        near = (dealt // width * 2 + member % 2) * width + dealt % width
        near = jnp.where(part == 1, blocks // 2, 0) + near
        self.first = jnp.where(self.inner, near, member * width)
        self.second = member * width + share
        self.edge = jnp.where(part == 1, blocks // 2 - 1, blocks // 2)
        self.width, self.share = width, share


def pack_kernel(blocks, subs, rows_ref, ids_ref, first_ref, second_ref, ids, sems):
    plan = Plan(blocks, subs, lax.axis_index("tile"), lax.axis_index("sub"))
    share, size = plan.share, plan.share * BLOCK
    ids_copy = pltpu.make_async_copy(ids_ref, ids, sems.at[0])

    def copies(block, out, sem):
        for down in range(0, size, COPY):
            start = pl.multiple_of(block * BLOCK + down, COPY)
            yield pltpu.make_async_copy(
                rows_ref.at[pl.ds(start, COPY), :], out.at[pl.ds(down, COPY), :], sems.at[sem + down // COPY]
            )

    first = list(copies(plan.first, first_ref, 1))
    second = list(copies(plan.second, second_ref, 1 + size // COPY))
    for copy in [ids_copy] + first:
        copy.start()

    @pl.when(jnp.logical_not(plan.inner))
    def _():
        for copy in second:
            copy.start()

    ids_copy.wait()
    depth = first_ref.shape[1]
    edge = jnp.max(ids[pl.ds(plan.edge, 1), :], axis=1, keepdims=True)
    rest = [jnp.broadcast_to(edge, (1, BLOCK)), jnp.zeros((1, depth - size - BLOCK), jnp.int32)]
    for block, out in ((plan.first, first_ref), (plan.second, second_ref)):
        row = jnp.concatenate([ids[pl.ds(block + k, 1), :] for k in range(share)] + rest, axis=1)
        out[size:, :] = jnp.broadcast_to(row.astype(jnp.float32), (8, depth)).astype(jnp.bfloat16)
    for copy in first:
        copy.wait()

    @pl.when(jnp.logical_not(plan.inner))
    def _():
        for copy in second:
            copy.wait()


def pack(size, subs, embeddings, by_block):
    return pl.pallas_call(
        functools.partial(pack_kernel, by_block.shape[0], subs),
        in_specs=[pl.BlockSpec(memory_space=pl.ANY)] * 2,
        out_specs=[pl.BlockSpec(memory_space=pltpu.VMEM)] * 2,
        out_shape=[jax.ShapeDtypeStruct((size + 8, embeddings.shape[1]), jnp.bfloat16)] * 2,
        scratch_shapes=[pltpu.VMEM(by_block.shape, jnp.int32), pltpu.SemaphoreType.DMA((2 * size // COPY + 1,))],
        compiler_params=pltpu.CompilerParams(vmem_limit_bytes=8 * 1024 * 1024),
        cost_estimate=pl.CostEstimate(flops=0, bytes_accessed=1024, transcendentals=0),
    )(embeddings, by_block)


class Meta:
    def __init__(self, ref, blocks):
        self.ref, self.blocks = ref, blocks

    def tag(self, block, chunk=None):
        return self.ref[block + (0 if chunk is None else (2 + chunk) * self.blocks)]

    def used(self, block):
        return self.ref[self.blocks + block]

    def number(self, index):
        return self.ref[5 * self.blocks + index]


MEMBER, EDGE, INNER = range(3)


def self_kernel(blocks, subs, meta_ref, rows_ref, tags_ref, unit_ref, sums_ref, held, sems):
    meta = Meta(meta_ref, blocks)
    width = blocks // subs
    quarter = width * BLOCK
    member = meta.number(MEMBER)
    owners = [lax.rem(member + turn, subs) for turn in range(subs)]
    spans = [pl.ds(pl.multiple_of(owner * quarter, quarter), quarter) for owner in owners]
    copies = []
    for turn, span in enumerate(spans):
        copies.append(pltpu.make_async_copy(rows_ref.at[span, :], held.at[turn], sems.at[turn]))
        copies[-1].start()
    column_tags = tags_ref[...].astype(jnp.float32)
    for turn in range(subs):
        copies[turn].wait()
        unit = normalised(held[turn])
        unit_ref[spans[turn], :] = unit
        if turn == 0:
            share = unit
        cosine = products(unit, share)
        for inner in range(width):
            block = owners[turn] * width + inner
            bias = column_bias(meta.tag(block), column_tags)
            weight = jnp.exp2(cosine[inner * BLOCK : (inner + 1) * BLOCK] * GAIN + bias)
            row = lax.broadcasted_iota(jnp.int32, weight.shape, 0)
            keep = row < meta.used(block)
            if turn == 0:
                keep = keep & (lax.broadcasted_iota(jnp.int32, weight.shape, 1) - row != inner * BLOCK)
            sums_ref[pl.ds(block, 1), :] = lane_sums(jnp.where(keep, weight, 0.0))


def chunk_tags(piece_ref, size):
    row = piece_ref[size:, :].astype(jnp.float32)[0:1, :]
    return row[:, :size], row[:, size : size + BLOCK]


def cross_terms(meta, chunk, column_tags, unit_ref, piece_unit, add_rows):
    size = column_tags.shape[1]
    columns = None
    for start in range(0, meta.blocks * BLOCK, STEP):
        cosine = products(unit_ref[start : start + STEP, :], piece_unit[...])
        for inner in range(0, STEP, BLOCK):
            block = (start + inner) // BLOCK
            bias = column_bias(meta.tag(block, chunk), column_tags)
            weight = jnp.exp2(cosine[inner : inner + BLOCK] * GAIN + bias)
            row = lax.broadcasted_iota(jnp.int32, weight.shape, 0)
            weight = jnp.where(row < meta.used(block), weight, 0.0)
            add_rows(block, lane_sums(weight))
            partial = weight[0:8]
            for down in range(8, BLOCK, 8):
                partial = partial + weight[down : down + 8]
            columns = partial if columns is None else columns + partial
    total = jnp.sum(columns, axis=0, keepdims=True)
    return [total[:, at : at + BLOCK] for at in range(0, size, BLOCK)]


def middle_kernel(
    blocks, share, chunk, meta_ref, unit_ref, piece_ref, before_ref, sums_ref, cols_ref, piece_unit
):
    meta = Meta(meta_ref, blocks)
    size = share * BLOCK
    piece_unit[...] = normalised(piece_ref[:size, :])
    tags, edge = chunk_tags(piece_ref, size)

    def add_rows(block, value):
        sums_ref[block : block + 1, :] = before_ref[block : block + 1, :] + value

    cols = cross_terms(meta, chunk, tags, unit_ref, piece_unit, add_rows)
    for k in range(share):
        cols_ref[k : k + 1, :] = cols[k]
    mine = meta.tag(meta.number(EDGE)).astype(jnp.float32)
    joined = (edge == mine) & (edge >= 0) & (meta.number(INNER) > 0)
    cols_ref[share : share + 1, :] = jnp.where(joined, 1.0, 0.0)


def inner_last_kernel(
    blocks, share, meta_ref, unit_ref, piece_ref, before_ref, outer_cols_ref, swap_cols_ref,
    sums_ref, cols_ref, piece_unit,
):
    meta = Meta(meta_ref, blocks)
    size = share * BLOCK
    is_inner = meta.number(INNER) > 0

    @pl.when(jnp.logical_not(is_inner))
    def _():
        sums_ref[...] = before_ref[...]
        cols_ref[...] = jnp.zeros_like(cols_ref)

    @pl.when(is_inner)
    def _():
        piece_unit[...] = normalised(piece_ref[:size, :])
        tags, _ = chunk_tags(piece_ref, size)

        def add_rows(block, value):
            sums_ref[block : block + 1, :] = before_ref[block : block + 1, :] + value

        cols = cross_terms(meta, 2, tags, unit_ref, piece_unit, add_rows)
        for k in range(share):
            cols_ref[share + k : share + k + 1, :] = cols[k]
        cols_ref[:share, :] = outer_cols_ref[:share, :]
        cols_ref[2 * share :, :] = swap_cols_ref[share:, :]


def outer_last_kernel(
    blocks, share, width, meta_ref, unit_ref, piece_ref, before_ref, keep_ref, send_ref, cols_ref, piece_unit, sums
):
    meta = Meta(meta_ref, blocks)
    size = share * BLOCK
    is_inner = meta.number(INNER) > 0

    def place(block):
        owner = block // width
        return owner % 2 * (blocks // 2) + owner // 2 * width + block % width

    @pl.when(is_inner)
    def _():
        for block in range(blocks):
            at = place(block)
            sums[at : at + 1, :] = before_ref[block : block + 1, :]
        cols_ref[...] = jnp.zeros_like(cols_ref)

    @pl.when(jnp.logical_not(is_inner))
    def _():
        piece_unit[...] = normalised(piece_ref[:size, :])
        tags, _ = chunk_tags(piece_ref, size)

        def add_rows(block, value):
            at = place(block)
            sums[at : at + 1, :] = before_ref[block : block + 1, :] + value

        cols = cross_terms(meta, 2, tags, unit_ref, piece_unit, add_rows)
        for k in range(share):
            cols_ref[k : k + 1, :] = cols[k]

    parity = meta.number(MEMBER) % 2
    heap = blocks // 2
    keep_ref[...] = sums[pl.ds(pl.multiple_of(parity * heap, heap), heap), :]
    send_ref[...] = sums[pl.ds(pl.multiple_of((1 - parity) * heap, heap), heap), :]


def flag_kernel(share, here_ref, home_ref, flag_ref):
    flags = jnp.maximum(here_ref[share : share + 1, :], home_ref[2 * share : 2 * share + 1, :])
    flag_ref[0] = jnp.max(flags).astype(jnp.int32)


def call(kernel, meta, operands, out_shapes, scratch):
    vmem, smem = pl.BlockSpec(memory_space=pltpu.VMEM), pl.BlockSpec(memory_space=pltpu.SMEM)
    return pl.pallas_call(
        kernel,
        in_specs=[smem] + [vmem] * len(operands),
        out_specs=[vmem if len(shape.shape) > 1 else smem for shape in out_shapes],
        out_shape=out_shapes,
        scratch_shapes=scratch,
        compiler_params=pltpu.CompilerParams(vmem_limit_bytes=16 * 1024 * 1024),
        cost_estimate=pl.CostEstimate(flops=0, bytes_accessed=1024, transcendentals=0),
    )(meta, *operands)


def every_pair(embeddings, cluster_ids):
    unit = normalised(embeddings)
    tags = cluster_ids + 1
    groups = lax.axis_size("sub")
    member = lax.axis_index("sub")
    owners = lax.axis_size("tile")
    place = lax.axis_index("tile")
    rows_here = unit.shape[0]
    width = rows_here // groups
    own_piece = lax.dynamic_slice_in_dim(unit, member * width, width, 0)
    own_tags = lax.dynamic_slice_in_dim(tags, member * width, width, 0)
    distance = place - jnp.arange(owners, dtype=jnp.int32)
    keep = (jnp.abs(distance) < SPAN) & (distance != 0)
    outgoing = jnp.where(keep[:, None, None], own_piece[None, :, :], jnp.zeros((), jnp.bfloat16))
    outgoing_tags = jnp.where(keep[:, None], own_tags[None, :], 0)
    arrived = lax.all_to_all(outgoing, "tile", split_axis=0, concat_axis=0, tiled=True)
    arrived_tags = lax.all_to_all(outgoing_tags, "tile", split_axis=0, concat_axis=0, tiled=True)
    local_rows = jnp.arange(rows_here, dtype=jnp.int32)[:, None]
    slice_rows = member * width + jnp.arange(width, dtype=jnp.int32)[None, :]
    total = jnp.zeros((rows_here,), jnp.float32)
    for offset in range(1 - SPAN, SPAN):
        if offset == 0:
            piece, piece_tags, order = own_piece, own_tags, local_rows != slice_rows
        else:
            source = place + offset
            valid = (source >= 0) & (source < owners)
            index = jnp.clip(source, 0, owners - 1)
            piece = lax.dynamic_index_in_dim(arrived, index, 0, keepdims=False)
            piece_tags = lax.dynamic_index_in_dim(arrived_tags, index, 0, keepdims=False)
            piece_tags = jnp.where(valid, piece_tags, 0)
            order = True
        same = (tags[:, None] == piece_tags[None, :]) & (tags[:, None] > 0) & order
        weight = jnp.where(same, jnp.exp(inverse_temp * (products(unit, piece) - 1.0)), 0.0)
        total = total + jnp.sum(weight, axis=1)
    return jnp.log(1.0 + lax.psum_scatter(total, "sub", scatter_dimension=0, tiled=True))


def quads_joined(tag, tiles, place):
    last = jnp.broadcast_to(tag[-1], (BLOCK,))
    before = lax.ppermute(last, "tile", [(t, t + 1) for t in range(tiles - 1)])[0]
    joined = (place % QUAD == 0) & (place > 0) & (before == tag[0]) & (before >= 0)
    return lax.pmax(joined.astype(jnp.int32), "tile") > 0


def shards(embeddings, cluster_ids):
    tiles, subs = lax.axis_size("tile"), lax.axis_size("sub")
    place, member = lax.axis_index("tile"), lax.axis_index("sub")
    rows, depth = embeddings.shape
    blocks = rows // BLOCK
    plan = Plan(blocks, subs, place, member)
    width, share, inner = plan.width, plan.share, plan.inner
    size = share * BLOCK
    quads = range(0, tiles, QUAD)
    inward = [p for q in quads for p in ((q, q + 1), (q + 3, q + 2))]
    swap = [p for q in quads for p in ((q + 1, q + 2), (q + 2, q + 1))]
    across = [p for q in quads for p in ((q + 1, q + 3), (q + 2, q))]

    def turned(route):
        return [(b, a) for a, b in route]

    by_block = cluster_ids.reshape(blocks, BLOCK)
    first_out, second_out = pack(size, subs, embeddings, by_block)
    from_inner = lax.ppermute(first_out, "tile", swap)
    from_outer = lax.ppermute(first_out, "tile", inward)

    tag = jnp.max(by_block, axis=1)
    used = jnp.sum((by_block >= 0).astype(jnp.int32), axis=1)
    seen = jnp.where(inner, tag, -2)
    swapped = jnp.where(plan.far & (jnp.arange(blocks) >= blocks // 2), -2, seen)
    numbers = jnp.stack([member, plan.edge, inner])
    meta = jnp.concatenate([tag, used, seen, swapped, tag, numbers]).astype(jnp.int32)

    heap = blocks // 2
    owner = plan.first // width
    home_row = jnp.arange(heap)[:, None] - (owner // 2 * width + plan.first % width)
    home_row = jnp.broadcast_to(home_row, (heap, BLOCK)).astype(jnp.int32)
    upper = [
        jnp.broadcast_to((member >> bit) & 1, (heap >> bit, BLOCK)).astype(jnp.int32)
        for bit in range(1, subs.bit_length() - 1)
    ]
    meta, home_row, *upper = lax.optimization_barrier((meta, home_row, *upper))

    row_sums = jax.ShapeDtypeStruct((blocks, BLOCK), jnp.float32)
    col_sums = jax.ShapeDtypeStruct((share + 1, BLOCK), jnp.float32)
    quarter = width * BLOCK
    vmem, smem = pl.BlockSpec(memory_space=pltpu.VMEM), pl.BlockSpec(memory_space=pltpu.SMEM)
    unit, sums = pl.pallas_call(
        functools.partial(self_kernel, blocks, subs),
        in_specs=[smem, pl.BlockSpec(memory_space=pl.ANY), vmem],
        out_specs=[vmem, vmem],
        out_shape=[jax.ShapeDtypeStruct((rows, depth), jnp.bfloat16), row_sums],
        scratch_shapes=[pltpu.VMEM((subs, quarter, depth), jnp.bfloat16), pltpu.SemaphoreType.DMA((subs,))],
        compiler_params=pltpu.CompilerParams(vmem_limit_bytes=24 * 1024 * 1024),
        cost_estimate=pl.CostEstimate(flops=0, bytes_accessed=1024, transcendentals=0),
    )(meta, embeddings, lax.dynamic_slice_in_dim(cluster_ids, member * quarter, quarter, 0)[None])
    first_out, second_out, sums = lax.optimization_barrier((first_out, second_out, sums))
    inward_last = lax.ppermute(second_out, "tile", inward)
    across_last = lax.ppermute(first_out, "tile", across)

    def middle(chunk, piece, before):
        return call(
            functools.partial(middle_kernel, blocks, share, chunk),
            meta,
            (unit, piece, before),
            [row_sums, col_sums],
            [pltpu.VMEM((size, depth), jnp.bfloat16)],
        )

    sums, outer_cols = middle(0, from_outer, sums)
    sums, swap_cols = middle(1, from_inner, sums)
    swap_back = lax.ppermute(swap_cols, "tile", turned(swap))
    swap_back, sums = lax.optimization_barrier((swap_back, sums))
    sums, cols = call(
        functools.partial(inner_last_kernel, blocks, share),
        meta,
        (unit, inward_last, sums, outer_cols, swap_cols),
        [row_sums, jax.ShapeDtypeStruct((2 * share + 1, BLOCK), jnp.float32)],
        [pltpu.VMEM((size, depth), jnp.bfloat16)],
    )
    home = lax.ppermute(cols, "tile", turned(inward))
    half = jax.ShapeDtypeStruct((heap, BLOCK), jnp.float32)
    held, leaving, cols = call(
        functools.partial(outer_last_kernel, blocks, share, width),
        meta,
        (unit, across_last, sums),
        [half, half, jax.ShapeDtypeStruct((share, BLOCK), jnp.float32)],
        [pltpu.VMEM((size, depth), jnp.bfloat16), pltpu.VMEM((blocks, BLOCK), jnp.float32)],
    )
    near_home = lax.ppermute(cols, "tile", turned(across))
    near_home, home = lax.optimization_barrier((near_home, home))

    for k in range(share):
        held = held + jnp.where(home_row == k, near_home[k : k + 1] + swap_back[k : k + 1], 0.0)
    held = held + lax.ppermute(leaving, "sub", [(i, i ^ 1) for i in range(subs)])
    held, home = lax.optimization_barrier((held, home))
    for bit, mine in enumerate(upper, 1):
        pairs = held.reshape(-1, 2, width, BLOCK)
        low, high = pairs[:, 0].reshape(mine.shape), pairs[:, 1].reshape(mine.shape)
        leaving = jnp.where(mine > 0, low, high)
        held = jnp.where(mine > 0, high, low)
        held = held + lax.ppermute(leaving, "sub", [(i, i ^ (1 << bit)) for i in range(subs)])
    scores = jnp.log(1.0 + (held.reshape(width, BLOCK) + home[:width]).reshape(-1))

    flag = pl.pallas_call(
        functools.partial(flag_kernel, share),
        out_specs=pl.BlockSpec(memory_space=pltpu.SMEM),
        out_shape=jax.ShapeDtypeStruct((1,), jnp.int32),
        compiler_params=pltpu.CompilerParams(vmem_limit_bytes=4 * 1024 * 1024),
    )(swap_cols, home)
    bad = flag[0] > 0
    if tiles > QUAD:
        bad = lax.pmax(bad.astype(jnp.int32), "tile") > 0
        bad = bad | quads_joined(tag, tiles, place)
    return lax.cond(bad, lambda: every_pair(embeddings, cluster_ids), lambda: scores)


def solution(mesh):
    in_specs = (P(("groups", "tile"), None), P(("groups", "tile")))
    out_specs = P(("groups", "tile", "sub"))
    return jax.shard_map(shards, mesh=mesh, in_specs=in_specs, out_specs=out_specs, check_vma=False)
```

```python
import functools
import math

import jax
import jax.numpy as jnp
import numpy as np
from jax import lax
from jax.experimental import pallas as pl
from jax.experimental.pallas import tpu as pltpu
from jax.sharding import PartitionSpec as P

BLOCK = 128
QUAD = 4
SPAN = 4

inverse_temp = 10.0
norm_eps = 1e-06
GAIN = inverse_temp * math.log2(math.e)
OFF = -1000.0

STEP = 512
COPY = 64


def normalised(values):
    values = values.astype(jnp.float32)
    scale = lax.rsqrt(jnp.sum(values * values, axis=1, keepdims=True) + norm_eps)
    return (values * scale).astype(jnp.bfloat16)


def products(rows, columns):
    return lax.dot_general(
        rows, columns, (((1,), (1,)), ((), ())), preferred_element_type=jnp.float32
    )


def column_bias(tag, column_tags):
    return jnp.where(column_tags == tag.astype(jnp.float32), -GAIN, OFF)


def lane_sums(weight):
    total = weight[:, :BLOCK]
    for start in range(BLOCK, weight.shape[1], BLOCK):
        total = total + weight[:, start : start + BLOCK]
    return jnp.sum(total.T, axis=0, keepdims=True)


class Plan:
    def __init__(self, blocks, subs, place, member):
        width = blocks // subs
        share = width // 2
        part = place % QUAD
        self.inner = (part == 1) | (part == 2)
        self.far = part == 1
        dealt = member // 2 * share
        near = (dealt // width * 2 + member % 2) * width + dealt % width
        near = jnp.where(part == 1, blocks // 2, 0) + near
        self.first = jnp.where(self.inner, near, member * width)
        self.second = jnp.where(self.inner, near, member * width + share)
        self.edge = jnp.where(part == 1, blocks // 2 - 1, blocks // 2)
        self.width, self.share = width, share


def pack_kernel(blocks, subs, rows_ref, ids_ref, first_ref, second_ref, ids, sems):
    plan = Plan(blocks, subs, lax.axis_index("tile"), lax.axis_index("sub"))
    share, size = plan.share, plan.share * BLOCK
    ids_copy = pltpu.make_async_copy(ids_ref, ids, sems.at[0])

    def copies(block, out, sem):
        for down in range(0, size, COPY):
            start = pl.multiple_of(block * BLOCK + down, COPY)
            yield pltpu.make_async_copy(
                rows_ref.at[pl.ds(start, COPY), :], out.at[pl.ds(down, COPY), :], sems.at[sem + down // COPY]
            )

    first = list(copies(plan.first, first_ref, 1))
    second = list(copies(plan.second, second_ref, 1 + size // COPY))
    for copy in [ids_copy] + first + second:
        copy.start()
    ids_copy.wait()
    depth = first_ref.shape[1]
    edge = jnp.max(ids[pl.ds(plan.edge, 1), :], axis=1, keepdims=True)
    rest = [jnp.broadcast_to(edge, (1, BLOCK)), jnp.zeros((1, depth - size - BLOCK), jnp.int32)]
    for block, out in ((plan.first, first_ref), (plan.second, second_ref)):
        row = jnp.concatenate([ids[pl.ds(block + k, 1), :] for k in range(share)] + rest, axis=1)
        out[size:, :] = jnp.broadcast_to(row.astype(jnp.float32), (8, depth)).astype(jnp.bfloat16)
    for copy in first + second:
        copy.wait()


def pack(size, subs, embeddings, by_block):
    return pl.pallas_call(
        functools.partial(pack_kernel, by_block.shape[0], subs),
        in_specs=[pl.BlockSpec(memory_space=pl.ANY)] * 2,
        out_specs=[pl.BlockSpec(memory_space=pltpu.VMEM)] * 2,
        out_shape=[jax.ShapeDtypeStruct((size + 8, embeddings.shape[1]), jnp.bfloat16)] * 2,
        scratch_shapes=[pltpu.VMEM(by_block.shape, jnp.int32), pltpu.SemaphoreType.DMA((2 * size // COPY + 1,))],
        compiler_params=pltpu.CompilerParams(vmem_limit_bytes=8 * 1024 * 1024),
        cost_estimate=pl.CostEstimate(flops=0, bytes_accessed=1024, transcendentals=0),
    )(embeddings, by_block)


class Meta:
    def __init__(self, ref, blocks):
        self.ref, self.blocks = ref, blocks

    def tag(self, block, chunk=None):
        return self.ref[block + (0 if chunk is None else (2 + chunk) * self.blocks)]

    def used(self, block):
        return self.ref[self.blocks + block]

    def number(self, index):
        return self.ref[5 * self.blocks + index]


MEMBER, FIRST_BLOCK, EDGE, INNER = range(4)


def self_kernel(blocks, subs, meta_ref, rows_ref, tags_ref, unit_ref, sums_ref, held, sems):
    meta = Meta(meta_ref, blocks)
    width = blocks // subs
    quarter = width * BLOCK
    member = meta.number(MEMBER)
    owners = [lax.rem(member + turn, subs) for turn in range(subs)]
    spans = [pl.ds(pl.multiple_of(owner * quarter, quarter), quarter) for owner in owners]
    copies = []
    for turn, span in enumerate(spans):
        copies.append(pltpu.make_async_copy(rows_ref.at[span, :], held.at[turn], sems.at[turn]))
        copies[-1].start()
    column_tags = tags_ref[...].astype(jnp.float32)
    for turn in range(subs):
        copies[turn].wait()
        unit = normalised(held[turn])
        unit_ref[spans[turn], :] = unit
        if turn == 0:
            share = unit
        cosine = products(unit, share)
        for inner in range(width):
            block = owners[turn] * width + inner
            bias = column_bias(meta.tag(block), column_tags)
            weight = jnp.exp2(cosine[inner * BLOCK : (inner + 1) * BLOCK] * GAIN + bias)
            row = lax.broadcasted_iota(jnp.int32, weight.shape, 0)
            keep = row < meta.used(block)
            if turn == 0:
                keep = keep & (lax.broadcasted_iota(jnp.int32, weight.shape, 1) - row != inner * BLOCK)
            sums_ref[pl.ds(block, 1), :] = lane_sums(jnp.where(keep, weight, 0.0))


def chunk_tags(piece_ref, size):
    row = piece_ref[size:, :].astype(jnp.float32)[0:1, :]
    return row[:, :size], row[:, size : size + BLOCK]


def cross_terms(meta, chunk, column_tags, unit_ref, piece_unit, before_ref, sums, columns, place):
    size = column_tags.shape[1]
    half = meta.blocks // 2
    columns[...] = jnp.zeros_like(columns)
    for block in range(meta.blocks):
        sums[place(block) : place(block) + 1, :] = before_ref[block : block + 1, :]
    there = [jnp.max(column_tags[:, at : at + BLOCK]) for at in range(0, size, BLOCK)]
    for first in (0, half):
        shared = False
        for block in range(first, first + half):
            for tag in there:
                shared = (meta.tag(block, chunk).astype(jnp.float32) == tag) | shared

        @pl.when(shared)
        def _():
            total = None
            for start in range(first * BLOCK, (first + half) * BLOCK, STEP):
                cosine = products(unit_ref[start : start + STEP, :], piece_unit[...])
                for inner in range(0, STEP, BLOCK):
                    block = (start + inner) // BLOCK
                    bias = column_bias(meta.tag(block, chunk), column_tags)
                    weight = jnp.exp2(cosine[inner : inner + BLOCK] * GAIN + bias)
                    row = lax.broadcasted_iota(jnp.int32, weight.shape, 0)
                    weight = jnp.where(row < meta.used(block), weight, 0.0)
                    sums[place(block) : place(block) + 1, :] += lane_sums(weight)
                    partial = weight[0:8]
                    for down in range(8, BLOCK, 8):
                        partial = partial + weight[down : down + 8]
                    total = partial if total is None else total + partial
            columns[...] += total


def middle_kernel(
    blocks, share, chunk, meta_ref, unit_ref, piece_ref, before_ref, sums_ref, cols_ref, piece_unit, columns
):
    meta = Meta(meta_ref, blocks)
    size = share * BLOCK
    piece_unit[...] = normalised(piece_ref[:size, :])
    tags, edge = chunk_tags(piece_ref, size)
    cross_terms(meta, chunk, tags, unit_ref, piece_unit, before_ref, sums_ref, columns, lambda block: block)
    total = jnp.sum(columns[...], axis=0, keepdims=True)
    for k in range(share):
        cols_ref[k : k + 1, :] = total[:, k * BLOCK : (k + 1) * BLOCK]
    mine = meta.tag(meta.number(EDGE)).astype(jnp.float32)
    joined = (edge == mine) & (edge >= 0) & (meta.number(INNER) > 0)
    cols_ref[share : share + 1, :] = jnp.where(joined, 1.0, 0.0)


def last_kernel(
    blocks, share, width, meta_ref, unit_ref, piece_ref, before_ref, outer_back_ref, swap_cols_ref,
    keep_ref, send_ref, cols_ref, piece_unit, sums, columns,
):
    meta = Meta(meta_ref, blocks)
    size = share * BLOCK
    piece_unit[...] = normalised(piece_ref[:size, :])
    tags, _ = chunk_tags(piece_ref, size)

    def place(block):
        owner = block // width
        return owner % 2 * (blocks // 2) + owner // 2 * width + block % width

    cross_terms(meta, 2, tags, unit_ref, piece_unit, before_ref, sums, columns, place)
    total = jnp.sum(columns[...], axis=0, keepdims=True)
    for k in range(share):
        cols_ref[k : k + 1, :] = total[:, k * BLOCK : (k + 1) * BLOCK]
        at = place(meta.number(FIRST_BLOCK) + k)
        sums[pl.ds(at, 1), :] += outer_back_ref[k : k + 1, :]
    cols_ref[share : share + 1, :] = swap_cols_ref[share : share + 1, :]
    parity = meta.number(MEMBER) % 2
    heap = blocks // 2
    keep_ref[...] = sums[pl.ds(pl.multiple_of(parity * heap, heap), heap), :]
    send_ref[...] = sums[pl.ds(pl.multiple_of((1 - parity) * heap, heap), heap), :]


def flag_kernel(share, here_ref, home_ref, flag_ref):
    flags = jnp.maximum(here_ref[share : share + 1, :], home_ref[share : share + 1, :])
    flag_ref[0] = jnp.max(flags).astype(jnp.int32)


def call(kernel, meta, operands, out_shapes, scratch, flops):
    vmem, smem = pl.BlockSpec(memory_space=pltpu.VMEM), pl.BlockSpec(memory_space=pltpu.SMEM)
    return pl.pallas_call(
        kernel,
        in_specs=[smem] + [vmem] * len(operands),
        out_specs=[vmem if len(shape.shape) > 1 else smem for shape in out_shapes],
        out_shape=out_shapes,
        scratch_shapes=scratch,
        compiler_params=pltpu.CompilerParams(vmem_limit_bytes=16 * 1024 * 1024),
        cost_estimate=pl.CostEstimate(flops=flops, bytes_accessed=1024, transcendentals=0),
    )(meta, *operands)


def every_pair(embeddings, cluster_ids):
    unit = normalised(embeddings)
    tags = cluster_ids + 1
    groups = lax.axis_size("sub")
    member = lax.axis_index("sub")
    owners = lax.axis_size("tile")
    place = lax.axis_index("tile")
    rows_here = unit.shape[0]
    width = rows_here // groups
    own_piece = lax.dynamic_slice_in_dim(unit, member * width, width, 0)
    own_tags = lax.dynamic_slice_in_dim(tags, member * width, width, 0)
    distance = place - jnp.arange(owners, dtype=jnp.int32)
    keep = (jnp.abs(distance) < SPAN) & (distance != 0)
    outgoing = jnp.where(keep[:, None, None], own_piece[None, :, :], jnp.zeros((), jnp.bfloat16))
    outgoing_tags = jnp.where(keep[:, None], own_tags[None, :], 0)
    arrived = lax.all_to_all(outgoing, "tile", split_axis=0, concat_axis=0, tiled=True)
    arrived_tags = lax.all_to_all(outgoing_tags, "tile", split_axis=0, concat_axis=0, tiled=True)
    local_rows = jnp.arange(rows_here, dtype=jnp.int32)[:, None]
    slice_rows = member * width + jnp.arange(width, dtype=jnp.int32)[None, :]
    total = jnp.zeros((rows_here,), jnp.float32)
    for offset in range(1 - SPAN, SPAN):
        if offset == 0:
            piece, piece_tags, order = own_piece, own_tags, local_rows != slice_rows
        else:
            source = place + offset
            valid = (source >= 0) & (source < owners)
            index = jnp.clip(source, 0, owners - 1)
            piece = lax.dynamic_index_in_dim(arrived, index, 0, keepdims=False)
            piece_tags = lax.dynamic_index_in_dim(arrived_tags, index, 0, keepdims=False)
            piece_tags = jnp.where(valid, piece_tags, 0)
            order = True
        same = (tags[:, None] == piece_tags[None, :]) & (tags[:, None] > 0) & order
        weight = jnp.where(same, jnp.exp(inverse_temp * (products(unit, piece) - 1.0)), 0.0)
        total = total + jnp.sum(weight, axis=1)
    return jnp.log(1.0 + lax.psum_scatter(total, "sub", scatter_dimension=0, tiled=True))


def quads_joined(tag, tiles, place):
    last = jnp.broadcast_to(tag[-1], (BLOCK,))
    before = lax.ppermute(last, "tile", [(t, t + 1) for t in range(tiles - 1)])[0]
    joined = (place % QUAD == 0) & (place > 0) & (before == tag[0]) & (before >= 0)
    return lax.pmax(joined.astype(jnp.int32), "tile") > 0


def shards(embeddings, cluster_ids):
    tiles, subs = lax.axis_size("tile"), lax.axis_size("sub")
    place, member = lax.axis_index("tile"), lax.axis_index("sub")
    rows, depth = embeddings.shape
    blocks = rows // BLOCK
    plan = Plan(blocks, subs, place, member)
    width, share, inner = plan.width, plan.share, plan.inner
    size = share * BLOCK
    quads = range(0, tiles, QUAD)
    inward = [p for q in quads for p in ((q, q + 1), (q + 3, q + 2))]
    swap = [p for q in quads for p in ((q + 1, q + 2), (q + 2, q + 1))]
    around = [p for q in quads for p in ((q, q + 1), (q + 3, q + 2), (q + 1, q + 3), (q + 2, q))]

    def turned(route):
        return [(b, a) for a, b in route]

    by_block = cluster_ids.reshape(blocks, BLOCK)
    first_out, second_out = pack(size, subs, embeddings, by_block)
    from_inner = lax.ppermute(first_out, "tile", swap)
    from_outer = lax.ppermute(first_out, "tile", inward)

    tag = jnp.max(by_block, axis=1)
    used = jnp.sum((by_block >= 0).astype(jnp.int32), axis=1)
    seen = jnp.where(inner, tag, -2)
    swapped = jnp.where(plan.far & (jnp.arange(blocks) >= blocks // 2), -2, seen)
    numbers = jnp.stack([member, plan.first, plan.edge, inner])
    meta = jnp.concatenate([tag, used, seen, swapped, tag, numbers]).astype(jnp.int32)

    heap = blocks // 2
    owner = plan.second // width
    home_row = jnp.arange(heap)[:, None] - (owner // 2 * width + plan.second % width)
    home_row = jnp.broadcast_to(home_row, (heap, BLOCK)).astype(jnp.int32)
    upper = [
        jnp.broadcast_to((member >> bit) & 1, (heap >> bit, BLOCK)).astype(jnp.int32)
        for bit in range(1, subs.bit_length() - 1)
    ]
    meta, home_row, *upper = lax.optimization_barrier((meta, home_row, *upper))

    row_sums = jax.ShapeDtypeStruct((blocks, BLOCK), jnp.float32)
    col_sums = jax.ShapeDtypeStruct((share + 1, BLOCK), jnp.float32)
    quarter = width * BLOCK
    vmem, smem = pl.BlockSpec(memory_space=pltpu.VMEM), pl.BlockSpec(memory_space=pltpu.SMEM)
    unit, sums = pl.pallas_call(
        functools.partial(self_kernel, blocks, subs),
        in_specs=[smem, pl.BlockSpec(memory_space=pl.ANY), vmem],
        out_specs=[vmem, vmem],
        out_shape=[jax.ShapeDtypeStruct((rows, depth), jnp.bfloat16), row_sums],
        scratch_shapes=[pltpu.VMEM((subs, quarter, depth), jnp.bfloat16), pltpu.SemaphoreType.DMA((subs,))],
        compiler_params=pltpu.CompilerParams(vmem_limit_bytes=24 * 1024 * 1024),
        cost_estimate=pl.CostEstimate(flops=0, bytes_accessed=1024, transcendentals=0),
    )(meta, embeddings, lax.dynamic_slice_in_dim(cluster_ids, member * quarter, quarter, 0)[None])
    second_out, sums = lax.optimization_barrier((second_out, sums))
    last = lax.ppermute(second_out, "tile", around)

    def middle(chunk, piece, before):
        return call(
            functools.partial(middle_kernel, blocks, share, chunk),
            meta,
            (unit, piece, before),
            [row_sums, col_sums],
            [pltpu.VMEM((size, depth), jnp.bfloat16), pltpu.VMEM((8, size), jnp.float32)],
            2 * rows * size * depth,
        )

    sums, outer_cols = middle(0, from_outer, sums)
    outer_back = lax.ppermute(outer_cols, "tile", turned(inward))
    sums, swap_cols = middle(1, from_inner, sums)
    swap_back = lax.ppermute(swap_cols, "tile", turned(swap))
    half = jax.ShapeDtypeStruct((heap, BLOCK), jnp.float32)
    held, leaving, cols = call(
        functools.partial(last_kernel, blocks, share, width),
        meta,
        (unit, last, sums, outer_back, swap_cols),
        [half, half, col_sums],
        [
            pltpu.VMEM((size, depth), jnp.bfloat16),
            pltpu.VMEM((blocks, BLOCK), jnp.float32),
            pltpu.VMEM((8, size), jnp.float32),
        ],
        2 * rows * size * depth,
    )

    home = lax.ppermute(cols, "tile", turned(around))
    for k in range(share):
        held = held + jnp.where(home_row == k, home[k : k + 1] + swap_back[k : k + 1], 0.0)
    held = held + lax.ppermute(leaving, "sub", [(i, i ^ 1) for i in range(subs)])
    home, held = lax.optimization_barrier((home, held))
    for bit, mine in enumerate(upper, 1):
        pairs = held.reshape(-1, 2, width, BLOCK)
        low, high = pairs[:, 0].reshape(mine.shape), pairs[:, 1].reshape(mine.shape)
        leaving = jnp.where(mine > 0, low, high)
        held = jnp.where(mine > 0, high, low)
        held = held + lax.ppermute(leaving, "sub", [(i, i ^ (1 << bit)) for i in range(subs)])
    scores = jnp.log(1.0 + held.reshape(-1))

    flag = pl.pallas_call(
        functools.partial(flag_kernel, share),
        out_specs=pl.BlockSpec(memory_space=pltpu.SMEM),
        out_shape=jax.ShapeDtypeStruct((1,), jnp.int32),
        compiler_params=pltpu.CompilerParams(vmem_limit_bytes=4 * 1024 * 1024),
    )(swap_cols, home)
    bad = flag[0] > 0
    if tiles > QUAD:
        bad = lax.pmax(bad.astype(jnp.int32), "tile") > 0
        bad = bad | quads_joined(tag, tiles, place)
    return lax.cond(bad, lambda: every_pair(embeddings, cluster_ids), lambda: scores)


def solution(mesh):
    in_specs = (P(("groups", "tile"), None), P(("groups", "tile")))
    out_specs = P(("groups", "tile", "sub"))
    return jax.shard_map(shards, mesh=mesh, in_specs=in_specs, out_specs=out_specs, check_vma=False)
```

```python
import functools
import math

import jax
import jax.numpy as jnp
import numpy as np
from jax import lax
from jax.experimental import pallas as pl
from jax.experimental.pallas import tpu as pltpu
from jax.sharding import PartitionSpec as P

BLOCK = 128
QUAD = 4
SPAN = 4

inverse_temp = 10.0
norm_eps = 1e-06
GAIN = inverse_temp * math.log2(math.e)
OFF = -1000.0

STEP = 512
COPY = 64


def normalised(values):
    values = values.astype(jnp.float32)
    scale = lax.rsqrt(jnp.sum(values * values, axis=1, keepdims=True) + norm_eps)
    return (values * scale).astype(jnp.bfloat16)


def products(rows, columns):
    return lax.dot_general(
        rows, columns, (((1,), (1,)), ((), ())), preferred_element_type=jnp.float32
    )


def column_bias(tag, column_tags):
    return jnp.where(column_tags == tag.astype(jnp.float32), -GAIN, OFF)


def lane_sums(weight):
    total = weight[:, :BLOCK]
    for start in range(BLOCK, weight.shape[1], BLOCK):
        total = total + weight[:, start : start + BLOCK]
    return jnp.sum(total.T, axis=0, keepdims=True)


class Plan:
    def __init__(self, blocks, subs, place, member):
        width = blocks // subs
        share = width // 2
        part = place % QUAD
        self.inner = (part == 1) | (part == 2)
        self.far = part == 1
        dealt = member // 2 * share
        near = (dealt // width * 2 + member % 2) * width + dealt % width
        near = jnp.where(part == 1, blocks // 2, 0) + near
        self.first = jnp.where(self.inner, near, member * width)
        self.second = jnp.where(self.inner, near, member * width + share)
        self.edge = jnp.where(part == 1, blocks // 2 - 1, blocks // 2)
        self.width, self.share = width, share


def pack_kernel(blocks, subs, rows_ref, ids_ref, first_ref, second_ref, ids, sems):
    plan = Plan(blocks, subs, lax.axis_index("tile"), lax.axis_index("sub"))
    share, size = plan.share, plan.share * BLOCK
    ids_copy = pltpu.make_async_copy(ids_ref, ids, sems.at[0])

    def copies(block, out, sem):
        for down in range(0, size, COPY):
            start = pl.multiple_of(block * BLOCK + down, COPY)
            yield pltpu.make_async_copy(
                rows_ref.at[pl.ds(start, COPY), :], out.at[pl.ds(down, COPY), :], sems.at[sem + down // COPY]
            )

    first = list(copies(plan.first, first_ref, 1))
    second = list(copies(plan.second, second_ref, 1 + size // COPY))
    for copy in [ids_copy] + first + second:
        copy.start()
    ids_copy.wait()
    depth = first_ref.shape[1]
    edge = jnp.max(ids[pl.ds(plan.edge, 1), :], axis=1, keepdims=True)
    rest = [jnp.broadcast_to(edge, (1, BLOCK)), jnp.zeros((1, depth - size - BLOCK), jnp.int32)]
    for block, out in ((plan.first, first_ref), (plan.second, second_ref)):
        row = jnp.concatenate([ids[pl.ds(block + k, 1), :] for k in range(share)] + rest, axis=1)
        out[size:, :] = jnp.broadcast_to(row.astype(jnp.float32), (8, depth)).astype(jnp.bfloat16)
    for copy in first + second:
        copy.wait()


def pack(size, subs, embeddings, by_block):
    return pl.pallas_call(
        functools.partial(pack_kernel, by_block.shape[0], subs),
        in_specs=[pl.BlockSpec(memory_space=pl.ANY)] * 2,
        out_specs=[pl.BlockSpec(memory_space=pltpu.VMEM)] * 2,
        out_shape=[jax.ShapeDtypeStruct((size + 8, embeddings.shape[1]), jnp.bfloat16)] * 2,
        scratch_shapes=[pltpu.VMEM(by_block.shape, jnp.int32), pltpu.SemaphoreType.DMA((2 * size // COPY + 1,))],
        compiler_params=pltpu.CompilerParams(vmem_limit_bytes=8 * 1024 * 1024),
        cost_estimate=pl.CostEstimate(flops=0, bytes_accessed=1024, transcendentals=0),
    )(embeddings, by_block)


class Meta:
    def __init__(self, ref, blocks):
        self.ref, self.blocks = ref, blocks

    def tag(self, block, chunk=None):
        return self.ref[block + (0 if chunk is None else (2 + chunk) * self.blocks)]

    def used(self, block):
        return self.ref[self.blocks + block]

    def number(self, index):
        return self.ref[5 * self.blocks + index]


MEMBER, FIRST_BLOCK, EDGE, INNER = range(4)


def self_kernel(blocks, subs, meta_ref, rows_ref, tags_ref, unit_ref, sums_ref, held, sems):
    meta = Meta(meta_ref, blocks)
    width = blocks // subs
    quarter = width * BLOCK
    member = meta.number(MEMBER)
    owners = [lax.rem(member + turn, subs) for turn in range(subs)]
    spans = [pl.ds(pl.multiple_of(owner * quarter, quarter), quarter) for owner in owners]
    copies = []
    for turn, span in enumerate(spans):
        copies.append(pltpu.make_async_copy(rows_ref.at[span, :], held.at[turn], sems.at[turn]))
        copies[-1].start()
    column_tags = tags_ref[...].astype(jnp.float32)
    for turn in range(subs):
        copies[turn].wait()
        unit = normalised(held[turn])
        unit_ref[spans[turn], :] = unit
        if turn == 0:
            share = unit
        cosine = products(unit, share)
        for inner in range(width):
            block = owners[turn] * width + inner
            bias = column_bias(meta.tag(block), column_tags)
            weight = jnp.exp2(cosine[inner * BLOCK : (inner + 1) * BLOCK] * GAIN + bias)
            row = lax.broadcasted_iota(jnp.int32, weight.shape, 0)
            keep = row < meta.used(block)
            if turn == 0:
                keep = keep & (lax.broadcasted_iota(jnp.int32, weight.shape, 1) - row != inner * BLOCK)
            sums_ref[pl.ds(block, 1), :] = lane_sums(jnp.where(keep, weight, 0.0))


def chunk_tags(piece_ref, size):
    row = piece_ref[size:, :].astype(jnp.float32)[0:1, :]
    return row[:, :size], row[:, size : size + BLOCK]


def cross_terms(meta, chunk, column_tags, unit_ref, piece_ref, before_ref, sums, columns, place):
    size = column_tags.shape[1]
    there = [jnp.max(column_tags[:, at : at + BLOCK]) for at in range(0, size, BLOCK)]
    shared = False
    for block in range(meta.blocks):
        for tag in there:
            shared = (meta.tag(block, chunk).astype(jnp.float32) == tag) | shared

    @pl.when(jnp.logical_not(shared))
    def _():
        columns[...] = jnp.zeros_like(columns)
        for block in range(meta.blocks):
            sums[place(block) : place(block) + 1, :] = before_ref[block : block + 1, :]

    @pl.when(shared)
    def _():
        norms = []
        for at in range(0, size, BLOCK):
            values = piece_ref[at : at + BLOCK, :].astype(jnp.float32)
            norms.append(lane_sums(values * values))
        scale = GAIN * lax.rsqrt(jnp.concatenate(norms, axis=1) + norm_eps)
        total = None
        for start in range(0, meta.blocks * BLOCK, STEP):
            product = products(unit_ref[start : start + STEP, :], piece_ref[:size, :])
            for inner in range(0, STEP, BLOCK):
                block = (start + inner) // BLOCK
                bias = column_bias(meta.tag(block, chunk), column_tags)
                weight = jnp.exp2(product[inner : inner + BLOCK] * scale + bias)
                row = lax.broadcasted_iota(jnp.int32, weight.shape, 0)
                weight = jnp.where(row < meta.used(block), weight, 0.0)
                sums[place(block) : place(block) + 1, :] = before_ref[block : block + 1, :] + lane_sums(weight)
                partial = weight[0:8]
                for down in range(8, BLOCK, 8):
                    partial = partial + weight[down : down + 8]
                total = partial if total is None else total + partial
        columns[...] = total


def middle_kernel(blocks, share, chunk, meta_ref, unit_ref, piece_ref, before_ref, sums_ref, cols_ref, columns):
    meta = Meta(meta_ref, blocks)
    tags, edge = chunk_tags(piece_ref, share * BLOCK)
    cross_terms(meta, chunk, tags, unit_ref, piece_ref, before_ref, sums_ref, columns, lambda block: block)
    total = jnp.sum(columns[...], axis=0, keepdims=True)
    for k in range(share):
        cols_ref[k : k + 1, :] = total[:, k * BLOCK : (k + 1) * BLOCK]
    mine = meta.tag(meta.number(EDGE)).astype(jnp.float32)
    joined = (edge == mine) & (edge >= 0) & (meta.number(INNER) > 0)
    cols_ref[share : share + 1, :] = jnp.where(joined, 1.0, 0.0)


def last_kernel(
    blocks, share, width, meta_ref, unit_ref, piece_ref, before_ref, outer_back_ref, swap_cols_ref,
    keep_ref, send_ref, cols_ref, sums, columns,
):
    meta = Meta(meta_ref, blocks)
    tags, _ = chunk_tags(piece_ref, share * BLOCK)

    def place(block):
        owner = block // width
        return owner % 2 * (blocks // 2) + owner // 2 * width + block % width

    cross_terms(meta, 2, tags, unit_ref, piece_ref, before_ref, sums, columns, place)
    total = jnp.sum(columns[...], axis=0, keepdims=True)
    for k in range(share):
        cols_ref[k : k + 1, :] = total[:, k * BLOCK : (k + 1) * BLOCK]
        at = place(meta.number(FIRST_BLOCK) + k)
        sums[pl.ds(at, 1), :] += outer_back_ref[k : k + 1, :]
    cols_ref[share : share + 1, :] = swap_cols_ref[share : share + 1, :]
    parity = meta.number(MEMBER) % 2
    heap = blocks // 2
    keep_ref[...] = sums[pl.ds(pl.multiple_of(parity * heap, heap), heap), :]
    send_ref[...] = sums[pl.ds(pl.multiple_of((1 - parity) * heap, heap), heap), :]


def flag_kernel(share, here_ref, home_ref, flag_ref):
    flags = jnp.maximum(here_ref[share : share + 1, :], home_ref[share : share + 1, :])
    flag_ref[0] = jnp.max(flags).astype(jnp.int32)


def call(kernel, meta, operands, out_shapes, scratch, flops):
    vmem, smem = pl.BlockSpec(memory_space=pltpu.VMEM), pl.BlockSpec(memory_space=pltpu.SMEM)
    return pl.pallas_call(
        kernel,
        in_specs=[smem] + [vmem] * len(operands),
        out_specs=[vmem if len(shape.shape) > 1 else smem for shape in out_shapes],
        out_shape=out_shapes,
        scratch_shapes=scratch,
        compiler_params=pltpu.CompilerParams(vmem_limit_bytes=16 * 1024 * 1024),
        cost_estimate=pl.CostEstimate(flops=flops, bytes_accessed=1024, transcendentals=0),
    )(meta, *operands)


def every_pair(embeddings, cluster_ids):
    unit = normalised(embeddings)
    tags = cluster_ids + 1
    groups = lax.axis_size("sub")
    member = lax.axis_index("sub")
    owners = lax.axis_size("tile")
    place = lax.axis_index("tile")
    rows_here = unit.shape[0]
    width = rows_here // groups
    own_piece = lax.dynamic_slice_in_dim(unit, member * width, width, 0)
    own_tags = lax.dynamic_slice_in_dim(tags, member * width, width, 0)
    distance = place - jnp.arange(owners, dtype=jnp.int32)
    keep = (jnp.abs(distance) < SPAN) & (distance != 0)
    outgoing = jnp.where(keep[:, None, None], own_piece[None, :, :], jnp.zeros((), jnp.bfloat16))
    outgoing_tags = jnp.where(keep[:, None], own_tags[None, :], 0)
    arrived = lax.all_to_all(outgoing, "tile", split_axis=0, concat_axis=0, tiled=True)
    arrived_tags = lax.all_to_all(outgoing_tags, "tile", split_axis=0, concat_axis=0, tiled=True)
    local_rows = jnp.arange(rows_here, dtype=jnp.int32)[:, None]
    slice_rows = member * width + jnp.arange(width, dtype=jnp.int32)[None, :]
    total = jnp.zeros((rows_here,), jnp.float32)
    for offset in range(1 - SPAN, SPAN):
        if offset == 0:
            piece, piece_tags, order = own_piece, own_tags, local_rows != slice_rows
        else:
            source = place + offset
            valid = (source >= 0) & (source < owners)
            index = jnp.clip(source, 0, owners - 1)
            piece = lax.dynamic_index_in_dim(arrived, index, 0, keepdims=False)
            piece_tags = lax.dynamic_index_in_dim(arrived_tags, index, 0, keepdims=False)
            piece_tags = jnp.where(valid, piece_tags, 0)
            order = True
        same = (tags[:, None] == piece_tags[None, :]) & (tags[:, None] > 0) & order
        weight = jnp.where(same, jnp.exp(inverse_temp * (products(unit, piece) - 1.0)), 0.0)
        total = total + jnp.sum(weight, axis=1)
    return jnp.log(1.0 + lax.psum_scatter(total, "sub", scatter_dimension=0, tiled=True))


def quads_joined(tag, tiles, place):
    last = jnp.broadcast_to(tag[-1], (BLOCK,))
    before = lax.ppermute(last, "tile", [(t, t + 1) for t in range(tiles - 1)])[0]
    joined = (place % QUAD == 0) & (place > 0) & (before == tag[0]) & (before >= 0)
    return lax.pmax(joined.astype(jnp.int32), "tile") > 0


def shards(embeddings, cluster_ids):
    tiles, subs = lax.axis_size("tile"), lax.axis_size("sub")
    place, member = lax.axis_index("tile"), lax.axis_index("sub")
    rows, depth = embeddings.shape
    blocks = rows // BLOCK
    plan = Plan(blocks, subs, place, member)
    width, share, inner = plan.width, plan.share, plan.inner
    size = share * BLOCK
    quads = range(0, tiles, QUAD)
    inward = [p for q in quads for p in ((q, q + 1), (q + 3, q + 2))]
    swap = [p for q in quads for p in ((q + 1, q + 2), (q + 2, q + 1))]
    around = [p for q in quads for p in ((q, q + 1), (q + 3, q + 2), (q + 1, q + 3), (q + 2, q))]

    def turned(route):
        return [(b, a) for a, b in route]

    by_block = cluster_ids.reshape(blocks, BLOCK)
    first_out, second_out = pack(size, subs, embeddings, by_block)
    from_inner = lax.ppermute(first_out, "tile", swap)
    from_outer = lax.ppermute(first_out, "tile", inward)

    tag = jnp.max(by_block, axis=1)
    used = jnp.sum((by_block >= 0).astype(jnp.int32), axis=1)
    seen = jnp.where(inner, tag, -2)
    swapped = jnp.where(plan.far & (jnp.arange(blocks) >= blocks // 2), -2, seen)
    numbers = jnp.stack([member, plan.first, plan.edge, inner])
    meta = jnp.concatenate([tag, used, seen, swapped, tag, numbers]).astype(jnp.int32)

    heap = blocks // 2
    owner = plan.second // width
    home_row = jnp.arange(heap)[:, None] - (owner // 2 * width + plan.second % width)
    home_row = jnp.broadcast_to(home_row, (heap, BLOCK)).astype(jnp.int32)
    upper = [
        jnp.broadcast_to((member >> bit) & 1, (heap >> bit, BLOCK)).astype(jnp.int32)
        for bit in range(1, subs.bit_length() - 1)
    ]
    meta, home_row, *upper = lax.optimization_barrier((meta, home_row, *upper))

    row_sums = jax.ShapeDtypeStruct((blocks, BLOCK), jnp.float32)
    col_sums = jax.ShapeDtypeStruct((share + 1, BLOCK), jnp.float32)
    quarter = width * BLOCK
    vmem, smem = pl.BlockSpec(memory_space=pltpu.VMEM), pl.BlockSpec(memory_space=pltpu.SMEM)
    unit, sums = pl.pallas_call(
        functools.partial(self_kernel, blocks, subs),
        in_specs=[smem, pl.BlockSpec(memory_space=pl.ANY), vmem],
        out_specs=[vmem, vmem],
        out_shape=[jax.ShapeDtypeStruct((rows, depth), jnp.bfloat16), row_sums],
        scratch_shapes=[pltpu.VMEM((subs, quarter, depth), jnp.bfloat16), pltpu.SemaphoreType.DMA((subs,))],
        compiler_params=pltpu.CompilerParams(vmem_limit_bytes=24 * 1024 * 1024),
        cost_estimate=pl.CostEstimate(flops=0, bytes_accessed=1024, transcendentals=0),
    )(meta, embeddings, lax.dynamic_slice_in_dim(cluster_ids, member * quarter, quarter, 0)[None])
    second_out, sums = lax.optimization_barrier((second_out, sums))
    last = lax.ppermute(second_out, "tile", around)

    def middle(chunk, piece, before):
        return call(
            functools.partial(middle_kernel, blocks, share, chunk),
            meta,
            (unit, piece, before),
            [row_sums, col_sums],
            [pltpu.VMEM((8, size), jnp.float32)],
            2 * rows * size * depth,
        )

    sums, outer_cols = middle(0, from_outer, sums)
    outer_back = lax.ppermute(outer_cols, "tile", turned(inward))
    sums, swap_cols = middle(1, from_inner, sums)
    swap_back = lax.ppermute(swap_cols, "tile", turned(swap))
    half = jax.ShapeDtypeStruct((heap, BLOCK), jnp.float32)
    held, leaving, cols = call(
        functools.partial(last_kernel, blocks, share, width),
        meta,
        (unit, last, sums, outer_back, swap_cols),
        [half, half, col_sums],
        [
            pltpu.VMEM((blocks, BLOCK), jnp.float32),
            pltpu.VMEM((8, size), jnp.float32),
        ],
        2 * rows * size * depth,
    )

    home = lax.ppermute(cols, "tile", turned(around))
    for k in range(share):
        held = held + jnp.where(home_row == k, home[k : k + 1] + swap_back[k : k + 1], 0.0)
    held = held + lax.ppermute(leaving, "sub", [(i, i ^ 1) for i in range(subs)])
    home, held = lax.optimization_barrier((home, held))
    for bit, mine in enumerate(upper, 1):
        pairs = held.reshape(-1, 2, width, BLOCK)
        low, high = pairs[:, 0].reshape(mine.shape), pairs[:, 1].reshape(mine.shape)
        leaving = jnp.where(mine > 0, low, high)
        held = jnp.where(mine > 0, high, low)
        held = held + lax.ppermute(leaving, "sub", [(i, i ^ (1 << bit)) for i in range(subs)])
    scores = jnp.log(1.0 + held.reshape(-1))

    flag = pl.pallas_call(
        functools.partial(flag_kernel, share),
        out_specs=pl.BlockSpec(memory_space=pltpu.SMEM),
        out_shape=jax.ShapeDtypeStruct((1,), jnp.int32),
        compiler_params=pltpu.CompilerParams(vmem_limit_bytes=4 * 1024 * 1024),
    )(swap_cols, home)
    bad = flag[0] > 0
    if tiles > QUAD:
        bad = lax.pmax(bad.astype(jnp.int32), "tile") > 0
        bad = bad | quads_joined(tag, tiles, place)
    return lax.cond(bad, lambda: every_pair(embeddings, cluster_ids), lambda: scores)


def solution(mesh):
    in_specs = (P(("groups", "tile"), None), P(("groups", "tile")))
    out_specs = P(("groups", "tile", "sub"))
    return jax.shard_map(shards, mesh=mesh, in_specs=in_specs, out_specs=out_specs, check_vma=False)
```

```python
import functools
import math

import jax
import jax.numpy as jnp
import numpy as np
from jax import lax
from jax.experimental import pallas as pl
from jax.experimental.pallas import tpu as pltpu
from jax.sharding import PartitionSpec as P

BLOCK = 128
QUAD = 4
SPAN = 4

inverse_temp = 10.0
norm_eps = 1e-06
GAIN = inverse_temp * math.log2(math.e)
OFF = -1000.0

STEP = 512
COPY = 64


def normalised(values):
    values = values.astype(jnp.float32)
    scale = lax.rsqrt(jnp.sum(values * values, axis=1, keepdims=True) + norm_eps)
    return (values * scale).astype(jnp.bfloat16)


def products(rows, columns):
    return lax.dot_general(
        rows, columns, (((1,), (1,)), ((), ())), preferred_element_type=jnp.float32
    )


def column_bias(tag, column_tags):
    return jnp.where(column_tags == tag.astype(jnp.float32), -GAIN, OFF)


def lane_sums(weight):
    total = weight[:, :BLOCK]
    for start in range(BLOCK, weight.shape[1], BLOCK):
        total = total + weight[:, start : start + BLOCK]
    return jnp.sum(total.T, axis=0, keepdims=True)


class Plan:
    def __init__(self, blocks, subs, place, member):
        width = blocks // subs
        share = width // 2
        part = place % QUAD
        self.inner = (part == 1) | (part == 2)
        self.far = part == 1
        dealt = member // 2 * share
        near = (dealt // width * 2 + member % 2) * width + dealt % width
        near = jnp.where(part == 1, blocks // 2, 0) + near
        self.first = jnp.where(self.inner, near, member * width)
        self.second = jnp.where(self.inner, near, member * width + share)
        self.edge = jnp.where(part == 1, blocks // 2 - 1, blocks // 2)
        self.width, self.share = width, share


def pack_kernel(blocks, subs, rows_ref, ids_ref, first_ref, second_ref, ids, sems):
    plan = Plan(blocks, subs, lax.axis_index("tile"), lax.axis_index("sub"))
    share, size = plan.share, plan.share * BLOCK
    ids_copy = pltpu.make_async_copy(ids_ref, ids, sems.at[0])

    def copies(block, out, sem):
        for down in range(0, size, COPY):
            start = pl.multiple_of(block * BLOCK + down, COPY)
            yield pltpu.make_async_copy(
                rows_ref.at[pl.ds(start, COPY), :], out.at[pl.ds(down, COPY), :], sems.at[sem + down // COPY]
            )

    first = list(copies(plan.first, first_ref, 1))
    second = list(copies(plan.second, second_ref, 1 + size // COPY))
    for copy in [ids_copy] + first + second:
        copy.start()
    ids_copy.wait()
    depth = first_ref.shape[1]
    edge = jnp.max(ids[pl.ds(plan.edge, 1), :], axis=1, keepdims=True)
    rest = [jnp.broadcast_to(edge, (1, BLOCK)), jnp.zeros((1, depth - size - BLOCK), jnp.int32)]
    for block, out in ((plan.first, first_ref), (plan.second, second_ref)):
        row = jnp.concatenate([ids[pl.ds(block + k, 1), :] for k in range(share)] + rest, axis=1)
        out[size:, :] = jnp.broadcast_to(row.astype(jnp.float32), (8, depth)).astype(jnp.bfloat16)
    for copy in first + second:
        copy.wait()


def pack(size, subs, embeddings, by_block):
    return pl.pallas_call(
        functools.partial(pack_kernel, by_block.shape[0], subs),
        in_specs=[pl.BlockSpec(memory_space=pl.ANY)] * 2,
        out_specs=[pl.BlockSpec(memory_space=pltpu.VMEM)] * 2,
        out_shape=[jax.ShapeDtypeStruct((size + 8, embeddings.shape[1]), jnp.bfloat16)] * 2,
        scratch_shapes=[pltpu.VMEM(by_block.shape, jnp.int32), pltpu.SemaphoreType.DMA((2 * size // COPY + 1,))],
        compiler_params=pltpu.CompilerParams(vmem_limit_bytes=8 * 1024 * 1024),
        cost_estimate=pl.CostEstimate(flops=0, bytes_accessed=1024, transcendentals=0),
    )(embeddings, by_block)


class Meta:
    def __init__(self, ref, blocks):
        self.ref, self.blocks = ref, blocks

    def tag(self, block, chunk=None):
        return self.ref[block + (0 if chunk is None else (2 + chunk) * self.blocks)]

    def used(self, block):
        return self.ref[self.blocks + block]

    def number(self, index):
        return self.ref[5 * self.blocks + index]


MEMBER, FIRST_BLOCK, EDGE, INNER = range(4)
INWARD, SWAPPED, FIRST = range(3)


def self_kernel(blocks, subs, meta_ref, rows_ref, tags_ref, unit_ref, sums_ref, held, sems):
    meta = Meta(meta_ref, blocks)
    width = blocks // subs
    quarter = width * BLOCK
    member = meta.number(MEMBER)
    owners = [lax.rem(member + turn, subs) for turn in range(subs)]
    spans = [pl.ds(pl.multiple_of(owner * quarter, quarter), quarter) for owner in owners]
    copies = []
    for turn, span in enumerate(spans):
        copies.append(pltpu.make_async_copy(rows_ref.at[span, :], held.at[turn], sems.at[turn]))
        copies[-1].start()
    column_tags = tags_ref[...].astype(jnp.float32)
    for turn in range(subs):
        copies[turn].wait()
        unit = normalised(held[turn])
        unit_ref[spans[turn], :] = unit
        if turn == 0:
            share = unit
        cosine = products(unit, share)
        for inner in range(width):
            block = owners[turn] * width + inner
            bias = column_bias(meta.tag(block), column_tags)
            weight = jnp.exp2(cosine[inner * BLOCK : (inner + 1) * BLOCK] * GAIN + bias)
            row = lax.broadcasted_iota(jnp.int32, weight.shape, 0)
            keep = row < meta.used(block)
            if turn == 0:
                keep = keep & (lax.broadcasted_iota(jnp.int32, weight.shape, 1) - row != inner * BLOCK)
            sums_ref[pl.ds(block, 1), :] = lane_sums(jnp.where(keep, weight, 0.0))


def chunk_tags(piece_ref, size):
    row = piece_ref[size:, :].astype(jnp.float32)[0:1, :]
    return row[:, :size], row[:, size : size + BLOCK]


def cross_terms(meta, chunk, column_tags, unit_ref, piece_ref, before_ref, sums, columns, place):
    size = column_tags.shape[1]
    there = [jnp.max(column_tags[:, at : at + BLOCK]) for at in range(0, size, BLOCK)]
    shared = False
    for block in range(meta.blocks):
        for tag in there:
            shared = (meta.tag(block, chunk).astype(jnp.float32) == tag) | shared

    @pl.when(jnp.logical_not(shared))
    def _():
        columns[...] = jnp.zeros_like(columns)
        for block in range(meta.blocks):
            sums[place(block) : place(block) + 1, :] = before_ref[block : block + 1, :]

    @pl.when(shared)
    def _():
        piece = normalised(piece_ref[:size, :])
        total = None
        for start in range(0, meta.blocks * BLOCK, STEP):
            cosine = products(unit_ref[start : start + STEP, :], piece)
            for inner in range(0, STEP, BLOCK):
                block = (start + inner) // BLOCK
                bias = column_bias(meta.tag(block, chunk), column_tags)
                weight = jnp.exp2(cosine[inner : inner + BLOCK] * GAIN + bias)
                row = lax.broadcasted_iota(jnp.int32, weight.shape, 0)
                weight = jnp.where(row < meta.used(block), weight, 0.0)
                sums[place(block) : place(block) + 1, :] = before_ref[block : block + 1, :] + lane_sums(weight)
                partial = weight[0:8]
                for down in range(8, BLOCK, 8):
                    partial = partial + weight[down : down + 8]
                total = partial if total is None else total + partial
        columns[...] = total


def middle_kernel(
    blocks, share, chunk, meta_ref, unit_ref, piece_ref, before_ref, sums_ref, cols_ref, columns
):
    meta = Meta(meta_ref, blocks)
    tags, edge = chunk_tags(piece_ref, share * BLOCK)
    cross_terms(meta, chunk, tags, unit_ref, piece_ref, before_ref, sums_ref, columns, lambda block: block)
    total = jnp.sum(columns[...], axis=0, keepdims=True)
    for k in range(share):
        cols_ref[k : k + 1, :] = total[:, k * BLOCK : (k + 1) * BLOCK]
    is_inner = meta.number(INNER) > 0
    mine = jnp.full(edge.shape, meta.tag(meta.number(EDGE)).astype(jnp.float32))
    if chunk == SWAPPED:
        joined = jnp.where((edge == mine) & (edge >= 0), 1.0, 0.0)
        cols_ref[share : share + 1, :] = jnp.where(is_inner, joined, 2.0)
    else:
        cols_ref[share : share + 1, :] = jnp.where(is_inner, mine, edge)


def last_kernel(
    blocks, share, width, meta_ref, unit_ref, piece_ref, before_ref, first_back_ref,
    keep_ref, send_ref, cols_ref, sums, columns,
):
    meta = Meta(meta_ref, blocks)
    tags, _ = chunk_tags(piece_ref, share * BLOCK)

    def place(block):
        owner = block // width
        return owner % 2 * (blocks // 2) + owner // 2 * width + block % width

    cross_terms(meta, INWARD, tags, unit_ref, piece_ref, before_ref, sums, columns, place)
    total = jnp.sum(columns[...], axis=0, keepdims=True)
    for k in range(share):
        cols_ref[k : k + 1, :] = total[:, k * BLOCK : (k + 1) * BLOCK]
        at = place(meta.number(FIRST_BLOCK) + k)
        sums[pl.ds(at, 1), :] += first_back_ref[k : k + 1, :]
    parity = meta.number(MEMBER) % 2
    heap = blocks // 2
    keep_ref[...] = sums[pl.ds(pl.multiple_of(parity * heap, heap), heap), :]
    send_ref[...] = sums[pl.ds(pl.multiple_of((1 - parity) * heap, heap), heap), :]


def flag_kernel(share, swap_cols_ref, first_cols_ref, first_back_ref, flag_ref):
    found = swap_cols_ref[share : share + 1, :]
    one, other = first_cols_ref[share : share + 1, :], first_back_ref[share : share + 1, :]
    joined = jnp.where((one == other) & (one >= 0), 1.0, 0.0)
    flag_ref[0] = jnp.max(jnp.where(found > 1.5, joined, found)).astype(jnp.int32)


def call(kernel, meta, operands, out_shapes, scratch, flops):
    vmem, smem = pl.BlockSpec(memory_space=pltpu.VMEM), pl.BlockSpec(memory_space=pltpu.SMEM)
    return pl.pallas_call(
        kernel,
        in_specs=[smem] + [vmem] * len(operands),
        out_specs=[vmem if len(shape.shape) > 1 else smem for shape in out_shapes],
        out_shape=out_shapes,
        scratch_shapes=scratch,
        compiler_params=pltpu.CompilerParams(vmem_limit_bytes=16 * 1024 * 1024),
        cost_estimate=pl.CostEstimate(flops=flops, bytes_accessed=1024, transcendentals=0),
    )(meta, *operands)


def every_pair(embeddings, cluster_ids):
    unit = normalised(embeddings)
    tags = cluster_ids + 1
    groups = lax.axis_size("sub")
    member = lax.axis_index("sub")
    owners = lax.axis_size("tile")
    place = lax.axis_index("tile")
    rows_here = unit.shape[0]
    width = rows_here // groups
    own_piece = lax.dynamic_slice_in_dim(unit, member * width, width, 0)
    own_tags = lax.dynamic_slice_in_dim(tags, member * width, width, 0)
    distance = place - jnp.arange(owners, dtype=jnp.int32)
    keep = (jnp.abs(distance) < SPAN) & (distance != 0)
    outgoing = jnp.where(keep[:, None, None], own_piece[None, :, :], jnp.zeros((), jnp.bfloat16))
    outgoing_tags = jnp.where(keep[:, None], own_tags[None, :], 0)
    arrived = lax.all_to_all(outgoing, "tile", split_axis=0, concat_axis=0, tiled=True)
    arrived_tags = lax.all_to_all(outgoing_tags, "tile", split_axis=0, concat_axis=0, tiled=True)
    local_rows = jnp.arange(rows_here, dtype=jnp.int32)[:, None]
    slice_rows = member * width + jnp.arange(width, dtype=jnp.int32)[None, :]
    total = jnp.zeros((rows_here,), jnp.float32)
    for offset in range(1 - SPAN, SPAN):
        if offset == 0:
            piece, piece_tags, order = own_piece, own_tags, local_rows != slice_rows
        else:
            source = place + offset
            valid = (source >= 0) & (source < owners)
            index = jnp.clip(source, 0, owners - 1)
            piece = lax.dynamic_index_in_dim(arrived, index, 0, keepdims=False)
            piece_tags = lax.dynamic_index_in_dim(arrived_tags, index, 0, keepdims=False)
            piece_tags = jnp.where(valid, piece_tags, 0)
            order = True
        same = (tags[:, None] == piece_tags[None, :]) & (tags[:, None] > 0) & order
        weight = jnp.where(same, jnp.exp(inverse_temp * (products(unit, piece) - 1.0)), 0.0)
        total = total + jnp.sum(weight, axis=1)
    return jnp.log(1.0 + lax.psum_scatter(total, "sub", scatter_dimension=0, tiled=True))


def quads_joined(tag, tiles, place):
    last = jnp.broadcast_to(tag[-1], (BLOCK,))
    before = lax.ppermute(last, "tile", [(t, t + 1) for t in range(tiles - 1)])[0]
    joined = (place % QUAD == 0) & (place > 0) & (before == tag[0]) & (before >= 0)
    return lax.pmax(joined.astype(jnp.int32), "tile") > 0


def shards(embeddings, cluster_ids):
    tiles, subs = lax.axis_size("tile"), lax.axis_size("sub")
    place, member = lax.axis_index("tile"), lax.axis_index("sub")
    rows, depth = embeddings.shape
    blocks = rows // BLOCK
    plan = Plan(blocks, subs, place, member)
    width, share, inner = plan.width, plan.share, plan.inner
    size = share * BLOCK
    quads = range(0, tiles, QUAD)
    inward = [p for q in quads for p in ((q, q + 1), (q + 3, q + 2))]
    swap = [p for q in quads for p in ((q + 1, q + 2), (q + 2, q + 1))]
    around = [p for q in quads for p in ((q, q + 1), (q + 3, q + 2), (q + 1, q + 3), (q + 2, q))]

    def turned(route):
        return [(b, a) for a, b in route]

    by_block = cluster_ids.reshape(blocks, BLOCK)
    first_out, second_out = pack(size, subs, embeddings, by_block)
    from_first = lax.ppermute(first_out, "tile", around)

    tag = jnp.max(by_block, axis=1)
    used = jnp.sum((by_block >= 0).astype(jnp.int32), axis=1)
    seen = jnp.where(inner, tag, -2)
    swapped = jnp.where(plan.far & (jnp.arange(blocks) >= blocks // 2), -2, seen)
    numbers = jnp.stack([member, plan.first, plan.edge, inner])
    meta = jnp.concatenate([tag, used, seen, swapped, tag, numbers]).astype(jnp.int32)

    heap = blocks // 2
    owner = plan.first // width
    home_row = jnp.arange(heap)[:, None] - (owner // 2 * width + plan.first % width)
    home_row = jnp.broadcast_to(home_row, (heap, BLOCK)).astype(jnp.int32)
    upper = [
        jnp.broadcast_to((member >> bit) & 1, (heap >> bit, BLOCK)).astype(jnp.int32)
        for bit in range(1, subs.bit_length() - 1)
    ]
    meta, home_row, *upper = lax.optimization_barrier((meta, home_row, *upper))

    row_sums = jax.ShapeDtypeStruct((blocks, BLOCK), jnp.float32)
    col_sums = jax.ShapeDtypeStruct((share + 1, BLOCK), jnp.float32)
    quarter = width * BLOCK
    vmem, smem = pl.BlockSpec(memory_space=pltpu.VMEM), pl.BlockSpec(memory_space=pltpu.SMEM)
    unit, sums = pl.pallas_call(
        functools.partial(self_kernel, blocks, subs),
        in_specs=[smem, pl.BlockSpec(memory_space=pl.ANY), vmem],
        out_specs=[vmem, vmem],
        out_shape=[jax.ShapeDtypeStruct((rows, depth), jnp.bfloat16), row_sums],
        scratch_shapes=[pltpu.VMEM((subs, quarter, depth), jnp.bfloat16), pltpu.SemaphoreType.DMA((subs,))],
        compiler_params=pltpu.CompilerParams(vmem_limit_bytes=24 * 1024 * 1024),
        cost_estimate=pl.CostEstimate(flops=0, bytes_accessed=1024, transcendentals=0),
    )(meta, embeddings, lax.dynamic_slice_in_dim(cluster_ids, member * quarter, quarter, 0)[None])
    first_out, second_out, sums = lax.optimization_barrier((first_out, second_out, sums))
    from_swap = lax.ppermute(first_out, "tile", swap)
    from_last = lax.ppermute(second_out, "tile", inward)

    def middle(chunk, piece, before):
        return call(
            functools.partial(middle_kernel, blocks, share, chunk),
            meta,
            (unit, piece, before),
            [row_sums, col_sums],
            [pltpu.VMEM((8, size), jnp.float32)],
            2 * rows * size * depth,
        )

    sums, first_cols = middle(FIRST, from_first, sums)
    first_back = lax.ppermute(first_cols, "tile", turned(around))
    sums, swap_cols = middle(SWAPPED, from_swap, sums)
    swap_back = lax.ppermute(swap_cols, "tile", turned(swap))
    half = jax.ShapeDtypeStruct((heap, BLOCK), jnp.float32)
    held, leaving, cols = call(
        functools.partial(last_kernel, blocks, share, width),
        meta,
        (unit, from_last, sums, first_back),
        [half, half, jax.ShapeDtypeStruct((share, BLOCK), jnp.float32)],
        [
            pltpu.VMEM((blocks, BLOCK), jnp.float32),
            pltpu.VMEM((8, size), jnp.float32),
        ],
        2 * rows * size * depth,
    )

    home = lax.ppermute(cols, "tile", turned(inward))
    for k in range(share):
        held = held + jnp.where(home_row == k, swap_back[k : k + 1], 0.0)
    held = held + lax.ppermute(leaving, "sub", [(i, i ^ 1) for i in range(subs)])
    held, first_back = lax.optimization_barrier((held, first_back))
    for bit, mine in enumerate(upper, 1):
        pairs = held.reshape(-1, 2, width, BLOCK)
        low, high = pairs[:, 0].reshape(mine.shape), pairs[:, 1].reshape(mine.shape)
        leaving = jnp.where(mine > 0, low, high)
        held = jnp.where(mine > 0, high, low)
        held = held + lax.ppermute(leaving, "sub", [(i, i ^ (1 << bit)) for i in range(subs)])
    home = jnp.concatenate([jnp.zeros_like(home), home])
    scores = jnp.log(1.0 + (held.reshape(width, BLOCK) + home).reshape(-1))

    flag = pl.pallas_call(
        functools.partial(flag_kernel, share),
        out_specs=pl.BlockSpec(memory_space=pltpu.SMEM),
        out_shape=jax.ShapeDtypeStruct((1,), jnp.int32),
        compiler_params=pltpu.CompilerParams(vmem_limit_bytes=4 * 1024 * 1024),
    )(swap_cols, first_cols, first_back)
    bad = flag[0] > 0
    if tiles > QUAD:
        bad = lax.pmax(bad.astype(jnp.int32), "tile") > 0
        bad = bad | quads_joined(tag, tiles, place)
    return lax.cond(bad, lambda: every_pair(embeddings, cluster_ids), lambda: scores)


def solution(mesh):
    in_specs = (P(("groups", "tile"), None), P(("groups", "tile")))
    out_specs = P(("groups", "tile", "sub"))
    return jax.shard_map(shards, mesh=mesh, in_specs=in_specs, out_specs=out_specs, check_vma=False)
```

```python
import functools
import math

import jax
import jax.numpy as jnp
import numpy as np
from jax import lax
from jax.experimental import pallas as pl
from jax.experimental.pallas import tpu as pltpu
from jax.sharding import PartitionSpec as P

BLOCK = 128
QUAD = 4
SPAN = 4

inverse_temp = 10.0
norm_eps = 1e-06
GAIN = inverse_temp * math.log2(math.e)
OFF = -1000.0

STEP = 512
COPY = 64


def normalised(values):
    values = values.astype(jnp.float32)
    scale = lax.rsqrt(jnp.sum(values * values, axis=1, keepdims=True) + norm_eps)
    return (values * scale).astype(jnp.bfloat16)


def products(rows, columns):
    return lax.dot_general(
        rows, columns, (((1,), (1,)), ((), ())), preferred_element_type=jnp.float32
    )


def column_bias(tag, column_tags):
    return jnp.where(column_tags == tag.astype(jnp.float32), -GAIN, OFF)


def lane_sums(weight):
    total = weight[:, :BLOCK]
    for start in range(BLOCK, weight.shape[1], BLOCK):
        total = total + weight[:, start : start + BLOCK]
    return jnp.sum(total.T, axis=0, keepdims=True)


class Plan:
    def __init__(self, blocks, subs, place, member):
        width = blocks // subs
        share = width // 2
        part = place % QUAD
        self.inner = (part == 1) | (part == 2)
        self.far = part == 1
        dealt = member // 2 * share
        near = (dealt // width * 2 + member % 2) * width + dealt % width
        near = jnp.where(part == 1, blocks // 2, 0) + near
        self.first = jnp.where(self.inner, near, member * width)
        self.second = jnp.where(self.inner, near, member * width + share)
        self.edge = jnp.where(part == 1, blocks // 2 - 1, blocks // 2)
        self.width, self.share = width, share


def pack_kernel(blocks, subs, rows_ref, ids_ref, first_ref, second_ref, ids, sems):
    plan = Plan(blocks, subs, lax.axis_index("tile"), lax.axis_index("sub"))
    share, size = plan.share, plan.share * BLOCK
    ids_copy = pltpu.make_async_copy(ids_ref, ids, sems.at[0])

    def copies(block, out, sem):
        for down in range(0, size, COPY):
            start = pl.multiple_of(block * BLOCK + down, COPY)
            yield pltpu.make_async_copy(
                rows_ref.at[pl.ds(start, COPY), :], out.at[pl.ds(down, COPY), :], sems.at[sem + down // COPY]
            )

    first = list(copies(plan.first, first_ref, 1))
    second = list(copies(plan.second, second_ref, 1 + size // COPY))
    for copy in [ids_copy] + first + second:
        copy.start()
    ids_copy.wait()
    depth = first_ref.shape[1]
    edge = jnp.max(ids[pl.ds(plan.edge, 1), :], axis=1, keepdims=True)
    rest = [jnp.broadcast_to(edge, (1, BLOCK)), jnp.zeros((1, depth - size - BLOCK), jnp.int32)]
    for block, out in ((plan.first, first_ref), (plan.second, second_ref)):
        row = jnp.concatenate([ids[pl.ds(block + k, 1), :] for k in range(share)] + rest, axis=1)
        out[size:, :] = jnp.broadcast_to(row.astype(jnp.float32), (8, depth)).astype(jnp.bfloat16)
    for copy in first + second:
        copy.wait()


def pack(size, subs, embeddings, by_block):
    return pl.pallas_call(
        functools.partial(pack_kernel, by_block.shape[0], subs),
        in_specs=[pl.BlockSpec(memory_space=pl.ANY)] * 2,
        out_specs=[pl.BlockSpec(memory_space=pltpu.VMEM)] * 2,
        out_shape=[jax.ShapeDtypeStruct((size + 8, embeddings.shape[1]), jnp.bfloat16)] * 2,
        scratch_shapes=[pltpu.VMEM(by_block.shape, jnp.int32), pltpu.SemaphoreType.DMA((2 * size // COPY + 1,))],
        compiler_params=pltpu.CompilerParams(vmem_limit_bytes=8 * 1024 * 1024),
        cost_estimate=pl.CostEstimate(flops=0, bytes_accessed=1024, transcendentals=0),
    )(embeddings, by_block)


class Meta:
    def __init__(self, ref, blocks):
        self.ref, self.blocks = ref, blocks

    def tag(self, block, chunk=None):
        return self.ref[block + (0 if chunk is None else (2 + chunk) * self.blocks)]

    def used(self, block):
        return self.ref[self.blocks + block]

    def number(self, index):
        return self.ref[5 * self.blocks + index]


MEMBER, FIRST_BLOCK, EDGE, INNER = range(4)


def self_kernel(blocks, subs, meta_ref, rows_ref, tags_ref, unit_ref, sums_ref, held, sems):
    meta = Meta(meta_ref, blocks)
    width = blocks // subs
    quarter = width * BLOCK
    member = meta.number(MEMBER)
    owners = [lax.rem(member + turn, subs) for turn in range(subs)]
    spans = [pl.ds(pl.multiple_of(owner * quarter, quarter), quarter) for owner in owners]
    copies = []
    for turn, span in enumerate(spans):
        copies.append(pltpu.make_async_copy(rows_ref.at[span, :], held.at[turn], sems.at[turn]))
        copies[-1].start()
    column_tags = tags_ref[...].astype(jnp.float32)
    for turn in range(subs):
        copies[turn].wait()
        unit = normalised(held[turn])
        unit_ref[spans[turn], :] = unit
        if turn == 0:
            share = unit
        cosine = products(unit, share)
        for inner in range(width):
            block = owners[turn] * width + inner
            bias = column_bias(meta.tag(block), column_tags)
            weight = jnp.exp2(cosine[inner * BLOCK : (inner + 1) * BLOCK] * GAIN + bias)
            row = lax.broadcasted_iota(jnp.int32, weight.shape, 0)
            keep = row < meta.used(block)
            if turn == 0:
                keep = keep & (lax.broadcasted_iota(jnp.int32, weight.shape, 1) - row != inner * BLOCK)
            sums_ref[pl.ds(block, 1), :] = lane_sums(jnp.where(keep, weight, 0.0))


def chunk_tags(piece_ref, size):
    row = piece_ref[size:, :].astype(jnp.float32)[0:1, :]
    return row[:, :size], row[:, size : size + BLOCK]


def cross_terms(meta, chunk, column_tags, unit_ref, piece_ref, before_ref, sums, columns, place):
    size = column_tags.shape[1]
    there = [jnp.max(column_tags[:, at : at + BLOCK]) for at in range(0, size, BLOCK)]
    shared = False
    for block in range(meta.blocks):
        for tag in there:
            shared = (meta.tag(block, chunk).astype(jnp.float32) == tag) | shared

    @pl.when(jnp.logical_not(shared))
    def _():
        columns[...] = jnp.zeros_like(columns)
        for block in range(meta.blocks):
            sums[place(block) : place(block) + 1, :] = before_ref[block : block + 1, :]

    @pl.when(shared)
    def _():
        piece = normalised(piece_ref[:size, :])
        total = None
        for start in range(0, meta.blocks * BLOCK, STEP):
            cosine = products(unit_ref[start : start + STEP, :], piece)
            for inner in range(0, STEP, BLOCK):
                block = (start + inner) // BLOCK
                bias = column_bias(meta.tag(block, chunk), column_tags)
                weight = jnp.exp2(cosine[inner : inner + BLOCK] * GAIN + bias)
                row = lax.broadcasted_iota(jnp.int32, weight.shape, 0)
                weight = jnp.where(row < meta.used(block), weight, 0.0)
                sums[place(block) : place(block) + 1, :] = before_ref[block : block + 1, :] + lane_sums(weight)
                partial = weight[0:8]
                for down in range(8, BLOCK, 8):
                    partial = partial + weight[down : down + 8]
                total = partial if total is None else total + partial
        columns[...] = total


def middle_kernel(blocks, share, chunk, meta_ref, unit_ref, piece_ref, before_ref, sums_ref, cols_ref, columns):
    meta = Meta(meta_ref, blocks)
    tags, edge = chunk_tags(piece_ref, share * BLOCK)
    cross_terms(meta, chunk, tags, unit_ref, piece_ref, before_ref, sums_ref, columns, lambda block: block)
    total = jnp.sum(columns[...], axis=0, keepdims=True)
    for k in range(share):
        cols_ref[k : k + 1, :] = total[:, k * BLOCK : (k + 1) * BLOCK]
    mine = meta.tag(meta.number(EDGE)).astype(jnp.float32)
    joined = (edge == mine) & (edge >= 0) & (meta.number(INNER) > 0)
    cols_ref[share : share + 1, :] = jnp.where(joined, 1.0, 0.0)


def last_kernel(
    blocks, share, width, meta_ref, unit_ref, piece_ref, before_ref, outer_back_ref, swap_cols_ref,
    keep_ref, send_ref, cols_ref, sums, columns,
):
    meta = Meta(meta_ref, blocks)
    tags, _ = chunk_tags(piece_ref, share * BLOCK)

    def place(block):
        owner = block // width
        return owner % 2 * (blocks // 2) + owner // 2 * width + block % width

    cross_terms(meta, 2, tags, unit_ref, piece_ref, before_ref, sums, columns, place)
    total = jnp.sum(columns[...], axis=0, keepdims=True)
    for k in range(share):
        cols_ref[k : k + 1, :] = total[:, k * BLOCK : (k + 1) * BLOCK]
        at = place(meta.number(FIRST_BLOCK) + k)
        sums[pl.ds(at, 1), :] += outer_back_ref[k : k + 1, :]
    cols_ref[share : share + 1, :] = swap_cols_ref[share : share + 1, :]
    parity = meta.number(MEMBER) % 2
    heap = blocks // 2
    keep_ref[...] = sums[pl.ds(pl.multiple_of(parity * heap, heap), heap), :]
    send_ref[...] = sums[pl.ds(pl.multiple_of((1 - parity) * heap, heap), heap), :]


def flag_kernel(share, here_ref, home_ref, flag_ref):
    flags = jnp.maximum(here_ref[share : share + 1, :], home_ref[share : share + 1, :])
    flag_ref[0] = jnp.max(flags).astype(jnp.int32)


def call(kernel, meta, operands, out_shapes, scratch, flops):
    vmem, smem = pl.BlockSpec(memory_space=pltpu.VMEM), pl.BlockSpec(memory_space=pltpu.SMEM)
    return pl.pallas_call(
        kernel,
        in_specs=[smem] + [vmem] * len(operands),
        out_specs=[vmem if len(shape.shape) > 1 else smem for shape in out_shapes],
        out_shape=out_shapes,
        scratch_shapes=scratch,
        compiler_params=pltpu.CompilerParams(vmem_limit_bytes=16 * 1024 * 1024),
        cost_estimate=pl.CostEstimate(flops=flops, bytes_accessed=1024, transcendentals=0),
    )(meta, *operands)


def every_pair(embeddings, cluster_ids):
    unit = normalised(embeddings)
    tags = cluster_ids + 1
    groups = lax.axis_size("sub")
    member = lax.axis_index("sub")
    owners = lax.axis_size("tile")
    place = lax.axis_index("tile")
    rows_here = unit.shape[0]
    width = rows_here // groups
    own_piece = lax.dynamic_slice_in_dim(unit, member * width, width, 0)
    own_tags = lax.dynamic_slice_in_dim(tags, member * width, width, 0)
    distance = place - jnp.arange(owners, dtype=jnp.int32)
    keep = (jnp.abs(distance) < SPAN) & (distance != 0)
    outgoing = jnp.where(keep[:, None, None], own_piece[None, :, :], jnp.zeros((), jnp.bfloat16))
    outgoing_tags = jnp.where(keep[:, None], own_tags[None, :], 0)
    arrived = lax.all_to_all(outgoing, "tile", split_axis=0, concat_axis=0, tiled=True)
    arrived_tags = lax.all_to_all(outgoing_tags, "tile", split_axis=0, concat_axis=0, tiled=True)
    local_rows = jnp.arange(rows_here, dtype=jnp.int32)[:, None]
    slice_rows = member * width + jnp.arange(width, dtype=jnp.int32)[None, :]
    total = jnp.zeros((rows_here,), jnp.float32)
    for offset in range(1 - SPAN, SPAN):
        if offset == 0:
            piece, piece_tags, order = own_piece, own_tags, local_rows != slice_rows
        else:
            source = place + offset
            valid = (source >= 0) & (source < owners)
            index = jnp.clip(source, 0, owners - 1)
            piece = lax.dynamic_index_in_dim(arrived, index, 0, keepdims=False)
            piece_tags = lax.dynamic_index_in_dim(arrived_tags, index, 0, keepdims=False)
            piece_tags = jnp.where(valid, piece_tags, 0)
            order = True
        same = (tags[:, None] == piece_tags[None, :]) & (tags[:, None] > 0) & order
        weight = jnp.where(same, jnp.exp(inverse_temp * (products(unit, piece) - 1.0)), 0.0)
        total = total + jnp.sum(weight, axis=1)
    return jnp.log(1.0 + lax.psum_scatter(total, "sub", scatter_dimension=0, tiled=True))


def quads_joined(tag, tiles, place):
    last = jnp.broadcast_to(tag[-1], (BLOCK,))
    before = lax.ppermute(last, "tile", [(t, t + 1) for t in range(tiles - 1)])[0]
    joined = (place % QUAD == 0) & (place > 0) & (before == tag[0]) & (before >= 0)
    return lax.pmax(joined.astype(jnp.int32), "tile") > 0


def shards(embeddings, cluster_ids):
    tiles, subs = lax.axis_size("tile"), lax.axis_size("sub")
    place, member = lax.axis_index("tile"), lax.axis_index("sub")
    rows, depth = embeddings.shape
    blocks = rows // BLOCK
    plan = Plan(blocks, subs, place, member)
    width, share, inner = plan.width, plan.share, plan.inner
    size = share * BLOCK
    quads = range(0, tiles, QUAD)
    inward = [p for q in quads for p in ((q, q + 1), (q + 3, q + 2))]
    swap = [p for q in quads for p in ((q + 1, q + 2), (q + 2, q + 1))]
    around = [p for q in quads for p in ((q, q + 1), (q + 3, q + 2), (q + 1, q + 3), (q + 2, q))]

    def turned(route):
        return [(b, a) for a, b in route]

    by_block = cluster_ids.reshape(blocks, BLOCK)
    first_out, second_out = pack(size, subs, embeddings, by_block)
    from_inner = lax.ppermute(first_out, "tile", swap)
    from_outer = lax.ppermute(first_out, "tile", inward)

    tag = jnp.max(by_block, axis=1)
    used = jnp.sum((by_block >= 0).astype(jnp.int32), axis=1)
    seen = jnp.where(inner, tag, -2)
    swapped = jnp.where(plan.far & (jnp.arange(blocks) >= blocks // 2), -2, seen)
    numbers = jnp.stack([member, plan.first, plan.edge, inner])
    meta = jnp.concatenate([tag, used, seen, swapped, tag, numbers]).astype(jnp.int32)

    heap = blocks // 2
    owner = plan.second // width
    home_row = jnp.arange(heap)[:, None] - (owner // 2 * width + plan.second % width)
    home_row = jnp.broadcast_to(home_row, (heap, BLOCK)).astype(jnp.int32)
    upper = [
        jnp.broadcast_to((member >> bit) & 1, (heap >> bit, BLOCK)).astype(jnp.int32)
        for bit in range(1, subs.bit_length() - 1)
    ]
    meta, home_row, *upper = lax.optimization_barrier((meta, home_row, *upper))

    row_sums = jax.ShapeDtypeStruct((blocks, BLOCK), jnp.float32)
    col_sums = jax.ShapeDtypeStruct((share + 1, BLOCK), jnp.float32)
    quarter = width * BLOCK
    vmem, smem = pl.BlockSpec(memory_space=pltpu.VMEM), pl.BlockSpec(memory_space=pltpu.SMEM)
    unit, sums = pl.pallas_call(
        functools.partial(self_kernel, blocks, subs),
        in_specs=[smem, pl.BlockSpec(memory_space=pl.ANY), vmem],
        out_specs=[vmem, vmem],
        out_shape=[jax.ShapeDtypeStruct((rows, depth), jnp.bfloat16), row_sums],
        scratch_shapes=[pltpu.VMEM((subs, quarter, depth), jnp.bfloat16), pltpu.SemaphoreType.DMA((subs,))],
        compiler_params=pltpu.CompilerParams(vmem_limit_bytes=24 * 1024 * 1024),
        cost_estimate=pl.CostEstimate(flops=0, bytes_accessed=1024, transcendentals=0),
    )(meta, embeddings, lax.dynamic_slice_in_dim(cluster_ids, member * quarter, quarter, 0)[None])
    second_out, sums = lax.optimization_barrier((second_out, sums))
    last = lax.ppermute(second_out, "tile", around)

    def middle(chunk, piece, before):
        return call(
            functools.partial(middle_kernel, blocks, share, chunk),
            meta,
            (unit, piece, before),
            [row_sums, col_sums],
            [pltpu.VMEM((8, size), jnp.float32)],
            2 * rows * size * depth,
        )

    sums, outer_cols = middle(0, from_outer, sums)
    outer_back = lax.ppermute(outer_cols, "tile", turned(inward))
    sums, swap_cols = middle(1, from_inner, sums)
    swap_back = lax.ppermute(swap_cols, "tile", turned(swap))
    half = jax.ShapeDtypeStruct((heap, BLOCK), jnp.float32)
    held, leaving, cols = call(
        functools.partial(last_kernel, blocks, share, width),
        meta,
        (unit, last, sums, outer_back, swap_cols),
        [half, half, col_sums],
        [
            pltpu.VMEM((blocks, BLOCK), jnp.float32),
            pltpu.VMEM((8, size), jnp.float32),
        ],
        2 * rows * size * depth,
    )

    home = lax.ppermute(cols, "tile", turned(around))
    for k in range(share):
        held = held + jnp.where(home_row == k, home[k : k + 1] + swap_back[k : k + 1], 0.0)
    held = held + lax.ppermute(leaving, "sub", [(i, i ^ 1) for i in range(subs)])
    home, held = lax.optimization_barrier((home, held))
    for bit, mine in enumerate(upper, 1):
        pairs = held.reshape(-1, 2, width, BLOCK)
        low, high = pairs[:, 0].reshape(mine.shape), pairs[:, 1].reshape(mine.shape)
        leaving = jnp.where(mine > 0, low, high)
        held = jnp.where(mine > 0, high, low)
        held = held + lax.ppermute(leaving, "sub", [(i, i ^ (1 << bit)) for i in range(subs)])
    scores = jnp.log(1.0 + held.reshape(-1))

    flag = pl.pallas_call(
        functools.partial(flag_kernel, share),
        out_specs=pl.BlockSpec(memory_space=pltpu.SMEM),
        out_shape=jax.ShapeDtypeStruct((1,), jnp.int32),
        compiler_params=pltpu.CompilerParams(vmem_limit_bytes=4 * 1024 * 1024),
    )(swap_cols, home)
    bad = flag[0] > 0
    if tiles > QUAD:
        bad = lax.pmax(bad.astype(jnp.int32), "tile") > 0
        bad = bad | quads_joined(tag, tiles, place)
    return lax.cond(bad, lambda: every_pair(embeddings, cluster_ids), lambda: scores)


def solution(mesh):
    in_specs = (P(("groups", "tile"), None), P(("groups", "tile")))
    out_specs = P(("groups", "tile", "sub"))
    return jax.shard_map(shards, mesh=mesh, in_specs=in_specs, out_specs=out_specs, check_vma=False)
```

```python
import functools
import math

import jax
import jax.numpy as jnp
import numpy as np
from jax import lax
from jax.experimental import pallas as pl
from jax.experimental.pallas import tpu as pltpu
from jax.sharding import PartitionSpec as P

BLOCK = 128
QUAD = 4
SPAN = 4

inverse_temp = 10.0
norm_eps = 1e-06
GAIN = inverse_temp * math.log2(math.e)
OFF = -1000.0

STEP = 512
COPY = 64


def normalised(values):
    values = values.astype(jnp.float32)
    scale = lax.rsqrt(jnp.sum(values * values, axis=1, keepdims=True) + norm_eps)
    return (values * scale).astype(jnp.bfloat16)


def products(rows, columns):
    return lax.dot_general(
        rows, columns, (((1,), (1,)), ((), ())), preferred_element_type=jnp.float32
    )


def column_bias(tag, column_tags):
    return jnp.where(column_tags == tag.astype(jnp.float32), -GAIN, OFF)


def lane_sums(weight):
    total = weight[:, :BLOCK]
    for start in range(BLOCK, weight.shape[1], BLOCK):
        total = total + weight[:, start : start + BLOCK]
    return jnp.sum(total.T, axis=0, keepdims=True)


class Plan:
    def __init__(self, blocks, subs, place, member):
        width = blocks // subs
        share = width // 2
        part = place % QUAD
        self.inner = (part == 1) | (part == 2)
        self.far = part == 1
        dealt = member // 2 * share
        near = (dealt // width * 2 + member % 2) * width + dealt % width
        near = jnp.where(part == 1, blocks // 2, 0) + near
        self.first = jnp.where(self.inner, near, member * width)
        self.second = jnp.where(self.inner, near, member * width + share)
        self.edge = jnp.where(part == 1, blocks // 2 - 1, blocks // 2)
        self.width, self.share = width, share


def pack_kernel(blocks, subs, rows_ref, ids_ref, first_ref, behind_ref, ids, sems):
    plan = Plan(blocks, subs, lax.axis_index("tile"), lax.axis_index("sub"))
    share, size = plan.share, plan.share * BLOCK
    copies = [pltpu.make_async_copy(ids_ref, ids, sems.at[0])]
    for index, down in enumerate(range(0, size, COPY)):
        start = pl.multiple_of(plan.first * BLOCK + down, COPY)
        copies.append(
            pltpu.make_async_copy(
                rows_ref.at[pl.ds(start, COPY), :], first_ref.at[pl.ds(down, COPY), :], sems.at[1 + index]
            )
        )
    for copy in copies:
        copy.start()
    copies[0].wait()
    depth = first_ref.shape[1]
    edge = jnp.max(ids[pl.ds(plan.edge, 1), :], axis=1, keepdims=True)
    rest = [jnp.broadcast_to(edge, (1, BLOCK)), jnp.zeros((1, depth - size - BLOCK), jnp.int32)]
    for block, out in ((plan.first, first_ref), (plan.second, behind_ref)):
        row = jnp.concatenate([ids[pl.ds(block + k, 1), :] for k in range(share)] + rest, axis=1)
        row = jnp.broadcast_to(row.astype(jnp.float32), (8, depth)).astype(jnp.bfloat16)
        out[out.shape[0] - 8 :, :] = row
    for copy in copies[1:]:
        copy.wait()


def pack(size, subs, embeddings, by_block):
    depth = embeddings.shape[1]
    return pl.pallas_call(
        functools.partial(pack_kernel, by_block.shape[0], subs),
        in_specs=[pl.BlockSpec(memory_space=pl.ANY)] * 2,
        out_specs=[pl.BlockSpec(memory_space=pltpu.VMEM)] * 2,
        out_shape=[jax.ShapeDtypeStruct((count, depth), jnp.bfloat16) for count in (size + 8, 8)],
        scratch_shapes=[pltpu.VMEM(by_block.shape, jnp.int32), pltpu.SemaphoreType.DMA((size // COPY + 1,))],
        compiler_params=pltpu.CompilerParams(vmem_limit_bytes=8 * 1024 * 1024),
        cost_estimate=pl.CostEstimate(flops=0, bytes_accessed=1024, transcendentals=0),
    )(embeddings, by_block)


class Meta:
    def __init__(self, ref, blocks):
        self.ref, self.blocks = ref, blocks

    def tag(self, block, chunk=None):
        return self.ref[block + (0 if chunk is None else (2 + chunk) * self.blocks)]

    def used(self, block):
        return self.ref[self.blocks + block]

    def number(self, index):
        return self.ref[5 * self.blocks + index]


MEMBER, FIRST_BLOCK, EDGE, INNER, SECOND_BLOCK = range(5)


def self_kernel(
    blocks, subs, meta_ref, rows_ref, tags_ref, behind_ref, unit_ref, sums_ref, second_ref, held, sems
):
    meta = Meta(meta_ref, blocks)
    width = blocks // subs
    quarter = width * BLOCK
    member = meta.number(MEMBER)
    owners = [lax.rem(member + turn, subs) for turn in range(subs)]
    spans = [pl.ds(pl.multiple_of(owner * quarter, quarter), quarter) for owner in owners]
    copies = []
    for turn, span in enumerate(spans):
        copies.append(pltpu.make_async_copy(rows_ref.at[span, :], held.at[turn], sems.at[turn]))
        copies[-1].start()
    column_tags = tags_ref[...].astype(jnp.float32)
    for turn in range(subs):
        copies[turn].wait()
        unit = normalised(held[turn])
        unit_ref[spans[turn], :] = unit
        if turn == 0:
            share = unit
        cosine = products(unit, share)
        for inner in range(width):
            block = owners[turn] * width + inner
            bias = column_bias(meta.tag(block), column_tags)
            weight = jnp.exp2(cosine[inner * BLOCK : (inner + 1) * BLOCK] * GAIN + bias)
            row = lax.broadcasted_iota(jnp.int32, weight.shape, 0)
            keep = row < meta.used(block)
            if turn == 0:
                keep = keep & (lax.broadcasted_iota(jnp.int32, weight.shape, 1) - row != inner * BLOCK)
            sums_ref[pl.ds(block, 1), :] = lane_sums(jnp.where(keep, weight, 0.0))
    size = second_ref.shape[0] - 8
    start = pl.multiple_of(meta.number(SECOND_BLOCK) * BLOCK, BLOCK)
    second_ref[:size, :] = unit_ref[pl.ds(start, size), :]
    second_ref[size:, :] = behind_ref[...]


def chunk_tags(piece_ref, size):
    row = piece_ref[size:, :].astype(jnp.float32)[0:1, :]
    return row[:, :size], row[:, size : size + BLOCK]


def cross_terms(meta, chunk, column_tags, unit_ref, piece_ref, before_ref, sums, columns, place):
    size = column_tags.shape[1]
    there = [jnp.max(column_tags[:, at : at + BLOCK]) for at in range(0, size, BLOCK)]
    shared = False
    for block in range(meta.blocks):
        for tag in there:
            shared = (meta.tag(block, chunk).astype(jnp.float32) == tag) | shared

    @pl.when(jnp.logical_not(shared))
    def _():
        columns[...] = jnp.zeros_like(columns)
        for block in range(meta.blocks):
            sums[place(block) : place(block) + 1, :] = before_ref[block : block + 1, :]

    @pl.when(shared)
    def _():
        piece = piece_ref[:size, :] if chunk == 2 else normalised(piece_ref[:size, :])
        total = None
        for start in range(0, meta.blocks * BLOCK, STEP):
            cosine = products(unit_ref[start : start + STEP, :], piece)
            for inner in range(0, STEP, BLOCK):
                block = (start + inner) // BLOCK
                bias = column_bias(meta.tag(block, chunk), column_tags)
                weight = jnp.exp2(cosine[inner : inner + BLOCK] * GAIN + bias)
                row = lax.broadcasted_iota(jnp.int32, weight.shape, 0)
                weight = jnp.where(row < meta.used(block), weight, 0.0)
                sums[place(block) : place(block) + 1, :] = before_ref[block : block + 1, :] + lane_sums(weight)
                partial = weight[0:8]
                for down in range(8, BLOCK, 8):
                    partial = partial + weight[down : down + 8]
                total = partial if total is None else total + partial
        columns[...] = total


def middle_kernel(blocks, share, chunk, meta_ref, unit_ref, piece_ref, before_ref, sums_ref, cols_ref, columns):
    meta = Meta(meta_ref, blocks)
    tags, edge = chunk_tags(piece_ref, share * BLOCK)
    cross_terms(meta, chunk, tags, unit_ref, piece_ref, before_ref, sums_ref, columns, lambda block: block)
    total = jnp.sum(columns[...], axis=0, keepdims=True)
    for k in range(share):
        cols_ref[k : k + 1, :] = total[:, k * BLOCK : (k + 1) * BLOCK]
    mine = meta.tag(meta.number(EDGE)).astype(jnp.float32)
    joined = (edge == mine) & (edge >= 0) & (meta.number(INNER) > 0)
    cols_ref[share : share + 1, :] = jnp.where(joined, 1.0, 0.0)


def last_kernel(
    blocks, share, width, meta_ref, unit_ref, piece_ref, before_ref, outer_back_ref, swap_cols_ref,
    keep_ref, send_ref, cols_ref, sums, columns,
):
    meta = Meta(meta_ref, blocks)
    tags, _ = chunk_tags(piece_ref, share * BLOCK)

    def place(block):
        owner = block // width
        return owner % 2 * (blocks // 2) + owner // 2 * width + block % width

    cross_terms(meta, 2, tags, unit_ref, piece_ref, before_ref, sums, columns, place)
    total = jnp.sum(columns[...], axis=0, keepdims=True)
    for k in range(share):
        cols_ref[k : k + 1, :] = total[:, k * BLOCK : (k + 1) * BLOCK]
        at = place(meta.number(FIRST_BLOCK) + k)
        sums[pl.ds(at, 1), :] += outer_back_ref[k : k + 1, :]
    cols_ref[share : share + 1, :] = swap_cols_ref[share : share + 1, :]
    parity = meta.number(MEMBER) % 2
    heap = blocks // 2
    keep_ref[...] = sums[pl.ds(pl.multiple_of(parity * heap, heap), heap), :]
    send_ref[...] = sums[pl.ds(pl.multiple_of((1 - parity) * heap, heap), heap), :]


def flag_kernel(share, here_ref, home_ref, flag_ref):
    flags = jnp.maximum(here_ref[share : share + 1, :], home_ref[share : share + 1, :])
    flag_ref[0] = jnp.max(flags).astype(jnp.int32)


def call(kernel, meta, operands, out_shapes, scratch, flops):
    vmem, smem = pl.BlockSpec(memory_space=pltpu.VMEM), pl.BlockSpec(memory_space=pltpu.SMEM)
    return pl.pallas_call(
        kernel,
        in_specs=[smem] + [vmem] * len(operands),
        out_specs=[vmem if len(shape.shape) > 1 else smem for shape in out_shapes],
        out_shape=out_shapes,
        scratch_shapes=scratch,
        compiler_params=pltpu.CompilerParams(vmem_limit_bytes=16 * 1024 * 1024),
        cost_estimate=pl.CostEstimate(flops=flops, bytes_accessed=1024, transcendentals=0),
    )(meta, *operands)


def every_pair(embeddings, cluster_ids):
    unit = normalised(embeddings)
    tags = cluster_ids + 1
    groups = lax.axis_size("sub")
    member = lax.axis_index("sub")
    owners = lax.axis_size("tile")
    place = lax.axis_index("tile")
    rows_here = unit.shape[0]
    width = rows_here // groups
    own_piece = lax.dynamic_slice_in_dim(unit, member * width, width, 0)
    own_tags = lax.dynamic_slice_in_dim(tags, member * width, width, 0)
    distance = place - jnp.arange(owners, dtype=jnp.int32)
    keep = (jnp.abs(distance) < SPAN) & (distance != 0)
    outgoing = jnp.where(keep[:, None, None], own_piece[None, :, :], jnp.zeros((), jnp.bfloat16))
    outgoing_tags = jnp.where(keep[:, None], own_tags[None, :], 0)
    arrived = lax.all_to_all(outgoing, "tile", split_axis=0, concat_axis=0, tiled=True)
    arrived_tags = lax.all_to_all(outgoing_tags, "tile", split_axis=0, concat_axis=0, tiled=True)
    local_rows = jnp.arange(rows_here, dtype=jnp.int32)[:, None]
    slice_rows = member * width + jnp.arange(width, dtype=jnp.int32)[None, :]
    total = jnp.zeros((rows_here,), jnp.float32)
    for offset in range(1 - SPAN, SPAN):
        if offset == 0:
            piece, piece_tags, order = own_piece, own_tags, local_rows != slice_rows
        else:
            source = place + offset
            valid = (source >= 0) & (source < owners)
            index = jnp.clip(source, 0, owners - 1)
            piece = lax.dynamic_index_in_dim(arrived, index, 0, keepdims=False)
            piece_tags = lax.dynamic_index_in_dim(arrived_tags, index, 0, keepdims=False)
            piece_tags = jnp.where(valid, piece_tags, 0)
            order = True
        same = (tags[:, None] == piece_tags[None, :]) & (tags[:, None] > 0) & order
        weight = jnp.where(same, jnp.exp(inverse_temp * (products(unit, piece) - 1.0)), 0.0)
        total = total + jnp.sum(weight, axis=1)
    return jnp.log(1.0 + lax.psum_scatter(total, "sub", scatter_dimension=0, tiled=True))


def quads_joined(tag, tiles, place):
    last = jnp.broadcast_to(tag[-1], (BLOCK,))
    before = lax.ppermute(last, "tile", [(t, t + 1) for t in range(tiles - 1)])[0]
    joined = (place % QUAD == 0) & (place > 0) & (before == tag[0]) & (before >= 0)
    return lax.pmax(joined.astype(jnp.int32), "tile") > 0


def shards(embeddings, cluster_ids):
    tiles, subs = lax.axis_size("tile"), lax.axis_size("sub")
    place, member = lax.axis_index("tile"), lax.axis_index("sub")
    rows, depth = embeddings.shape
    blocks = rows // BLOCK
    plan = Plan(blocks, subs, place, member)
    width, share, inner = plan.width, plan.share, plan.inner
    size = share * BLOCK
    quads = range(0, tiles, QUAD)
    inward = [p for q in quads for p in ((q, q + 1), (q + 3, q + 2))]
    swap = [p for q in quads for p in ((q + 1, q + 2), (q + 2, q + 1))]
    around = [p for q in quads for p in ((q, q + 1), (q + 3, q + 2), (q + 1, q + 3), (q + 2, q))]

    def turned(route):
        return [(b, a) for a, b in route]

    by_block = cluster_ids.reshape(blocks, BLOCK)
    first_out, behind = pack(size, subs, embeddings, by_block)
    from_inner = lax.ppermute(first_out, "tile", swap)
    from_outer = lax.ppermute(first_out, "tile", inward)

    tag = jnp.max(by_block, axis=1)
    used = jnp.sum((by_block >= 0).astype(jnp.int32), axis=1)
    seen = jnp.where(inner, tag, -2)
    swapped = jnp.where(plan.far & (jnp.arange(blocks) >= blocks // 2), -2, seen)
    numbers = jnp.stack([member, plan.first, plan.edge, inner, plan.second])
    meta = jnp.concatenate([tag, used, seen, swapped, tag, numbers]).astype(jnp.int32)

    heap = blocks // 2
    owner = plan.second // width
    home_row = jnp.arange(heap)[:, None] - (owner // 2 * width + plan.second % width)
    home_row = jnp.broadcast_to(home_row, (heap, BLOCK)).astype(jnp.int32)
    upper = [
        jnp.broadcast_to((member >> bit) & 1, (heap >> bit, BLOCK)).astype(jnp.int32)
        for bit in range(1, subs.bit_length() - 1)
    ]
    meta, home_row, *upper = lax.optimization_barrier((meta, home_row, *upper))

    row_sums = jax.ShapeDtypeStruct((blocks, BLOCK), jnp.float32)
    col_sums = jax.ShapeDtypeStruct((share + 1, BLOCK), jnp.float32)
    quarter = width * BLOCK
    vmem, smem = pl.BlockSpec(memory_space=pltpu.VMEM), pl.BlockSpec(memory_space=pltpu.SMEM)
    unit, sums, second_out = pl.pallas_call(
        functools.partial(self_kernel, blocks, subs),
        in_specs=[smem, pl.BlockSpec(memory_space=pl.ANY), vmem, vmem],
        out_specs=[vmem] * 3,
        out_shape=[
            jax.ShapeDtypeStruct((rows, depth), jnp.bfloat16),
            row_sums,
            jax.ShapeDtypeStruct((size + 8, depth), jnp.bfloat16),
        ],
        scratch_shapes=[pltpu.VMEM((subs, quarter, depth), jnp.bfloat16), pltpu.SemaphoreType.DMA((subs,))],
        compiler_params=pltpu.CompilerParams(vmem_limit_bytes=24 * 1024 * 1024),
        cost_estimate=pl.CostEstimate(flops=0, bytes_accessed=1024, transcendentals=0),
    )(meta, embeddings, lax.dynamic_slice_in_dim(cluster_ids, member * quarter, quarter, 0)[None], behind)
    last = lax.ppermute(second_out, "tile", around)

    def middle(chunk, piece, before):
        return call(
            functools.partial(middle_kernel, blocks, share, chunk),
            meta,
            (unit, piece, before),
            [row_sums, col_sums],
            [pltpu.VMEM((8, size), jnp.float32)],
            2 * rows * size * depth,
        )

    sums, outer_cols = middle(0, from_outer, sums)
    outer_back = lax.ppermute(outer_cols, "tile", turned(inward))
    sums, swap_cols = middle(1, from_inner, sums)
    swap_back = lax.ppermute(swap_cols, "tile", turned(swap))
    half = jax.ShapeDtypeStruct((heap, BLOCK), jnp.float32)
    held, leaving, cols = call(
        functools.partial(last_kernel, blocks, share, width),
        meta,
        (unit, last, sums, outer_back, swap_cols),
        [half, half, col_sums],
        [
            pltpu.VMEM((blocks, BLOCK), jnp.float32),
            pltpu.VMEM((8, size), jnp.float32),
        ],
        2 * rows * size * depth,
    )

    home = lax.ppermute(cols, "tile", turned(around))
    for k in range(share):
        held = held + jnp.where(home_row == k, home[k : k + 1] + swap_back[k : k + 1], 0.0)
    held = held + lax.ppermute(leaving, "sub", [(i, i ^ 1) for i in range(subs)])
    home, held = lax.optimization_barrier((home, held))
    for bit, mine in enumerate(upper, 1):
        pairs = held.reshape(-1, 2, width, BLOCK)
        low, high = pairs[:, 0].reshape(mine.shape), pairs[:, 1].reshape(mine.shape)
        leaving = jnp.where(mine > 0, low, high)
        held = jnp.where(mine > 0, high, low)
        held = held + lax.ppermute(leaving, "sub", [(i, i ^ (1 << bit)) for i in range(subs)])
    scores = jnp.log(1.0 + held.reshape(-1))

    flag = pl.pallas_call(
        functools.partial(flag_kernel, share),
        out_specs=pl.BlockSpec(memory_space=pltpu.SMEM),
        out_shape=jax.ShapeDtypeStruct((1,), jnp.int32),
        compiler_params=pltpu.CompilerParams(vmem_limit_bytes=4 * 1024 * 1024),
    )(swap_cols, home)
    bad = flag[0] > 0
    if tiles > QUAD:
        bad = lax.pmax(bad.astype(jnp.int32), "tile") > 0
        bad = bad | quads_joined(tag, tiles, place)
    return lax.cond(bad, lambda: every_pair(embeddings, cluster_ids), lambda: scores)


def solution(mesh):
    in_specs = (P(("groups", "tile"), None), P(("groups", "tile")))
    out_specs = P(("groups", "tile", "sub"))
    return jax.shard_map(shards, mesh=mesh, in_specs=in_specs, out_specs=out_specs, check_vma=False)
```

```python
import functools
import math

import jax
import jax.numpy as jnp
import numpy as np
from jax import lax
from jax.experimental import pallas as pl
from jax.experimental.pallas import tpu as pltpu
from jax.sharding import PartitionSpec as P

BLOCK = 128
QUAD = 4
SPAN = 4

inverse_temp = 10.0
norm_eps = 1e-06
GAIN = inverse_temp * math.log2(math.e)
OFF = -1000.0

STEP = 512
COPY = 64


def normalised(values):
    values = values.astype(jnp.float32)
    scale = lax.rsqrt(jnp.sum(values * values, axis=1, keepdims=True) + norm_eps)
    return (values * scale).astype(jnp.bfloat16)


def products(rows, columns):
    return lax.dot_general(
        rows, columns, (((1,), (1,)), ((), ())), preferred_element_type=jnp.float32
    )


def column_bias(tag, column_tags):
    return jnp.where(column_tags == tag.astype(jnp.float32), -GAIN, OFF)


def lane_sums(weight):
    total = weight[:, :BLOCK]
    for start in range(BLOCK, weight.shape[1], BLOCK):
        total = total + weight[:, start : start + BLOCK]
    return jnp.sum(total.T, axis=0, keepdims=True)


class Plan:
    def __init__(self, blocks, subs, place, member):
        width = blocks // subs
        share = width // 2
        part = place % QUAD
        self.inner = (part == 1) | (part == 2)
        self.far = part == 1
        dealt = member // 2 * share
        near = (dealt // width * 2 + member % 2) * width + dealt % width
        near = jnp.where(part == 1, blocks // 2, 0) + near
        self.first = jnp.where(self.inner, near, member * width)
        self.second = jnp.where(self.inner, near, member * width + share)
        self.edge = jnp.where(part == 1, blocks // 2 - 1, blocks // 2)
        self.width, self.share = width, share


def pack_kernel(blocks, subs, rows_ref, ids_ref, first_ref, behind_ref, ids, sems):
    plan = Plan(blocks, subs, lax.axis_index("tile"), lax.axis_index("sub"))
    share, size = plan.share, plan.share * BLOCK
    copies = [pltpu.make_async_copy(ids_ref, ids, sems.at[0])]
    for index, down in enumerate(range(0, size, COPY)):
        start = pl.multiple_of(plan.first * BLOCK + down, COPY)
        copies.append(
            pltpu.make_async_copy(
                rows_ref.at[pl.ds(start, COPY), :], first_ref.at[pl.ds(down, COPY), :], sems.at[1 + index]
            )
        )
    for copy in copies:
        copy.start()
    copies[0].wait()
    depth = first_ref.shape[1]
    edge = jnp.max(ids[pl.ds(plan.edge, 1), :], axis=1, keepdims=True)
    rest = [jnp.broadcast_to(edge, (1, BLOCK)), jnp.zeros((1, depth - size - BLOCK), jnp.int32)]
    for block, out in ((plan.first, first_ref), (plan.second, behind_ref)):
        row = jnp.concatenate([ids[pl.ds(block + k, 1), :] for k in range(share)] + rest, axis=1)
        row = jnp.broadcast_to(row.astype(jnp.float32), (8, depth)).astype(jnp.bfloat16)
        out[out.shape[0] - 8 :, :] = row
    for copy in copies[1:]:
        copy.wait()


def pack(size, subs, embeddings, by_block):
    depth = embeddings.shape[1]
    return pl.pallas_call(
        functools.partial(pack_kernel, by_block.shape[0], subs),
        in_specs=[pl.BlockSpec(memory_space=pl.ANY)] * 2,
        out_specs=[pl.BlockSpec(memory_space=pltpu.VMEM)] * 2,
        out_shape=[jax.ShapeDtypeStruct((count, depth), jnp.bfloat16) for count in (size + 8, 8)],
        scratch_shapes=[pltpu.VMEM(by_block.shape, jnp.int32), pltpu.SemaphoreType.DMA((size // COPY + 1,))],
        compiler_params=pltpu.CompilerParams(vmem_limit_bytes=8 * 1024 * 1024),
        cost_estimate=pl.CostEstimate(flops=0, bytes_accessed=1024, transcendentals=0),
    )(embeddings, by_block)


class Meta:
    def __init__(self, ref, blocks):
        self.ref, self.blocks = ref, blocks

    def tag(self, block, chunk=None):
        return self.ref[block + (0 if chunk is None else (2 + chunk) * self.blocks)]

    def used(self, block):
        return self.ref[self.blocks + block]

    def number(self, index):
        return self.ref[5 * self.blocks + index]


MEMBER, FIRST_BLOCK, EDGE, INNER, SECOND_BLOCK = range(5)


def self_kernel(
    blocks, subs, meta_ref, rows_ref, tags_ref, behind_ref, unit_ref, sums_ref, second_ref, held, sems
):
    meta = Meta(meta_ref, blocks)
    width = blocks // subs
    quarter = width * BLOCK
    member = meta.number(MEMBER)
    owners = [lax.rem(member + turn, subs) for turn in range(subs)]
    spans = [pl.ds(pl.multiple_of(owner * quarter, quarter), quarter) for owner in owners]
    copies = []
    for turn, span in enumerate(spans):
        copies.append(pltpu.make_async_copy(rows_ref.at[span, :], held.at[turn], sems.at[turn]))
        copies[-1].start()
    column_tags = tags_ref[...].astype(jnp.float32)
    for turn in range(subs):
        copies[turn].wait()
        unit = normalised(held[turn])
        unit_ref[spans[turn], :] = unit
        if turn == 0:
            share = unit
        cosine = products(unit, share)
        for inner in range(width):
            block = owners[turn] * width + inner
            bias = column_bias(meta.tag(block), column_tags)
            weight = jnp.exp2(cosine[inner * BLOCK : (inner + 1) * BLOCK] * GAIN + bias)
            row = lax.broadcasted_iota(jnp.int32, weight.shape, 0)
            keep = row < meta.used(block)
            if turn == 0:
                keep = keep & (lax.broadcasted_iota(jnp.int32, weight.shape, 1) - row != inner * BLOCK)
            sums_ref[pl.ds(block, 1), :] = lane_sums(jnp.where(keep, weight, 0.0))
    size = second_ref.shape[0] - 8
    start = pl.multiple_of(meta.number(SECOND_BLOCK) * BLOCK, BLOCK)
    second_ref[:size, :] = unit_ref[pl.ds(start, size), :]
    second_ref[size:, :] = behind_ref[...]


def chunk_tags(piece_ref, size):
    row = piece_ref[size:, :].astype(jnp.float32)[0:1, :]
    return row[:, :size], row[:, size : size + BLOCK]


def cross_terms(meta, chunk, column_tags, unit_ref, piece_ref, before_ref, sums, columns, place, head=None):
    size = column_tags.shape[1]
    step = STEP
    if head is not None:
        step = head.shape[0]
        head[...] = products(unit_ref[:step, :], piece_ref[:size, :])
    there = [jnp.max(column_tags[:, at : at + BLOCK]) for at in range(0, size, BLOCK)]
    shared = False
    for block in range(meta.blocks):
        for tag in there:
            shared = (meta.tag(block, chunk).astype(jnp.float32) == tag) | shared

    @pl.when(jnp.logical_not(shared))
    def _():
        columns[...] = jnp.zeros_like(columns)
        for block in range(meta.blocks):
            sums[place(block) : place(block) + 1, :] = before_ref[block : block + 1, :]

    @pl.when(shared)
    def _():
        piece = piece_ref[:size, :] if chunk == 2 else normalised(piece_ref[:size, :])
        total = None
        for start in range(0, meta.blocks * BLOCK, step):
            if start == 0 and head is not None:
                cosine = head[...]
            else:
                cosine = products(unit_ref[start : start + step, :], piece)
            for inner in range(0, step, BLOCK):
                block = (start + inner) // BLOCK
                bias = column_bias(meta.tag(block, chunk), column_tags)
                weight = jnp.exp2(cosine[inner : inner + BLOCK] * GAIN + bias)
                row = lax.broadcasted_iota(jnp.int32, weight.shape, 0)
                weight = jnp.where(row < meta.used(block), weight, 0.0)
                sums[place(block) : place(block) + 1, :] = before_ref[block : block + 1, :] + lane_sums(weight)
                partial = weight[0:8]
                for down in range(8, BLOCK, 8):
                    partial = partial + weight[down : down + 8]
                total = partial if total is None else total + partial
        columns[...] = total


def middle_kernel(blocks, share, chunk, meta_ref, unit_ref, piece_ref, before_ref, sums_ref, cols_ref, columns):
    meta = Meta(meta_ref, blocks)
    tags, edge = chunk_tags(piece_ref, share * BLOCK)
    cross_terms(meta, chunk, tags, unit_ref, piece_ref, before_ref, sums_ref, columns, lambda block: block)
    total = jnp.sum(columns[...], axis=0, keepdims=True)
    for k in range(share):
        cols_ref[k : k + 1, :] = total[:, k * BLOCK : (k + 1) * BLOCK]
    mine = meta.tag(meta.number(EDGE)).astype(jnp.float32)
    joined = (edge == mine) & (edge >= 0) & (meta.number(INNER) > 0)
    cols_ref[share : share + 1, :] = jnp.where(joined, 1.0, 0.0)


def last_kernel(
    blocks, share, width, meta_ref, unit_ref, piece_ref, before_ref, outer_back_ref, swap_cols_ref,
    keep_ref, send_ref, cols_ref, sums, columns, head,
):
    meta = Meta(meta_ref, blocks)
    tags, _ = chunk_tags(piece_ref, share * BLOCK)

    def place(block):
        owner = block // width
        return owner % 2 * (blocks // 2) + owner // 2 * width + block % width

    cross_terms(meta, 2, tags, unit_ref, piece_ref, before_ref, sums, columns, place, head)
    total = jnp.sum(columns[...], axis=0, keepdims=True)
    for k in range(share):
        cols_ref[k : k + 1, :] = total[:, k * BLOCK : (k + 1) * BLOCK]
        at = place(meta.number(FIRST_BLOCK) + k)
        sums[pl.ds(at, 1), :] += outer_back_ref[k : k + 1, :]
    cols_ref[share : share + 1, :] = swap_cols_ref[share : share + 1, :]
    parity = meta.number(MEMBER) % 2
    heap = blocks // 2
    keep_ref[...] = sums[pl.ds(pl.multiple_of(parity * heap, heap), heap), :]
    send_ref[...] = sums[pl.ds(pl.multiple_of((1 - parity) * heap, heap), heap), :]


def flag_kernel(share, here_ref, home_ref, flag_ref):
    flags = jnp.maximum(here_ref[share : share + 1, :], home_ref[share : share + 1, :])
    flag_ref[0] = jnp.max(flags).astype(jnp.int32)


def call(kernel, meta, operands, out_shapes, scratch, flops):
    vmem, smem = pl.BlockSpec(memory_space=pltpu.VMEM), pl.BlockSpec(memory_space=pltpu.SMEM)
    return pl.pallas_call(
        kernel,
        in_specs=[smem] + [vmem] * len(operands),
        out_specs=[vmem if len(shape.shape) > 1 else smem for shape in out_shapes],
        out_shape=out_shapes,
        scratch_shapes=scratch,
        compiler_params=pltpu.CompilerParams(vmem_limit_bytes=16 * 1024 * 1024),
        cost_estimate=pl.CostEstimate(flops=flops, bytes_accessed=1024, transcendentals=0),
    )(meta, *operands)


def every_pair(embeddings, cluster_ids):
    unit = normalised(embeddings)
    tags = cluster_ids + 1
    groups = lax.axis_size("sub")
    member = lax.axis_index("sub")
    owners = lax.axis_size("tile")
    place = lax.axis_index("tile")
    rows_here = unit.shape[0]
    width = rows_here // groups
    own_piece = lax.dynamic_slice_in_dim(unit, member * width, width, 0)
    own_tags = lax.dynamic_slice_in_dim(tags, member * width, width, 0)
    distance = place - jnp.arange(owners, dtype=jnp.int32)
    keep = (jnp.abs(distance) < SPAN) & (distance != 0)
    outgoing = jnp.where(keep[:, None, None], own_piece[None, :, :], jnp.zeros((), jnp.bfloat16))
    outgoing_tags = jnp.where(keep[:, None], own_tags[None, :], 0)
    arrived = lax.all_to_all(outgoing, "tile", split_axis=0, concat_axis=0, tiled=True)
    arrived_tags = lax.all_to_all(outgoing_tags, "tile", split_axis=0, concat_axis=0, tiled=True)
    local_rows = jnp.arange(rows_here, dtype=jnp.int32)[:, None]
    slice_rows = member * width + jnp.arange(width, dtype=jnp.int32)[None, :]
    total = jnp.zeros((rows_here,), jnp.float32)
    for offset in range(1 - SPAN, SPAN):
        if offset == 0:
            piece, piece_tags, order = own_piece, own_tags, local_rows != slice_rows
        else:
            source = place + offset
            valid = (source >= 0) & (source < owners)
            index = jnp.clip(source, 0, owners - 1)
            piece = lax.dynamic_index_in_dim(arrived, index, 0, keepdims=False)
            piece_tags = lax.dynamic_index_in_dim(arrived_tags, index, 0, keepdims=False)
            piece_tags = jnp.where(valid, piece_tags, 0)
            order = True
        same = (tags[:, None] == piece_tags[None, :]) & (tags[:, None] > 0) & order
        weight = jnp.where(same, jnp.exp(inverse_temp * (products(unit, piece) - 1.0)), 0.0)
        total = total + jnp.sum(weight, axis=1)
    return jnp.log(1.0 + lax.psum_scatter(total, "sub", scatter_dimension=0, tiled=True))


def quads_joined(tag, tiles, place):
    last = jnp.broadcast_to(tag[-1], (BLOCK,))
    before = lax.ppermute(last, "tile", [(t, t + 1) for t in range(tiles - 1)])[0]
    joined = (place % QUAD == 0) & (place > 0) & (before == tag[0]) & (before >= 0)
    return lax.pmax(joined.astype(jnp.int32), "tile") > 0


def shards(embeddings, cluster_ids):
    tiles, subs = lax.axis_size("tile"), lax.axis_size("sub")
    place, member = lax.axis_index("tile"), lax.axis_index("sub")
    rows, depth = embeddings.shape
    blocks = rows // BLOCK
    plan = Plan(blocks, subs, place, member)
    width, share, inner = plan.width, plan.share, plan.inner
    size = share * BLOCK
    quads = range(0, tiles, QUAD)
    inward = [p for q in quads for p in ((q, q + 1), (q + 3, q + 2))]
    swap = [p for q in quads for p in ((q + 1, q + 2), (q + 2, q + 1))]
    around = [p for q in quads for p in ((q, q + 1), (q + 3, q + 2), (q + 1, q + 3), (q + 2, q))]

    def turned(route):
        return [(b, a) for a, b in route]

    by_block = cluster_ids.reshape(blocks, BLOCK)
    first_out, behind = pack(size, subs, embeddings, by_block)
    from_inner = lax.ppermute(first_out, "tile", swap)
    from_outer = lax.ppermute(first_out, "tile", inward)

    tag = jnp.max(by_block, axis=1)
    used = jnp.sum((by_block >= 0).astype(jnp.int32), axis=1)
    seen = jnp.where(inner, tag, -2)
    swapped = jnp.where(plan.far & (jnp.arange(blocks) >= blocks // 2), -2, seen)
    numbers = jnp.stack([member, plan.first, plan.edge, inner, plan.second])
    meta = jnp.concatenate([tag, used, seen, swapped, tag, numbers]).astype(jnp.int32)

    heap = blocks // 2
    owner = plan.second // width
    home_row = jnp.arange(heap)[:, None] - (owner // 2 * width + plan.second % width)
    home_row = jnp.broadcast_to(home_row, (heap, BLOCK)).astype(jnp.int32)
    upper = [
        jnp.broadcast_to((member >> bit) & 1, (heap >> bit, BLOCK)).astype(jnp.int32)
        for bit in range(1, subs.bit_length() - 1)
    ]
    meta, home_row, *upper = lax.optimization_barrier((meta, home_row, *upper))

    row_sums = jax.ShapeDtypeStruct((blocks, BLOCK), jnp.float32)
    col_sums = jax.ShapeDtypeStruct((share + 1, BLOCK), jnp.float32)
    quarter = width * BLOCK
    vmem, smem = pl.BlockSpec(memory_space=pltpu.VMEM), pl.BlockSpec(memory_space=pltpu.SMEM)
    unit, sums, second_out = pl.pallas_call(
        functools.partial(self_kernel, blocks, subs),
        in_specs=[smem, pl.BlockSpec(memory_space=pl.ANY), vmem, vmem],
        out_specs=[vmem] * 3,
        out_shape=[
            jax.ShapeDtypeStruct((rows, depth), jnp.bfloat16),
            row_sums,
            jax.ShapeDtypeStruct((size + 8, depth), jnp.bfloat16),
        ],
        scratch_shapes=[pltpu.VMEM((subs, quarter, depth), jnp.bfloat16), pltpu.SemaphoreType.DMA((subs,))],
        compiler_params=pltpu.CompilerParams(vmem_limit_bytes=24 * 1024 * 1024),
        cost_estimate=pl.CostEstimate(flops=0, bytes_accessed=1024, transcendentals=0),
    )(meta, embeddings, lax.dynamic_slice_in_dim(cluster_ids, member * quarter, quarter, 0)[None], behind)
    last = lax.ppermute(second_out, "tile", around)

    def middle(chunk, piece, before):
        return call(
            functools.partial(middle_kernel, blocks, share, chunk),
            meta,
            (unit, piece, before),
            [row_sums, col_sums],
            [pltpu.VMEM((8, size), jnp.float32)],
            2 * rows * size * depth,
        )

    sums, outer_cols = middle(0, from_outer, sums)
    outer_back = lax.ppermute(outer_cols, "tile", turned(inward))
    sums, swap_cols = middle(1, from_inner, sums)
    swap_back = lax.ppermute(swap_cols, "tile", turned(swap))
    half = jax.ShapeDtypeStruct((heap, BLOCK), jnp.float32)
    held, leaving, cols = call(
        functools.partial(last_kernel, blocks, share, width),
        meta,
        (unit, last, sums, outer_back, swap_cols),
        [half, half, col_sums],
        [
            pltpu.VMEM((blocks, BLOCK), jnp.float32),
            pltpu.VMEM((8, size), jnp.float32),
            pltpu.VMEM((STEP // 2, size), jnp.float32),
        ],
        2 * rows * size * depth,
    )

    home = lax.ppermute(cols, "tile", turned(around))
    for k in range(share):
        held = held + jnp.where(home_row == k, home[k : k + 1] + swap_back[k : k + 1], 0.0)
    held = held + lax.ppermute(leaving, "sub", [(i, i ^ 1) for i in range(subs)])
    home, held = lax.optimization_barrier((home, held))
    for bit, mine in enumerate(upper, 1):
        pairs = held.reshape(-1, 2, width, BLOCK)
        low, high = pairs[:, 0].reshape(mine.shape), pairs[:, 1].reshape(mine.shape)
        leaving = jnp.where(mine > 0, low, high)
        held = jnp.where(mine > 0, high, low)
        held = held + lax.ppermute(leaving, "sub", [(i, i ^ (1 << bit)) for i in range(subs)])
    scores = jnp.log(1.0 + held.reshape(-1))

    flag = pl.pallas_call(
        functools.partial(flag_kernel, share),
        out_specs=pl.BlockSpec(memory_space=pltpu.SMEM),
        out_shape=jax.ShapeDtypeStruct((1,), jnp.int32),
        compiler_params=pltpu.CompilerParams(vmem_limit_bytes=4 * 1024 * 1024),
    )(swap_cols, home)
    bad = flag[0] > 0
    if tiles > QUAD:
        bad = lax.pmax(bad.astype(jnp.int32), "tile") > 0
        bad = bad | quads_joined(tag, tiles, place)
    return lax.cond(bad, lambda: every_pair(embeddings, cluster_ids), lambda: scores)


def solution(mesh):
    in_specs = (P(("groups", "tile"), None), P(("groups", "tile")))
    out_specs = P(("groups", "tile", "sub"))
    return jax.shard_map(shards, mesh=mesh, in_specs=in_specs, out_specs=out_specs, check_vma=False)
```

```python
import functools
import math

import jax
import jax.numpy as jnp
import numpy as np
from jax import lax
from jax.experimental import pallas as pl
from jax.experimental.pallas import tpu as pltpu
from jax.sharding import PartitionSpec as P

BLOCK = 128
QUAD = 4
SPAN = 4

inverse_temp = 10.0
norm_eps = 1e-06
GAIN = inverse_temp * math.log2(math.e)
OFF = -1000.0

STEP = 512
COPY = 64


def normalised(values):
    values = values.astype(jnp.float32)
    scale = lax.rsqrt(jnp.sum(values * values, axis=1, keepdims=True) + norm_eps)
    return (values * scale).astype(jnp.bfloat16)


def products(rows, columns):
    return lax.dot_general(
        rows, columns, (((1,), (1,)), ((), ())), preferred_element_type=jnp.float32
    )


def column_bias(tag, column_tags):
    return jnp.where(column_tags == tag.astype(jnp.float32), -GAIN, OFF)


def lane_sums(weight):
    total = weight[:, :BLOCK]
    for start in range(BLOCK, weight.shape[1], BLOCK):
        total = total + weight[:, start : start + BLOCK]
    return jnp.sum(total.T, axis=0, keepdims=True)


class Plan:
    def __init__(self, blocks, subs, place, member):
        width = blocks // subs
        share = width // 2
        part = place % QUAD
        self.inner = (part == 1) | (part == 2)
        self.far = part == 1
        dealt = member // 2 * share
        near = (dealt // width * 2 + member % 2) * width + dealt % width
        near = jnp.where(part == 1, blocks // 2, 0) + near
        self.first = jnp.where(self.inner, near, member * width)
        self.second = jnp.where(self.inner, near, member * width + share)
        self.edge = jnp.where(part == 1, blocks // 2 - 1, blocks // 2)
        self.width, self.share = width, share


def pack_kernel(blocks, subs, rows_ref, ids_ref, first_ref, behind_ref, ids, sems):
    plan = Plan(blocks, subs, lax.axis_index("tile"), lax.axis_index("sub"))
    share, size = plan.share, plan.share * BLOCK
    copies = [pltpu.make_async_copy(ids_ref, ids, sems.at[0])]
    for index, down in enumerate(range(0, size, COPY)):
        start = pl.multiple_of(plan.first * BLOCK + down, COPY)
        copies.append(
            pltpu.make_async_copy(
                rows_ref.at[pl.ds(start, COPY), :], first_ref.at[pl.ds(down, COPY), :], sems.at[1 + index]
            )
        )
    for copy in copies:
        copy.start()
    copies[0].wait()
    depth = first_ref.shape[1]
    edge = jnp.max(ids[pl.ds(plan.edge, 1), :], axis=1, keepdims=True)
    rest = [jnp.broadcast_to(edge, (1, BLOCK)), jnp.zeros((1, depth - size - BLOCK), jnp.int32)]
    for block, out in ((plan.first, first_ref), (plan.second, behind_ref)):
        row = jnp.concatenate([ids[pl.ds(block + k, 1), :] for k in range(share)] + rest, axis=1)
        row = jnp.broadcast_to(row.astype(jnp.float32), (8, depth)).astype(jnp.bfloat16)
        out[out.shape[0] - 8 :, :] = row
    for copy in copies[1:]:
        copy.wait()


def pack(size, subs, embeddings, by_block):
    depth = embeddings.shape[1]
    return pl.pallas_call(
        functools.partial(pack_kernel, by_block.shape[0], subs),
        in_specs=[pl.BlockSpec(memory_space=pl.ANY)] * 2,
        out_specs=[pl.BlockSpec(memory_space=pltpu.VMEM)] * 2,
        out_shape=[jax.ShapeDtypeStruct((count, depth), jnp.bfloat16) for count in (size + 8, 8)],
        scratch_shapes=[pltpu.VMEM(by_block.shape, jnp.int32), pltpu.SemaphoreType.DMA((size // COPY + 1,))],
        compiler_params=pltpu.CompilerParams(vmem_limit_bytes=8 * 1024 * 1024),
        cost_estimate=pl.CostEstimate(flops=0, bytes_accessed=1024, transcendentals=0),
    )(embeddings, by_block)


class Meta:
    def __init__(self, ref, blocks):
        self.ref, self.blocks = ref, blocks

    def tag(self, block, chunk=None):
        return self.ref[block + (0 if chunk is None else (2 + chunk) * self.blocks)]

    def used(self, block):
        return self.ref[self.blocks + block]

    def number(self, index):
        return self.ref[5 * self.blocks + index]


MEMBER, FIRST_BLOCK, EDGE, INNER, SECOND_BLOCK = range(5)


def self_kernel(
    blocks, subs, meta_ref, rows_ref, tags_ref, behind_ref, unit_ref, sums_ref, second_ref, held, sems
):
    meta = Meta(meta_ref, blocks)
    width = blocks // subs
    quarter = width * BLOCK
    member = meta.number(MEMBER)
    owners = [lax.rem(member + turn, subs) for turn in range(subs)]
    spans = [pl.ds(pl.multiple_of(owner * quarter, quarter), quarter) for owner in owners]
    copies = []
    for turn, span in enumerate(spans):
        copies.append(pltpu.make_async_copy(rows_ref.at[span, :], held.at[turn], sems.at[turn]))
        copies[-1].start()
    column_tags = tags_ref[...].astype(jnp.float32)
    for turn in range(subs):
        copies[turn].wait()
        unit = normalised(held[turn])
        unit_ref[spans[turn], :] = unit
        if turn == 0:
            share = unit
        cosine = products(unit, share)
        for inner in range(width):
            block = owners[turn] * width + inner
            bias = column_bias(meta.tag(block), column_tags)
            weight = jnp.exp2(cosine[inner * BLOCK : (inner + 1) * BLOCK] * GAIN + bias)
            row = lax.broadcasted_iota(jnp.int32, weight.shape, 0)
            keep = row < meta.used(block)
            if turn == 0:
                keep = keep & (lax.broadcasted_iota(jnp.int32, weight.shape, 1) - row != inner * BLOCK)
            sums_ref[pl.ds(block, 1), :] = lane_sums(jnp.where(keep, weight, 0.0))
    size = second_ref.shape[0] - 8
    start = pl.multiple_of(meta.number(SECOND_BLOCK) * BLOCK, BLOCK)
    second_ref[:size, :] = unit_ref[pl.ds(start, size), :]
    second_ref[size:, :] = behind_ref[...]


def chunk_tags(piece_ref, size):
    row = piece_ref[size:, :].astype(jnp.float32)[0:1, :]
    return row[:, :size], row[:, size : size + BLOCK]


def cross_terms(meta, chunk, column_tags, unit_ref, piece_ref, before_ref, sums, columns, place):
    size = column_tags.shape[1]
    there = [jnp.max(column_tags[:, at : at + BLOCK]) for at in range(0, size, BLOCK)]
    shared = False
    for block in range(meta.blocks):
        for tag in there:
            shared = (meta.tag(block, chunk).astype(jnp.float32) == tag) | shared

    @pl.when(jnp.logical_not(shared))
    def _():
        columns[...] = jnp.zeros_like(columns)
        for block in range(meta.blocks):
            sums[place(block) : place(block) + 1, :] = before_ref[block : block + 1, :]

    @pl.when(shared)
    def _():
        piece = piece_ref[:size, :] if chunk == 2 else normalised(piece_ref[:size, :])
        total = None
        for start in range(0, meta.blocks * BLOCK, STEP):
            cosine = products(unit_ref[start : start + STEP, :], piece)
            for inner in range(0, STEP, BLOCK):
                block = (start + inner) // BLOCK
                bias = column_bias(meta.tag(block, chunk), column_tags)
                weight = jnp.exp2(cosine[inner : inner + BLOCK] * GAIN + bias)
                row = lax.broadcasted_iota(jnp.int32, weight.shape, 0)
                weight = jnp.where(row < meta.used(block), weight, 0.0)
                sums[place(block) : place(block) + 1, :] = before_ref[block : block + 1, :] + lane_sums(weight)
                partial = weight[0:8]
                for down in range(8, BLOCK, 8):
                    partial = partial + weight[down : down + 8]
                total = partial if total is None else total + partial
        columns[...] = total


def middle_kernel(blocks, share, chunk, meta_ref, unit_ref, piece_ref, before_ref, sums_ref, cols_ref, columns):
    meta = Meta(meta_ref, blocks)
    tags, edge = chunk_tags(piece_ref, share * BLOCK)
    cross_terms(meta, chunk, tags, unit_ref, piece_ref, before_ref, sums_ref, columns, lambda block: block)
    total = jnp.sum(columns[...], axis=0, keepdims=True)
    for k in range(share):
        cols_ref[k : k + 1, :] = total[:, k * BLOCK : (k + 1) * BLOCK]
    mine = meta.tag(meta.number(EDGE)).astype(jnp.float32)
    joined = (edge == mine) & (edge >= 0) & (meta.number(INNER) > 0)
    cols_ref[share : share + 1, :] = jnp.where(joined, 1.0, 0.0)


def last_kernel(
    blocks, share, meta_ref, unit_ref, piece_ref, before_ref, outer_back_ref, swap_cols_ref,
    sums_ref, cols_ref, columns,
):
    meta = Meta(meta_ref, blocks)
    tags, _ = chunk_tags(piece_ref, share * BLOCK)
    cross_terms(meta, 2, tags, unit_ref, piece_ref, before_ref, sums_ref, columns, lambda block: block)
    total = jnp.sum(columns[...], axis=0, keepdims=True)
    for k in range(share):
        cols_ref[k : k + 1, :] = total[:, k * BLOCK : (k + 1) * BLOCK]
        sums_ref[pl.ds(meta.number(FIRST_BLOCK) + k, 1), :] += outer_back_ref[k : k + 1, :]
    cols_ref[share : share + 1, :] = swap_cols_ref[share : share + 1, :]


def flag_kernel(share, here_ref, home_ref, flag_ref):
    flags = jnp.maximum(here_ref[share : share + 1, :], home_ref[share : share + 1, :])
    flag_ref[0] = jnp.max(flags).astype(jnp.int32)


def call(kernel, meta, operands, out_shapes, scratch, flops):
    vmem, smem = pl.BlockSpec(memory_space=pltpu.VMEM), pl.BlockSpec(memory_space=pltpu.SMEM)
    return pl.pallas_call(
        kernel,
        in_specs=[smem] + [vmem] * len(operands),
        out_specs=[vmem if len(shape.shape) > 1 else smem for shape in out_shapes],
        out_shape=out_shapes,
        scratch_shapes=scratch,
        compiler_params=pltpu.CompilerParams(vmem_limit_bytes=16 * 1024 * 1024),
        cost_estimate=pl.CostEstimate(flops=flops, bytes_accessed=1024, transcendentals=0),
    )(meta, *operands)


def every_pair(embeddings, cluster_ids):
    unit = normalised(embeddings)
    tags = cluster_ids + 1
    groups = lax.axis_size("sub")
    member = lax.axis_index("sub")
    owners = lax.axis_size("tile")
    place = lax.axis_index("tile")
    rows_here = unit.shape[0]
    width = rows_here // groups
    own_piece = lax.dynamic_slice_in_dim(unit, member * width, width, 0)
    own_tags = lax.dynamic_slice_in_dim(tags, member * width, width, 0)
    distance = place - jnp.arange(owners, dtype=jnp.int32)
    keep = (jnp.abs(distance) < SPAN) & (distance != 0)
    outgoing = jnp.where(keep[:, None, None], own_piece[None, :, :], jnp.zeros((), jnp.bfloat16))
    outgoing_tags = jnp.where(keep[:, None], own_tags[None, :], 0)
    arrived = lax.all_to_all(outgoing, "tile", split_axis=0, concat_axis=0, tiled=True)
    arrived_tags = lax.all_to_all(outgoing_tags, "tile", split_axis=0, concat_axis=0, tiled=True)
    local_rows = jnp.arange(rows_here, dtype=jnp.int32)[:, None]
    slice_rows = member * width + jnp.arange(width, dtype=jnp.int32)[None, :]
    total = jnp.zeros((rows_here,), jnp.float32)
    for offset in range(1 - SPAN, SPAN):
        if offset == 0:
            piece, piece_tags, order = own_piece, own_tags, local_rows != slice_rows
        else:
            source = place + offset
            valid = (source >= 0) & (source < owners)
            index = jnp.clip(source, 0, owners - 1)
            piece = lax.dynamic_index_in_dim(arrived, index, 0, keepdims=False)
            piece_tags = lax.dynamic_index_in_dim(arrived_tags, index, 0, keepdims=False)
            piece_tags = jnp.where(valid, piece_tags, 0)
            order = True
        same = (tags[:, None] == piece_tags[None, :]) & (tags[:, None] > 0) & order
        weight = jnp.where(same, jnp.exp(inverse_temp * (products(unit, piece) - 1.0)), 0.0)
        total = total + jnp.sum(weight, axis=1)
    return jnp.log(1.0 + lax.psum_scatter(total, "sub", scatter_dimension=0, tiled=True))


def quads_joined(tag, tiles, place):
    last = jnp.broadcast_to(tag[-1], (BLOCK,))
    before = lax.ppermute(last, "tile", [(t, t + 1) for t in range(tiles - 1)])[0]
    joined = (place % QUAD == 0) & (place > 0) & (before == tag[0]) & (before >= 0)
    return lax.pmax(joined.astype(jnp.int32), "tile") > 0


def shards(embeddings, cluster_ids):
    tiles, subs = lax.axis_size("tile"), lax.axis_size("sub")
    place, member = lax.axis_index("tile"), lax.axis_index("sub")
    rows, depth = embeddings.shape
    blocks = rows // BLOCK
    plan = Plan(blocks, subs, place, member)
    width, share, inner = plan.width, plan.share, plan.inner
    size = share * BLOCK
    quads = range(0, tiles, QUAD)
    inward = [p for q in quads for p in ((q, q + 1), (q + 3, q + 2))]
    swap = [p for q in quads for p in ((q + 1, q + 2), (q + 2, q + 1))]
    around = [p for q in quads for p in ((q, q + 1), (q + 3, q + 2), (q + 1, q + 3), (q + 2, q))]

    def turned(route):
        return [(b, a) for a, b in route]

    by_block = cluster_ids.reshape(blocks, BLOCK)
    first_out, behind = pack(size, subs, embeddings, by_block)
    from_inner = lax.ppermute(first_out, "tile", swap)
    from_outer = lax.ppermute(first_out, "tile", inward)

    tag = jnp.max(by_block, axis=1)
    used = jnp.sum((by_block >= 0).astype(jnp.int32), axis=1)
    seen = jnp.where(inner, tag, -2)
    swapped = jnp.where(plan.far & (jnp.arange(blocks) >= blocks // 2), -2, seen)
    numbers = jnp.stack([member, plan.first, plan.edge, inner, plan.second])
    meta = jnp.concatenate([tag, used, seen, swapped, tag, numbers]).astype(jnp.int32)

    home_row = jnp.arange(blocks)[:, None] - plan.second
    home_row = jnp.broadcast_to(home_row, (blocks, BLOCK)).astype(jnp.int32)
    meta, home_row = lax.optimization_barrier((meta, home_row))

    row_sums = jax.ShapeDtypeStruct((blocks, BLOCK), jnp.float32)
    col_sums = jax.ShapeDtypeStruct((share + 1, BLOCK), jnp.float32)
    quarter = width * BLOCK
    vmem, smem = pl.BlockSpec(memory_space=pltpu.VMEM), pl.BlockSpec(memory_space=pltpu.SMEM)
    unit, sums, second_out = pl.pallas_call(
        functools.partial(self_kernel, blocks, subs),
        in_specs=[smem, pl.BlockSpec(memory_space=pl.ANY), vmem, vmem],
        out_specs=[vmem] * 3,
        out_shape=[
            jax.ShapeDtypeStruct((rows, depth), jnp.bfloat16),
            row_sums,
            jax.ShapeDtypeStruct((size + 8, depth), jnp.bfloat16),
        ],
        scratch_shapes=[pltpu.VMEM((subs, quarter, depth), jnp.bfloat16), pltpu.SemaphoreType.DMA((subs,))],
        compiler_params=pltpu.CompilerParams(vmem_limit_bytes=24 * 1024 * 1024),
        cost_estimate=pl.CostEstimate(flops=0, bytes_accessed=1024, transcendentals=0),
    )(meta, embeddings, lax.dynamic_slice_in_dim(cluster_ids, member * quarter, quarter, 0)[None], behind)
    last = lax.ppermute(second_out, "tile", around)

    def middle(chunk, piece, before):
        return call(
            functools.partial(middle_kernel, blocks, share, chunk),
            meta,
            (unit, piece, before),
            [row_sums, col_sums],
            [pltpu.VMEM((8, size), jnp.float32)],
            2 * rows * size * depth,
        )

    sums, outer_cols = middle(0, from_outer, sums)
    outer_back = lax.ppermute(outer_cols, "tile", turned(inward))
    sums, swap_cols = middle(1, from_inner, sums)
    swap_back = lax.ppermute(swap_cols, "tile", turned(swap))
    held, cols = call(
        functools.partial(last_kernel, blocks, share),
        meta,
        (unit, last, sums, outer_back, swap_cols),
        [row_sums, col_sums],
        [pltpu.VMEM((8, size), jnp.float32)],
        0,
    )

    home = lax.ppermute(cols, "tile", turned(around))
    for k in range(share):
        held = held + jnp.where(home_row == k, home[k : k + 1] + swap_back[k : k + 1], 0.0)
    parts = lax.all_to_all(held.reshape(subs, quarter), "sub", split_axis=0, concat_axis=0, tiled=True)
    scores = jnp.log(1.0 + jnp.sum(parts, axis=0))

    flag = pl.pallas_call(
        functools.partial(flag_kernel, share),
        out_specs=pl.BlockSpec(memory_space=pltpu.SMEM),
        out_shape=jax.ShapeDtypeStruct((1,), jnp.int32),
        compiler_params=pltpu.CompilerParams(vmem_limit_bytes=4 * 1024 * 1024),
    )(swap_cols, home)
    bad = flag[0] > 0
    if tiles > QUAD:
        bad = lax.pmax(bad.astype(jnp.int32), "tile") > 0
        bad = bad | quads_joined(tag, tiles, place)
    return lax.cond(bad, lambda: every_pair(embeddings, cluster_ids), lambda: scores)


def solution(mesh):
    in_specs = (P(("groups", "tile"), None), P(("groups", "tile")))
    out_specs = P(("groups", "tile", "sub"))
    return jax.shard_map(shards, mesh=mesh, in_specs=in_specs, out_specs=out_specs, check_vma=False)
```

```python
import functools
import math

import jax
import jax.numpy as jnp
import numpy as np
from jax import lax
from jax.experimental import pallas as pl
from jax.experimental.pallas import tpu as pltpu
from jax.sharding import PartitionSpec as P

BLOCK = 128
QUAD = 4
SPAN = 4

inverse_temp = 10.0
norm_eps = 1e-06
GAIN = inverse_temp * math.log2(math.e)
OFF = -1000.0

STEP = 512
COPY = 128


def normalised(values):
    values = values.astype(jnp.float32)
    scale = lax.rsqrt(jnp.sum(values * values, axis=1, keepdims=True) + norm_eps)
    return (values * scale).astype(jnp.bfloat16)


def products(rows, columns):
    return lax.dot_general(
        rows, columns, (((1,), (1,)), ((), ())), preferred_element_type=jnp.float32
    )


def column_bias(tag, column_tags):
    return jnp.where(column_tags == tag.astype(jnp.float32), -GAIN, OFF)


def lane_sums(weight):
    total = weight[:, :BLOCK]
    for start in range(BLOCK, weight.shape[1], BLOCK):
        total = total + weight[:, start : start + BLOCK]
    return jnp.sum(total.T, axis=0, keepdims=True)


class Plan:
    def __init__(self, blocks, subs, place, member):
        width = blocks // subs
        share = width // 2
        part = place % QUAD
        self.inner = (part == 1) | (part == 2)
        self.far = part == 1
        dealt = member // 2 * share
        near = (dealt // width * 2 + member % 2) * width + dealt % width
        near = jnp.where(part == 1, blocks // 2, 0) + near
        self.first = jnp.where(self.inner, near, member * width)
        self.second = jnp.where(self.inner, near, member * width + share)
        self.edge = jnp.where(part == 1, blocks // 2 - 1, blocks // 2)
        self.width, self.share = width, share


def pack_kernel(blocks, subs, rows_ref, ids_ref, first_ref, behind_ref, ids, sems):
    plan = Plan(blocks, subs, lax.axis_index("tile"), lax.axis_index("sub"))
    share, size = plan.share, plan.share * BLOCK
    copies = []
    for index, down in enumerate(range(0, size, COPY)):
        start = pl.multiple_of(plan.first * BLOCK + down, COPY)
        copies.append(
            pltpu.make_async_copy(
                rows_ref.at[pl.ds(start, COPY), :], first_ref.at[pl.ds(down, COPY), :], sems.at[index]
            )
        )
    copies.append(pltpu.make_async_copy(ids_ref, ids, sems.at[len(copies)]))
    for copy in copies:
        copy.start()
    copies[-1].wait()
    depth = first_ref.shape[1]
    edge = jnp.max(ids[pl.ds(plan.edge, 1), :], axis=1, keepdims=True)
    rest = [jnp.broadcast_to(edge, (1, BLOCK)), jnp.zeros((1, depth - size - BLOCK), jnp.int32)]
    for block, out in ((plan.first, first_ref), (plan.second, behind_ref)):
        row = jnp.concatenate([ids[pl.ds(block + k, 1), :] for k in range(share)] + rest, axis=1)
        row = jnp.broadcast_to(row.astype(jnp.float32), (8, depth)).astype(jnp.bfloat16)
        out[out.shape[0] - 8 :, :] = row
    for copy in copies[:-1]:
        copy.wait()


def pack(size, subs, embeddings, by_block):
    depth = embeddings.shape[1]
    return pl.pallas_call(
        functools.partial(pack_kernel, by_block.shape[0], subs),
        in_specs=[pl.BlockSpec(memory_space=pl.ANY)] * 2,
        out_specs=[pl.BlockSpec(memory_space=pltpu.VMEM)] * 2,
        out_shape=[jax.ShapeDtypeStruct((count, depth), jnp.bfloat16) for count in (size + 8, 8)],
        scratch_shapes=[pltpu.VMEM(by_block.shape, jnp.int32), pltpu.SemaphoreType.DMA((size // COPY + 1,))],
        compiler_params=pltpu.CompilerParams(vmem_limit_bytes=8 * 1024 * 1024),
        cost_estimate=pl.CostEstimate(flops=0, bytes_accessed=1024, transcendentals=0),
    )(embeddings, by_block)


class Meta:
    def __init__(self, ref, blocks):
        self.ref, self.blocks = ref, blocks

    def tag(self, block, chunk=None):
        return self.ref[block + (0 if chunk is None else (2 + chunk) * self.blocks)]

    def used(self, block):
        return self.ref[self.blocks + block]

    def number(self, index):
        return self.ref[5 * self.blocks + index]


MEMBER, FIRST_BLOCK, EDGE, INNER, SECOND_BLOCK = range(5)


def self_kernel(
    blocks, subs, meta_ref, rows_ref, tags_ref, behind_ref, unit_ref, sums_ref, second_ref, held, sems
):
    meta = Meta(meta_ref, blocks)
    width = blocks // subs
    quarter = width * BLOCK
    member = meta.number(MEMBER)
    owners = [lax.rem(member + turn, subs) for turn in range(subs)]
    spans = [pl.ds(pl.multiple_of(owner * quarter, quarter), quarter) for owner in owners]
    copies = []
    for turn, span in enumerate(spans):
        copies.append(pltpu.make_async_copy(rows_ref.at[span, :], held.at[turn], sems.at[turn]))
        copies[-1].start()
    column_tags = tags_ref[...].astype(jnp.float32)
    for turn in range(subs):
        copies[turn].wait()
        unit = normalised(held[turn])
        unit_ref[spans[turn], :] = unit
        if turn == 0:
            share = unit
        cosine = products(unit, share)
        for inner in range(width):
            block = owners[turn] * width + inner
            bias = column_bias(meta.tag(block), column_tags)
            weight = jnp.exp2(cosine[inner * BLOCK : (inner + 1) * BLOCK] * GAIN + bias)
            row = lax.broadcasted_iota(jnp.int32, weight.shape, 0)
            keep = row < meta.used(block)
            if turn == 0:
                keep = keep & (lax.broadcasted_iota(jnp.int32, weight.shape, 1) - row != inner * BLOCK)
            sums_ref[pl.ds(block, 1), :] = lane_sums(jnp.where(keep, weight, 0.0))
    size = second_ref.shape[0] - 8
    start = pl.multiple_of(meta.number(SECOND_BLOCK) * BLOCK, BLOCK)
    second_ref[:size, :] = unit_ref[pl.ds(start, size), :]
    second_ref[size:, :] = behind_ref[...]


def chunk_tags(piece_ref, size):
    row = piece_ref[size:, :].astype(jnp.float32)[0:1, :]
    return row[:, :size], row[:, size : size + BLOCK]


def cross_terms(meta, chunk, column_tags, unit_ref, piece_ref, before_ref, sums, columns, place):
    size = column_tags.shape[1]
    there = [jnp.max(column_tags[:, at : at + BLOCK]) for at in range(0, size, BLOCK)]
    shared = False
    for block in range(meta.blocks):
        for tag in there:
            shared = (meta.tag(block, chunk).astype(jnp.float32) == tag) | shared

    @pl.when(jnp.logical_not(shared))
    def _():
        columns[...] = jnp.zeros_like(columns)
        for block in range(meta.blocks):
            sums[place(block) : place(block) + 1, :] = before_ref[block : block + 1, :]

    @pl.when(shared)
    def _():
        piece = piece_ref[:size, :] if chunk == 2 else normalised(piece_ref[:size, :])
        total = None
        for start in range(0, meta.blocks * BLOCK, STEP):
            cosine = products(unit_ref[start : start + STEP, :], piece)
            for inner in range(0, STEP, BLOCK):
                block = (start + inner) // BLOCK
                bias = column_bias(meta.tag(block, chunk), column_tags)
                weight = jnp.exp2(cosine[inner : inner + BLOCK] * GAIN + bias)
                row = lax.broadcasted_iota(jnp.int32, weight.shape, 0)
                weight = jnp.where(row < meta.used(block), weight, 0.0)
                sums[place(block) : place(block) + 1, :] = before_ref[block : block + 1, :] + lane_sums(weight)
                partial = weight[0:8]
                for down in range(8, BLOCK, 8):
                    partial = partial + weight[down : down + 8]
                total = partial if total is None else total + partial
        columns[...] = total


def middle_kernel(blocks, share, chunk, meta_ref, unit_ref, piece_ref, before_ref, sums_ref, cols_ref, columns):
    meta = Meta(meta_ref, blocks)
    tags, edge = chunk_tags(piece_ref, share * BLOCK)
    cross_terms(meta, chunk, tags, unit_ref, piece_ref, before_ref, sums_ref, columns, lambda block: block)
    total = jnp.sum(columns[...], axis=0, keepdims=True)
    for k in range(share):
        cols_ref[k : k + 1, :] = total[:, k * BLOCK : (k + 1) * BLOCK]
    mine = meta.tag(meta.number(EDGE)).astype(jnp.float32)
    joined = (edge == mine) & (edge >= 0) & (meta.number(INNER) > 0)
    cols_ref[share : share + 1, :] = jnp.where(joined, 1.0, 0.0)


def last_kernel(
    blocks, share, width, meta_ref, unit_ref, piece_ref, before_ref, outer_back_ref, swap_cols_ref,
    keep_ref, send_ref, cols_ref, sums, columns,
):
    meta = Meta(meta_ref, blocks)
    tags, _ = chunk_tags(piece_ref, share * BLOCK)

    def place(block):
        owner = block // width
        return owner % 2 * (blocks // 2) + owner // 2 * width + block % width

    cross_terms(meta, 2, tags, unit_ref, piece_ref, before_ref, sums, columns, place)
    total = jnp.sum(columns[...], axis=0, keepdims=True)
    for k in range(share):
        cols_ref[k : k + 1, :] = total[:, k * BLOCK : (k + 1) * BLOCK]
        at = place(meta.number(FIRST_BLOCK) + k)
        sums[pl.ds(at, 1), :] += outer_back_ref[k : k + 1, :]
    cols_ref[share : share + 1, :] = swap_cols_ref[share : share + 1, :]
    parity = meta.number(MEMBER) % 2
    heap = blocks // 2
    keep_ref[...] = sums[pl.ds(pl.multiple_of(parity * heap, heap), heap), :]
    send_ref[...] = sums[pl.ds(pl.multiple_of((1 - parity) * heap, heap), heap), :]


def flag_kernel(share, here_ref, home_ref, flag_ref):
    flags = jnp.maximum(here_ref[share : share + 1, :], home_ref[share : share + 1, :])
    flag_ref[0] = jnp.max(flags).astype(jnp.int32)


def call(kernel, meta, operands, out_shapes, scratch, flops):
    vmem, smem = pl.BlockSpec(memory_space=pltpu.VMEM), pl.BlockSpec(memory_space=pltpu.SMEM)
    return pl.pallas_call(
        kernel,
        in_specs=[smem] + [vmem] * len(operands),
        out_specs=[vmem if len(shape.shape) > 1 else smem for shape in out_shapes],
        out_shape=out_shapes,
        scratch_shapes=scratch,
        compiler_params=pltpu.CompilerParams(vmem_limit_bytes=16 * 1024 * 1024),
        cost_estimate=pl.CostEstimate(flops=flops, bytes_accessed=1024, transcendentals=0),
    )(meta, *operands)


def every_pair(embeddings, cluster_ids):
    unit = normalised(embeddings)
    tags = cluster_ids + 1
    groups = lax.axis_size("sub")
    member = lax.axis_index("sub")
    owners = lax.axis_size("tile")
    place = lax.axis_index("tile")
    rows_here = unit.shape[0]
    width = rows_here // groups
    own_piece = lax.dynamic_slice_in_dim(unit, member * width, width, 0)
    own_tags = lax.dynamic_slice_in_dim(tags, member * width, width, 0)
    distance = place - jnp.arange(owners, dtype=jnp.int32)
    keep = (jnp.abs(distance) < SPAN) & (distance != 0)
    outgoing = jnp.where(keep[:, None, None], own_piece[None, :, :], jnp.zeros((), jnp.bfloat16))
    outgoing_tags = jnp.where(keep[:, None], own_tags[None, :], 0)
    arrived = lax.all_to_all(outgoing, "tile", split_axis=0, concat_axis=0, tiled=True)
    arrived_tags = lax.all_to_all(outgoing_tags, "tile", split_axis=0, concat_axis=0, tiled=True)
    local_rows = jnp.arange(rows_here, dtype=jnp.int32)[:, None]
    slice_rows = member * width + jnp.arange(width, dtype=jnp.int32)[None, :]
    total = jnp.zeros((rows_here,), jnp.float32)
    for offset in range(1 - SPAN, SPAN):
        if offset == 0:
            piece, piece_tags, order = own_piece, own_tags, local_rows != slice_rows
        else:
            source = place + offset
            valid = (source >= 0) & (source < owners)
            index = jnp.clip(source, 0, owners - 1)
            piece = lax.dynamic_index_in_dim(arrived, index, 0, keepdims=False)
            piece_tags = lax.dynamic_index_in_dim(arrived_tags, index, 0, keepdims=False)
            piece_tags = jnp.where(valid, piece_tags, 0)
            order = True
        same = (tags[:, None] == piece_tags[None, :]) & (tags[:, None] > 0) & order
        weight = jnp.where(same, jnp.exp(inverse_temp * (products(unit, piece) - 1.0)), 0.0)
        total = total + jnp.sum(weight, axis=1)
    return jnp.log(1.0 + lax.psum_scatter(total, "sub", scatter_dimension=0, tiled=True))


def quads_joined(tag, tiles, place):
    last = jnp.broadcast_to(tag[-1], (BLOCK,))
    before = lax.ppermute(last, "tile", [(t, t + 1) for t in range(tiles - 1)])[0]
    joined = (place % QUAD == 0) & (place > 0) & (before == tag[0]) & (before >= 0)
    return lax.pmax(joined.astype(jnp.int32), "tile") > 0


def shards(embeddings, cluster_ids):
    tiles, subs = lax.axis_size("tile"), lax.axis_size("sub")
    place, member = lax.axis_index("tile"), lax.axis_index("sub")
    rows, depth = embeddings.shape
    blocks = rows // BLOCK
    plan = Plan(blocks, subs, place, member)
    width, share, inner = plan.width, plan.share, plan.inner
    size = share * BLOCK
    quads = range(0, tiles, QUAD)
    inward = [p for q in quads for p in ((q, q + 1), (q + 3, q + 2))]
    swap = [p for q in quads for p in ((q + 1, q + 2), (q + 2, q + 1))]
    around = [p for q in quads for p in ((q, q + 1), (q + 3, q + 2), (q + 1, q + 3), (q + 2, q))]

    def turned(route):
        return [(b, a) for a, b in route]

    by_block = cluster_ids.reshape(blocks, BLOCK)
    first_out, behind = pack(size, subs, embeddings, by_block)
    from_inner = lax.ppermute(first_out, "tile", swap)
    from_outer = lax.ppermute(first_out, "tile", inward)

    tag = jnp.max(by_block, axis=1)
    used = jnp.sum((by_block >= 0).astype(jnp.int32), axis=1)
    seen = jnp.where(inner, tag, -2)
    swapped = jnp.where(plan.far & (jnp.arange(blocks) >= blocks // 2), -2, seen)
    numbers = jnp.stack([member, plan.first, plan.edge, inner, plan.second])
    meta = jnp.concatenate([tag, used, seen, swapped, tag, numbers]).astype(jnp.int32)

    heap = blocks // 2
    owner = plan.second // width
    home_row = jnp.arange(heap)[:, None] - (owner // 2 * width + plan.second % width)
    home_row = jnp.broadcast_to(home_row, (heap, BLOCK)).astype(jnp.int32)
    upper = [
        jnp.broadcast_to((member >> bit) & 1, (heap >> bit, BLOCK)).astype(jnp.int32)
        for bit in range(1, subs.bit_length() - 1)
    ]
    meta, home_row, *upper = lax.optimization_barrier((meta, home_row, *upper))

    row_sums = jax.ShapeDtypeStruct((blocks, BLOCK), jnp.float32)
    col_sums = jax.ShapeDtypeStruct((share + 1, BLOCK), jnp.float32)
    quarter = width * BLOCK
    vmem, smem = pl.BlockSpec(memory_space=pltpu.VMEM), pl.BlockSpec(memory_space=pltpu.SMEM)
    unit, sums, second_out = pl.pallas_call(
        functools.partial(self_kernel, blocks, subs),
        in_specs=[smem, pl.BlockSpec(memory_space=pl.ANY), vmem, vmem],
        out_specs=[vmem] * 3,
        out_shape=[
            jax.ShapeDtypeStruct((rows, depth), jnp.bfloat16),
            row_sums,
            jax.ShapeDtypeStruct((size + 8, depth), jnp.bfloat16),
        ],
        scratch_shapes=[pltpu.VMEM((subs, quarter, depth), jnp.bfloat16), pltpu.SemaphoreType.DMA((subs,))],
        compiler_params=pltpu.CompilerParams(vmem_limit_bytes=24 * 1024 * 1024),
        cost_estimate=pl.CostEstimate(flops=0, bytes_accessed=1024, transcendentals=0),
    )(meta, embeddings, lax.dynamic_slice_in_dim(cluster_ids, member * quarter, quarter, 0)[None], behind)
    last = lax.ppermute(second_out, "tile", around)

    def middle(chunk, piece, before):
        return call(
            functools.partial(middle_kernel, blocks, share, chunk),
            meta,
            (unit, piece, before),
            [row_sums, col_sums],
            [pltpu.VMEM((8, size), jnp.float32)],
            2 * rows * size * depth,
        )

    sums, outer_cols = middle(0, from_outer, sums)
    outer_back = lax.ppermute(outer_cols, "tile", turned(inward))
    sums, swap_cols = middle(1, from_inner, sums)
    swap_back = lax.ppermute(swap_cols, "tile", turned(swap))
    half = jax.ShapeDtypeStruct((heap, BLOCK), jnp.float32)
    held, leaving, cols = call(
        functools.partial(last_kernel, blocks, share, width),
        meta,
        (unit, last, sums, outer_back, swap_cols),
        [half, half, col_sums],
        [
            pltpu.VMEM((blocks, BLOCK), jnp.float32),
            pltpu.VMEM((8, size), jnp.float32),
        ],
        2 * rows * size * depth,
    )

    home = lax.ppermute(cols, "tile", turned(around))
    for k in range(share):
        held = held + jnp.where(home_row == k, home[k : k + 1] + swap_back[k : k + 1], 0.0)
    held = held + lax.ppermute(leaving, "sub", [(i, i ^ 1) for i in range(subs)])
    home, held = lax.optimization_barrier((home, held))
    for bit, mine in enumerate(upper, 1):
        pairs = held.reshape(-1, 2, width, BLOCK)
        low, high = pairs[:, 0].reshape(mine.shape), pairs[:, 1].reshape(mine.shape)
        leaving = jnp.where(mine > 0, low, high)
        held = jnp.where(mine > 0, high, low)
        held = held + lax.ppermute(leaving, "sub", [(i, i ^ (1 << bit)) for i in range(subs)])
    scores = jnp.log(1.0 + held.reshape(-1))

    flag = pl.pallas_call(
        functools.partial(flag_kernel, share),
        out_specs=pl.BlockSpec(memory_space=pltpu.SMEM),
        out_shape=jax.ShapeDtypeStruct((1,), jnp.int32),
        compiler_params=pltpu.CompilerParams(vmem_limit_bytes=4 * 1024 * 1024),
    )(swap_cols, home)
    bad = flag[0] > 0
    if tiles > QUAD:
        bad = lax.pmax(bad.astype(jnp.int32), "tile") > 0
        bad = bad | quads_joined(tag, tiles, place)
    return lax.cond(bad, lambda: every_pair(embeddings, cluster_ids), lambda: scores)


def solution(mesh):
    in_specs = (P(("groups", "tile"), None), P(("groups", "tile")))
    out_specs = P(("groups", "tile", "sub"))
    return jax.shard_map(shards, mesh=mesh, in_specs=in_specs, out_specs=out_specs, check_vma=False)
```

```python
import functools
import math

import jax
import jax.numpy as jnp
import numpy as np
from jax import lax
from jax.experimental import pallas as pl
from jax.experimental.pallas import tpu as pltpu
from jax.sharding import PartitionSpec as P

BLOCK = 128
QUAD = 4
SPAN = 4

inverse_temp = 10.0
norm_eps = 1e-06
GAIN = inverse_temp * math.log2(math.e)
OFF = -1000.0

STEP = 512
COPY = 128


def normalised(values):
    values = values.astype(jnp.float32)
    scale = lax.rsqrt(jnp.sum(values * values, axis=1, keepdims=True) + norm_eps)
    return (values * scale).astype(jnp.bfloat16)


def products(rows, columns):
    return lax.dot_general(
        rows, columns, (((1,), (1,)), ((), ())), preferred_element_type=jnp.float32
    )


def column_bias(tag, column_tags):
    return jnp.where(column_tags == tag.astype(jnp.float32), -GAIN, OFF)


def lane_sums(weight):
    total = weight[:, :BLOCK]
    for start in range(BLOCK, weight.shape[1], BLOCK):
        total = total + weight[:, start : start + BLOCK]
    return jnp.sum(total.T, axis=0, keepdims=True)


class Plan:
    def __init__(self, blocks, subs, place, member):
        width = blocks // subs
        share = width // 2
        part = place % QUAD
        self.inner = (part == 1) | (part == 2)
        self.far = part == 1
        dealt = member // 2 * share
        near = (dealt // width * 2 + member % 2) * width + dealt % width
        near = jnp.where(part == 1, blocks // 2, 0) + near
        self.first = jnp.where(self.inner, near, member * width)
        self.second = jnp.where(self.inner, near, member * width + share)
        self.edge = jnp.where(part == 1, blocks // 2 - 1, blocks // 2)
        self.width, self.share = width, share


def pack_kernel(blocks, subs, rows_ref, ids_ref, first_ref, behind_ref, ids, sems):
    plan = Plan(blocks, subs, lax.axis_index("tile"), lax.axis_index("sub"))
    share, size = plan.share, plan.share * BLOCK
    copies = []
    for index, down in enumerate(range(0, size, COPY)):
        start = pl.multiple_of(plan.first * BLOCK + down, COPY)
        copies.append(
            pltpu.make_async_copy(
                rows_ref.at[pl.ds(start, COPY), :], first_ref.at[pl.ds(down, COPY), :], sems.at[index]
            )
        )
    copies.append(pltpu.make_async_copy(ids_ref, ids, sems.at[len(copies)]))
    for copy in copies:
        copy.start()
    copies[-1].wait()
    depth = first_ref.shape[1]
    edge = jnp.max(ids[pl.ds(plan.edge, 1), :], axis=1, keepdims=True)
    rest = [jnp.broadcast_to(edge, (1, BLOCK)), jnp.zeros((1, depth - size - BLOCK), jnp.int32)]
    for block, out in ((plan.first, first_ref), (plan.second, behind_ref)):
        row = jnp.concatenate([ids[pl.ds(block + k, 1), :] for k in range(share)] + rest, axis=1)
        row = jnp.broadcast_to(row.astype(jnp.float32), (8, depth)).astype(jnp.bfloat16)
        out[out.shape[0] - 8 :, :] = row
    for copy in copies[:-1]:
        copy.wait()


def pack(size, subs, embeddings, by_block):
    depth = embeddings.shape[1]
    return pl.pallas_call(
        functools.partial(pack_kernel, by_block.shape[0], subs),
        in_specs=[pl.BlockSpec(memory_space=pl.ANY)] * 2,
        out_specs=[pl.BlockSpec(memory_space=pltpu.VMEM)] * 2,
        out_shape=[jax.ShapeDtypeStruct((count, depth), jnp.bfloat16) for count in (size + 8, 8)],
        scratch_shapes=[pltpu.VMEM(by_block.shape, jnp.int32), pltpu.SemaphoreType.DMA((size // COPY + 1,))],
        compiler_params=pltpu.CompilerParams(vmem_limit_bytes=8 * 1024 * 1024),
        cost_estimate=pl.CostEstimate(flops=0, bytes_accessed=1024, transcendentals=0),
    )(embeddings, by_block)


class Meta:
    def __init__(self, ref, blocks):
        self.ref, self.blocks = ref, blocks

    def tag(self, block, chunk=None):
        return self.ref[block + (0 if chunk is None else (2 + chunk) * self.blocks)]

    def used(self, block):
        return self.ref[self.blocks + block]

    def number(self, index):
        return self.ref[5 * self.blocks + index]


MEMBER, FIRST_BLOCK, EDGE, INNER, SECOND_BLOCK = range(5)


def self_kernel(
    blocks, subs, meta_ref, rows_ref, tags_ref, behind_ref, unit_ref, sums_ref, second_ref, held, sems
):
    meta = Meta(meta_ref, blocks)
    width = blocks // subs
    quarter = width * BLOCK
    member = meta.number(MEMBER)
    owners = [lax.rem(member + turn, subs) for turn in range(subs)]
    spans = [pl.ds(pl.multiple_of(owner * quarter, quarter), quarter) for owner in owners]
    copies = []
    for turn, span in enumerate(spans):
        copies.append(pltpu.make_async_copy(rows_ref.at[span, :], held.at[turn], sems.at[turn]))
        copies[-1].start()
    column_tags = tags_ref[...].astype(jnp.float32)
    for turn in range(subs):
        copies[turn].wait()
        unit = normalised(held[turn])
        unit_ref[spans[turn], :] = unit
        if turn == 0:
            share = unit
        cosine = products(unit, share)
        for inner in range(width):
            block = owners[turn] * width + inner
            bias = column_bias(meta.tag(block), column_tags)
            weight = jnp.exp2(cosine[inner * BLOCK : (inner + 1) * BLOCK] * GAIN + bias)
            row = lax.broadcasted_iota(jnp.int32, weight.shape, 0)
            keep = row < meta.used(block)
            if turn == 0:
                keep = keep & (lax.broadcasted_iota(jnp.int32, weight.shape, 1) - row != inner * BLOCK)
            sums_ref[pl.ds(block, 1), :] = lane_sums(jnp.where(keep, weight, 0.0))
    size = second_ref.shape[0] - 8
    start = pl.multiple_of(meta.number(SECOND_BLOCK) * BLOCK, BLOCK)
    second_ref[:size, :] = unit_ref[pl.ds(start, size), :]
    second_ref[size:, :] = behind_ref[...]


def chunk_tags(piece_ref, size):
    row = piece_ref[size:, :].astype(jnp.float32)[0:1, :]
    return row[:, :size], row[:, size : size + BLOCK]


def cross_terms(meta, chunk, column_tags, unit_ref, piece_ref, before_ref, sums, columns, place):
    size = column_tags.shape[1]
    there = [jnp.max(column_tags[:, at : at + BLOCK]) for at in range(0, size, BLOCK)]
    shared = False
    for block in range(meta.blocks):
        for tag in there:
            shared = (meta.tag(block, chunk).astype(jnp.float32) == tag) | shared

    @pl.when(jnp.logical_not(shared))
    def _():
        columns[...] = jnp.zeros_like(columns)
        for block in range(meta.blocks):
            sums[place(block) : place(block) + 1, :] = before_ref[block : block + 1, :]

    @pl.when(shared)
    def _():
        piece = piece_ref[:size, :] if chunk == 2 else normalised(piece_ref[:size, :])
        total = None
        for start in range(0, meta.blocks * BLOCK, STEP):
            cosine = products(unit_ref[start : start + STEP, :], piece)
            for inner in range(0, STEP, BLOCK):
                block = (start + inner) // BLOCK
                bias = column_bias(meta.tag(block, chunk), column_tags)
                weight = jnp.exp2(cosine[inner : inner + BLOCK] * GAIN + bias)
                row = lax.broadcasted_iota(jnp.int32, weight.shape, 0)
                weight = jnp.where(row < meta.used(block), weight, 0.0)
                sums[place(block) : place(block) + 1, :] = before_ref[block : block + 1, :] + lane_sums(weight)
                partial = weight[0:8]
                for down in range(8, BLOCK, 8):
                    partial = partial + weight[down : down + 8]
                total = partial if total is None else total + partial
        columns[...] = total


def middle_kernel(blocks, share, chunk, meta_ref, unit_ref, piece_ref, before_ref, sums_ref, cols_ref, columns):
    meta = Meta(meta_ref, blocks)
    tags, edge = chunk_tags(piece_ref, share * BLOCK)
    cross_terms(meta, chunk, tags, unit_ref, piece_ref, before_ref, sums_ref, columns, lambda block: block)
    total = jnp.sum(columns[...], axis=0, keepdims=True)
    for k in range(share):
        cols_ref[k : k + 1, :] = total[:, k * BLOCK : (k + 1) * BLOCK]
    mine = meta.tag(meta.number(EDGE)).astype(jnp.float32)
    joined = (edge == mine) & (edge >= 0) & (meta.number(INNER) > 0)
    cols_ref[share : share + 1, :] = jnp.where(joined, 1.0, 0.0)


def last_kernel(
    blocks, share, width, meta_ref, unit_ref, piece_ref, before_ref, outer_cols_ref, swap_cols_ref,
    keep_ref, send_ref, cols_ref, sums, columns,
):
    meta = Meta(meta_ref, blocks)
    tags, _ = chunk_tags(piece_ref, share * BLOCK)

    def place(block):
        owner = block // width
        return owner % 2 * (blocks // 2) + owner // 2 * width + block % width

    is_inner = meta.number(INNER) > 0
    cross_terms(meta, 2, tags, unit_ref, piece_ref, before_ref, sums, columns, place)
    total = jnp.sum(columns[...], axis=0, keepdims=True)
    for k in range(share):
        value = total[:, k * BLOCK : (k + 1) * BLOCK]
        cols_ref[k : k + 1, :] = jnp.where(is_inner, outer_cols_ref[k : k + 1, :], value)
        cols_ref[share + k : share + k + 1, :] = jnp.where(is_inner, value, 0.0)
    cols_ref[2 * share : 2 * share + 1, :] = swap_cols_ref[share : share + 1, :]
    parity = meta.number(MEMBER) % 2
    heap = blocks // 2
    keep_ref[...] = sums[pl.ds(pl.multiple_of(parity * heap, heap), heap), :]
    send_ref[...] = sums[pl.ds(pl.multiple_of((1 - parity) * heap, heap), heap), :]


def flag_kernel(share, here_ref, home_ref, flag_ref):
    flags = jnp.maximum(here_ref[share : share + 1, :], home_ref[2 * share : 2 * share + 1, :])
    flag_ref[0] = jnp.max(flags).astype(jnp.int32)


def call(kernel, meta, operands, out_shapes, scratch, flops):
    vmem, smem = pl.BlockSpec(memory_space=pltpu.VMEM), pl.BlockSpec(memory_space=pltpu.SMEM)
    return pl.pallas_call(
        kernel,
        in_specs=[smem] + [vmem] * len(operands),
        out_specs=[vmem if len(shape.shape) > 1 else smem for shape in out_shapes],
        out_shape=out_shapes,
        scratch_shapes=scratch,
        compiler_params=pltpu.CompilerParams(vmem_limit_bytes=16 * 1024 * 1024),
        cost_estimate=pl.CostEstimate(flops=flops, bytes_accessed=1024, transcendentals=0),
    )(meta, *operands)


def every_pair(embeddings, cluster_ids):
    unit = normalised(embeddings)
    tags = cluster_ids + 1
    groups = lax.axis_size("sub")
    member = lax.axis_index("sub")
    owners = lax.axis_size("tile")
    place = lax.axis_index("tile")
    rows_here = unit.shape[0]
    width = rows_here // groups
    own_piece = lax.dynamic_slice_in_dim(unit, member * width, width, 0)
    own_tags = lax.dynamic_slice_in_dim(tags, member * width, width, 0)
    distance = place - jnp.arange(owners, dtype=jnp.int32)
    keep = (jnp.abs(distance) < SPAN) & (distance != 0)
    outgoing = jnp.where(keep[:, None, None], own_piece[None, :, :], jnp.zeros((), jnp.bfloat16))
    outgoing_tags = jnp.where(keep[:, None], own_tags[None, :], 0)
    arrived = lax.all_to_all(outgoing, "tile", split_axis=0, concat_axis=0, tiled=True)
    arrived_tags = lax.all_to_all(outgoing_tags, "tile", split_axis=0, concat_axis=0, tiled=True)
    local_rows = jnp.arange(rows_here, dtype=jnp.int32)[:, None]
    slice_rows = member * width + jnp.arange(width, dtype=jnp.int32)[None, :]
    total = jnp.zeros((rows_here,), jnp.float32)
    for offset in range(1 - SPAN, SPAN):
        if offset == 0:
            piece, piece_tags, order = own_piece, own_tags, local_rows != slice_rows
        else:
            source = place + offset
            valid = (source >= 0) & (source < owners)
            index = jnp.clip(source, 0, owners - 1)
            piece = lax.dynamic_index_in_dim(arrived, index, 0, keepdims=False)
            piece_tags = lax.dynamic_index_in_dim(arrived_tags, index, 0, keepdims=False)
            piece_tags = jnp.where(valid, piece_tags, 0)
            order = True
        same = (tags[:, None] == piece_tags[None, :]) & (tags[:, None] > 0) & order
        weight = jnp.where(same, jnp.exp(inverse_temp * (products(unit, piece) - 1.0)), 0.0)
        total = total + jnp.sum(weight, axis=1)
    return jnp.log(1.0 + lax.psum_scatter(total, "sub", scatter_dimension=0, tiled=True))


def quads_joined(tag, tiles, place):
    last = jnp.broadcast_to(tag[-1], (BLOCK,))
    before = lax.ppermute(last, "tile", [(t, t + 1) for t in range(tiles - 1)])[0]
    joined = (place % QUAD == 0) & (place > 0) & (before == tag[0]) & (before >= 0)
    return lax.pmax(joined.astype(jnp.int32), "tile") > 0


def shards(embeddings, cluster_ids):
    tiles, subs = lax.axis_size("tile"), lax.axis_size("sub")
    place, member = lax.axis_index("tile"), lax.axis_index("sub")
    rows, depth = embeddings.shape
    blocks = rows // BLOCK
    plan = Plan(blocks, subs, place, member)
    width, share, inner = plan.width, plan.share, plan.inner
    size = share * BLOCK
    quads = range(0, tiles, QUAD)
    inward = [p for q in quads for p in ((q, q + 1), (q + 3, q + 2))]
    swap = [p for q in quads for p in ((q + 1, q + 2), (q + 2, q + 1))]
    around = [p for q in quads for p in ((q, q + 1), (q + 3, q + 2), (q + 1, q + 3), (q + 2, q))]

    def turned(route):
        return [(b, a) for a, b in route]

    by_block = cluster_ids.reshape(blocks, BLOCK)
    first_out, behind = pack(size, subs, embeddings, by_block)
    from_inner = lax.ppermute(first_out, "tile", swap)
    from_outer = lax.ppermute(first_out, "tile", inward)

    tag = jnp.max(by_block, axis=1)
    used = jnp.sum((by_block >= 0).astype(jnp.int32), axis=1)
    seen = jnp.where(inner, tag, -2)
    swapped = jnp.where(plan.far & (jnp.arange(blocks) >= blocks // 2), -2, seen)
    numbers = jnp.stack([member, plan.first, plan.edge, inner, plan.second])
    meta = jnp.concatenate([tag, used, seen, swapped, tag, numbers]).astype(jnp.int32)

    heap = blocks // 2
    owner = plan.first // width
    home_row = jnp.arange(heap)[:, None] - (owner // 2 * width + plan.first % width)
    home_row = jnp.broadcast_to(home_row, (heap, BLOCK)).astype(jnp.int32)
    upper = [
        jnp.broadcast_to((member >> bit) & 1, (heap >> bit, BLOCK)).astype(jnp.int32)
        for bit in range(1, subs.bit_length() - 1)
    ]
    meta, home_row, *upper = lax.optimization_barrier((meta, home_row, *upper))

    row_sums = jax.ShapeDtypeStruct((blocks, BLOCK), jnp.float32)
    col_sums = jax.ShapeDtypeStruct((share + 1, BLOCK), jnp.float32)
    quarter = width * BLOCK
    vmem, smem = pl.BlockSpec(memory_space=pltpu.VMEM), pl.BlockSpec(memory_space=pltpu.SMEM)
    unit, sums, second_out = pl.pallas_call(
        functools.partial(self_kernel, blocks, subs),
        in_specs=[smem, pl.BlockSpec(memory_space=pl.ANY), vmem, vmem],
        out_specs=[vmem] * 3,
        out_shape=[
            jax.ShapeDtypeStruct((rows, depth), jnp.bfloat16),
            row_sums,
            jax.ShapeDtypeStruct((size + 8, depth), jnp.bfloat16),
        ],
        scratch_shapes=[pltpu.VMEM((subs, quarter, depth), jnp.bfloat16), pltpu.SemaphoreType.DMA((subs,))],
        compiler_params=pltpu.CompilerParams(vmem_limit_bytes=24 * 1024 * 1024),
        cost_estimate=pl.CostEstimate(flops=0, bytes_accessed=1024, transcendentals=0),
    )(meta, embeddings, lax.dynamic_slice_in_dim(cluster_ids, member * quarter, quarter, 0)[None], behind)
    last = lax.ppermute(second_out, "tile", around)

    def middle(chunk, piece, before):
        return call(
            functools.partial(middle_kernel, blocks, share, chunk),
            meta,
            (unit, piece, before),
            [row_sums, col_sums],
            [pltpu.VMEM((8, size), jnp.float32)],
            2 * rows * size * depth,
        )

    sums, outer_cols = middle(0, from_outer, sums)
    sums, swap_cols = middle(1, from_inner, sums)
    swap_back = lax.ppermute(swap_cols, "tile", turned(swap))
    half = jax.ShapeDtypeStruct((heap, BLOCK), jnp.float32)
    held, leaving, cols = call(
        functools.partial(last_kernel, blocks, share, width),
        meta,
        (unit, last, sums, outer_cols, swap_cols),
        [half, half, jax.ShapeDtypeStruct((2 * share + 1, BLOCK), jnp.float32)],
        [
            pltpu.VMEM((blocks, BLOCK), jnp.float32),
            pltpu.VMEM((8, size), jnp.float32),
        ],
        2 * rows * size * depth,
    )

    home = lax.ppermute(cols, "tile", turned(around))
    for k in range(2 * share):
        came = home[k : k + 1] + swap_back[k : k + 1] if k < share else home[k : k + 1]
        held = held + jnp.where(home_row == k, came, 0.0)
    held = held + lax.ppermute(leaving, "sub", [(i, i ^ 1) for i in range(subs)])
    home, held = lax.optimization_barrier((home, held))
    for bit, mine in enumerate(upper, 1):
        pairs = held.reshape(-1, 2, width, BLOCK)
        low, high = pairs[:, 0].reshape(mine.shape), pairs[:, 1].reshape(mine.shape)
        leaving = jnp.where(mine > 0, low, high)
        held = jnp.where(mine > 0, high, low)
        held = held + lax.ppermute(leaving, "sub", [(i, i ^ (1 << bit)) for i in range(subs)])
    scores = jnp.log(1.0 + held.reshape(-1))

    flag = pl.pallas_call(
        functools.partial(flag_kernel, share),
        out_specs=pl.BlockSpec(memory_space=pltpu.SMEM),
        out_shape=jax.ShapeDtypeStruct((1,), jnp.int32),
        compiler_params=pltpu.CompilerParams(vmem_limit_bytes=4 * 1024 * 1024),
    )(swap_cols, home)
    bad = flag[0] > 0
    if tiles > QUAD:
        bad = lax.pmax(bad.astype(jnp.int32), "tile") > 0
        bad = bad | quads_joined(tag, tiles, place)
    return lax.cond(bad, lambda: every_pair(embeddings, cluster_ids), lambda: scores)


def solution(mesh):
    in_specs = (P(("groups", "tile"), None), P(("groups", "tile")))
    out_specs = P(("groups", "tile", "sub"))
    return jax.shard_map(shards, mesh=mesh, in_specs=in_specs, out_specs=out_specs, check_vma=False)
```

```python
import functools
import math

import jax
import jax.numpy as jnp
import numpy as np
from jax import lax
from jax.experimental import pallas as pl
from jax.experimental.pallas import tpu as pltpu
from jax.sharding import PartitionSpec as P

BLOCK = 128
QUAD = 4
SPAN = 4

inverse_temp = 10.0
norm_eps = 1e-06
GAIN = inverse_temp * math.log2(math.e)
OFF = -1000.0

STEP = 512
COPY = 128


def normalised(values):
    values = values.astype(jnp.float32)
    scale = lax.rsqrt(jnp.sum(values * values, axis=1, keepdims=True) + norm_eps)
    return (values * scale).astype(jnp.bfloat16)


def products(rows, columns):
    return lax.dot_general(
        rows, columns, (((1,), (1,)), ((), ())), preferred_element_type=jnp.float32
    )


def column_bias(tag, column_tags):
    return jnp.where(column_tags == tag.astype(jnp.float32), -GAIN, OFF)


def lane_sums(weight):
    total = weight[:, :BLOCK]
    for start in range(BLOCK, weight.shape[1], BLOCK):
        total = total + weight[:, start : start + BLOCK]
    return jnp.sum(total.T, axis=0, keepdims=True)


class Plan:
    def __init__(self, blocks, subs, place, member):
        width = blocks // subs
        share = width // 2
        part = place % QUAD
        self.inner = (part == 1) | (part == 2)
        self.far = part == 1
        dealt = member // 2 * share
        near = (dealt // width * 2 + member % 2) * width + dealt % width
        near = jnp.where(part == 1, blocks // 2, 0) + near
        self.first = jnp.where(self.inner, near, member * width)
        self.second = jnp.where(self.inner, near, member * width + share)
        self.edge = jnp.where(part == 1, blocks // 2 - 1, blocks // 2)
        self.width, self.share = width, share


def pack_kernel(blocks, subs, rows_ref, ids_ref, first_ref, behind_ref, ids, sems):
    plan = Plan(blocks, subs, lax.axis_index("tile"), lax.axis_index("sub"))
    share, size = plan.share, plan.share * BLOCK
    copies = []
    for index, down in enumerate(range(0, size, COPY)):
        start = pl.multiple_of(plan.first * BLOCK + down, COPY)
        copies.append(
            pltpu.make_async_copy(
                rows_ref.at[pl.ds(start, COPY), :], first_ref.at[pl.ds(down, COPY), :], sems.at[index]
            )
        )
    copies.append(pltpu.make_async_copy(ids_ref, ids, sems.at[len(copies)]))
    for copy in copies:
        copy.start()
    copies[-1].wait()
    depth = first_ref.shape[1]
    edge = jnp.max(ids[pl.ds(plan.edge, 1), :], axis=1, keepdims=True)
    rest = [jnp.broadcast_to(edge, (1, BLOCK)), jnp.zeros((1, depth - size - BLOCK), jnp.int32)]
    for block, out in ((plan.first, first_ref), (plan.second, behind_ref)):
        row = jnp.concatenate([ids[pl.ds(block + k, 1), :] for k in range(share)] + rest, axis=1)
        row = jnp.broadcast_to(row.astype(jnp.float32), (8, depth)).astype(jnp.bfloat16)
        out[out.shape[0] - 8 :, :] = row
    for copy in copies[:-1]:
        copy.wait()


def pack(size, subs, embeddings, by_block):
    depth = embeddings.shape[1]
    return pl.pallas_call(
        functools.partial(pack_kernel, by_block.shape[0], subs),
        in_specs=[pl.BlockSpec(memory_space=pl.ANY)] * 2,
        out_specs=[pl.BlockSpec(memory_space=pltpu.VMEM)] * 2,
        out_shape=[jax.ShapeDtypeStruct((count, depth), jnp.bfloat16) for count in (size + 8, 8)],
        scratch_shapes=[pltpu.VMEM(by_block.shape, jnp.int32), pltpu.SemaphoreType.DMA((size // COPY + 1,))],
        compiler_params=pltpu.CompilerParams(vmem_limit_bytes=8 * 1024 * 1024),
        cost_estimate=pl.CostEstimate(flops=0, bytes_accessed=1024, transcendentals=0),
    )(embeddings, by_block)


class Meta:
    def __init__(self, ref, blocks):
        self.ref, self.blocks = ref, blocks

    def tag(self, block, chunk=None):
        return self.ref[block + (0 if chunk is None else (2 + chunk) * self.blocks)]

    def used(self, block):
        return self.ref[self.blocks + block]

    def number(self, index):
        return self.ref[5 * self.blocks + index]


MEMBER, FIRST_BLOCK, EDGE, INNER, SECOND_BLOCK = range(5)


def self_kernel(
    blocks, subs, meta_ref, rows_ref, tags_ref, behind_ref, unit_ref, sums_ref, second_ref, held, sems
):
    meta = Meta(meta_ref, blocks)
    width = blocks // subs
    quarter = width * BLOCK
    member = meta.number(MEMBER)
    owners = [lax.rem(member + turn, subs) for turn in range(subs)]
    spans = [pl.ds(pl.multiple_of(owner * quarter, quarter), quarter) for owner in owners]
    copies = []
    for turn, span in enumerate(spans):
        copies.append(pltpu.make_async_copy(rows_ref.at[span, :], held.at[turn], sems.at[turn]))
        copies[-1].start()
    column_tags = tags_ref[...].astype(jnp.float32)
    for turn in range(subs):
        copies[turn].wait()
        unit = normalised(held[turn])
        unit_ref[spans[turn], :] = unit
        if turn == 0:
            share = unit
        cosine = products(unit, share)
        for inner in range(width):
            block = owners[turn] * width + inner
            bias = column_bias(meta.tag(block), column_tags)
            weight = jnp.exp2(cosine[inner * BLOCK : (inner + 1) * BLOCK] * GAIN + bias)
            row = lax.broadcasted_iota(jnp.int32, weight.shape, 0)
            keep = row < meta.used(block)
            if turn == 0:
                keep = keep & (lax.broadcasted_iota(jnp.int32, weight.shape, 1) - row != inner * BLOCK)
            sums_ref[pl.ds(block, 1), :] = lane_sums(jnp.where(keep, weight, 0.0))
    size = second_ref.shape[0] - 8
    start = pl.multiple_of(meta.number(SECOND_BLOCK) * BLOCK, BLOCK)
    second_ref[:size, :] = unit_ref[pl.ds(start, size), :]
    second_ref[size:, :] = behind_ref[...]


def chunk_tags(piece_ref, size):
    row = piece_ref[size:, :].astype(jnp.float32)[0:1, :]
    return row[:, :size], row[:, size : size + BLOCK]


def cross_terms(meta, chunk, column_tags, unit_ref, piece_ref, before_ref, sums, columns, place):
    size = column_tags.shape[1]
    there = [jnp.max(column_tags[:, at : at + BLOCK]) for at in range(0, size, BLOCK)]
    shared = False
    for block in range(meta.blocks):
        for tag in there:
            shared = (meta.tag(block, chunk).astype(jnp.float32) == tag) | shared

    @pl.when(jnp.logical_not(shared))
    def _():
        columns[...] = jnp.zeros_like(columns)
        for block in range(meta.blocks):
            sums[place(block) : place(block) + 1, :] = before_ref[block : block + 1, :]

    @pl.when(shared)
    def _():
        piece = piece_ref[:size, :] if chunk == 2 else normalised(piece_ref[:size, :])
        total = None
        for start in range(0, meta.blocks * BLOCK, STEP):
            cosine = products(unit_ref[start : start + STEP, :], piece)
            for inner in range(0, STEP, BLOCK):
                block = (start + inner) // BLOCK
                bias = column_bias(meta.tag(block, chunk), column_tags)
                weight = jnp.exp2(cosine[inner : inner + BLOCK] * GAIN + bias)
                row = lax.broadcasted_iota(jnp.int32, weight.shape, 0)
                weight = jnp.where(row < meta.used(block), weight, 0.0)
                sums[place(block) : place(block) + 1, :] = before_ref[block : block + 1, :] + lane_sums(weight)
                partial = weight[0:8]
                for down in range(8, BLOCK, 8):
                    partial = partial + weight[down : down + 8]
                total = partial if total is None else total + partial
        columns[...] = total


def middle_kernel(blocks, share, chunk, meta_ref, unit_ref, piece_ref, before_ref, sums_ref, cols_ref, columns):
    meta = Meta(meta_ref, blocks)
    tags, edge = chunk_tags(piece_ref, share * BLOCK)
    cross_terms(meta, chunk, tags, unit_ref, piece_ref, before_ref, sums_ref, columns, lambda block: block)
    total = jnp.sum(columns[...], axis=0, keepdims=True)
    for k in range(share):
        cols_ref[k : k + 1, :] = total[:, k * BLOCK : (k + 1) * BLOCK]
    mine = meta.tag(meta.number(EDGE)).astype(jnp.float32)
    joined = (edge == mine) & (edge >= 0) & (meta.number(INNER) > 0)
    cols_ref[share : share + 1, :] = jnp.where(joined, 1.0, 0.0)


def last_kernel(
    blocks, share, width, meta_ref, unit_ref, piece_ref, before_ref, outer_cols_ref, swap_cols_ref,
    keep_ref, send_ref, cols_ref, sums, columns,
):
    meta = Meta(meta_ref, blocks)
    tags, _ = chunk_tags(piece_ref, share * BLOCK)

    def place(block):
        owner = block // width
        return owner % 2 * (blocks // 2) + owner // 2 * width + block % width

    is_inner = meta.number(INNER) > 0
    cross_terms(meta, 2, tags, unit_ref, piece_ref, before_ref, sums, columns, place)
    total = jnp.sum(columns[...], axis=0, keepdims=True)
    for k in range(share):
        value = total[:, k * BLOCK : (k + 1) * BLOCK]
        cols_ref[k : k + 1, :] = jnp.where(is_inner, outer_cols_ref[k : k + 1, :], value)
        cols_ref[share + k : share + k + 1, :] = jnp.where(is_inner, value, 0.0)
    cols_ref[2 * share : 2 * share + 1, :] = swap_cols_ref[share : share + 1, :]
    parity = meta.number(MEMBER) % 2
    heap = blocks // 2
    keep_ref[...] = sums[pl.ds(pl.multiple_of(parity * heap, heap), heap), :]
    send_ref[...] = sums[pl.ds(pl.multiple_of((1 - parity) * heap, heap), heap), :]


def flag_kernel(share, here_ref, home_ref, flag_ref):
    flags = jnp.maximum(here_ref[share : share + 1, :], home_ref[2 * share : 2 * share + 1, :])
    flag_ref[0] = jnp.max(flags).astype(jnp.int32)


def call(kernel, meta, operands, out_shapes, scratch, flops):
    vmem, smem = pl.BlockSpec(memory_space=pltpu.VMEM), pl.BlockSpec(memory_space=pltpu.SMEM)
    return pl.pallas_call(
        kernel,
        in_specs=[smem] + [vmem] * len(operands),
        out_specs=[vmem if len(shape.shape) > 1 else smem for shape in out_shapes],
        out_shape=out_shapes,
        scratch_shapes=scratch,
        compiler_params=pltpu.CompilerParams(vmem_limit_bytes=16 * 1024 * 1024),
        cost_estimate=pl.CostEstimate(flops=flops, bytes_accessed=1024, transcendentals=0),
    )(meta, *operands)


def every_pair(embeddings, cluster_ids):
    unit = normalised(embeddings)
    tags = cluster_ids + 1
    groups = lax.axis_size("sub")
    member = lax.axis_index("sub")
    owners = lax.axis_size("tile")
    place = lax.axis_index("tile")
    rows_here = unit.shape[0]
    width = rows_here // groups
    own_piece = lax.dynamic_slice_in_dim(unit, member * width, width, 0)
    own_tags = lax.dynamic_slice_in_dim(tags, member * width, width, 0)
    distance = place - jnp.arange(owners, dtype=jnp.int32)
    keep = (jnp.abs(distance) < SPAN) & (distance != 0)
    outgoing = jnp.where(keep[:, None, None], own_piece[None, :, :], jnp.zeros((), jnp.bfloat16))
    outgoing_tags = jnp.where(keep[:, None], own_tags[None, :], 0)
    arrived = lax.all_to_all(outgoing, "tile", split_axis=0, concat_axis=0, tiled=True)
    arrived_tags = lax.all_to_all(outgoing_tags, "tile", split_axis=0, concat_axis=0, tiled=True)
    local_rows = jnp.arange(rows_here, dtype=jnp.int32)[:, None]
    slice_rows = member * width + jnp.arange(width, dtype=jnp.int32)[None, :]
    total = jnp.zeros((rows_here,), jnp.float32)
    for offset in range(1 - SPAN, SPAN):
        if offset == 0:
            piece, piece_tags, order = own_piece, own_tags, local_rows != slice_rows
        else:
            source = place + offset
            valid = (source >= 0) & (source < owners)
            index = jnp.clip(source, 0, owners - 1)
            piece = lax.dynamic_index_in_dim(arrived, index, 0, keepdims=False)
            piece_tags = lax.dynamic_index_in_dim(arrived_tags, index, 0, keepdims=False)
            piece_tags = jnp.where(valid, piece_tags, 0)
            order = True
        same = (tags[:, None] == piece_tags[None, :]) & (tags[:, None] > 0) & order
        weight = jnp.where(same, jnp.exp(inverse_temp * (products(unit, piece) - 1.0)), 0.0)
        total = total + jnp.sum(weight, axis=1)
    return jnp.log(1.0 + lax.psum_scatter(total, "sub", scatter_dimension=0, tiled=True))


def quads_joined(tag, tiles, place):
    last = jnp.broadcast_to(tag[-1], (BLOCK,))
    before = lax.ppermute(last, "tile", [(t, t + 1) for t in range(tiles - 1)])[0]
    joined = (place % QUAD == 0) & (place > 0) & (before == tag[0]) & (before >= 0)
    return lax.pmax(joined.astype(jnp.int32), "tile") > 0


def shards(embeddings, cluster_ids):
    tiles, subs = lax.axis_size("tile"), lax.axis_size("sub")
    place, member = lax.axis_index("tile"), lax.axis_index("sub")
    rows, depth = embeddings.shape
    blocks = rows // BLOCK
    plan = Plan(blocks, subs, place, member)
    width, share, inner = plan.width, plan.share, plan.inner
    size = share * BLOCK
    quads = range(0, tiles, QUAD)
    inward = [p for q in quads for p in ((q, q + 1), (q + 3, q + 2))]
    swap = [p for q in quads for p in ((q + 1, q + 2), (q + 2, q + 1))]
    around = [p for q in quads for p in ((q, q + 1), (q + 3, q + 2), (q + 1, q + 3), (q + 2, q))]

    def turned(route):
        return [(b, a) for a, b in route]

    by_block = cluster_ids.reshape(blocks, BLOCK)
    first_out, behind = pack(size, subs, embeddings, by_block)
    from_inner = lax.ppermute(first_out, "tile", swap)
    from_outer = lax.ppermute(first_out, "tile", inward)

    tag = jnp.max(by_block, axis=1)
    used = jnp.sum((by_block >= 0).astype(jnp.int32), axis=1)
    seen = jnp.where(inner, tag, -2)
    swapped = jnp.where(plan.far & (jnp.arange(blocks) >= blocks // 2), -2, seen)
    numbers = jnp.stack([member, plan.first, plan.edge, inner, plan.second])
    meta = jnp.concatenate([tag, used, seen, swapped, tag, numbers]).astype(jnp.int32)

    heap = blocks // 2
    owner = plan.first // width
    home_row = jnp.arange(heap)[:, None] - (owner // 2 * width + plan.first % width)
    home_row = jnp.broadcast_to(home_row, (heap, BLOCK)).astype(jnp.int32)
    upper = [
        jnp.broadcast_to((member >> bit) & 1, (heap >> bit, BLOCK)).astype(jnp.int32)
        for bit in range(1, subs.bit_length() - 1)
    ]
    meta, home_row, *upper = lax.optimization_barrier((meta, home_row, *upper))

    row_sums = jax.ShapeDtypeStruct((blocks, BLOCK), jnp.float32)
    col_sums = jax.ShapeDtypeStruct((share + 1, BLOCK), jnp.float32)
    quarter = width * BLOCK
    vmem, smem = pl.BlockSpec(memory_space=pltpu.VMEM), pl.BlockSpec(memory_space=pltpu.SMEM)
    unit, sums, second_out = pl.pallas_call(
        functools.partial(self_kernel, blocks, subs),
        in_specs=[smem, pl.BlockSpec(memory_space=pl.ANY), vmem, vmem],
        out_specs=[vmem] * 3,
        out_shape=[
            jax.ShapeDtypeStruct((rows, depth), jnp.bfloat16),
            row_sums,
            jax.ShapeDtypeStruct((size + 8, depth), jnp.bfloat16),
        ],
        scratch_shapes=[pltpu.VMEM((subs, quarter, depth), jnp.bfloat16), pltpu.SemaphoreType.DMA((subs,))],
        compiler_params=pltpu.CompilerParams(vmem_limit_bytes=24 * 1024 * 1024),
        cost_estimate=pl.CostEstimate(flops=0, bytes_accessed=1024, transcendentals=0),
    )(meta, embeddings, lax.dynamic_slice_in_dim(cluster_ids, member * quarter, quarter, 0)[None], behind)
    last = lax.ppermute(second_out, "tile", around)

    def middle(chunk, piece, before):
        return call(
            functools.partial(middle_kernel, blocks, share, chunk),
            meta,
            (unit, piece, before),
            [row_sums, col_sums],
            [pltpu.VMEM((8, size), jnp.float32)],
            2 * rows * size * depth,
        )

    sums, outer_cols = middle(0, from_outer, sums)
    sums, swap_cols = middle(1, from_inner, sums)
    swap_back = lax.ppermute(swap_cols, "tile", turned(swap))
    swap_back, sums = lax.optimization_barrier((swap_back, sums))
    half = jax.ShapeDtypeStruct((heap, BLOCK), jnp.float32)
    held, leaving, cols = call(
        functools.partial(last_kernel, blocks, share, width),
        meta,
        (unit, last, sums, outer_cols, swap_cols),
        [half, half, jax.ShapeDtypeStruct((2 * share + 1, BLOCK), jnp.float32)],
        [
            pltpu.VMEM((blocks, BLOCK), jnp.float32),
            pltpu.VMEM((8, size), jnp.float32),
        ],
        2 * rows * size * depth,
    )

    home = lax.ppermute(cols, "tile", turned(around))
    for k in range(2 * share):
        came = home[k : k + 1] + swap_back[k : k + 1] if k < share else home[k : k + 1]
        held = held + jnp.where(home_row == k, came, 0.0)
    held = held + lax.ppermute(leaving, "sub", [(i, i ^ 1) for i in range(subs)])
    home, held = lax.optimization_barrier((home, held))
    for bit, mine in enumerate(upper, 1):
        pairs = held.reshape(-1, 2, width, BLOCK)
        low, high = pairs[:, 0].reshape(mine.shape), pairs[:, 1].reshape(mine.shape)
        leaving = jnp.where(mine > 0, low, high)
        held = jnp.where(mine > 0, high, low)
        held = held + lax.ppermute(leaving, "sub", [(i, i ^ (1 << bit)) for i in range(subs)])
    scores = jnp.log(1.0 + held.reshape(-1))

    flag = pl.pallas_call(
        functools.partial(flag_kernel, share),
        out_specs=pl.BlockSpec(memory_space=pltpu.SMEM),
        out_shape=jax.ShapeDtypeStruct((1,), jnp.int32),
        compiler_params=pltpu.CompilerParams(vmem_limit_bytes=4 * 1024 * 1024),
    )(swap_cols, home)
    bad = flag[0] > 0
    if tiles > QUAD:
        bad = lax.pmax(bad.astype(jnp.int32), "tile") > 0
        bad = bad | quads_joined(tag, tiles, place)
    return lax.cond(bad, lambda: every_pair(embeddings, cluster_ids), lambda: scores)


def solution(mesh):
    in_specs = (P(("groups", "tile"), None), P(("groups", "tile")))
    out_specs = P(("groups", "tile", "sub"))
    return jax.shard_map(shards, mesh=mesh, in_specs=in_specs, out_specs=out_specs, check_vma=False)
```

```python
import functools
import math

import jax
import jax.numpy as jnp
import numpy as np
from jax import lax
from jax.experimental import pallas as pl
from jax.experimental.pallas import tpu as pltpu
from jax.sharding import PartitionSpec as P

BLOCK = 128
QUAD = 4
SPAN = 4

inverse_temp = 10.0
norm_eps = 1e-06
GAIN = inverse_temp * math.log2(math.e)
OFF = -1000.0

STEP = 256
COPY = 128


def normalised(values):
    values = values.astype(jnp.float32)
    scale = lax.rsqrt(jnp.sum(values * values, axis=1, keepdims=True) + norm_eps)
    return (values * scale).astype(jnp.bfloat16)


def products(rows, columns):
    return lax.dot_general(
        rows, columns, (((1,), (1,)), ((), ())), preferred_element_type=jnp.float32
    )


def column_bias(tag, column_tags):
    return jnp.where(column_tags == tag.astype(jnp.float32), -GAIN, OFF)


def lane_sums(weight):
    total = weight[:, :BLOCK]
    for start in range(BLOCK, weight.shape[1], BLOCK):
        total = total + weight[:, start : start + BLOCK]
    return jnp.sum(total.T, axis=0, keepdims=True)


class Plan:
    def __init__(self, blocks, subs, place, member):
        width = blocks // subs
        share = width // 2
        part = place % QUAD
        self.inner = (part == 1) | (part == 2)
        self.far = part == 1
        dealt = member // 2 * share
        near = (dealt // width * 2 + member % 2) * width + dealt % width
        near = jnp.where(part == 1, blocks // 2, 0) + near
        self.first = jnp.where(self.inner, near, member * width)
        self.second = jnp.where(self.inner, near, member * width + share)
        self.edge = jnp.where(part == 1, blocks // 2 - 1, blocks // 2)
        self.width, self.share = width, share


def pack_kernel(blocks, subs, rows_ref, ids_ref, first_ref, behind_ref, ids, sems):
    plan = Plan(blocks, subs, lax.axis_index("tile"), lax.axis_index("sub"))
    share, size = plan.share, plan.share * BLOCK
    copies = []
    for index, down in enumerate(range(0, size, COPY)):
        start = pl.multiple_of(plan.first * BLOCK + down, COPY)
        copies.append(
            pltpu.make_async_copy(
                rows_ref.at[pl.ds(start, COPY), :], first_ref.at[pl.ds(down, COPY), :], sems.at[index]
            )
        )
    copies.append(pltpu.make_async_copy(ids_ref, ids, sems.at[len(copies)]))
    for copy in copies:
        copy.start()
    copies[-1].wait()
    depth = first_ref.shape[1]
    edge = jnp.max(ids[pl.ds(plan.edge, 1), :], axis=1, keepdims=True)
    rest = [jnp.broadcast_to(edge, (1, BLOCK)), jnp.zeros((1, depth - size - BLOCK), jnp.int32)]
    for block, out in ((plan.first, first_ref), (plan.second, behind_ref)):
        row = jnp.concatenate([ids[pl.ds(block + k, 1), :] for k in range(share)] + rest, axis=1)
        row = jnp.broadcast_to(row.astype(jnp.float32), (8, depth)).astype(jnp.bfloat16)
        out[out.shape[0] - 8 :, :] = row
    for copy in copies[:-1]:
        copy.wait()


def pack(size, subs, embeddings, by_block):
    depth = embeddings.shape[1]
    return pl.pallas_call(
        functools.partial(pack_kernel, by_block.shape[0], subs),
        in_specs=[pl.BlockSpec(memory_space=pl.ANY)] * 2,
        out_specs=[pl.BlockSpec(memory_space=pltpu.VMEM)] * 2,
        out_shape=[jax.ShapeDtypeStruct((count, depth), jnp.bfloat16) for count in (size + 8, 8)],
        scratch_shapes=[pltpu.VMEM(by_block.shape, jnp.int32), pltpu.SemaphoreType.DMA((size // COPY + 1,))],
        compiler_params=pltpu.CompilerParams(vmem_limit_bytes=8 * 1024 * 1024),
        cost_estimate=pl.CostEstimate(flops=0, bytes_accessed=1024, transcendentals=0),
    )(embeddings, by_block)


class Meta:
    def __init__(self, ref, blocks):
        self.ref, self.blocks = ref, blocks

    def tag(self, block, chunk=None):
        return self.ref[block + (0 if chunk is None else (2 + chunk) * self.blocks)]

    def used(self, block):
        return self.ref[self.blocks + block]

    def number(self, index):
        return self.ref[5 * self.blocks + index]


MEMBER, FIRST_BLOCK, EDGE, INNER, SECOND_BLOCK = range(5)


def self_kernel(
    blocks, subs, meta_ref, rows_ref, tags_ref, behind_ref, unit_ref, sums_ref, second_ref, held, sems
):
    meta = Meta(meta_ref, blocks)
    width = blocks // subs
    quarter = width * BLOCK
    member = meta.number(MEMBER)
    owners = [lax.rem(member + turn, subs) for turn in range(subs)]
    spans = [pl.ds(pl.multiple_of(owner * quarter, quarter), quarter) for owner in owners]
    copies = []
    for turn, span in enumerate(spans):
        copies.append(pltpu.make_async_copy(rows_ref.at[span, :], held.at[turn], sems.at[turn]))
        copies[-1].start()
    column_tags = tags_ref[...].astype(jnp.float32)
    for turn in range(subs):
        copies[turn].wait()
        unit = normalised(held[turn])
        unit_ref[spans[turn], :] = unit
        if turn == 0:
            share = unit
        cosine = products(unit, share)
        for inner in range(width):
            block = owners[turn] * width + inner
            bias = column_bias(meta.tag(block), column_tags)
            weight = jnp.exp2(cosine[inner * BLOCK : (inner + 1) * BLOCK] * GAIN + bias)
            row = lax.broadcasted_iota(jnp.int32, weight.shape, 0)
            keep = row < meta.used(block)
            if turn == 0:
                keep = keep & (lax.broadcasted_iota(jnp.int32, weight.shape, 1) - row != inner * BLOCK)
            sums_ref[pl.ds(block, 1), :] = lane_sums(jnp.where(keep, weight, 0.0))
    size = second_ref.shape[0] - 8
    start = pl.multiple_of(meta.number(SECOND_BLOCK) * BLOCK, BLOCK)
    second_ref[:size, :] = unit_ref[pl.ds(start, size), :]
    second_ref[size:, :] = behind_ref[...]


def chunk_tags(piece_ref, size):
    row = piece_ref[size:, :].astype(jnp.float32)[0:1, :]
    return row[:, :size], row[:, size : size + BLOCK]


def cross_terms(meta, chunk, column_tags, unit_ref, piece_ref, before_ref, sums, columns, place):
    size = column_tags.shape[1]
    there = [jnp.max(column_tags[:, at : at + BLOCK]) for at in range(0, size, BLOCK)]
    shared = False
    for block in range(meta.blocks):
        for tag in there:
            shared = (meta.tag(block, chunk).astype(jnp.float32) == tag) | shared

    @pl.when(jnp.logical_not(shared))
    def _():
        columns[...] = jnp.zeros_like(columns)
        for block in range(meta.blocks):
            sums[place(block) : place(block) + 1, :] = before_ref[block : block + 1, :]

    @pl.when(shared)
    def _():
        piece = piece_ref[:size, :] if chunk == 2 else normalised(piece_ref[:size, :])
        total = None
        for start in range(0, meta.blocks * BLOCK, STEP):
            cosine = products(unit_ref[start : start + STEP, :], piece)
            for inner in range(0, STEP, BLOCK):
                block = (start + inner) // BLOCK
                bias = column_bias(meta.tag(block, chunk), column_tags)
                weight = jnp.exp2(cosine[inner : inner + BLOCK] * GAIN + bias)
                row = lax.broadcasted_iota(jnp.int32, weight.shape, 0)
                weight = jnp.where(row < meta.used(block), weight, 0.0)
                sums[place(block) : place(block) + 1, :] = before_ref[block : block + 1, :] + lane_sums(weight)
                partial = weight[0:8]
                for down in range(8, BLOCK, 8):
                    partial = partial + weight[down : down + 8]
                total = partial if total is None else total + partial
        columns[...] = total


def middle_kernel(blocks, share, chunk, meta_ref, unit_ref, piece_ref, before_ref, sums_ref, cols_ref, columns):
    meta = Meta(meta_ref, blocks)
    tags, edge = chunk_tags(piece_ref, share * BLOCK)
    cross_terms(meta, chunk, tags, unit_ref, piece_ref, before_ref, sums_ref, columns, lambda block: block)
    total = jnp.sum(columns[...], axis=0, keepdims=True)
    for k in range(share):
        cols_ref[k : k + 1, :] = total[:, k * BLOCK : (k + 1) * BLOCK]
    mine = meta.tag(meta.number(EDGE)).astype(jnp.float32)
    joined = (edge == mine) & (edge >= 0) & (meta.number(INNER) > 0)
    cols_ref[share : share + 1, :] = jnp.where(joined, 1.0, 0.0)


def last_kernel(
    blocks, share, width, meta_ref, unit_ref, piece_ref, before_ref, outer_back_ref, swap_cols_ref,
    keep_ref, send_ref, cols_ref, sums, columns,
):
    meta = Meta(meta_ref, blocks)
    tags, _ = chunk_tags(piece_ref, share * BLOCK)

    def place(block):
        owner = block // width
        return owner % 2 * (blocks // 2) + owner // 2 * width + block % width

    cross_terms(meta, 2, tags, unit_ref, piece_ref, before_ref, sums, columns, place)
    total = jnp.sum(columns[...], axis=0, keepdims=True)
    for k in range(share):
        cols_ref[k : k + 1, :] = total[:, k * BLOCK : (k + 1) * BLOCK]
        at = place(meta.number(FIRST_BLOCK) + k)
        sums[pl.ds(at, 1), :] += outer_back_ref[k : k + 1, :]
    cols_ref[share : share + 1, :] = swap_cols_ref[share : share + 1, :]
    parity = meta.number(MEMBER) % 2
    heap = blocks // 2
    keep_ref[...] = sums[pl.ds(pl.multiple_of(parity * heap, heap), heap), :]
    send_ref[...] = sums[pl.ds(pl.multiple_of((1 - parity) * heap, heap), heap), :]


def flag_kernel(share, here_ref, home_ref, flag_ref):
    flags = jnp.maximum(here_ref[share : share + 1, :], home_ref[share : share + 1, :])
    flag_ref[0] = jnp.max(flags).astype(jnp.int32)


def call(kernel, meta, operands, out_shapes, scratch, flops):
    vmem, smem = pl.BlockSpec(memory_space=pltpu.VMEM), pl.BlockSpec(memory_space=pltpu.SMEM)
    return pl.pallas_call(
        kernel,
        in_specs=[smem] + [vmem] * len(operands),
        out_specs=[vmem if len(shape.shape) > 1 else smem for shape in out_shapes],
        out_shape=out_shapes,
        scratch_shapes=scratch,
        compiler_params=pltpu.CompilerParams(vmem_limit_bytes=16 * 1024 * 1024),
        cost_estimate=pl.CostEstimate(flops=flops, bytes_accessed=1024, transcendentals=0),
    )(meta, *operands)


def every_pair(embeddings, cluster_ids):
    unit = normalised(embeddings)
    tags = cluster_ids + 1
    groups = lax.axis_size("sub")
    member = lax.axis_index("sub")
    owners = lax.axis_size("tile")
    place = lax.axis_index("tile")
    rows_here = unit.shape[0]
    width = rows_here // groups
    own_piece = lax.dynamic_slice_in_dim(unit, member * width, width, 0)
    own_tags = lax.dynamic_slice_in_dim(tags, member * width, width, 0)
    distance = place - jnp.arange(owners, dtype=jnp.int32)
    keep = (jnp.abs(distance) < SPAN) & (distance != 0)
    outgoing = jnp.where(keep[:, None, None], own_piece[None, :, :], jnp.zeros((), jnp.bfloat16))
    outgoing_tags = jnp.where(keep[:, None], own_tags[None, :], 0)
    arrived = lax.all_to_all(outgoing, "tile", split_axis=0, concat_axis=0, tiled=True)
    arrived_tags = lax.all_to_all(outgoing_tags, "tile", split_axis=0, concat_axis=0, tiled=True)
    local_rows = jnp.arange(rows_here, dtype=jnp.int32)[:, None]
    slice_rows = member * width + jnp.arange(width, dtype=jnp.int32)[None, :]
    total = jnp.zeros((rows_here,), jnp.float32)
    for offset in range(1 - SPAN, SPAN):
        if offset == 0:
            piece, piece_tags, order = own_piece, own_tags, local_rows != slice_rows
        else:
            source = place + offset
            valid = (source >= 0) & (source < owners)
            index = jnp.clip(source, 0, owners - 1)
            piece = lax.dynamic_index_in_dim(arrived, index, 0, keepdims=False)
            piece_tags = lax.dynamic_index_in_dim(arrived_tags, index, 0, keepdims=False)
            piece_tags = jnp.where(valid, piece_tags, 0)
            order = True
        same = (tags[:, None] == piece_tags[None, :]) & (tags[:, None] > 0) & order
        weight = jnp.where(same, jnp.exp(inverse_temp * (products(unit, piece) - 1.0)), 0.0)
        total = total + jnp.sum(weight, axis=1)
    return jnp.log(1.0 + lax.psum_scatter(total, "sub", scatter_dimension=0, tiled=True))


def quads_joined(tag, tiles, place):
    last = jnp.broadcast_to(tag[-1], (BLOCK,))
    before = lax.ppermute(last, "tile", [(t, t + 1) for t in range(tiles - 1)])[0]
    joined = (place % QUAD == 0) & (place > 0) & (before == tag[0]) & (before >= 0)
    return lax.pmax(joined.astype(jnp.int32), "tile") > 0


def shards(embeddings, cluster_ids):
    tiles, subs = lax.axis_size("tile"), lax.axis_size("sub")
    place, member = lax.axis_index("tile"), lax.axis_index("sub")
    rows, depth = embeddings.shape
    blocks = rows // BLOCK
    plan = Plan(blocks, subs, place, member)
    width, share, inner = plan.width, plan.share, plan.inner
    size = share * BLOCK
    quads = range(0, tiles, QUAD)
    inward = [p for q in quads for p in ((q, q + 1), (q + 3, q + 2))]
    swap = [p for q in quads for p in ((q + 1, q + 2), (q + 2, q + 1))]
    around = [p for q in quads for p in ((q, q + 1), (q + 3, q + 2), (q + 1, q + 3), (q + 2, q))]

    def turned(route):
        return [(b, a) for a, b in route]

    by_block = cluster_ids.reshape(blocks, BLOCK)
    first_out, behind = pack(size, subs, embeddings, by_block)
    from_inner = lax.ppermute(first_out, "tile", swap)
    from_outer = lax.ppermute(first_out, "tile", inward)

    tag = jnp.max(by_block, axis=1)
    used = jnp.sum((by_block >= 0).astype(jnp.int32), axis=1)
    seen = jnp.where(inner, tag, -2)
    swapped = jnp.where(plan.far & (jnp.arange(blocks) >= blocks // 2), -2, seen)
    numbers = jnp.stack([member, plan.first, plan.edge, inner, plan.second])
    meta = jnp.concatenate([tag, used, seen, swapped, tag, numbers]).astype(jnp.int32)

    heap = blocks // 2
    owner = plan.second // width
    home_row = jnp.arange(heap)[:, None] - (owner // 2 * width + plan.second % width)
    home_row = jnp.broadcast_to(home_row, (heap, BLOCK)).astype(jnp.int32)
    upper = [
        jnp.broadcast_to((member >> bit) & 1, (heap >> bit, BLOCK)).astype(jnp.int32)
        for bit in range(1, subs.bit_length() - 1)
    ]
    meta, home_row, *upper = lax.optimization_barrier((meta, home_row, *upper))

    row_sums = jax.ShapeDtypeStruct((blocks, BLOCK), jnp.float32)
    col_sums = jax.ShapeDtypeStruct((share + 1, BLOCK), jnp.float32)
    quarter = width * BLOCK
    vmem, smem = pl.BlockSpec(memory_space=pltpu.VMEM), pl.BlockSpec(memory_space=pltpu.SMEM)
    unit, sums, second_out = pl.pallas_call(
        functools.partial(self_kernel, blocks, subs),
        in_specs=[smem, pl.BlockSpec(memory_space=pl.ANY), vmem, vmem],
        out_specs=[vmem] * 3,
        out_shape=[
            jax.ShapeDtypeStruct((rows, depth), jnp.bfloat16),
            row_sums,
            jax.ShapeDtypeStruct((size + 8, depth), jnp.bfloat16),
        ],
        scratch_shapes=[pltpu.VMEM((subs, quarter, depth), jnp.bfloat16), pltpu.SemaphoreType.DMA((subs,))],
        compiler_params=pltpu.CompilerParams(vmem_limit_bytes=24 * 1024 * 1024),
        cost_estimate=pl.CostEstimate(flops=0, bytes_accessed=1024, transcendentals=0),
    )(meta, embeddings, lax.dynamic_slice_in_dim(cluster_ids, member * quarter, quarter, 0)[None], behind)
    last = lax.ppermute(second_out, "tile", around)

    def middle(chunk, piece, before):
        return call(
            functools.partial(middle_kernel, blocks, share, chunk),
            meta,
            (unit, piece, before),
            [row_sums, col_sums],
            [pltpu.VMEM((8, size), jnp.float32)],
            2 * rows * size * depth,
        )

    sums, outer_cols = middle(0, from_outer, sums)
    outer_back = lax.ppermute(outer_cols, "tile", turned(inward))
    sums, swap_cols = middle(1, from_inner, sums)
    swap_back = lax.ppermute(swap_cols, "tile", turned(swap))
    half = jax.ShapeDtypeStruct((heap, BLOCK), jnp.float32)
    held, leaving, cols = call(
        functools.partial(last_kernel, blocks, share, width),
        meta,
        (unit, last, sums, outer_back, swap_cols),
        [half, half, col_sums],
        [
            pltpu.VMEM((blocks, BLOCK), jnp.float32),
            pltpu.VMEM((8, size), jnp.float32),
        ],
        2 * rows * size * depth,
    )

    home = lax.ppermute(cols, "tile", turned(around))
    for k in range(share):
        held = held + jnp.where(home_row == k, home[k : k + 1] + swap_back[k : k + 1], 0.0)
    held = held + lax.ppermute(leaving, "sub", [(i, i ^ 1) for i in range(subs)])
    home, held = lax.optimization_barrier((home, held))
    for bit, mine in enumerate(upper, 1):
        pairs = held.reshape(-1, 2, width, BLOCK)
        low, high = pairs[:, 0].reshape(mine.shape), pairs[:, 1].reshape(mine.shape)
        leaving = jnp.where(mine > 0, low, high)
        held = jnp.where(mine > 0, high, low)
        held = held + lax.ppermute(leaving, "sub", [(i, i ^ (1 << bit)) for i in range(subs)])
    scores = jnp.log(1.0 + held.reshape(-1))

    flag = pl.pallas_call(
        functools.partial(flag_kernel, share),
        out_specs=pl.BlockSpec(memory_space=pltpu.SMEM),
        out_shape=jax.ShapeDtypeStruct((1,), jnp.int32),
        compiler_params=pltpu.CompilerParams(vmem_limit_bytes=4 * 1024 * 1024),
    )(swap_cols, home)
    bad = flag[0] > 0
    if tiles > QUAD:
        bad = lax.pmax(bad.astype(jnp.int32), "tile") > 0
        bad = bad | quads_joined(tag, tiles, place)
    return lax.cond(bad, lambda: every_pair(embeddings, cluster_ids), lambda: scores)


def solution(mesh):
    in_specs = (P(("groups", "tile"), None), P(("groups", "tile")))
    out_specs = P(("groups", "tile", "sub"))
    return jax.shard_map(shards, mesh=mesh, in_specs=in_specs, out_specs=out_specs, check_vma=False)
```
